32 devices in a mesh: dp: 8 (over z, x), fsdp: 4 (over y, core).
Axes of the slice: x: 2, y: 2, z: 4, core: 2. Of those that a mesh axis runs over, the one named last changes fastest.
Arguments:
- block_in: bfloat16 [32, 768, 1152], P(('dp', 'fsdp')), may hold values from -6 to 6
- condition: bfloat16 [32, 3, 1152], P(('dp', 'fsdp')), may hold values from -6 to 6
- lengths: int32 [32, 3], P(('dp', 'fsdp')), may hold values from 1 to 512, 768 in all within a row
- head_mask: int32 [32, 3, 16], P(('dp', 'fsdp')), may hold values 0 or 1
- group_mask: int32 [32, 3, 16], P(('dp', 'fsdp')), may hold values 0 or 1
- buffer_slot: int32 [32, 768], P(('dp', 'fsdp')), may hold values from -1 to 511, as said below
- ada_weight: bfloat16 [1152, 6912], P('dp', 'fsdp'), may hold values from -0.1875 to 0.1875
- ada_bias: bfloat16 [6912], P('fsdp'), may hold values from -1.796875 to 1.796875
- qkv_weight: bfloat16 [1152, 3456], P('dp', 'fsdp'), may hold values from -0.1875 to 0.1875
- query_bias: bfloat16 [1152], P('fsdp'), may hold values from -1.796875 to 1.796875
- value_bias: bfloat16 [1152], P('fsdp'), may hold values from -1.796875 to 1.796875
- out_weight: bfloat16 [1152, 1152], P('dp', 'fsdp'), may hold values from -0.5 to 0.5
- out_bias: bfloat16 [1152], P('fsdp'), may hold values from -1.796875 to 1.796875
- up_weight: bfloat16 [1152, 4608], P('dp', 'fsdp'), may hold values from -0.1875 to 0.1875
- up_bias: bfloat16 [4608], P('fsdp'), may hold values from -3 to 3
- down_weight: bfloat16 [4608, 1152], P('dp', 'fsdp'), may hold values from -0.125 to 0.125
- down_bias: bfloat16 [1152], P('fsdp'), may hold values from -1.796875 to 1.796875
- cotangent: bfloat16 [32, 768, 1152], P(('dp', 'fsdp')), may hold values from -6 to 6
Outputs:
- block_out: bfloat16 [32, 768, 1152], P(('dp', 'fsdp'))
- grad_block_in: float32 [32, 768, 1152], P(('dp', 'fsdp'))
- grad_ada_weight: float32 [1152, 6912], P('dp', 'fsdp')
- grad_ada_bias: float32 [6912], P('fsdp')
- grad_qkv_weight: float32 [1152, 3456], P('dp', 'fsdp')
- grad_query_bias: float32 [1152], P('fsdp')
- grad_value_bias: float32 [1152], P('fsdp')
- grad_out_weight: float32 [1152, 1152], P('dp', 'fsdp')
- grad_out_bias: float32 [1152], P('fsdp')
- grad_up_weight: float32 [1152, 4608], P('dp', 'fsdp')
- grad_up_bias: float32 [4608], P('fsdp')
- grad_down_weight: float32 [4608, 1152], P('dp', 'fsdp')
- grad_down_bias: float32 [1152], P('fsdp')
The draws below stay inside these ranges and needn't reach their ends.
Inputs may be any that keep to these rules, and one draw needn't show every extreme that they name: The 3 crop lengths of a row add up to 768. `buffer_slot`: -1 where the router skips the token; else the token's place in its row's feed-forward buffer of 512 places: place // 64 is the dp index whose device runs its feed-forward, place % 64 its position among the at most 64 tokens that the row sends there. Places of a row are distinct. In every draw one dp index, and the last one, receive 64 tokens from every row.
All inputs are finite; a program needn't handle non-finite values. No bound on the sum of `head_mask` or of `group_mask` on one device may be relied on, other than what follows from the above.
Results may differ from the reference program's by a relative error of at most 0.014.
The reference program's roundings to bfloat16 on the way count: a program that leaves them out, or rounds other values in their place, can miss the bound.
Values may be sent and summed in bfloat16 or wider, within the bound.
A program may use at most 320 MiB of HBM per device.

```python
import math
import jax
import jax.numpy as jnp
import numpy as np
from jax import lax

D = 1152
HEADS = 16
HEAD_DIM = 72
FF = 4608
GROUPS = 16
CROP = 512
TOK_DEV = 768
SLOTS = 3
ROWS = 32
CAP = 64
N_DP = 8


def draw_buffer_slot(key, part):
    key = jax.random.fold_in(key, 7)
    count_key, choose_key, order_key = jax.random.split(key, 3)
    owners = N_DP
    counts = jax.random.randint(count_key, (ROWS, owners), CAP // 2, CAP + 1)
    chosen = jax.random.randint(choose_key, (), 0, owners)
    column = jnp.arange(owners, dtype=jnp.int32)
    filled = (column == chosen) | (column == owners - 1)
    counts = jnp.where(filled[None, :], CAP, counts).astype(jnp.int32)
    finish = jnp.cumsum(counts, axis=1).astype(jnp.int32)
    opening = finish - counts
    position = jnp.arange(TOK_DEV, dtype=jnp.int32)
    target = jnp.sum((position[None, :, None] >= finish[:, None, :]).astype(jnp.int32), axis=2)
    bounded = jnp.minimum(target, owners - 1)
    first_of = jnp.take_along_axis(opening, bounded, axis=1)
    places = jnp.where(target < owners, bounded * CAP + position[None, :] - first_of, -1).astype(jnp.int32)
    orders = jax.vmap(lambda single: jax.random.permutation(single, TOK_DEV))(jax.random.split(order_key, ROWS))
    return jax.vmap(lambda order_row, place_row: jnp.zeros((TOK_DEV,), jnp.int32).at[order_row].set(place_row))(orders, places)


def set_ends(values, key, smallest, high):
    shape = values.shape
    spot = [jax.random.randint(jax.random.fold_in(key, axis), (), 0, shape[axis]) for axis in range(len(shape))]
    values = values.at[tuple(spot)].set(smallest)
    longest = shape.index(max(shape))
    spot[longest] = (spot[longest] + 1) % shape[longest]
    return values.at[tuple(spot)].set(high)


def steps_of(stream_key, shape, shards, low, top_value):
    level, own = 1.0, jax.random.fold_in(stream_key, 6)
    for axis_at, shards_of in shards:
        draws = jnp.exp(jax.random.uniform(jax.random.fold_in(own, axis_at), (shards_of,), jnp.float32, low / len(shards), top_value / len(shards)))
        level = level * jnp.repeat(draws, shape[axis_at] // shards_of).reshape([-1 if axis == axis_at else 1 for axis in range(len(shape))])
    return level


def length_profile(amount, total, most, skew):
    loads = [(1 << 20) // math.isqrt(rank ** skew) + 1 for rank in range(2, amount + 1)]
    surplus, holding = total - most - (amount - 1), [1] * (amount - 1)
    while surplus > 0:
        movable = [i for i in range(amount - 1) if holding[i] < most]
        whole, budget = sum([loads[i] for i in movable]), surplus
        for i in movable:
            more = min(most - holding[i], max(1, budget * loads[i] // whole), surplus)
            holding[i] = holding[i] + more
            surplus = surplus - more
    return np.array([most] + holding)


def ragged_sizes(key, count, total, most, skew):
    if count == 2:
        one = jax.random.randint(key, (), max(1, total - most), min(most, total - 1) + 1)
        return jnp.stack([one, total - one])
    tallies = jnp.asarray(length_profile(count, total, most, skew), jnp.int32)
    pairs = (count - 1) // 2
    giver, sink = tallies[1:1 + 2 * pairs:2], tallies[2:2 + 2 * pairs:2]
    room = jnp.minimum(giver - 1, most - sink)
    shifted = jax.random.randint(jax.random.fold_in(key, 1), (pairs,), 0, 1 << 20) % (room + 1)
    tallies = tallies.at[1:1 + 2 * pairs:2].set(giver - shifted).at[2:2 + 2 * pairs:2].set(sink + shifted)
    return tallies[jax.random.permutation(jax.random.fold_in(key, 2), count)]


def scatter_about(rng, extent, width, limit, cuts=(), kind=jnp.bfloat16):
    level = steps_of(rng, extent, cuts, -0.22, 0.18) if cuts else 1.0
    drawn = jax.random.normal(rng, extent, jnp.float32) * width * level
    return jnp.minimum(jnp.maximum(drawn, -limit), limit).astype(kind)


def setup_inputs(seed: int = 0) -> dict:
    arg_keys = jax.random.split(jax.random.key(seed), 19)
    block_in = scatter_about(arg_keys[0], (ROWS, TOK_DEV, D), 1.0, 6.0, ((0, 32),))
    condition = scatter_about(arg_keys[1], (ROWS, SLOTS, D), 1.0, 6.0, ((0, 32),))
    lengths = jax.vmap(lambda own: ragged_sizes(own, SLOTS, TOK_DEV, CROP, 0))(jax.random.split(arg_keys[2], ROWS)).reshape((ROWS, SLOTS)).astype(jnp.int32)
    head_mask = set_ends((jax.random.randint(arg_keys[3], (ROWS, SLOTS, HEADS), 0, 4) < 3).astype(jnp.int32), jax.random.fold_in(arg_keys[3], 1), 0, 1)
    group_mask = set_ends((jax.random.randint(arg_keys[4], (ROWS, SLOTS, GROUPS), 0, 4) < 3).astype(jnp.int32), jax.random.fold_in(arg_keys[4], 1), 0, 1)
    buffer_slot = draw_buffer_slot(jax.random.fold_in(arg_keys[18], 71), 0)
    ada_weight = scatter_about(arg_keys[6], (D, 6 * D), D ** -0.5, 0.1875, ((0, 8), (1, 4)))
    ada_bias = scatter_about(arg_keys[7], (6 * D,), 0.3, 1.796875, ((0, 4),))
    qkv_weight = scatter_about(arg_keys[8], (D, 3 * D), D ** -0.5, 0.1875, ((0, 8), (1, 4)))
    query_bias = scatter_about(arg_keys[9], (D,), 0.3, 1.796875, ((0, 4),))
    value_bias = scatter_about(arg_keys[10], (D,), 0.3, 1.796875, ((0, 4),))
    out_weight = scatter_about(arg_keys[11], (D, D), (D // 8) ** -0.5, 0.5, ((0, 8), (1, 4)))
    out_bias = scatter_about(arg_keys[12], (D,), 0.3, 1.796875, ((0, 4),))
    up_weight = scatter_about(arg_keys[13], (D, FF), D ** -0.5, 0.1875, ((0, 8), (1, 4)))
    up_bias = scatter_about(arg_keys[14], (FF,), 0.5, 3.0, ((0, 4),))
    down_weight = scatter_about(arg_keys[15], (FF, D), (FF // 2) ** -0.5, 0.125, ((0, 8), (1, 4)))
    down_bias = scatter_about(arg_keys[16], (D,), 0.3, 1.796875, ((0, 4),))
    cotangent = scatter_about(arg_keys[17], (ROWS, TOK_DEV, D), 1.0, 6.0, ((0, 32),))
    return dict(block_in=block_in, condition=condition, lengths=lengths, head_mask=head_mask, group_mask=group_mask, buffer_slot=buffer_slot, ada_weight=ada_weight, ada_bias=ada_bias, qkv_weight=qkv_weight, query_bias=query_bias, value_bias=value_bias, out_weight=out_weight, out_bias=out_bias, up_weight=up_weight, up_bias=up_bias, down_weight=down_weight, down_bias=down_bias, cotangent=cotangent)


@jax.custom_vjp
def low(v):
    return lax.optimization_barrier(v.astype(jnp.bfloat16)).astype(jnp.float32)

@jax.custom_vjp
def low_back(v):
    return v

def low_keep(v):
    return (low(v), None)

def low_pass(kept, grad):
    return (grad,)

def back_keep(v):
    return (v, None)

def back_low(kept, grad):
    return (low(grad),)
low.defvjp(low_keep, low_pass)
low_back.defvjp(back_keep, back_low)
highest = lax.Precision.HIGHEST
epsilon = 1e-06

def layer_norm(values):
    center = values - lax.optimization_barrier(jnp.mean(values, axis=-1, keepdims=True))
    variance = lax.optimization_barrier(jnp.mean(center * center, axis=-1, keepdims=True))
    return center * lax.rsqrt(variance + epsilon)

def row_forward(row_in, cond_row, length_row, head_row, group_row, keep_row, params):
    ada_weight, ada_bias, qkv_weight, query_bias, value_bias, out_weight, out_bias, up_weight, up_bias, down_weight, down_bias = params
    finish = jnp.cumsum(length_row).astype(jnp.int32)
    opening = finish - length_row
    position = jnp.arange(TOK_DEV, dtype=jnp.int32)
    member = ((position[:, None] >= opening[None, :]) & (position[:, None] < finish[None, :])).astype(jnp.float32)
    segment = lax.optimization_barrier(jnp.sum((position[:, None] >= finish[None, :]).astype(jnp.int32), axis=1))
    cond_act = low(jax.nn.silu(cond_row))
    modulation = jnp.dot(cond_act, ada_weight, precision=highest) + ada_bias
    pieces = [jnp.dot(member, modulation[:, number * D:(number + 1) * D], precision=highest) for number in range(6)]
    shift_one, scale_one, gate_one, shift_two, scale_two, gate_two = pieces
    head_keep = jnp.dot(member, head_row.astype(jnp.float32), precision=highest)
    group_keep = jnp.dot(member, group_row.astype(jnp.float32), precision=highest)
    first_in = low(layer_norm(row_in) * (1.0 + scale_one) + shift_one)
    qkv_bias = jnp.concatenate([query_bias, jnp.zeros_like(query_bias), value_bias])
    triple = low(low_back(jnp.dot(first_in, qkv_weight, precision=highest) + qkv_bias))
    queries = triple[:, :D].reshape(TOK_DEV, HEADS, HEAD_DIM)
    keys_all = triple[:, D:2 * D].reshape(TOK_DEV, HEADS, HEAD_DIM)
    values_all = triple[:, 2 * D:].reshape(TOK_DEV, HEADS, HEAD_DIM)
    allowed = segment[:, None] == segment[None, :]
    raw_scores = jnp.einsum('qhd,khd->hqk', queries, keys_all, precision=highest) * HEAD_DIM ** (-0.5)
    scores = low_back(jnp.where(allowed[None], raw_scores, -1e+30))
    row_max = lax.optimization_barrier(jnp.max(scores, axis=-1, keepdims=True))
    log_total = row_max + jnp.log(lax.optimization_barrier(jnp.sum(jnp.exp(scores - row_max), axis=-1, keepdims=True)))
    probs = low(jnp.exp(scores - log_total))
    attended = jnp.einsum('hqk,khd->qhd', probs, values_all, precision=highest)
    mixed = low(low_back(attended * head_keep[:, :, None])).reshape(TOK_DEV, D)
    attn_out = low_back(jnp.dot(mixed, out_weight, precision=highest) + out_bias)
    after_attn = row_in + gate_one * attn_out
    second_in = low(low_back(layer_norm(after_attn) * (1.0 + scale_two) + shift_two))
    hidden = low_back(jnp.dot(second_in, up_weight, precision=highest) + up_bias)
    channel_keep = jnp.repeat(group_keep, FF // GROUPS, axis=1)
    active = low(jax.nn.gelu(hidden, approximate=True) * channel_keep)
    branch = low(low_back(jnp.dot(active, down_weight, precision=highest) + down_bias))
    return after_attn + gate_two * keep_row[:, None] * branch

def reference(block_in, condition, lengths, head_mask, group_mask, buffer_slot, ada_weight, ada_bias, qkv_weight, query_bias, value_bias, out_weight, out_bias, up_weight, up_bias, down_weight, down_bias, cotangent):
    params = tuple((array.astype(jnp.float32) for array in (ada_weight, ada_bias, qkv_weight, query_bias, value_bias, out_weight, out_bias, up_weight, up_bias, down_weight, down_bias)))
    conditions = condition.astype(jnp.float32)
    kept = (buffer_slot >= 0).astype(jnp.float32)

    def forward(inputs, weights):

        def one_row(carry, packed):
            row_in, cond_row, length_row, head_row, group_row, keep_row = packed
            return (carry, row_forward(row_in, cond_row, length_row, head_row, group_row, keep_row, weights))
        _, outputs = lax.scan(jax.checkpoint(one_row), jnp.zeros((), jnp.float32), (inputs, conditions, lengths, head_mask, group_mask, kept))
        return outputs
    outputs, pullback = jax.vjp(forward, block_in.astype(jnp.float32), params)
    grad_inputs, grads = pullback(cotangent.astype(jnp.float32))
    return (outputs.astype(jnp.bfloat16), grad_inputs, grads[0], grads[1], grads[2], grads[3], grads[4], grads[5], grads[6], grads[7], grads[8], grads[9], grads[10])
```

```python
import jax
import jax.numpy as jnp
from jax import lax
from jax.sharding import PartitionSpec as P

D = 1152
HEADS = 16
HEAD_DIM = 72
FF = 4608
GROUPS = 16
TOK_DEV = 768


highest = lax.Precision.HIGHEST
epsilon = 1e-06


def layer_norm(values):
    center = values - jnp.mean(values, axis=-1, keepdims=True)
    variance = jnp.mean(center * center, axis=-1, keepdims=True)
    inverse = lax.rsqrt(variance + epsilon)
    return (center * inverse, inverse)


def norm_back(grad_normed, normed, inverse):
    first_mean = jnp.mean(grad_normed, axis=-1, keepdims=True)
    second_mean = jnp.mean(grad_normed * normed, axis=-1, keepdims=True)
    return inverse * (grad_normed - first_mean - normed * second_mean)


def attention_scores(query_part, key_part, allowed, factor):
    raw_scores = (
        jnp.einsum("qhd,khd->hqk", query_part, key_part, preferred_element_type=jnp.float32)
        * factor
    )
    return jnp.where(allowed[None], raw_scores, -1e30)


def gelu_tanh(values):
    return jax.nn.gelu(values, approximate=True)


def shards(
    block_in,
    condition,
    lengths,
    head_mask,
    group_mask,
    buffer_slot,
    ada_weight,
    ada_bias,
    qkv_weight,
    query_bias,
    value_bias,
    out_weight,
    out_bias,
    up_weight,
    up_bias,
    down_weight,
    down_bias,
    cotangent,
):
    peers = lax.axis_size("dp")
    mates = lax.axis_size("fsdp")

    def gather_matrix(shard):
        stacked = lax.all_gather(shard, ("dp", "fsdp"), axis=0, tiled=False)
        rows, columns = shard.shape
        stacked = stacked.reshape(peers, mates, rows, columns).transpose(0, 2, 1, 3)
        return stacked.reshape(peers * rows, mates * columns)

    full_qkv, full_out, full_up, full_down = [
        gather_matrix(shard) for shard in (qkv_weight, out_weight, up_weight, down_weight)
    ]
    vectors = (query_bias, value_bias, out_bias, up_bias, down_bias)
    packed_bias = lax.all_gather(jnp.concatenate(vectors), "fsdp", axis=0, tiled=False)
    edges = [0]
    for vector in vectors:
        edges.append(edges[-1] + vector.shape[0])
    bias_query, bias_value, bias_out, bias_up, bias_down = [
        packed_bias[:, low:high].reshape(-1).astype(jnp.float32)
        for low, high in zip(edges[:-1], edges[1:])
    ]
    inputs = block_in[0].astype(jnp.float32)
    crop_length = lengths[0]
    finish = jnp.cumsum(crop_length)
    opening = finish - crop_length
    position = jnp.arange(TOK_DEV, dtype=jnp.int32)
    member = (
        (position[:, None] >= opening[None, :]) & (position[:, None] < finish[None, :])
    ).astype(jnp.float32)
    segment = jnp.sum((position[:, None] >= finish[None, :]).astype(jnp.int32), axis=1)
    cond_act = jax.nn.silu(condition[0].astype(jnp.float32)).astype(jnp.bfloat16)
    crops = cond_act.shape[0]
    cond_all = lax.all_gather(cond_act, ("dp", "fsdp"), axis=0, tiled=True)
    depth = ada_weight.shape[0]
    cond_slice = lax.dynamic_slice_in_dim(cond_all, lax.axis_index("dp") * depth, depth, axis=1)
    partial_mod = jnp.dot(cond_slice, ada_weight, preferred_element_type=jnp.float32)
    column_mod = lax.psum_scatter(partial_mod, "dp", scatter_dimension=0, tiled=True)
    column_mod = column_mod + ada_bias.astype(jnp.float32)
    modulation = lax.all_to_all(column_mod, "fsdp", split_axis=0, concat_axis=1, tiled=True)
    pieces = [
        jnp.dot(member, modulation[:, number * D : (number + 1) * D], precision=highest)
        for number in range(6)
    ]
    shift_one, scale_one, gate_one, shift_two, scale_two, gate_two = pieces
    head_keep = jnp.dot(member, head_mask[0].astype(jnp.float32), precision=highest)
    group_keep = jnp.dot(member, group_mask[0].astype(jnp.float32), precision=highest)
    normed_one, inverse_one = layer_norm(inputs)
    first_in = (normed_one * (1.0 + scale_one) + shift_one).astype(jnp.bfloat16)
    qkv_bias = jnp.concatenate([bias_query, jnp.zeros_like(bias_query), bias_value])
    triple = (jnp.dot(first_in, full_qkv, preferred_element_type=jnp.float32) + qkv_bias).astype(
        jnp.bfloat16
    )
    queries = triple[:, :D].reshape(TOK_DEV, HEADS, HEAD_DIM)
    keys_all = triple[:, D : 2 * D].reshape(TOK_DEV, HEADS, HEAD_DIM)
    values_all = triple[:, 2 * D :].reshape(TOK_DEV, HEADS, HEAD_DIM)
    factor = HEAD_DIM ** (-0.5)
    row_block = min(768, TOK_DEV)
    group_size = min(4, HEADS)
    log_totals = {}
    head_parts = []
    for head_start in range(0, HEADS, group_size):
        heads_here = slice(head_start, head_start + group_size)
        row_start = 0
        rows_here = slice(row_start, row_start + row_block)
        allowed = segment[:, None] == segment[None, :]
        scores = attention_scores(
            queries[rows_here, heads_here], keys_all[:, heads_here], allowed, factor
        )
        row_max = jnp.max(scores, axis=-1, keepdims=True)
        log_total = row_max + jnp.log(jnp.sum(jnp.exp(scores - row_max), axis=-1, keepdims=True))
        weights_low = jnp.exp(scores - log_total).astype(jnp.bfloat16)
        row_parts = jnp.einsum(
            "hqk,khd->qhd",
            weights_low,
            values_all[:, heads_here],
            preferred_element_type=jnp.float32,
        )
        log_totals[head_start, row_start] = log_total
        head_parts.append(row_parts)
    attended = jnp.concatenate(head_parts, axis=1)
    mixed = (attended * head_keep[:, :, None]).astype(jnp.bfloat16).reshape(TOK_DEV, D)
    attn_out = jnp.dot(mixed, full_out, preferred_element_type=jnp.float32) + bias_out
    after_attn = inputs + gate_one * attn_out
    normed_two, inverse_two = layer_norm(after_attn)
    second_in = (normed_two * (1.0 + scale_two) + shift_two).astype(jnp.bfloat16)
    keep = (buffer_slot[0] >= 0).astype(jnp.float32)[:, None]
    places = 2 * TOK_DEV // 3
    chooser = (buffer_slot[0][:, None] == jnp.arange(places, dtype=jnp.int32)[None, :]).astype(
        jnp.bfloat16
    )
    arrived = jnp.einsum(
        "tb,td->bd", chooser, second_in, preferred_element_type=jnp.float32
    ).astype(jnp.bfloat16)
    groups_float = jnp.einsum(
        "tb,tg->bg",
        chooser,
        group_keep.astype(jnp.bfloat16),
        preferred_element_type=jnp.float32,
    )
    channel_keep = jnp.repeat(groups_float, FF // GROUPS, axis=1)
    hidden = jnp.dot(arrived, full_up, preferred_element_type=jnp.float32) + bias_up
    active = (gelu_tanh(hidden) * channel_keep).astype(jnp.bfloat16)
    branch = (jnp.dot(active, full_down, preferred_element_type=jnp.float32) + bias_down).astype(
        jnp.bfloat16
    )
    branch_tok = jnp.einsum(
        "tb,bd->td", chooser, branch, preferred_element_type=jnp.float32
    )
    after_mlp = after_attn + gate_two * branch_tok
    block_out = after_mlp.astype(jnp.bfloat16)[None]
    grad_after = cotangent[0].astype(jnp.float32)
    grad_gate_two = grad_after * branch_tok
    grad_branch = (gate_two * keep * grad_after).astype(jnp.bfloat16)
    grad_rows = jnp.einsum(
        "tb,td->bd", chooser, grad_branch, preferred_element_type=jnp.float32
    ).astype(jnp.bfloat16)
    back_qkv, back_out, back_up, back_down = full_qkv, full_out, full_up, full_down
    grad_down_bias = jnp.sum(grad_rows.astype(jnp.float32), axis=0)
    grad_down = jnp.einsum("bf,bd->fd", active, grad_rows, preferred_element_type=jnp.float32)
    grad_active = jnp.einsum("bd,fd->bf", grad_rows, back_down, preferred_element_type=jnp.float32)
    gelu_pull = jax.vjp(gelu_tanh, hidden)[1]
    grad_hidden = gelu_pull(grad_active * channel_keep)[0].astype(jnp.bfloat16)
    grad_up_bias = jnp.sum(grad_hidden.astype(jnp.float32), axis=0)
    grad_up = jnp.einsum("bd,bf->df", arrived, grad_hidden, preferred_element_type=jnp.float32)
    grad_arrived = jnp.einsum(
        "bf,df->bd", grad_hidden, back_up, preferred_element_type=jnp.float32
    ).astype(jnp.bfloat16)
    grad_second = jnp.einsum(
        "tb,bd->td", chooser, grad_arrived, preferred_element_type=jnp.float32
    )
    grad_scale_two = grad_second * normed_two
    grad_mid = grad_after + norm_back(grad_second * (1.0 + scale_two), normed_two, inverse_two)
    grad_gate_one = grad_mid * attn_out
    grad_attn = (gate_one * grad_mid).astype(jnp.bfloat16)
    grad_out_bias = jnp.sum(grad_attn.astype(jnp.float32), axis=0)
    grad_out = jnp.einsum("te,tf->ef", mixed, grad_attn, preferred_element_type=jnp.float32)
    grad_mixed = jnp.einsum(
        "tf,ef->te", grad_attn, back_out, preferred_element_type=jnp.float32
    ).astype(jnp.bfloat16)
    grad_attended = (
        grad_mixed.reshape(TOK_DEV, HEADS, HEAD_DIM).astype(jnp.float32) * head_keep[:, :, None]
    ).astype(jnp.bfloat16)
    query_heads = []
    key_heads = []
    value_heads = []
    for head_start in range(0, HEADS, group_size):
        heads_here = slice(head_start, head_start + group_size)
        row_start = 0
        rows_here = slice(row_start, row_start + row_block)
        allowed = segment[:, None] == segment[None, :]
        scores = attention_scores(
            queries[rows_here, heads_here], keys_all[:, heads_here], allowed, factor
        )
        probs = jnp.exp(scores - log_totals[head_start, row_start])
        grad_piece = grad_attended[rows_here, heads_here]
        grad_values = jnp.einsum(
            "hqk,qhd->khd",
            probs.astype(jnp.bfloat16),
            grad_piece,
            preferred_element_type=jnp.float32,
        )
        grad_probs = jnp.einsum(
            "qhd,khd->hqk",
            grad_piece,
            values_all[:, heads_here],
            preferred_element_type=jnp.float32,
        )
        grad_scores = (
            probs * (grad_probs - jnp.sum(probs * grad_probs, axis=-1, keepdims=True))
        ).astype(jnp.bfloat16)
        query_rows = (
            jnp.einsum(
                "hqk,khd->qhd",
                grad_scores,
                keys_all[:, heads_here],
                preferred_element_type=jnp.float32,
            )
            * factor
        )
        grad_keys = (
            jnp.einsum(
                "hqk,qhd->khd",
                grad_scores,
                queries[rows_here, heads_here],
                preferred_element_type=jnp.float32,
            )
            * factor
        )
        query_heads.append(query_rows)
        key_heads.append(grad_keys)
        value_heads.append(grad_values)
    grad_triple = jnp.concatenate(
        [
            jnp.concatenate(query_heads, axis=1).reshape(TOK_DEV, D),
            jnp.concatenate(key_heads, axis=1).reshape(TOK_DEV, D),
            jnp.concatenate(value_heads, axis=1).reshape(TOK_DEV, D),
        ],
        axis=1,
    ).astype(jnp.bfloat16)
    grad_query_bias = jnp.sum(grad_triple[:, :D].astype(jnp.float32), axis=0)
    grad_value_bias = jnp.sum(grad_triple[:, 2 * D :].astype(jnp.float32), axis=0)
    grad_qkv = jnp.einsum("td,te->de", first_in, grad_triple, preferred_element_type=jnp.float32)
    grad_first = jnp.einsum("te,de->td", grad_triple, back_qkv, preferred_element_type=jnp.float32)
    grad_scale_one = grad_first * normed_one
    grad_inputs = grad_mid + norm_back(grad_first * (1.0 + scale_one), normed_one, inverse_one)
    token_grads = [
        grad_first,
        grad_scale_one,
        grad_gate_one,
        grad_second,
        grad_scale_two,
        grad_gate_two,
    ]
    grad_modulation = jnp.concatenate(
        [jnp.einsum("ts,td->sd", member, single, precision=highest) for single in token_grads],
        axis=1,
    )
    mod_columns = lax.all_to_all(
        grad_modulation, "fsdp", split_axis=1, concat_axis=0, tiled=True
    )
    mod_all = lax.all_gather(mod_columns, "dp", axis=0, tiled=True)
    grad_ada_bias = jnp.sum(mod_all, axis=0)
    grad_ada = jnp.einsum(
        "sd,se->de", cond_slice.astype(jnp.float32), mod_all, precision=highest
    )

    def scatter_matrix(full):
        rows, columns = full.shape[0] // peers, full.shape[1] // mates
        blocks = full.astype(jnp.bfloat16).reshape(peers, rows, mates, columns)
        blocks = blocks.transpose(0, 2, 1, 3).reshape(peers * mates * rows, columns)
        share = lax.psum_scatter(blocks, ("dp", "fsdp"), scatter_dimension=0, tiled=True)
        return share.astype(jnp.float32)

    shares = [scatter_matrix(full) for full in (grad_qkv, grad_out, grad_up, grad_down)]
    bias_grads = (grad_query_bias, grad_value_bias, grad_out_bias, grad_up_bias, grad_down_bias)
    packed = jnp.concatenate([vector.reshape(mates, -1) for vector in bias_grads], axis=1)
    packed = lax.psum_scatter(packed, "fsdp", scatter_dimension=0, tiled=True)
    packed = lax.psum(packed[0], "dp")
    totals = [packed[low:high] for low, high in zip(edges[:-1], edges[1:])]
    return (
        block_out,
        grad_inputs[None],
        grad_ada,
        grad_ada_bias,
        shares[0],
        totals[0],
        totals[1],
        shares[1],
        totals[2],
        shares[2],
        totals[3],
        shares[3],
        totals[4],
    )


def solution(mesh):
    placed = (
        P(("dp", "fsdp"), None, None),
        P(("dp", "fsdp"), None, None),
        P(("dp", "fsdp"), None),
        P(("dp", "fsdp"), None, None),
        P(("dp", "fsdp"), None, None),
        P(("dp", "fsdp"), None),
        P("dp", "fsdp"),
        P("fsdp"),
        P("dp", "fsdp"),
        P("fsdp"),
        P("fsdp"),
        P("dp", "fsdp"),
        P("fsdp"),
        P("dp", "fsdp"),
        P("fsdp"),
        P("dp", "fsdp"),
        P("fsdp"),
        P(("dp", "fsdp"), None, None),
    )
    return jax.shard_map(
        shards,
        mesh=mesh,
        in_specs=placed,
        out_specs=(
            P(("dp", "fsdp"), None, None),
            P(("dp", "fsdp"), None, None),
            P("dp", "fsdp"),
            P("fsdp"),
            P("dp", "fsdp"),
            P("fsdp"),
            P("fsdp"),
            P("dp", "fsdp"),
            P("fsdp"),
            P("dp", "fsdp"),
            P("fsdp"),
            P("dp", "fsdp"),
            P("fsdp"),
        ),
        check_vma=False,
    )
```

```python
import functools

import jax
import jax.numpy as jnp
from jax import lax
from jax.experimental import pallas as pl
from jax.experimental.pallas import tpu as pltpu
from jax.sharding import PartitionSpec as P

D = 1152
HEADS = 16
HEAD_DIM = 72
FF = 4608
GROUPS = 16
TOK_DEV = 768


highest = lax.Precision.HIGHEST
epsilon = 1e-06


MESH = pl.DeviceIdType.MESH
SHARD = 144
UPPER = 80


class Place:
    def __init__(self):
        dp, fsdp = lax.axis_index("dp"), lax.axis_index("fsdp")
        self.z, self.x = lax.div(dp, 2), lax.rem(dp, 2)
        self.y, self.c = lax.div(fsdp, 2), lax.rem(fsdp, 2)
        z = self.z
        self.zs = (z, z + 1 - 2 * lax.rem(z, 2), lax.rem(z + 2, 4), 3 - z)

    def device(self, z=None, x=None, y=None, c=None):
        z, x = self.z if z is None else z, self.x if x is None else x
        y, c = self.y if y is None else y, self.c if c is None else c
        return (2 * z + x, 2 * y + c)

    def meet(self):
        barrier = pltpu.get_barrier_semaphore()
        others = [self.device(z=self.zs[k]) for k in (1, 2, 3)]
        others += [self.device(x=1 - self.x), self.device(y=1 - self.y), self.device(c=1 - self.c)]
        for other in others:
            pl.semaphore_signal(barrier, inc=1, device_id=other, device_id_type=MESH)
        pl.semaphore_wait(barrier, len(others))


class Copies:
    def __init__(self, send_sems, recv_sems):
        self.send_sems, self.recv_sems, self.made = send_sems, recv_sems, []

    def make(self, source, target, device):
        index = len(self.made)
        copy = pltpu.make_async_remote_copy(
            src_ref=source,
            dst_ref=target,
            send_sem=self.send_sems.at[index],
            recv_sem=self.recv_sems.at[index],
            device_id=device,
            device_id_type=MESH,
        )
        self.made.append(copy)
        return copy


GATHER_COPIES = 35


class Gather:
    def __init__(self, place, source, slot, send_sems, recv_sems, local_sem, swap):
        x, y, c, zs = place.x, place.y, place.c, place.zs
        self.copies = Copies(send_sems, recv_sems)
        make = self.copies.make
        first, second = (SHARD - UPPER, UPPER) if swap else (0, UPPER)
        upper = pl.ds(first, second)
        lower = pl.ds(0, SHARD - UPPER) if swap else pl.ds(UPPER, SHARD - UPPER)
        over_x, over_y, beside = (
            place.device(x=1 - x),
            place.device(y=1 - y),
            place.device(c=1 - c),
        )
        own = [slot(y, c, zs[k], x) for k in range(4)]
        held = [source] + own[1:]
        from_x = [slot(y, c, zs[k], 1 - x) for k in range(4)]
        from_y = [slot(1 - y, c, zs[k], x) for k in range(4)]
        across = [slot(1 - y, c, zs[k], 1 - x) for k in range(4)]
        self.local = pltpu.make_async_copy(source, own[0], local_sem)
        self.along = [None] + [make(source, own[0], place.device(z=zs[k])) for k in (1, 2, 3)]
        self.to_x = [make(held[k], own[k], over_x) for k in range(4)]
        self.to_y = [make(held[k], own[k], over_y) for k in range(4)]
        self.x_to_y = [make(s.at[upper], s.at[upper], over_y) for s in from_x]
        self.y_to_x = [make(s.at[lower], s.at[lower], over_x) for s in from_y]
        self.pair = [make(held[k], own[k], beside) for k in range(4)]
        self.pair_x = [make(s, s, beside) for s in from_x]
        self.pair_y = [make(s, s, beside) for s in from_y]
        self.pair_across = [make(s, s, beside) for s in across]

    def start(self):
        self.along[1].start()
        self.to_x[0].start()
        self.to_y[0].start()
        self.along[2].start()
        self.along[3].start()
        self.pair[0].start()
        self.local.start()

    def pass_along(self, k):
        self.along[k].wait_recv()
        self.to_x[k].start()
        self.to_y[k].start()
        self.pair[k].start()

    def pass_across(self, k):
        self.to_x[k].wait_recv()
        self.x_to_y[k].start()
        self.pair_x[k].start()
        self.to_y[k].wait_recv()
        self.y_to_x[k].start()
        self.pair_y[k].start()

    def pass_pair(self, k):
        self.x_to_y[k].wait_recv()
        self.y_to_x[k].wait_recv()
        self.pair_across[k].start()

    def finish(self):
        self.local.wait()
        for copy in self.pair + self.pair_x + self.pair_y + self.pair_across:
            copy.wait_recv()
        for copy in self.copies.made:
            copy.wait_send()


def gather_kernel(*refs):
    sources, targets = refs[:3], refs[3:6]
    send_sems, recv_sems, local_sems = refs[6:]
    place = Place()
    place.meet()

    def slot_of(r):
        if r == 2:
            return lambda y, c, z, x: targets[r].at[z, x, y, c]
        return lambda y, c, z, x: targets[r].at[y, c, z, x]

    rounds = [
        Gather(
            place,
            sources[r],
            slot_of(r),
            send_sems.at[r],
            recv_sems.at[r],
            local_sems.at[r],
            r % 2 == 1,
        )
        for r in range(3)
    ]
    rounds[0].start()
    for k in (1, 2, 3):
        rounds[0].pass_along(k)
    for r in range(3):
        if r < 2:
            rounds[r + 1].start()
        for k in range(4):
            rounds[r].pass_across(k)
        if r < 2:
            for k in (1, 2, 3):
                rounds[r + 1].pass_along(k)
        for k in range(4):
            rounds[r].pass_pair(k)
    for each in rounds:
        each.finish()


def gather_block(qkv_weight, out_weight, up_weight, down_weight):
    down_rows = lax.all_to_all(down_weight, "fsdp", split_axis=0, concat_axis=1, tiled=True)
    sources = (jnp.concatenate([qkv_weight, out_weight], axis=1), up_weight, down_rows)
    shapes = ((2, 2, 4, 2), (2, 2, 4, 2), (4, 2, 2, 2))
    anywhere = pl.BlockSpec(memory_space=pl.ANY)
    mixed, ups, downs = pl.pallas_call(
        gather_kernel,
        out_shape=[
            jax.ShapeDtypeStruct(shape + (SHARD, D), jnp.bfloat16) for shape in shapes
        ],
        in_specs=[anywhere] * 3,
        out_specs=[anywhere] * 3,
        scratch_shapes=[
            pltpu.SemaphoreType.DMA((3, GATHER_COPIES)),
            pltpu.SemaphoreType.DMA((3, GATHER_COPIES)),
            pltpu.SemaphoreType.DMA((3,)),
        ],
        compiler_params=pltpu.CompilerParams(collective_id=1, has_side_effects=True),
    )(*sources)
    mixed, ups = mixed.reshape(4, D, D), ups.reshape(4, D, D)
    own = qkv_weight.shape[1]
    return (
        mixed[:, :, :own].transpose(1, 0, 2).reshape(D, 3 * D),
        mixed[:, :, own:].transpose(1, 0, 2).reshape(D, D),
        ups.transpose(1, 0, 2).reshape(D, FF),
        downs.reshape(FF, D),
    )


def gather_any(*shards):
    peers, mates = lax.axis_size("dp"), lax.axis_size("fsdp")
    results = []
    for shard in shards:
        stacked = lax.all_gather(shard, ("dp", "fsdp"), axis=0, tiled=False)
        rows, columns = shard.shape
        stacked = stacked.reshape(peers, mates, rows, columns).transpose(0, 2, 1, 3)
        results.append(stacked.reshape(peers * rows, mates * columns))
    return results


SCATTER_COPIES = 27


class Scatter:
    def __init__(self, place, parts, bufs, out, send_sems, recv_sems, swap):
        x, y, zs = place.x, place.y, place.zs
        self.place, self.parts, self.out = place, parts, out
        self.by_x, self.by_y, self.from_x, self.from_y, self.from_z = bufs
        self.copies = Copies(send_sems, recv_sems)
        make = self.copies.make
        self.upper = (SHARD - UPPER, UPPER) if swap else (0, UPPER)
        self.lower = (0, SHARD - UPPER) if swap else (UPPER, SHARD - UPPER)
        a, b = pl.ds(*self.upper), pl.ds(*self.lower)
        over_x, over_y = place.device(x=1 - x), place.device(y=1 - y)
        four = range(4)
        self.across_y = [
            make(parts.at[1 - y, zs[k], 1 - x, a], self.by_y.at[k, a], over_y) for k in four
        ]
        self.across_x = [
            make(parts.at[1 - y, zs[k], 1 - x, b], self.by_x.at[k, b], over_x) for k in four
        ]
        self.x_lower = [make(parts.at[y, zs[k], 1 - x, b], self.from_x.at[k, b], over_x) for k in four]
        self.y_upper = [make(parts.at[1 - y, zs[k], x, a], self.from_y.at[k, a], over_y) for k in four]
        self.x_upper = [make(parts.at[y, zs[k], 1 - x, a], self.from_x.at[k, a], over_x) for k in four]
        self.y_lower = [make(parts.at[1 - y, zs[k], x, b], self.from_y.at[k, b], over_y) for k in four]
        self.along = [None] + [
            make(parts.at[y, zs[k], x], self.from_z.at[k - 1], place.device(z=zs[k]))
            for k in (1, 2, 3)
        ]

    def start(self, k):
        self.across_y[k].start()
        self.across_x[k].start()
        self.x_lower[k].start()
        self.y_upper[k].start()

    def add(self, index, rows, terms):
        for at in range(0, rows[1], 16):
            here = pl.ds(rows[0] + at, 16)
            total = self.parts[(*index, here)].astype(jnp.float32)
            for term, k in terms:
                total = total + term[k, here].astype(jnp.float32)
            self.parts[(*index, here)] = total.astype(jnp.bfloat16)

    def pass_across(self, k):
        x, y, z = self.place.x, self.place.y, self.place.zs[k]
        self.across_y[k].wait_recv()
        self.add((y, z, 1 - x), self.upper, ((self.by_y, k),))
        self.x_upper[k].start()
        self.across_x[k].wait_recv()
        self.add((1 - y, z, x), self.lower, ((self.by_x, k),))
        self.y_lower[k].start()

    def pass_along(self, k):
        x, y, z = self.place.x, self.place.y, self.place.zs[k]
        for copy in (self.x_upper[k], self.x_lower[k], self.y_upper[k], self.y_lower[k]):
            copy.wait_recv()
        self.add((y, z, x), (0, SHARD), ((self.from_x, k), (self.from_y, k)))
        if k:
            self.along[k].start()

    def close(self):
        x, y, z = self.place.x, self.place.y, self.place.z
        for k in (1, 2, 3):
            self.along[k].wait_recv()
        for at in range(0, SHARD, 16):
            here = pl.ds(at, 16)
            total = self.parts[y, z, x, here].astype(jnp.float32)
            for k in range(3):
                total = total + self.from_z[k, here].astype(jnp.float32)
            self.out[here] = total

    def finish(self):
        for copy in self.copies.made:
            copy.wait_send()


ORDER = (1, 2, 3, 0)


def scatter_kernel(*refs):
    grads, outs = refs[:3], refs[3:6]
    parts, halves, bufs = refs[6], refs[7], refs[8:13]
    send_sems, recv_sems, pair_send, pair_recv, local_sems = refs[13:]
    place = Place()
    place.meet()
    rounds, pairs, locals_ = [], [], []
    for r in range(3):
        rounds.append(
            Scatter(
                place,
                parts.at[r],
                [buf.at[r] for buf in bufs],
                outs[r],
                send_sems.at[r],
                recv_sems.at[r],
                r % 2 == 1,
            )
        )

        def blocks(y, c, grad=grads[r], natural=r == 0):
            return grad.at[:, :, y, c] if natural else grad.at[y, c]

        pairs.append(
            [
                pltpu.make_async_remote_copy(
                    src_ref=blocks(y, 1 - place.c),
                    dst_ref=halves.at[r, y],
                    send_sem=pair_send.at[r, y],
                    recv_sem=pair_recv.at[r, y],
                    device_id=place.device(c=1 - place.c),
                    device_id_type=MESH,
                )
                for y in range(2)
            ]
        )
        locals_.append(
            [
                pltpu.make_async_copy(blocks(y, place.c), parts.at[r, y], local_sems.at[r, y])
                for y in range(2)
            ]
        )

    def pair(r):
        for y in range(2):
            pairs[r][y].wait_recv()
            locals_[r][y].wait()

            def body(i, carry):
                z, x = lax.div(i, 2), lax.rem(i, 2)
                for at in range(0, SHARD, 16):
                    here = pl.ds(at, 16)
                    total = parts[r, y, z, x, here].astype(jnp.float32)
                    total = total + halves[r, y, z, x, here].astype(jnp.float32)
                    parts[r, y, z, x, here] = total.astype(jnp.bfloat16)
                return carry

            lax.fori_loop(0, 8, body, 0)

    for r in range(3):
        for y in range(2):
            pairs[r][y].start()
            locals_[r][y].start()
    pair(0)
    for k in ORDER:
        rounds[0].start(k)
    for r in range(3):
        if r < 2:
            pair(r + 1)
        for k in ORDER:
            rounds[r].pass_across(k)
        if r < 2:
            for k in ORDER:
                rounds[r + 1].start(k)
        for k in ORDER:
            rounds[r].pass_along(k)
        if r:
            rounds[r - 1].close()
    rounds[2].close()
    for r in range(3):
        rounds[r].finish()
        for copy in pairs[r]:
            copy.wait_send()


def scatter_block(grad_qkv, grad_out, grad_up, grad_down):
    def columns(full):
        return full.reshape(D, 4, -1).transpose(1, 0, 2)

    mixed = jnp.concatenate([columns(grad_qkv), columns(grad_out)], axis=2)
    blocks = (
        grad_down.reshape(4, 2, 2, 2, SHARD, D),
        columns(grad_up).reshape(2, 2, 4, 2, SHARD, D),
        mixed.reshape(2, 2, 4, 2, SHARD, D),
    )
    vmem, dma = pltpu.VMEM, pltpu.SemaphoreType.DMA
    shares = pl.pallas_call(
        scatter_kernel,
        out_shape=[jax.ShapeDtypeStruct((SHARD, D), jnp.float32)] * 3,
        in_specs=[pl.BlockSpec(memory_space=pl.ANY)] * 3,
        out_specs=[pl.BlockSpec(memory_space=pltpu.VMEM)] * 3,
        scratch_shapes=[vmem((3, 2, 4, 2, SHARD, D), jnp.bfloat16)] * 2
        + [vmem((3, 4, SHARD, D), jnp.bfloat16)] * 4
        + [vmem((3, 3, SHARD, D), jnp.bfloat16)]
        + [dma((3, SCATTER_COPIES))] * 2
        + [dma((3, 2))] * 3,
        compiler_params=pltpu.CompilerParams(
            collective_id=2, has_side_effects=True, vmem_limit_bytes=60 * 2**20
        ),
    )(*blocks)
    down = lax.all_to_all(shares[0], "fsdp", split_axis=1, concat_axis=0, tiled=True)
    own = grad_qkv.shape[1] // 4
    return (shares[2][:, :own], shares[2][:, own:], shares[1], down)


def scatter_any(*grads):
    peers, mates = lax.axis_size("dp"), lax.axis_size("fsdp")
    results = []
    for full in grads:
        rows, columns = full.shape[0] // peers, full.shape[1] // mates
        blocks = full.reshape(peers, rows, mates, columns)
        blocks = blocks.transpose(0, 2, 1, 3).reshape(peers * mates * rows, columns)
        share = lax.psum_scatter(blocks, ("dp", "fsdp"), scatter_dimension=0, tiled=True)
        results.append(share.astype(jnp.float32))
    return results


def layer_norm(values):
    center = values - jnp.mean(values, axis=-1, keepdims=True)
    variance = jnp.mean(center * center, axis=-1, keepdims=True)
    inverse = lax.rsqrt(variance + epsilon)
    return (center * inverse, inverse)


def norm_back(grad_normed, normed, inverse):
    first_mean = jnp.mean(grad_normed, axis=-1, keepdims=True)
    second_mean = jnp.mean(grad_normed * normed, axis=-1, keepdims=True)
    return inverse * (grad_normed - first_mean - normed * second_mean)


def attention_scores(query_part, key_part, allowed, factor):
    raw_scores = (
        jnp.einsum("qhd,khd->hqk", query_part, key_part, preferred_element_type=jnp.float32)
        * factor
    )
    return jnp.where(allowed[None], raw_scores, -1e30)


def gelu_tanh(values):
    return jax.nn.gelu(values, approximate=True)


def shards(
    block_in,
    condition,
    lengths,
    head_mask,
    group_mask,
    buffer_slot,
    ada_weight,
    ada_bias,
    qkv_weight,
    query_bias,
    value_bias,
    out_weight,
    out_bias,
    up_weight,
    up_bias,
    down_weight,
    down_bias,
    cotangent,
):
    peers = lax.axis_size("dp")
    mates = lax.axis_size("fsdp")

    on_block = peers == 8 and mates == 4
    gather = gather_block if on_block else gather_any
    full_qkv, full_out, full_up, full_down = gather(qkv_weight, out_weight, up_weight, down_weight)
    vectors = (query_bias, value_bias, out_bias, up_bias, down_bias)
    packed_bias = lax.all_gather(jnp.concatenate(vectors), "fsdp", axis=0, tiled=False)
    edges = [0]
    for vector in vectors:
        edges.append(edges[-1] + vector.shape[0])
    bias_query, bias_value, bias_out, bias_up, bias_down = [
        packed_bias[:, low:high].reshape(-1).astype(jnp.float32)
        for low, high in zip(edges[:-1], edges[1:])
    ]
    inputs = block_in[0].astype(jnp.float32)
    crop_length = lengths[0]
    finish = jnp.cumsum(crop_length)
    opening = finish - crop_length
    position = jnp.arange(TOK_DEV, dtype=jnp.int32)
    member = (
        (position[:, None] >= opening[None, :]) & (position[:, None] < finish[None, :])
    ).astype(jnp.float32)
    segment = jnp.sum((position[:, None] >= finish[None, :]).astype(jnp.int32), axis=1)
    cond_act = jax.nn.silu(condition[0].astype(jnp.float32)).astype(jnp.bfloat16)
    crops = cond_act.shape[0]
    cond_all = lax.all_gather(cond_act, ("dp", "fsdp"), axis=0, tiled=True)
    depth = ada_weight.shape[0]
    cond_slice = lax.dynamic_slice_in_dim(cond_all, lax.axis_index("dp") * depth, depth, axis=1)
    partial_mod = jnp.dot(cond_slice, ada_weight, preferred_element_type=jnp.float32)
    column_mod = lax.psum_scatter(partial_mod, "dp", scatter_dimension=0, tiled=True)
    column_mod = column_mod + ada_bias.astype(jnp.float32)
    modulation = lax.all_to_all(column_mod, "fsdp", split_axis=0, concat_axis=1, tiled=True)
    pieces = [
        jnp.dot(member, modulation[:, number * D : (number + 1) * D], precision=highest)
        for number in range(6)
    ]
    shift_one, scale_one, gate_one, shift_two, scale_two, gate_two = pieces
    head_keep = jnp.dot(member, head_mask[0].astype(jnp.float32), precision=highest)
    group_keep = jnp.dot(member, group_mask[0].astype(jnp.float32), precision=highest)
    normed_one, inverse_one = layer_norm(inputs)
    first_in = (normed_one * (1.0 + scale_one) + shift_one).astype(jnp.bfloat16)
    qkv_bias = jnp.concatenate([bias_query, jnp.zeros_like(bias_query), bias_value])
    triple = (jnp.dot(first_in, full_qkv, preferred_element_type=jnp.float32) + qkv_bias).astype(
        jnp.bfloat16
    )
    queries = triple[:, :D].reshape(TOK_DEV, HEADS, HEAD_DIM)
    keys_all = triple[:, D : 2 * D].reshape(TOK_DEV, HEADS, HEAD_DIM)
    values_all = triple[:, 2 * D :].reshape(TOK_DEV, HEADS, HEAD_DIM)
    factor = HEAD_DIM ** (-0.5)
    row_block = min(768, TOK_DEV)
    group_size = min(4, HEADS)
    log_totals = {}
    head_parts = []
    for head_start in range(0, HEADS, group_size):
        heads_here = slice(head_start, head_start + group_size)
        row_start = 0
        rows_here = slice(row_start, row_start + row_block)
        allowed = segment[:, None] == segment[None, :]
        scores = attention_scores(
            queries[rows_here, heads_here], keys_all[:, heads_here], allowed, factor
        )
        row_max = jnp.max(scores, axis=-1, keepdims=True)
        log_total = row_max + jnp.log(jnp.sum(jnp.exp(scores - row_max), axis=-1, keepdims=True))
        weights_low = jnp.exp(scores - log_total).astype(jnp.bfloat16)
        row_parts = jnp.einsum(
            "hqk,khd->qhd",
            weights_low,
            values_all[:, heads_here],
            preferred_element_type=jnp.float32,
        )
        log_totals[head_start, row_start] = log_total
        head_parts.append(row_parts)
    attended = jnp.concatenate(head_parts, axis=1)
    mixed = (attended * head_keep[:, :, None]).astype(jnp.bfloat16).reshape(TOK_DEV, D)
    attn_out = jnp.dot(mixed, full_out, preferred_element_type=jnp.float32) + bias_out
    after_attn = inputs + gate_one * attn_out
    normed_two, inverse_two = layer_norm(after_attn)
    second_in = (normed_two * (1.0 + scale_two) + shift_two).astype(jnp.bfloat16)
    keep = (buffer_slot[0] >= 0).astype(jnp.float32)[:, None]
    places = 2 * TOK_DEV // 3
    chooser = (buffer_slot[0][:, None] == jnp.arange(places, dtype=jnp.int32)[None, :]).astype(
        jnp.bfloat16
    )
    arrived = jnp.einsum(
        "tb,td->bd", chooser, second_in, preferred_element_type=jnp.float32
    ).astype(jnp.bfloat16)
    groups_float = jnp.einsum(
        "tb,tg->bg",
        chooser,
        group_keep.astype(jnp.bfloat16),
        preferred_element_type=jnp.float32,
    )
    channel_keep = jnp.repeat(groups_float, FF // GROUPS, axis=1)
    hidden = jnp.dot(arrived, full_up, preferred_element_type=jnp.float32) + bias_up
    active = (gelu_tanh(hidden) * channel_keep).astype(jnp.bfloat16)
    branch = (jnp.dot(active, full_down, preferred_element_type=jnp.float32) + bias_down).astype(
        jnp.bfloat16
    )
    branch_tok = jnp.einsum(
        "tb,bd->td", chooser, branch, preferred_element_type=jnp.float32
    )
    after_mlp = after_attn + gate_two * branch_tok
    block_out = after_mlp.astype(jnp.bfloat16)[None]
    grad_after = cotangent[0].astype(jnp.float32)
    grad_gate_two = grad_after * branch_tok
    grad_branch = (gate_two * keep * grad_after).astype(jnp.bfloat16)
    grad_rows = jnp.einsum(
        "tb,td->bd", chooser, grad_branch, preferred_element_type=jnp.float32
    ).astype(jnp.bfloat16)
    back_qkv, back_out, back_up, back_down = full_qkv, full_out, full_up, full_down
    grad_down_bias = jnp.sum(grad_rows.astype(jnp.float32), axis=0)
    grad_down = jnp.einsum("bf,bd->fd", active, grad_rows, preferred_element_type=jnp.float32)
    grad_active = jnp.einsum("bd,fd->bf", grad_rows, back_down, preferred_element_type=jnp.float32)
    gelu_pull = jax.vjp(gelu_tanh, hidden)[1]
    grad_hidden = gelu_pull(grad_active * channel_keep)[0].astype(jnp.bfloat16)
    grad_up_bias = jnp.sum(grad_hidden.astype(jnp.float32), axis=0)
    grad_up = jnp.einsum("bd,bf->df", arrived, grad_hidden, preferred_element_type=jnp.float32)
    grad_arrived = jnp.einsum(
        "bf,df->bd", grad_hidden, back_up, preferred_element_type=jnp.float32
    ).astype(jnp.bfloat16)
    grad_second = jnp.einsum(
        "tb,bd->td", chooser, grad_arrived, preferred_element_type=jnp.float32
    )
    grad_scale_two = grad_second * normed_two
    grad_mid = grad_after + norm_back(grad_second * (1.0 + scale_two), normed_two, inverse_two)
    grad_gate_one = grad_mid * attn_out
    grad_attn = (gate_one * grad_mid).astype(jnp.bfloat16)
    grad_out_bias = jnp.sum(grad_attn.astype(jnp.float32), axis=0)
    grad_out = jnp.einsum("te,tf->ef", mixed, grad_attn, preferred_element_type=jnp.float32)
    grad_mixed = jnp.einsum(
        "tf,ef->te", grad_attn, back_out, preferred_element_type=jnp.float32
    ).astype(jnp.bfloat16)
    grad_attended = (
        grad_mixed.reshape(TOK_DEV, HEADS, HEAD_DIM).astype(jnp.float32) * head_keep[:, :, None]
    ).astype(jnp.bfloat16)
    query_heads = []
    key_heads = []
    value_heads = []
    for head_start in range(0, HEADS, group_size):
        heads_here = slice(head_start, head_start + group_size)
        row_start = 0
        rows_here = slice(row_start, row_start + row_block)
        allowed = segment[:, None] == segment[None, :]
        scores = attention_scores(
            queries[rows_here, heads_here], keys_all[:, heads_here], allowed, factor
        )
        probs = jnp.exp(scores - log_totals[head_start, row_start])
        grad_piece = grad_attended[rows_here, heads_here]
        grad_values = jnp.einsum(
            "hqk,qhd->khd",
            probs.astype(jnp.bfloat16),
            grad_piece,
            preferred_element_type=jnp.float32,
        )
        grad_probs = jnp.einsum(
            "qhd,khd->hqk",
            grad_piece,
            values_all[:, heads_here],
            preferred_element_type=jnp.float32,
        )
        grad_scores = (
            probs * (grad_probs - jnp.sum(probs * grad_probs, axis=-1, keepdims=True))
        ).astype(jnp.bfloat16)
        query_rows = (
            jnp.einsum(
                "hqk,khd->qhd",
                grad_scores,
                keys_all[:, heads_here],
                preferred_element_type=jnp.float32,
            )
            * factor
        )
        grad_keys = (
            jnp.einsum(
                "hqk,qhd->khd",
                grad_scores,
                queries[rows_here, heads_here],
                preferred_element_type=jnp.float32,
            )
            * factor
        )
        query_heads.append(query_rows)
        key_heads.append(grad_keys)
        value_heads.append(grad_values)
    grad_triple = jnp.concatenate(
        [
            jnp.concatenate(query_heads, axis=1).reshape(TOK_DEV, D),
            jnp.concatenate(key_heads, axis=1).reshape(TOK_DEV, D),
            jnp.concatenate(value_heads, axis=1).reshape(TOK_DEV, D),
        ],
        axis=1,
    ).astype(jnp.bfloat16)
    grad_query_bias = jnp.sum(grad_triple[:, :D].astype(jnp.float32), axis=0)
    grad_value_bias = jnp.sum(grad_triple[:, 2 * D :].astype(jnp.float32), axis=0)
    grad_qkv = jnp.einsum("td,te->de", first_in, grad_triple, preferred_element_type=jnp.float32)
    grad_first = jnp.einsum("te,de->td", grad_triple, back_qkv, preferred_element_type=jnp.float32)
    grad_scale_one = grad_first * normed_one
    grad_inputs = grad_mid + norm_back(grad_first * (1.0 + scale_one), normed_one, inverse_one)
    token_grads = [
        grad_first,
        grad_scale_one,
        grad_gate_one,
        grad_second,
        grad_scale_two,
        grad_gate_two,
    ]
    grad_modulation = jnp.concatenate(
        [jnp.einsum("ts,td->sd", member, single, precision=highest) for single in token_grads],
        axis=1,
    )
    mod_columns = lax.all_to_all(
        grad_modulation, "fsdp", split_axis=1, concat_axis=0, tiled=True
    )
    mod_all = lax.all_gather(mod_columns, "dp", axis=0, tiled=True)
    grad_ada_bias = jnp.sum(mod_all, axis=0)
    grad_ada = jnp.einsum(
        "sd,se->de", cond_slice.astype(jnp.float32), mod_all, precision=highest
    )

    scatter = scatter_block if on_block else scatter_any
    shares = scatter(
        *[full.astype(jnp.bfloat16) for full in (grad_qkv, grad_out, grad_up, grad_down)]
    )
    bias_grads = (grad_query_bias, grad_value_bias, grad_out_bias, grad_up_bias, grad_down_bias)
    packed = jnp.concatenate([vector.reshape(mates, -1) for vector in bias_grads], axis=1)
    packed = lax.psum_scatter(packed, "fsdp", scatter_dimension=0, tiled=True)
    packed = lax.psum(packed[0], "dp")
    totals = [packed[low:high] for low, high in zip(edges[:-1], edges[1:])]
    return (
        block_out,
        grad_inputs[None],
        grad_ada,
        grad_ada_bias,
        shares[0],
        totals[0],
        totals[1],
        shares[1],
        totals[2],
        shares[2],
        totals[3],
        shares[3],
        totals[4],
    )


def solution(mesh):
    placed = (
        P(("dp", "fsdp"), None, None),
        P(("dp", "fsdp"), None, None),
        P(("dp", "fsdp"), None),
        P(("dp", "fsdp"), None, None),
        P(("dp", "fsdp"), None, None),
        P(("dp", "fsdp"), None),
        P("dp", "fsdp"),
        P("fsdp"),
        P("dp", "fsdp"),
        P("fsdp"),
        P("fsdp"),
        P("dp", "fsdp"),
        P("fsdp"),
        P("dp", "fsdp"),
        P("fsdp"),
        P("dp", "fsdp"),
        P("fsdp"),
        P(("dp", "fsdp"), None, None),
    )
    return jax.shard_map(
        shards,
        mesh=mesh,
        in_specs=placed,
        out_specs=(
            P(("dp", "fsdp"), None, None),
            P(("dp", "fsdp"), None, None),
            P("dp", "fsdp"),
            P("fsdp"),
            P("dp", "fsdp"),
            P("fsdp"),
            P("fsdp"),
            P("dp", "fsdp"),
            P("fsdp"),
            P("dp", "fsdp"),
            P("fsdp"),
            P("dp", "fsdp"),
            P("fsdp"),
        ),
        check_vma=False,
    )
```

```python
import math

import jax
import jax.numpy as jnp
from jax import lax
from jax.experimental import pallas as pl
from jax.experimental.pallas import tpu as pltpu
from jax.sharding import PartitionSpec as P

D = 1152
HEADS = 16
HEAD_DIM = 72
FF = 4608
GROUPS = 16
TOK_DEV = 768


highest = lax.Precision.HIGHEST
epsilon = 1e-06


NT = (((1,), (1,)), ((), ()))
TN = (((0,), (0,)), ((), ()))
NN = (((1,), (0,)), ((), ()))
PLACES = 512
BLOCK = 256
BF16, F32 = jnp.bfloat16, jnp.float32
SOFT = HEAD_DIM**-0.5 * math.log2(math.e)
QKV_SHARD, OUT_SHARD, PAD_SHARD = 864, 288, 896
VMEM_BYTES = 60 * 2**20


def dot(left, right, dims=NN):
    return lax.dot_general(left, right, dims, preferred_element_type=F32)


def rows_at(i):
    return pl.ds(pl.multiple_of(i * BLOCK, BLOCK), BLOCK)


def per_crop(table, segment):
    return jnp.where(
        segment == 0, table[0:1], jnp.where(segment == 1, table[1:2], table[2:3])
    )


def normalise(values):
    center = values - jnp.mean(values, axis=1, keepdims=True)
    variance = jnp.mean(center * center, axis=1, keepdims=True)
    inverse = lax.rsqrt(variance + epsilon)
    return center * inverse, inverse


def crop_sums(segment, values):
    lanes = lax.broadcasted_iota(jnp.int32, (values.shape[0], 128), 1)
    member = (lanes == segment).astype(BF16)
    high = values.astype(BF16)
    low = (values - high.astype(F32)).astype(BF16)
    return (dot(member, high, TN) + dot(member, low, TN))[:8]


def crop_mask(bias_ref, column_ref, row_ref):
    for i in range(TOK_DEV // BLOCK):
        here = pl.ds(i * BLOCK, BLOCK)
        bias_ref[here, :] = jnp.where(column_ref[here, :] == row_ref[...], 0.0, -1e30).astype(F32)


def places_of(slot_row, i):
    place = lax.broadcasted_iota(jnp.int32, (BLOCK, TOK_DEV), 0) + i * BLOCK
    return (place == slot_row).astype(BF16)


def tokens_of(slot_column):
    place = lax.broadcasted_iota(jnp.int32, (BLOCK, PLACES), 1)
    return (place == slot_column).astype(BF16)


def head_keep(mask_ref, h, segment):
    return jnp.where(
        segment == 0, mask_ref[h, 0], jnp.where(segment == 1, mask_ref[h, 1], mask_ref[h, 2])
    )


def attend_kernel(
    x_ref, weight_ref, mods_ref, qkv_bias_ref, out_bias_ref, column_ref, row_ref, slot_ref,
    groups_ref, mask_ref,
    first_ref, heads_ref, mixed_ref, lse_ref, attn_ref, after_ref, arrived_ref, picked_ref, out_weight_ref,
    bias_ref, parts_ref, second_ref,
):
    crop_mask(bias_ref, column_ref, row_ref)

    def norm(i, carry):
        here = rows_at(i)
        segment = column_ref[here, :]
        normed, _ = normalise(x_ref[here, :].astype(F32))
        shift, scale = per_crop(mods_ref[0], segment), per_crop(mods_ref[1], segment)
        first_ref[here, :] = (normed * (1.0 + scale) + shift).astype(BF16)
        return carry

    lax.fori_loop(0, 3, norm, 0)
    for j in range(4):
        out_weight_ref[:, OUT_SHARD * j : OUT_SHARD * (j + 1)] = weight_ref[j, :, QKV_SHARD:]

    def project(i, carry):
        j = lax.div(i, 3)
        here = rows_at(lax.rem(i, 3))
        triple = (dot(first_ref[here, :], weight_ref[j, :, :PAD_SHARD]) + qkv_bias_ref[j]).astype(BF16)
        zero = jnp.zeros((BLOCK, 128 - HEAD_DIM), BF16)
        for h in range(12):
            part = triple[:, HEAD_DIM * h : HEAD_DIM * (h + 1)]
            heads_ref[12 * j + h, here, :] = jnp.concatenate([part, zero], axis=1)
        return carry

    lax.fori_loop(0, 12, project, 0)

    def head(h, carry):
        keys, values = heads_ref[16 + h], heads_ref[32 + h]
        for i in range(3):
            here = pl.ds(i * BLOCK, BLOCK)
            scores = dot(heads_ref[h, here, :], keys, NT) * SOFT + bias_ref[here, :]
            top = jnp.max(scores, axis=1, keepdims=True)
            weights = jnp.exp2(scores - top)
            total = jnp.sum(weights, axis=1, keepdims=True)
            keep = head_keep(mask_ref, h, column_ref[here, :])
            parts_ref[h, here, :] = (dot(weights.astype(BF16), values) * (keep / total)).astype(BF16)
            spread = jnp.broadcast_to(top + jnp.log2(total), (BLOCK, 128))
            lse_ref[h, :, here] = jnp.transpose(spread)[:1, :]
        return carry

    lax.fori_loop(0, HEADS, head, 0)
    for h in range(HEADS):
        mixed_ref[:, HEAD_DIM * h : HEAD_DIM * (h + 1)] = parts_ref[h][:, :HEAD_DIM]

    def close(i, carry):
        here = rows_at(i)
        segment = column_ref[here, :]
        attn = dot(mixed_ref[here, :], out_weight_ref[...]) + out_bias_ref[...]
        attn_ref[here, :] = attn
        after = x_ref[here, :].astype(F32) + per_crop(mods_ref[2], segment) * attn
        after_ref[here, :] = after
        normed, _ = normalise(after)
        shift, scale = per_crop(mods_ref[3], segment), per_crop(mods_ref[4], segment)
        second_ref[here, :] = (normed * (1.0 + scale) + shift).astype(BF16)
        return carry

    lax.fori_loop(0, 3, close, 0)
    for i in range(2):
        here = pl.ds(i * BLOCK, BLOCK)
        choice = places_of(slot_ref[...], i)
        arrived_ref[here, :] = dot(choice, second_ref[...]).astype(BF16)
        picked_ref[here, :] = dot(choice, groups_ref[...]).astype(BF16)


def shape_of(*shape, dtype=BF16):
    return jax.ShapeDtypeStruct(shape, dtype)


IN_VMEM = pl.BlockSpec(memory_space=pltpu.VMEM)
IN_SMEM = pl.BlockSpec(memory_space=pltpu.SMEM)
ANYWHERE = pl.BlockSpec(memory_space=pl.ANY)


def attend(x, weight, mods, qkv_bias, out_bias, column, row, slot_row, groups, mask):
    return pl.pallas_call(
        attend_kernel,
        out_shape=[
            shape_of(TOK_DEV, D),
            shape_of(3 * HEADS, TOK_DEV, 128),
            shape_of(TOK_DEV, D),
            shape_of(HEADS, 1, TOK_DEV, dtype=F32),
            shape_of(TOK_DEV, D, dtype=F32),
            shape_of(TOK_DEV, D, dtype=F32),
            shape_of(PLACES, D),
            shape_of(PLACES, 128),
            shape_of(D, D),
        ],
        in_specs=[IN_VMEM] * 9 + [IN_SMEM],
        out_specs=[IN_VMEM] * 9,
        scratch_shapes=[
            pltpu.VMEM((TOK_DEV, TOK_DEV), F32),
            pltpu.VMEM((HEADS, TOK_DEV, 128), BF16),
            pltpu.VMEM((TOK_DEV, D), BF16),
        ],
        compiler_params=pltpu.CompilerParams(vmem_limit_bytes=VMEM_BYTES),
    )(x, weight, mods, qkv_bias, out_bias, column, row, slot_row, groups, mask)


ROOT = math.sqrt(2.0 / math.pi)


def feed_kernel(
    up_ref, down_ref, arrived_ref, picked_ref, up_bias_ref, down_bias_ref, cot_ref, after_ref,
    mods_ref, column_ref, slot_column_ref, slot_row_ref,
    pull_ref, grad_down_ref, grad_rows_ref, block_out_ref, gate_ref, bias_ref,
    active_ref, total_ref, branch_ref,
):
    step = pl.program_id(0)

    @pl.when(step == 0)
    def _():
        for i in range(3):
            here = pl.ds(i * BLOCK, BLOCK)
            gate = per_crop(mods_ref[5], column_ref[here, :])
            block_out_ref[here, :] = (gate * cot_ref[here, :].astype(F32)).astype(BF16)
        for i in range(2):
            here = pl.ds(i * BLOCK, BLOCK)
            choice = places_of(slot_row_ref[...], i)
            grad_rows_ref[here, :] = dot(choice, block_out_ref[...]).astype(BF16)
        bias_ref[...] = jnp.sum(grad_rows_ref[...].astype(F32), axis=0, keepdims=True)
        total_ref[...] = jnp.zeros_like(total_ref)

    @pl.when(step < 4)
    def _():
        group = lax.broadcasted_iota(jnp.int32, (128, D), 0) - 4 * step
        unit = lax.broadcasted_iota(jnp.int32, (128, D), 1)
        width = FF // GROUPS
        spread = ((unit >= group * width) & (unit < (group + 1) * width)).astype(BF16)
        for i in range(2):
            here = pl.ds(i * BLOCK, BLOCK)
            hidden = dot(arrived_ref[here, :], up_ref[0]) + up_bias_ref[0]
            keep = dot(picked_ref[here, :], spread)
            square = hidden * hidden
            curve = jnp.tanh(ROOT * hidden * (1.0 + 0.044715 * square))
            half = 0.5 * (1.0 + curve)
            slope = half + 0.5 * hidden * (1.0 - curve * curve) * (
                ROOT * (1.0 + 3.0 * 0.044715 * square)
            )
            active_ref[step, here, :] = (hidden * half * keep).astype(BF16)
            pull_ref[0, here, :] = (slope * keep).astype(BF16)

        def grad(i, carry):
            here = pl.ds(pl.multiple_of(i * 384, 384), 384)
            grad_down_ref[0, here, :] = dot(active_ref[step, :, here], grad_rows_ref[...], TN).astype(BF16)
            return carry

        lax.fori_loop(0, 3, grad, 0)

    @pl.when(step >= 4)
    def _():
        for i in range(2):
            here = pl.ds(i * BLOCK, BLOCK)
            total_ref[here, :] += dot(active_ref[step - 4, here, :], down_ref[0])

    @pl.when(step == 7)
    def _():
        branch_ref[...] = (total_ref[...] + down_bias_ref[...]).astype(BF16)
        gates = jnp.zeros((8, D), F32)
        for i in range(3):
            here = pl.ds(i * BLOCK, BLOCK)
            segment = column_ref[here, :]
            branch = dot(tokens_of(slot_column_ref[here, :]), branch_ref[...])
            gate = per_crop(mods_ref[5], segment)
            block_out_ref[here, :] = (after_ref[here, :] + gate * branch).astype(BF16)
            gates = gates + crop_sums(segment, cot_ref[here, :].astype(F32) * branch)
        gate_ref[...] = gates


def whole(*shape):
    return pl.BlockSpec(shape, lambda i: (0,) * len(shape))


def feed(up, down, arrived, picked, up_bias, down_bias, cot, after, mods, column, slot_column, slot_row):
    early = lambda *tail: pl.BlockSpec((1, *tail), lambda i: (jnp.minimum(i, 3), 0, 0))
    late = lambda *tail: pl.BlockSpec((1, *tail), lambda i: (jnp.maximum(i - 4, 0), 0, 0))
    return pl.pallas_call(
        feed_kernel,
        grid=(8,),
        out_shape=[
            shape_of(4, PLACES, D),
            shape_of(4, D, D),
            shape_of(PLACES, D),
            shape_of(TOK_DEV, D),
            shape_of(8, D, dtype=F32),
            shape_of(1, D, dtype=F32),
        ],
        in_specs=[
            early(D, D), late(D, D), whole(PLACES, D), whole(PLACES, 128), early(1, D), whole(1, D),
            whole(TOK_DEV, D), whole(TOK_DEV, D), whole(6, 8, D), whole(TOK_DEV, 1), whole(TOK_DEV, 1),
            whole(1, TOK_DEV),
        ],
        out_specs=[
            early(PLACES, D), early(D, D), whole(PLACES, D), whole(TOK_DEV, D), whole(8, D), whole(1, D),
        ],
        scratch_shapes=[
            pltpu.VMEM((4, PLACES, D), BF16),
            pltpu.VMEM((PLACES, D), F32),
            pltpu.VMEM((PLACES, D), BF16),
        ],
        compiler_params=pltpu.CompilerParams(vmem_limit_bytes=VMEM_BYTES),
    )(up, down, arrived, picked, up_bias, down_bias, cot, after, mods, column, slot_column, slot_row)


def unfeed_kernel(
    down_ref, up_ref, pull_ref, grad_rows_ref, arrived_ref, after_ref, cot_ref, attn_ref, mods_ref,
    column_ref, slot_column_ref,
    grad_up_ref, up_bias_ref, mid_ref, grad_attn_ref, grad_split_ref, sums_ref, out_bias_ref,
    hidden_ref, total_ref, back_ref,
):
    step = pl.program_id(0)

    @pl.when(step == 0)
    def _():
        total_ref[...] = jnp.zeros_like(total_ref)

    bias = jnp.zeros((1, D), F32)
    for i in range(2):
        here = pl.ds(i * BLOCK, BLOCK)
        grad = dot(grad_rows_ref[here, :], down_ref[0], NT) * pull_ref[0, here, :].astype(F32)
        low = grad.astype(BF16)
        hidden_ref[here, :] = low
        bias = bias + jnp.sum(low.astype(F32), axis=0, keepdims=True)
        total_ref[here, :] += dot(low, up_ref[0], NT)
    up_bias_ref[0] = bias

    def grad_of(i, carry):
        here = pl.ds(pl.multiple_of(i * 384, 384), 384)
        grad_up_ref[0, here, :] = dot(arrived_ref[:, here], hidden_ref[...], TN).astype(BF16)
        return carry

    lax.fori_loop(0, 3, grad_of, 0)

    @pl.when(step == 3)
    def _():
        back_ref[...] = total_ref[...].astype(BF16)
        shifts, scales = jnp.zeros((8, D), F32), jnp.zeros((8, D), F32)
        gates, out_bias = jnp.zeros((8, D), F32), jnp.zeros((1, D), F32)
        for i in range(3):
            here = pl.ds(i * BLOCK, BLOCK)
            segment = column_ref[here, :]
            second = dot(tokens_of(slot_column_ref[here, :]), back_ref[...])
            normed, inverse = normalise(after_ref[here, :])
            grad = second * (1.0 + per_crop(mods_ref[4], segment))
            mean = jnp.mean(grad, axis=1, keepdims=True)
            slant = jnp.mean(grad * normed, axis=1, keepdims=True)
            mid = cot_ref[here, :].astype(F32) + inverse * (grad - mean - normed * slant)
            mid_ref[here, :] = mid
            low = (per_crop(mods_ref[2], segment) * mid).astype(BF16)
            grad_attn_ref[here, :] = low
            for j in range(4):
                grad_split_ref[j, here, :] = low[:, OUT_SHARD * j : OUT_SHARD * (j + 1)]
            out_bias = out_bias + jnp.sum(low.astype(F32), axis=0, keepdims=True)
            shifts = shifts + crop_sums(segment, second)
            scales = scales + crop_sums(segment, second * normed)
            gates = gates + crop_sums(segment, mid * attn_ref[here, :])
        sums_ref[0], sums_ref[1], sums_ref[2] = gates, shifts, scales
        out_bias_ref[...] = out_bias


def unfeed(down, up, pull, grad_rows, arrived, after, cot, attn, mods, column, slot_column):
    block = lambda *tail: pl.BlockSpec((1, *tail), lambda i: (i, 0, 0))
    return pl.pallas_call(
        unfeed_kernel,
        grid=(4,),
        out_shape=[
            shape_of(4, D, D),
            shape_of(4, 1, D, dtype=F32),
            shape_of(TOK_DEV, D, dtype=F32),
            shape_of(TOK_DEV, D),
            shape_of(4, TOK_DEV, OUT_SHARD),
            shape_of(3, 8, D, dtype=F32),
            shape_of(1, D, dtype=F32),
        ],
        in_specs=[
            block(D, D), block(D, D), block(PLACES, D), whole(PLACES, D), whole(PLACES, D),
            whole(TOK_DEV, D), whole(TOK_DEV, D), whole(TOK_DEV, D), whole(6, 8, D), whole(TOK_DEV, 1),
            whole(TOK_DEV, 1),
        ],
        out_specs=[
            block(D, D), block(1, D), whole(TOK_DEV, D), whole(TOK_DEV, D), whole(4, TOK_DEV, OUT_SHARD),
            whole(3, 8, D), whole(1, D),
        ],
        scratch_shapes=[
            pltpu.VMEM((PLACES, D), BF16),
            pltpu.VMEM((PLACES, D), F32),
            pltpu.VMEM((PLACES, D), BF16),
        ],
        compiler_params=pltpu.CompilerParams(vmem_limit_bytes=VMEM_BYTES),
    )(down, up, pull, grad_rows, arrived, after, cot, attn, mods, column, slot_column)


def unattend_kernel(
    grad_ref, out_weight_ref, heads_ref, lse_ref, column_ref, row_ref, mask_ref,
    triple_ref, sums_ref,
    bias_ref, mixed_ref, grads_ref, key_ref, value_ref,
):
    crop_mask(bias_ref, column_ref, row_ref)

    def spread(i, carry):
        here = rows_at(i)
        segment = column_ref[here, :]
        mixed = dot(grad_ref[here, :], out_weight_ref[...], NT)
        zero = jnp.zeros((BLOCK, 128 - HEAD_DIM), BF16)
        for h in range(HEADS):
            part = mixed[:, HEAD_DIM * h : HEAD_DIM * (h + 1)] * head_keep(mask_ref, h, segment)
            mixed_ref[h, here, :] = jnp.concatenate([part.astype(BF16), zero], axis=1)
        return carry

    lax.fori_loop(0, 3, spread, 0)
    factor = HEAD_DIM**-0.5

    def head(h, carry):
        keys, values = heads_ref[16 + h], heads_ref[32 + h]
        turned = jnp.transpose(keys)
        for i in range(3):
            here = pl.ds(i * BLOCK, BLOCK)
            queries, grads = heads_ref[h, here, :], mixed_ref[h, here, :]
            scores = dot(keys, queries, NT) * SOFT + bias_ref[:, here]
            probs = jnp.exp2(scores - lse_ref[h, :, here])
            product = probs * dot(values, grads, NT)
            total = jnp.sum(product, axis=0, keepdims=True)
            low = (product - probs * total).astype(BF16)
            for_values, for_keys = dot(probs.astype(BF16), grads), dot(low, queries)
            if i == 0:
                value_ref[...], key_ref[...] = for_values, for_keys
            else:
                value_ref[...] += for_values
                key_ref[...] += for_keys
            grads_ref[h, here, :] = jnp.transpose(dot(turned, low) * factor).astype(BF16)
        grads_ref[16 + h] = (key_ref[...] * factor).astype(BF16)
        grads_ref[32 + h] = value_ref[...].astype(BF16)
        return carry

    lax.fori_loop(0, HEADS, head, 0)
    for j in range(4):
        triple_ref[j, :, QKV_SHARD:] = jnp.zeros((TOK_DEV, PAD_SHARD - QKV_SHARD), BF16)
        for h in range(12):
            triple_ref[j, :, HEAD_DIM * h : HEAD_DIM * (h + 1)] = grads_ref[12 * j + h][:, :HEAD_DIM]
        sums_ref[j] = jnp.sum(triple_ref[j].astype(F32), axis=0, keepdims=True)


def unattend(grad_attn, out_weight, heads, lse, column, row, mask):
    return pl.pallas_call(
        unattend_kernel,
        out_shape=[shape_of(4, TOK_DEV, PAD_SHARD), shape_of(4, 1, PAD_SHARD, dtype=F32)],
        in_specs=[IN_VMEM] * 6 + [IN_SMEM],
        out_specs=[IN_VMEM] * 2,
        scratch_shapes=[
            pltpu.VMEM((TOK_DEV, TOK_DEV), F32),
            pltpu.VMEM((HEADS, TOK_DEV, 128), BF16),
            pltpu.VMEM((3 * HEADS, TOK_DEV, 128), BF16),
            pltpu.VMEM((TOK_DEV, 128), F32),
            pltpu.VMEM((TOK_DEV, 128), F32),
        ],
        compiler_params=pltpu.CompilerParams(vmem_limit_bytes=VMEM_BYTES),
    )(grad_attn, out_weight, heads, lse, column, row, mask)


def unproject_kernel(
    weight_ref, triple_ref, split_ref, first_ref, mixed_ref, x_ref, mid_ref, mods_ref, column_ref,
    grad_ref, grad_in_ref, sums_ref,
    total_ref,
):
    step = pl.program_id(0)

    def grad(i, carry):
        here = pl.ds(pl.multiple_of(i * 384, 384), 384)
        part = dot(first_ref[:, here], triple_ref[0], TN).astype(BF16)
        grad_ref[0, here, :PAD_SHARD] = part
        grad_ref[0, here, QKV_SHARD:] = dot(mixed_ref[:, here], split_ref[0], TN).astype(BF16)
        return carry

    lax.fori_loop(0, 3, grad, 0)
    for i in range(3):
        here = pl.ds(i * BLOCK, BLOCK)
        part = dot(triple_ref[0, here, :], weight_ref[0, :, :PAD_SHARD], NT)
        total_ref[here, :] = jnp.where(step == 0, part, total_ref[here, :] + part)

    @pl.when(step == 3)
    def _():
        shifts, scales = jnp.zeros((8, D), F32), jnp.zeros((8, D), F32)
        for i in range(3):
            here = pl.ds(i * BLOCK, BLOCK)
            segment = column_ref[here, :]
            first = total_ref[here, :]
            normed, inverse = normalise(x_ref[here, :].astype(F32))
            grads = first * (1.0 + per_crop(mods_ref[1], segment))
            mean = jnp.mean(grads, axis=1, keepdims=True)
            slant = jnp.mean(grads * normed, axis=1, keepdims=True)
            grad_in_ref[here, :] = mid_ref[here, :] + inverse * (grads - mean - normed * slant)
            shifts = shifts + crop_sums(segment, first)
            scales = scales + crop_sums(segment, first * normed)
        sums_ref[0], sums_ref[1] = shifts, scales


def unproject(weight, triple, split, first, mixed, x, mid, mods, column):
    block = lambda *tail: pl.BlockSpec((1, *tail), lambda i: (i, 0, 0))
    return pl.pallas_call(
        unproject_kernel,
        grid=(4,),
        out_shape=[shape_of(4, D, D), shape_of(TOK_DEV, D, dtype=F32), shape_of(2, 8, D, dtype=F32)],
        in_specs=[
            block(D, D), block(TOK_DEV, PAD_SHARD), block(TOK_DEV, OUT_SHARD), whole(TOK_DEV, D),
            whole(TOK_DEV, D), whole(TOK_DEV, D), whole(TOK_DEV, D), whole(6, 8, D), whole(TOK_DEV, 1),
        ],
        out_specs=[block(D, D), whole(TOK_DEV, D), whole(2, 8, D)],
        scratch_shapes=[pltpu.VMEM((TOK_DEV, D), F32)],
        compiler_params=pltpu.CompilerParams(vmem_limit_bytes=VMEM_BYTES),
    )(weight, triple, split, first, mixed, x, mid, mods, column)


MESH = pl.DeviceIdType.MESH
SHARD = 144
UPPER = 80


class Place:
    def __init__(self):
        dp, fsdp = lax.axis_index("dp"), lax.axis_index("fsdp")
        self.z, self.x = lax.div(dp, 2), lax.rem(dp, 2)
        self.y, self.c = lax.div(fsdp, 2), lax.rem(fsdp, 2)
        z = self.z
        self.zs = (z, z + 1 - 2 * lax.rem(z, 2), lax.rem(z + 2, 4), 3 - z)
        self.mates = (
            self.device(c=1 - self.c),
            self.device(y=1 - self.y),
            self.device(y=1 - self.y, c=1 - self.c),
        )
        self.mate_index = (
            2 * self.y + 1 - self.c,
            2 * (1 - self.y) + self.c,
            2 * (1 - self.y) + 1 - self.c,
        )
        self.index = 2 * self.y + self.c
        self.peer = 2 * z + self.x

    def device(self, z=None, x=None, y=None, c=None):
        z, x = self.z if z is None else z, self.x if x is None else x
        y, c = self.y if y is None else y, self.c if c is None else c
        return (2 * z + x, 2 * y + c)

    def meet(self):
        barrier = pltpu.get_barrier_semaphore()
        others = [self.device(z=self.zs[k]) for k in (1, 2, 3)]
        others += [self.device(z=self.zs[k], x=1 - self.x) for k in range(4)]
        others += self.mates
        for other in others:
            pl.semaphore_signal(barrier, inc=1, device_id=other, device_id_type=MESH)
        pl.semaphore_wait(barrier, len(others))


class Copies:
    def __init__(self, send_sems, recv_sems):
        self.send_sems, self.recv_sems, self.made = send_sems, recv_sems, []

    def make(self, source, target, device):
        index = len(self.made)
        copy = pltpu.make_async_remote_copy(
            src_ref=source,
            dst_ref=target,
            send_sem=self.send_sems.at[index],
            recv_sem=self.recv_sems.at[index],
            device_id=device,
            device_id_type=MESH,
        )
        self.made.append(copy)
        return copy


GATHER_COPIES = 35


class Gather:
    def __init__(self, place, source, slot, send_sems, recv_sems, local_sem, swap):
        x, y, c, zs = place.x, place.y, place.c, place.zs
        self.copies = Copies(send_sems, recv_sems)
        make = self.copies.make
        first, second = (SHARD - UPPER, UPPER) if swap else (0, UPPER)
        upper = pl.ds(first, second)
        lower = pl.ds(0, SHARD - UPPER) if swap else pl.ds(UPPER, SHARD - UPPER)
        over_x, over_y, beside = (
            place.device(x=1 - x),
            place.device(y=1 - y),
            place.device(c=1 - c),
        )
        own = [slot(y, c, zs[k], x) for k in range(4)]
        held = [source] + own[1:]
        from_x = [slot(y, c, zs[k], 1 - x) for k in range(4)]
        from_y = [slot(1 - y, c, zs[k], x) for k in range(4)]
        across = [slot(1 - y, c, zs[k], 1 - x) for k in range(4)]
        self.local = pltpu.make_async_copy(source, own[0], local_sem)
        self.along = [None] + [make(source, own[0], place.device(z=zs[k])) for k in (1, 2, 3)]
        self.to_x = [make(held[k], own[k], over_x) for k in range(4)]
        self.to_y = [make(held[k], own[k], over_y) for k in range(4)]
        self.x_to_y = [make(s.at[upper], s.at[upper], over_y) for s in from_x]
        self.y_to_x = [make(s.at[lower], s.at[lower], over_x) for s in from_y]
        self.pair = [make(held[k], own[k], beside) for k in range(4)]
        self.pair_x = [make(s, s, beside) for s in from_x]
        self.pair_y = [make(s, s, beside) for s in from_y]
        self.pair_across = [make(s, s, beside) for s in across]

    def start(self):
        self.along[1].start()
        self.to_x[0].start()
        self.to_y[0].start()
        self.along[2].start()
        self.along[3].start()
        self.pair[0].start()
        self.local.start()

    def pass_along(self, k):
        self.along[k].wait_recv()
        self.to_x[k].start()
        self.to_y[k].start()
        self.pair[k].start()

    def pass_across(self, k):
        self.to_x[k].wait_recv()
        self.x_to_y[k].start()
        self.pair_x[k].start()
        self.to_y[k].wait_recv()
        self.y_to_x[k].start()
        self.pair_y[k].start()

    def pass_pair(self, k):
        self.x_to_y[k].wait_recv()
        self.y_to_x[k].wait_recv()
        self.pair_across[k].start()

    def finish(self):
        self.local.wait()
        for copy in self.pair + self.pair_x + self.pair_y + self.pair_across:
            copy.wait_recv()
        for copy in self.copies.made:
            copy.wait_send()

CROPS = 3


def gather_kernel(
    mixed_ref, up_ref, down_ref, cond_ref, ada_ref, ada_bias_ref, bias_ref,
    mixed_out, up_out, down_out, mods_ref, biases_ref, conds_ref,
    send_sems, recv_sems, local_sems, small_send, small_recv, local_small,
    all_cond, own_cond, partial_ref, from_x, from_z, column_ref,
):
    sources, targets = (mixed_ref, up_ref, down_ref), (mixed_out, up_out, down_out)
    place = Place()
    place.meet()
    x, zs = place.x, place.zs

    def slot_of(r):
        if r == 2:
            return lambda y, c, z, x: targets[r].at[z, x, y, c]
        return lambda y, c, z, x: targets[r].at[y, c, z, x]

    rounds = [
        Gather(
            place, sources[r], slot_of(r), send_sems.at[r], recv_sems.at[r], local_sems.at[r], r % 2 == 1
        )
        for r in range(3)
    ]
    small = Copies(small_send, small_recv)
    to_mates = [small.make(cond_ref, all_cond.at[place.index], mate) for mate in place.mates]
    to_mates += [small.make(bias_ref, biases_ref.at[place.index], mate) for mate in place.mates]
    others = [(k, far) for k in range(4) for far in (0, 1) if k or far]
    to_peers = []
    for k, far in others:
        there = 1 - x if far else x
        to_peers.append(
            small.make(
                own_cond.at[2 * zs[k] + there],
                conds_ref.at[place.peer],
                place.device(z=zs[k], x=there),
            )
        )
    over_x = [
        small.make(partial_ref.at[2 * zs[k] + 1 - x], from_x.at[k], place.device(x=1 - x))
        for k in range(4)
    ]
    along = [
        small.make(partial_ref.at[2 * zs[k] + x], from_z.at[k - 1], place.device(z=zs[k]))
        for k in (1, 2, 3)
    ]
    finals = [
        small.make(column_ref.at[other], mods_ref.at[place.index], mate)
        for other, mate in zip(place.mate_index, place.mates)
    ]
    own_bias = pltpu.make_async_copy(bias_ref, biases_ref.at[place.index], local_small.at[0])

    for copy in to_mates:
        copy.start()
    own_bias.start()
    rounds[0].start()
    all_cond[place.index] = cond_ref[...]
    own_cond[...] = jnp.zeros_like(own_cond)
    for copy in to_mates:
        copy.wait_recv()
    for j in range(4):
        own_cond[:, CROPS * j : CROPS * (j + 1), :] = all_cond[j, :, :CROPS, :]
    for copy in to_peers:
        copy.start()
    conds_ref[place.peer] = own_cond[place.peer]
    rounds[0].pass_along(1)
    for copy in to_peers:
        copy.wait_recv()
    for i in range(8):
        partial_ref[i] = dot(conds_ref[i][:, :SHARD].astype(BF16), ada_ref[...])
    for copy in over_x:
        copy.start()
    rounds[0].pass_along(2)
    rounds[0].pass_along(3)
    for k in range(4):
        over_x[k].wait_recv()
        partial_ref[2 * zs[k] + x] += from_x[k]
    for copy in along:
        copy.start()
    rounds[1].start()
    for k in range(2):
        rounds[0].pass_across(k)
    for copy in along:
        copy.wait_recv()
    total = partial_ref[place.peer] + from_z[0] + from_z[1] + from_z[2] + ada_bias_ref[...]
    column_ref[...] = jnp.zeros_like(column_ref)
    for j in range(4):
        column_ref[j, :CROPS, :] = total[CROPS * j : CROPS * (j + 1)]
    for copy in finals:
        copy.start()
    mods_ref[place.index] = column_ref[place.index]
    for k in range(2, 4):
        rounds[0].pass_across(k)
    for k in (1, 2, 3):
        rounds[1].pass_along(k)
    for k in range(4):
        rounds[0].pass_pair(k)
    rounds[2].start()
    for k in range(4):
        rounds[1].pass_across(k)
    for k in (1, 2, 3):
        rounds[2].pass_along(k)
    for k in range(4):
        rounds[1].pass_pair(k)
    for k in range(4):
        rounds[2].pass_across(k)
    for k in range(4):
        rounds[2].pass_pair(k)
    for copy in finals:
        copy.wait_recv()
    own_bias.wait()
    for each in rounds:
        each.finish()
    for copy in small.made:
        copy.wait_send()


def gather_all(mixed, up, down, cond, ada, ada_bias, bias):
    shapes = ((2, 2, 4, 2), (2, 2, 4, 2), (4, 2, 2, 2))
    vmem, dma = pltpu.VMEM, pltpu.SemaphoreType.DMA
    wide = ada.shape[1]
    return pl.pallas_call(
        gather_kernel,
        out_shape=[shape_of(*shape, SHARD, D) for shape in shapes]
        + [shape_of(4, 8, wide, dtype=F32), shape_of(4, 32, 128), shape_of(8, 16, 256, dtype=F32)],
        in_specs=[ANYWHERE] * 3 + [IN_VMEM] * 4,
        out_specs=[ANYWHERE] * 3 + [IN_VMEM] * 3,
        scratch_shapes=[dma((3, GATHER_COPIES))] * 2
        + [dma((3,)), dma((23,)), dma((23,)), dma((1,))]
        + [
            vmem((4, 8, 8, 256), F32),
            vmem((8, 16, 256), F32),
            vmem((8, 16, wide), F32),
            vmem((4, 16, wide), F32),
            vmem((3, 16, wide), F32),
            vmem((4, 8, wide), F32),
        ],
        compiler_params=pltpu.CompilerParams(
            collective_id=1, has_side_effects=True, vmem_limit_bytes=VMEM_BYTES
        ),
    )(mixed, up, down, cond, ada, ada_bias, bias)


SCATTER_COPIES = 27


class Scatter:
    def __init__(self, place, parts, bufs, out, send_sems, recv_sems, swap):
        x, y, zs = place.x, place.y, place.zs
        self.place, self.parts, self.out = place, parts, out
        self.by_x, self.by_y, self.from_x, self.from_y, self.from_z = bufs
        self.copies = Copies(send_sems, recv_sems)
        make = self.copies.make
        self.upper = (SHARD - UPPER, UPPER) if swap else (0, UPPER)
        self.lower = (0, SHARD - UPPER) if swap else (UPPER, SHARD - UPPER)
        a, b = pl.ds(*self.upper), pl.ds(*self.lower)
        over_x, over_y = place.device(x=1 - x), place.device(y=1 - y)
        four = range(4)
        self.across_y = [
            make(parts.at[1 - y, zs[k], 1 - x, a], self.by_y.at[k, a], over_y) for k in four
        ]
        self.across_x = [
            make(parts.at[1 - y, zs[k], 1 - x, b], self.by_x.at[k, b], over_x) for k in four
        ]
        self.x_lower = [make(parts.at[y, zs[k], 1 - x, b], self.from_x.at[k, b], over_x) for k in four]
        self.y_upper = [make(parts.at[1 - y, zs[k], x, a], self.from_y.at[k, a], over_y) for k in four]
        self.x_upper = [make(parts.at[y, zs[k], 1 - x, a], self.from_x.at[k, a], over_x) for k in four]
        self.y_lower = [make(parts.at[1 - y, zs[k], x, b], self.from_y.at[k, b], over_y) for k in four]
        self.along = [None] + [
            make(parts.at[y, zs[k], x], self.from_z.at[k - 1], place.device(z=zs[k]))
            for k in (1, 2, 3)
        ]

    def start(self, k):
        self.across_y[k].start()
        self.across_x[k].start()
        self.x_lower[k].start()
        self.y_upper[k].start()

    def add(self, index, rows, terms):
        for at in range(0, rows[1], 16):
            here = pl.ds(rows[0] + at, 16)
            total = self.parts[(*index, here)].astype(jnp.float32)
            for term, k in terms:
                total = total + term[k, here].astype(jnp.float32)
            self.parts[(*index, here)] = total.astype(jnp.bfloat16)

    def pass_across(self, k):
        x, y, z = self.place.x, self.place.y, self.place.zs[k]
        self.across_y[k].wait_recv()
        self.add((y, z, 1 - x), self.upper, ((self.by_y, k),))
        self.x_upper[k].start()
        self.across_x[k].wait_recv()
        self.add((1 - y, z, x), self.lower, ((self.by_x, k),))
        self.y_lower[k].start()

    def pass_along(self, k):
        x, y, z = self.place.x, self.place.y, self.place.zs[k]
        for copy in (self.x_upper[k], self.x_lower[k], self.y_upper[k], self.y_lower[k]):
            copy.wait_recv()
        self.add((y, z, x), (0, SHARD), ((self.from_x, k), (self.from_y, k)))
        if k:
            self.along[k].start()

    def close(self):
        x, y, z = self.place.x, self.place.y, self.place.z
        for k in (1, 2, 3):
            self.along[k].wait_recv()
        for at in range(0, SHARD, 16):
            here = pl.ds(at, 16)
            total = self.parts[y, z, x, here].astype(jnp.float32)
            for k in range(3):
                total = total + self.from_z[k, here].astype(jnp.float32)
            self.out[here] = total

    def finish(self):
        for copy in self.copies.made:
            copy.wait_send()


ORDER = (1, 2, 3, 0)


def close_ada(conds_ref, every, ada_ref, sums_ref):
    total = jnp.zeros(ada_ref.shape, F32)
    rows = jnp.zeros((16, ada_ref.shape[1]), F32)
    for i in range(0, 8, 2):
        rows = rows + every[i] + every[i + 1]
        cond = jnp.concatenate([conds_ref[i][:, :SHARD], conds_ref[i + 1][:, :SHARD]], axis=0)
        rest = jnp.concatenate([every[i], every[i + 1]], axis=0)
        for _ in range(3):
            part = rest.astype(BF16)
            total = total + dot(cond.astype(BF16), part, TN)
            rest = rest - part.astype(F32)
    ada_ref[...] = total
    sums_ref[...] = jnp.zeros_like(sums_ref)
    sums_ref[0:1, :] = jnp.sum(rows[:12], axis=0, keepdims=True)
    sums_ref[1:3, :] = rows[12:14]


def scatter_kernel(*refs):
    grads, mod_ref, conds_ref = refs[:3], refs[3], refs[4]
    outs, ada_ref, sums_ref = refs[5:8], refs[8], refs[9]
    parts, halves, bufs = refs[10], refs[11], refs[12:17]
    send_sems, recv_sems, pair_send, pair_recv, local_sems = refs[17:22]
    small_send, small_recv, from_mates, packed, every = refs[22:]
    place = Place()
    place.meet()
    small = Copies(small_send, small_recv)
    to_mates = [
        small.make(mod_ref.at[other], from_mates.at[place.index], mate)
        for other, mate in zip(place.mate_index, place.mates)
    ]
    along = [
        small.make(packed, every.at[place.peer], place.device(z=place.zs[k])) for k in (1, 2, 3)
    ]
    over_x = [
        small.make(
            every.at[2 * place.zs[k] + place.x],
            every.at[2 * place.zs[k] + place.x],
            place.device(x=1 - place.x),
        )
        for k in range(4)
    ]
    rounds, pairs, locals_ = [], [], []
    for r in range(3):
        rounds.append(
            Scatter(
                place,
                parts.at[r],
                [buf.at[r] for buf in bufs],
                outs[r],
                send_sems.at[r],
                recv_sems.at[r],
                r % 2 == 1,
            )
        )

        def blocks(y, c, grad=grads[r], natural=r == 0):
            return grad.at[:, :, y, c] if natural else grad.at[y, c]

        pairs.append(
            [
                pltpu.make_async_remote_copy(
                    src_ref=blocks(y, 1 - place.c),
                    dst_ref=halves.at[r, y],
                    send_sem=pair_send.at[r, y],
                    recv_sem=pair_recv.at[r, y],
                    device_id=place.device(c=1 - place.c),
                    device_id_type=MESH,
                )
                for y in range(2)
            ]
        )
        locals_.append(
            [
                pltpu.make_async_copy(blocks(y, place.c), parts.at[r, y], local_sems.at[r, y])
                for y in range(2)
            ]
        )

    def pair(r):
        for y in range(2):
            pairs[r][y].wait_recv()
            locals_[r][y].wait()

            def body(i, carry):
                z, x = lax.div(i, 2), lax.rem(i, 2)
                for at in range(0, SHARD, 16):
                    here = pl.ds(at, 16)
                    total = parts[r, y, z, x, here].astype(jnp.float32)
                    total = total + halves[r, y, z, x, here].astype(jnp.float32)
                    parts[r, y, z, x, here] = total.astype(jnp.bfloat16)
                return carry

            lax.fori_loop(0, 8, body, 0)

    for r in range(3):
        for y in range(2):
            pairs[r][y].start()
            locals_[r][y].start()
    for copy in to_mates:
        copy.start()
    from_mates[place.index] = mod_ref[place.index]
    packed[...] = jnp.zeros_like(packed)
    pair(0)
    for copy in to_mates:
        copy.wait_recv()
    for j in range(4):
        packed[CROPS * j : CROPS * (j + 1), :] = from_mates[j, :CROPS, :]
        packed[12:14, :] += from_mates[j, CROPS : CROPS + 2, :]
    for copy in along:
        copy.start()
    every[place.peer] = packed[...]
    for k in ORDER:
        rounds[0].start(k)
    pair(1)
    for copy in along:
        copy.wait_recv()
    for copy in over_x:
        copy.start()
    for r in range(3):
        if r == 1:
            pair(2)
        for k in ORDER:
            rounds[r].pass_across(k)
        if r < 2:
            for k in ORDER:
                rounds[r + 1].start(k)
        for k in ORDER:
            rounds[r].pass_along(k)
        if r == 0:
            for copy in over_x:
                copy.wait_recv()
            close_ada(conds_ref, every, ada_ref, sums_ref)
        if r:
            rounds[r - 1].close()
    rounds[2].close()
    for r in range(3):
        rounds[r].finish()
        for copy in pairs[r]:
            copy.wait_send()
    for copy in small.made:
        copy.wait_send()


def scatter_all(grad_down, grad_up, grad_mixed, mod_grads, conds):
    blocks = (
        grad_down.reshape(4, 2, 2, 2, SHARD, D),
        grad_up.reshape(2, 2, 4, 2, SHARD, D),
        grad_mixed.reshape(2, 2, 4, 2, SHARD, D),
    )
    vmem, dma = pltpu.VMEM, pltpu.SemaphoreType.DMA
    wide = mod_grads.shape[2]
    return pl.pallas_call(
        scatter_kernel,
        out_shape=[shape_of(SHARD, D, dtype=F32)] * 3
        + [shape_of(SHARD, wide, dtype=F32), shape_of(8, wide, dtype=F32)],
        in_specs=[ANYWHERE] * 3 + [IN_VMEM] * 2,
        out_specs=[IN_VMEM] * 5,
        scratch_shapes=[vmem((3, 2, 4, 2, SHARD, D), BF16)] * 2
        + [vmem((3, 4, SHARD, D), BF16)] * 4
        + [vmem((3, 3, SHARD, D), BF16)]
        + [dma((3, SCATTER_COPIES))] * 2
        + [dma((3, 2))] * 3
        + [dma((10,))] * 2
        + [vmem((4, 8, wide), F32), vmem((16, wide), F32), vmem((8, 16, wide), F32)],
        compiler_params=pltpu.CompilerParams(
            collective_id=2, has_side_effects=True, vmem_limit_bytes=VMEM_BYTES
        ),
    )(*blocks, mod_grads, conds)


def block_shards(
    block_in, condition, lengths, head_mask, group_mask, buffer_slot, ada_weight, ada_bias, qkv_weight,
    query_bias, value_bias, out_weight, out_bias, up_weight, up_bias, down_weight, down_bias, cotangent,
):
    x, cot = block_in[0], cotangent[0]
    finish = jnp.cumsum(lengths[0])
    position = jnp.arange(TOK_DEV, dtype=jnp.int32)
    segment = jnp.sum((position[:, None] >= finish[None, :]).astype(jnp.int32), axis=1)
    column, row = segment[:, None], segment[None, :]
    slot = buffer_slot[0].astype(jnp.int32)
    slot_column, slot_row = slot[:, None], slot[None, :]
    mask = head_mask[0].T.astype(F32)
    chosen = (segment[:, None] == jnp.arange(CROPS)[None, :])[:, :, None]
    groups = jnp.sum(jnp.where(chosen, group_mask[0].astype(F32)[None], 0.0), axis=1)
    groups = jnp.pad(groups, ((0, 0), (0, 128 - GROUPS))).astype(BF16)
    cond = jax.nn.silu(condition[0].astype(F32)).astype(BF16).astype(F32)
    cond = cond.reshape(CROPS, 8, SHARD).transpose(1, 0, 2)
    cond = jnp.pad(cond, ((0, 0), (0, 8 - CROPS), (0, 256 - SHARD)))
    vectors = jnp.concatenate([query_bias, value_bias, out_bias, up_bias, down_bias])
    packed = jnp.pad(vectors.reshape(18, 128), ((0, 14), (0, 0)))
    down_rows = lax.all_to_all(down_weight, "fsdp", split_axis=0, concat_axis=1, tiled=True)
    mixed_block = jnp.concatenate([qkv_weight, out_weight], axis=1)
    mixed_weight, up, down, mods, biases, conds = gather_all(
        mixed_block, up_weight, down_rows, cond, ada_weight, ada_bias.astype(F32)[None], packed
    )
    mixed_weight, up, down = mixed_weight.reshape(4, D, D), up.reshape(4, D, D), down.reshape(4, D, D)
    mods = mods.transpose(1, 0, 2).reshape(8, 6, D).transpose(1, 0, 2)
    biases = biases[:, :18].reshape(4, 2304).astype(F32)
    edges = (0, 288, 576, 864, 2016, 2304)
    bias_query, bias_value, bias_out, bias_up, bias_down = [
        biases[:, low:high].reshape(1, -1) for low, high in zip(edges[:-1], edges[1:])
    ]
    qkv_bias = jnp.concatenate([bias_query, jnp.zeros_like(bias_query), bias_value], axis=1)
    qkv_bias = jnp.pad(qkv_bias.reshape(4, 1, QKV_SHARD), ((0, 0), (0, 0), (0, PAD_SHARD - QKV_SHARD)))
    first, heads, mixed, lse, attn, after, arrived, picked, full_out = attend(
        x, mixed_weight, mods, qkv_bias, bias_out, column, row, slot_row, groups, mask
    )
    pull, grad_down, grad_rows, block_out, gate_two, grad_down_bias = feed(
        up, down, arrived, picked, bias_up.reshape(4, 1, D), bias_down, cot, after, mods, column,
        slot_column, slot_row,
    )
    grad_up, grad_up_bias, mid, grad_attn, grad_split, sums, grad_out_bias = unfeed(
        down, up, pull, grad_rows, arrived, after, cot, attn, mods, column, slot_column
    )
    triple, triple_sums = unattend(grad_attn, full_out, heads, lse, column, row, mask)
    grad_mixed, grad_in, first_sums = unproject(
        mixed_weight, triple, grad_split, first, mixed, x, mid, mods, column
    )
    triple_sums = triple_sums[:, 0, :QKV_SHARD].reshape(3 * D)
    mod_grads = jnp.concatenate(
        [first_sums[0], first_sums[1], sums[0], sums[1], sums[2], gate_two], axis=1
    )[:CROPS]
    mod_grads = mod_grads.reshape(CROPS, 4, -1).transpose(1, 0, 2)
    bias_grads = (
        triple_sums[:D], triple_sums[2 * D :], grad_out_bias, grad_up_bias, grad_down_bias,
    )
    bias_grads = jnp.concatenate([vector.reshape(4, -1) for vector in bias_grads], axis=1)
    wide = mod_grads.shape[2]
    bias_grads = jnp.pad(bias_grads, ((0, 0), (0, 5 * wide - 2304))).reshape(4, 5, wide)
    mod_grads = jnp.concatenate([mod_grads, bias_grads], axis=1)
    share_down, share_up, share_mixed, grad_ada, totals = scatter_all(
        grad_down, grad_up, grad_mixed, mod_grads, conds
    )
    share_down = lax.all_to_all(share_down, "fsdp", split_axis=1, concat_axis=0, tiled=True)
    bias_totals = totals[1:3].reshape(-1)
    grad_query, grad_value, grad_out, grad_ups, grad_downs = [
        bias_totals[low:high] for low, high in zip(edges[:-1], edges[1:])
    ]
    return (
        block_out[None],
        grad_in[None],
        grad_ada,
        totals[0],
        share_mixed[:, :QKV_SHARD],
        grad_query,
        grad_value,
        share_mixed[:, QKV_SHARD:],
        grad_out,
        share_up,
        grad_ups,
        share_down,
        grad_downs,
    )


def layer_norm(values):
    center = values - jnp.mean(values, axis=-1, keepdims=True)
    variance = jnp.mean(center * center, axis=-1, keepdims=True)
    inverse = lax.rsqrt(variance + epsilon)
    return (center * inverse, inverse)


def norm_back(grad_normed, normed, inverse):
    first_mean = jnp.mean(grad_normed, axis=-1, keepdims=True)
    second_mean = jnp.mean(grad_normed * normed, axis=-1, keepdims=True)
    return inverse * (grad_normed - first_mean - normed * second_mean)


def attention_scores(query_part, key_part, allowed, factor):
    raw_scores = (
        jnp.einsum("qhd,khd->hqk", query_part, key_part, preferred_element_type=jnp.float32)
        * factor
    )
    return jnp.where(allowed[None], raw_scores, -1e30)


def gelu_tanh(values):
    return jax.nn.gelu(values, approximate=True)


def shards(
    block_in,
    condition,
    lengths,
    head_mask,
    group_mask,
    buffer_slot,
    ada_weight,
    ada_bias,
    qkv_weight,
    query_bias,
    value_bias,
    out_weight,
    out_bias,
    up_weight,
    up_bias,
    down_weight,
    down_bias,
    cotangent,
):
    peers = lax.axis_size("dp")
    mates = lax.axis_size("fsdp")

    def gather_matrix(shard):
        stacked = lax.all_gather(shard, ("dp", "fsdp"), axis=0, tiled=False)
        rows, columns = shard.shape
        stacked = stacked.reshape(peers, mates, rows, columns).transpose(0, 2, 1, 3)
        return stacked.reshape(peers * rows, mates * columns)

    full_qkv, full_out, full_up, full_down = [
        gather_matrix(shard) for shard in (qkv_weight, out_weight, up_weight, down_weight)
    ]
    vectors = (query_bias, value_bias, out_bias, up_bias, down_bias)
    packed_bias = lax.all_gather(jnp.concatenate(vectors), "fsdp", axis=0, tiled=False)
    edges = [0]
    for vector in vectors:
        edges.append(edges[-1] + vector.shape[0])
    bias_query, bias_value, bias_out, bias_up, bias_down = [
        packed_bias[:, low:high].reshape(-1).astype(jnp.float32)
        for low, high in zip(edges[:-1], edges[1:])
    ]
    inputs = block_in[0].astype(jnp.float32)
    crop_length = lengths[0]
    finish = jnp.cumsum(crop_length)
    opening = finish - crop_length
    position = jnp.arange(TOK_DEV, dtype=jnp.int32)
    member = (
        (position[:, None] >= opening[None, :]) & (position[:, None] < finish[None, :])
    ).astype(jnp.float32)
    segment = jnp.sum((position[:, None] >= finish[None, :]).astype(jnp.int32), axis=1)
    cond_act = jax.nn.silu(condition[0].astype(jnp.float32)).astype(jnp.bfloat16)
    crops = cond_act.shape[0]
    cond_all = lax.all_gather(cond_act, ("dp", "fsdp"), axis=0, tiled=True)
    depth = ada_weight.shape[0]
    cond_slice = lax.dynamic_slice_in_dim(cond_all, lax.axis_index("dp") * depth, depth, axis=1)
    partial_mod = jnp.dot(cond_slice, ada_weight, preferred_element_type=jnp.float32)
    column_mod = lax.psum_scatter(partial_mod, "dp", scatter_dimension=0, tiled=True)
    column_mod = column_mod + ada_bias.astype(jnp.float32)
    modulation = lax.all_to_all(column_mod, "fsdp", split_axis=0, concat_axis=1, tiled=True)
    pieces = [
        jnp.dot(member, modulation[:, number * D : (number + 1) * D], precision=highest)
        for number in range(6)
    ]
    shift_one, scale_one, gate_one, shift_two, scale_two, gate_two = pieces
    head_keep = jnp.dot(member, head_mask[0].astype(jnp.float32), precision=highest)
    group_keep = jnp.dot(member, group_mask[0].astype(jnp.float32), precision=highest)
    normed_one, inverse_one = layer_norm(inputs)
    first_in = (normed_one * (1.0 + scale_one) + shift_one).astype(jnp.bfloat16)
    qkv_bias = jnp.concatenate([bias_query, jnp.zeros_like(bias_query), bias_value])
    triple = (jnp.dot(first_in, full_qkv, preferred_element_type=jnp.float32) + qkv_bias).astype(
        jnp.bfloat16
    )
    queries = triple[:, :D].reshape(TOK_DEV, HEADS, HEAD_DIM)
    keys_all = triple[:, D : 2 * D].reshape(TOK_DEV, HEADS, HEAD_DIM)
    values_all = triple[:, 2 * D :].reshape(TOK_DEV, HEADS, HEAD_DIM)
    factor = HEAD_DIM ** (-0.5)
    row_block = min(768, TOK_DEV)
    group_size = min(4, HEADS)
    log_totals = {}
    head_parts = []
    for head_start in range(0, HEADS, group_size):
        heads_here = slice(head_start, head_start + group_size)
        row_start = 0
        rows_here = slice(row_start, row_start + row_block)
        allowed = segment[:, None] == segment[None, :]
        scores = attention_scores(
            queries[rows_here, heads_here], keys_all[:, heads_here], allowed, factor
        )
        row_max = jnp.max(scores, axis=-1, keepdims=True)
        log_total = row_max + jnp.log(jnp.sum(jnp.exp(scores - row_max), axis=-1, keepdims=True))
        weights_low = jnp.exp(scores - log_total).astype(jnp.bfloat16)
        row_parts = jnp.einsum(
            "hqk,khd->qhd",
            weights_low,
            values_all[:, heads_here],
            preferred_element_type=jnp.float32,
        )
        log_totals[head_start, row_start] = log_total
        head_parts.append(row_parts)
    attended = jnp.concatenate(head_parts, axis=1)
    mixed = (attended * head_keep[:, :, None]).astype(jnp.bfloat16).reshape(TOK_DEV, D)
    attn_out = jnp.dot(mixed, full_out, preferred_element_type=jnp.float32) + bias_out
    after_attn = inputs + gate_one * attn_out
    normed_two, inverse_two = layer_norm(after_attn)
    second_in = (normed_two * (1.0 + scale_two) + shift_two).astype(jnp.bfloat16)
    keep = (buffer_slot[0] >= 0).astype(jnp.float32)[:, None]
    places = 2 * TOK_DEV // 3
    chooser = (buffer_slot[0][:, None] == jnp.arange(places, dtype=jnp.int32)[None, :]).astype(
        jnp.bfloat16
    )
    arrived = jnp.einsum(
        "tb,td->bd", chooser, second_in, preferred_element_type=jnp.float32
    ).astype(jnp.bfloat16)
    groups_float = jnp.einsum(
        "tb,tg->bg",
        chooser,
        group_keep.astype(jnp.bfloat16),
        preferred_element_type=jnp.float32,
    )
    channel_keep = jnp.repeat(groups_float, FF // GROUPS, axis=1)
    hidden = jnp.dot(arrived, full_up, preferred_element_type=jnp.float32) + bias_up
    active = (gelu_tanh(hidden) * channel_keep).astype(jnp.bfloat16)
    branch = (jnp.dot(active, full_down, preferred_element_type=jnp.float32) + bias_down).astype(
        jnp.bfloat16
    )
    branch_tok = jnp.einsum(
        "tb,bd->td", chooser, branch, preferred_element_type=jnp.float32
    )
    after_mlp = after_attn + gate_two * branch_tok
    block_out = after_mlp.astype(jnp.bfloat16)[None]
    grad_after = cotangent[0].astype(jnp.float32)
    grad_gate_two = grad_after * branch_tok
    grad_branch = (gate_two * keep * grad_after).astype(jnp.bfloat16)
    grad_rows = jnp.einsum(
        "tb,td->bd", chooser, grad_branch, preferred_element_type=jnp.float32
    ).astype(jnp.bfloat16)
    back_qkv, back_out, back_up, back_down = full_qkv, full_out, full_up, full_down
    grad_down_bias = jnp.sum(grad_rows.astype(jnp.float32), axis=0)
    grad_down = jnp.einsum("bf,bd->fd", active, grad_rows, preferred_element_type=jnp.float32)
    grad_active = jnp.einsum("bd,fd->bf", grad_rows, back_down, preferred_element_type=jnp.float32)
    gelu_pull = jax.vjp(gelu_tanh, hidden)[1]
    grad_hidden = gelu_pull(grad_active * channel_keep)[0].astype(jnp.bfloat16)
    grad_up_bias = jnp.sum(grad_hidden.astype(jnp.float32), axis=0)
    grad_up = jnp.einsum("bd,bf->df", arrived, grad_hidden, preferred_element_type=jnp.float32)
    grad_arrived = jnp.einsum(
        "bf,df->bd", grad_hidden, back_up, preferred_element_type=jnp.float32
    ).astype(jnp.bfloat16)
    grad_second = jnp.einsum(
        "tb,bd->td", chooser, grad_arrived, preferred_element_type=jnp.float32
    )
    grad_scale_two = grad_second * normed_two
    grad_mid = grad_after + norm_back(grad_second * (1.0 + scale_two), normed_two, inverse_two)
    grad_gate_one = grad_mid * attn_out
    grad_attn = (gate_one * grad_mid).astype(jnp.bfloat16)
    grad_out_bias = jnp.sum(grad_attn.astype(jnp.float32), axis=0)
    grad_out = jnp.einsum("te,tf->ef", mixed, grad_attn, preferred_element_type=jnp.float32)
    grad_mixed = jnp.einsum(
        "tf,ef->te", grad_attn, back_out, preferred_element_type=jnp.float32
    ).astype(jnp.bfloat16)
    grad_attended = (
        grad_mixed.reshape(TOK_DEV, HEADS, HEAD_DIM).astype(jnp.float32) * head_keep[:, :, None]
    ).astype(jnp.bfloat16)
    query_heads = []
    key_heads = []
    value_heads = []
    for head_start in range(0, HEADS, group_size):
        heads_here = slice(head_start, head_start + group_size)
        row_start = 0
        rows_here = slice(row_start, row_start + row_block)
        allowed = segment[:, None] == segment[None, :]
        scores = attention_scores(
            queries[rows_here, heads_here], keys_all[:, heads_here], allowed, factor
        )
        probs = jnp.exp(scores - log_totals[head_start, row_start])
        grad_piece = grad_attended[rows_here, heads_here]
        grad_values = jnp.einsum(
            "hqk,qhd->khd",
            probs.astype(jnp.bfloat16),
            grad_piece,
            preferred_element_type=jnp.float32,
        )
        grad_probs = jnp.einsum(
            "qhd,khd->hqk",
            grad_piece,
            values_all[:, heads_here],
            preferred_element_type=jnp.float32,
        )
        grad_scores = (
            probs * (grad_probs - jnp.sum(probs * grad_probs, axis=-1, keepdims=True))
        ).astype(jnp.bfloat16)
        query_rows = (
            jnp.einsum(
                "hqk,khd->qhd",
                grad_scores,
                keys_all[:, heads_here],
                preferred_element_type=jnp.float32,
            )
            * factor
        )
        grad_keys = (
            jnp.einsum(
                "hqk,qhd->khd",
                grad_scores,
                queries[rows_here, heads_here],
                preferred_element_type=jnp.float32,
            )
            * factor
        )
        query_heads.append(query_rows)
        key_heads.append(grad_keys)
        value_heads.append(grad_values)
    grad_triple = jnp.concatenate(
        [
            jnp.concatenate(query_heads, axis=1).reshape(TOK_DEV, D),
            jnp.concatenate(key_heads, axis=1).reshape(TOK_DEV, D),
            jnp.concatenate(value_heads, axis=1).reshape(TOK_DEV, D),
        ],
        axis=1,
    ).astype(jnp.bfloat16)
    grad_query_bias = jnp.sum(grad_triple[:, :D].astype(jnp.float32), axis=0)
    grad_value_bias = jnp.sum(grad_triple[:, 2 * D :].astype(jnp.float32), axis=0)
    grad_qkv = jnp.einsum("td,te->de", first_in, grad_triple, preferred_element_type=jnp.float32)
    grad_first = jnp.einsum("te,de->td", grad_triple, back_qkv, preferred_element_type=jnp.float32)
    grad_scale_one = grad_first * normed_one
    grad_inputs = grad_mid + norm_back(grad_first * (1.0 + scale_one), normed_one, inverse_one)
    token_grads = [
        grad_first,
        grad_scale_one,
        grad_gate_one,
        grad_second,
        grad_scale_two,
        grad_gate_two,
    ]
    grad_modulation = jnp.concatenate(
        [jnp.einsum("ts,td->sd", member, single, precision=highest) for single in token_grads],
        axis=1,
    )
    mod_columns = lax.all_to_all(
        grad_modulation, "fsdp", split_axis=1, concat_axis=0, tiled=True
    )
    mod_all = lax.all_gather(mod_columns, "dp", axis=0, tiled=True)
    grad_ada_bias = jnp.sum(mod_all, axis=0)
    grad_ada = jnp.einsum(
        "sd,se->de", cond_slice.astype(jnp.float32), mod_all, precision=highest
    )

    def scatter_matrix(full):
        rows, columns = full.shape[0] // peers, full.shape[1] // mates
        blocks = full.astype(jnp.bfloat16).reshape(peers, rows, mates, columns)
        blocks = blocks.transpose(0, 2, 1, 3).reshape(peers * mates * rows, columns)
        share = lax.psum_scatter(blocks, ("dp", "fsdp"), scatter_dimension=0, tiled=True)
        return share.astype(jnp.float32)

    shares = [scatter_matrix(full) for full in (grad_qkv, grad_out, grad_up, grad_down)]
    bias_grads = (grad_query_bias, grad_value_bias, grad_out_bias, grad_up_bias, grad_down_bias)
    packed = jnp.concatenate([vector.reshape(mates, -1) for vector in bias_grads], axis=1)
    packed = lax.psum_scatter(packed, "fsdp", scatter_dimension=0, tiled=True)
    packed = lax.psum(packed[0], "dp")
    totals = [packed[low:high] for low, high in zip(edges[:-1], edges[1:])]
    return (
        block_out,
        grad_inputs[None],
        grad_ada,
        grad_ada_bias,
        shares[0],
        totals[0],
        totals[1],
        shares[1],
        totals[2],
        shares[2],
        totals[3],
        shares[3],
        totals[4],
    )


def solution(mesh):
    placed = (
        P(("dp", "fsdp"), None, None),
        P(("dp", "fsdp"), None, None),
        P(("dp", "fsdp"), None),
        P(("dp", "fsdp"), None, None),
        P(("dp", "fsdp"), None, None),
        P(("dp", "fsdp"), None),
        P("dp", "fsdp"),
        P("fsdp"),
        P("dp", "fsdp"),
        P("fsdp"),
        P("fsdp"),
        P("dp", "fsdp"),
        P("fsdp"),
        P("dp", "fsdp"),
        P("fsdp"),
        P("dp", "fsdp"),
        P("fsdp"),
        P(("dp", "fsdp"), None, None),
    )
    on_block = dict(mesh.shape) == {"dp": 8, "fsdp": 4}
    return jax.shard_map(
        block_shards if on_block else shards,
        mesh=mesh,
        in_specs=placed,
        out_specs=(
            P(("dp", "fsdp"), None, None),
            P(("dp", "fsdp"), None, None),
            P("dp", "fsdp"),
            P("fsdp"),
            P("dp", "fsdp"),
            P("fsdp"),
            P("fsdp"),
            P("dp", "fsdp"),
            P("fsdp"),
            P("dp", "fsdp"),
            P("fsdp"),
            P("dp", "fsdp"),
            P("fsdp"),
        ),
        check_vma=False,
    )
```

```python
import math

import jax
import jax.numpy as jnp
from jax import lax
from jax.experimental import pallas as pl
from jax.experimental.pallas import tpu as pltpu
from jax.sharding import PartitionSpec as P

D = 1152
HEADS = 16
HEAD_DIM = 72
FF = 4608
GROUPS = 16
TOK_DEV = 768


highest = lax.Precision.HIGHEST
epsilon = 1e-06


NT = (((1,), (1,)), ((), ()))
TN = (((0,), (0,)), ((), ()))
NN = (((1,), (0,)), ((), ()))
PLACES = 512
BLOCK = 256
BF16, F32 = jnp.bfloat16, jnp.float32
SOFT = HEAD_DIM**-0.5 * math.log2(math.e)
QKV_SHARD, OUT_SHARD, PAD_SHARD = 864, 288, 896
VMEM_BYTES = 60 * 2**20


def dot(left, right, dims=NN):
    return lax.dot_general(left, right, dims, preferred_element_type=F32)


def rows_at(i):
    return pl.ds(pl.multiple_of(i * BLOCK, BLOCK), BLOCK)


def per_crop(table, segment):
    return jnp.where(
        segment == 0, table[0:1], jnp.where(segment == 1, table[1:2], table[2:3])
    )


def normalise(values):
    center = values - jnp.mean(values, axis=1, keepdims=True)
    variance = jnp.mean(center * center, axis=1, keepdims=True)
    inverse = lax.rsqrt(variance + epsilon)
    return center * inverse, inverse


def crop_sums(segment, values):
    lanes = lax.broadcasted_iota(jnp.int32, (values.shape[0], 128), 1)
    member = (lanes == segment).astype(BF16)
    high = values.astype(BF16)
    low = (values - high.astype(F32)).astype(BF16)
    return (dot(member, high, TN) + dot(member, low, TN))[:8]


def crop_mask(bias_ref, column_ref, row_ref):
    for i in range(TOK_DEV // BLOCK):
        here = pl.ds(i * BLOCK, BLOCK)
        bias_ref[here, :] = jnp.where(column_ref[here, :] == row_ref[...], 0.0, -1e30).astype(F32)


def places_of(slot_row, i):
    place = lax.broadcasted_iota(jnp.int32, (BLOCK, TOK_DEV), 0) + i * BLOCK
    return (place == slot_row).astype(BF16)


def tokens_of(slot_column):
    place = lax.broadcasted_iota(jnp.int32, (BLOCK, PLACES), 1)
    return (place == slot_column).astype(BF16)


def head_keep(mask_ref, h, segment):
    return jnp.where(
        segment == 0, mask_ref[h, 0], jnp.where(segment == 1, mask_ref[h, 1], mask_ref[h, 2])
    )


MESH = pl.DeviceIdType.MESH
SHARD = 144
UPPER = 80


class Place:
    def __init__(self):
        dp, fsdp = lax.axis_index("dp"), lax.axis_index("fsdp")
        self.z, self.x = lax.div(dp, 2), lax.rem(dp, 2)
        self.y, self.c = lax.div(fsdp, 2), lax.rem(fsdp, 2)
        z = self.z
        self.zs = (z, z + 1 - 2 * lax.rem(z, 2), lax.rem(z + 2, 4), 3 - z)
        self.mates = (
            self.device(c=1 - self.c),
            self.device(y=1 - self.y),
            self.device(y=1 - self.y, c=1 - self.c),
        )
        self.mate_index = (
            2 * self.y + 1 - self.c,
            2 * (1 - self.y) + self.c,
            2 * (1 - self.y) + 1 - self.c,
        )
        self.index = 2 * self.y + self.c
        self.peer = 2 * z + self.x

    def device(self, z=None, x=None, y=None, c=None):
        z, x = self.z if z is None else z, self.x if x is None else x
        y, c = self.y if y is None else y, self.c if c is None else c
        return (2 * z + x, 2 * y + c)

    def meet(self):
        barrier = pltpu.get_barrier_semaphore()
        others = [self.device(z=self.zs[k]) for k in (1, 2, 3)]
        others += [self.device(z=self.zs[k], x=1 - self.x) for k in range(4)]
        others += self.mates
        for other in others:
            pl.semaphore_signal(barrier, inc=1, device_id=other, device_id_type=MESH)
        pl.semaphore_wait(barrier, len(others))


class Copies:
    def __init__(self, send_sems, recv_sems):
        self.send_sems, self.recv_sems, self.made = send_sems, recv_sems, []

    def make(self, source, target, device):
        index = len(self.made)
        copy = pltpu.make_async_remote_copy(
            src_ref=source,
            dst_ref=target,
            send_sem=self.send_sems.at[index],
            recv_sem=self.recv_sems.at[index],
            device_id=device,
            device_id_type=MESH,
        )
        self.made.append(copy)
        return copy


GATHER_COPIES = 35


class Gather:
    def __init__(self, place, source, slot, send_sems, recv_sems, local_sem, swap):
        x, y, c, zs = place.x, place.y, place.c, place.zs
        self.copies = Copies(send_sems, recv_sems)
        make = self.copies.make
        first, second = (SHARD - UPPER, UPPER) if swap else (0, UPPER)
        upper = pl.ds(first, second)
        lower = pl.ds(0, SHARD - UPPER) if swap else pl.ds(UPPER, SHARD - UPPER)
        over_x, over_y, beside = (
            place.device(x=1 - x),
            place.device(y=1 - y),
            place.device(c=1 - c),
        )
        own = [slot(y, c, zs[k], x) for k in range(4)]
        held = [source] + own[1:]
        from_x = [slot(y, c, zs[k], 1 - x) for k in range(4)]
        from_y = [slot(1 - y, c, zs[k], x) for k in range(4)]
        across = [slot(1 - y, c, zs[k], 1 - x) for k in range(4)]
        self.local = pltpu.make_async_copy(source, own[0], local_sem)
        self.along = [None] + [make(source, own[0], place.device(z=zs[k])) for k in (1, 2, 3)]
        self.to_x = [make(held[k], own[k], over_x) for k in range(4)]
        self.to_y = [make(held[k], own[k], over_y) for k in range(4)]
        self.x_to_y = [make(s.at[upper], s.at[upper], over_y) for s in from_x]
        self.y_to_x = [make(s.at[lower], s.at[lower], over_x) for s in from_y]
        self.pair = [make(held[k], own[k], beside) for k in range(4)]
        self.pair_x = [make(s, s, beside) for s in from_x]
        self.pair_y = [make(s, s, beside) for s in from_y]
        self.pair_across = [make(s, s, beside) for s in across]

    def start(self):
        self.along[1].start()
        self.to_x[0].start()
        self.to_y[0].start()
        self.along[2].start()
        self.along[3].start()
        self.pair[0].start()
        self.local.start()

    def pass_along(self, k):
        self.along[k].wait_recv()
        self.to_x[k].start()
        self.to_y[k].start()
        self.pair[k].start()

    def pass_across(self, k):
        self.to_x[k].wait_recv()
        self.x_to_y[k].start()
        self.pair_x[k].start()
        self.to_y[k].wait_recv()
        self.y_to_x[k].start()
        self.pair_y[k].start()

    def pass_pair(self, k):
        self.x_to_y[k].wait_recv()
        self.y_to_x[k].wait_recv()
        self.pair_across[k].start()

    def finish(self):
        self.local.wait()
        for copy in self.pair + self.pair_x + self.pair_y + self.pair_across:
            copy.wait_recv()
        for copy in self.copies.made:
            copy.wait_send()


class Column:
    def __init__(self, place, source, column, send_sems, recv_sems, local_sem):
        copies = Copies(send_sems, recv_sems)
        self.local = pltpu.make_async_copy(source, column.at[place.z], local_sem)
        self.along = [
            copies.make(source, column.at[place.z], place.device(z=place.zs[k])) for k in (1, 2, 3)
        ]

    def start(self):
        for copy in self.along:
            copy.start()
        self.local.start()

    def finish(self):
        for copy in self.along:
            copy.wait()
        self.local.wait()


SPREAD_COPIES = 32


class Spread:
    def __init__(self, place, column, slot, send_sems, recv_sems, local_sems):
        x, y, c, zs = place.x, place.y, place.c, place.zs
        self.copies = Copies(send_sems, recv_sems)
        make = self.copies.make
        upper, lower = pl.ds(0, UPPER), pl.ds(UPPER, SHARD - UPPER)
        over_x, over_y, beside = place.device(x=1 - x), place.device(y=1 - y), place.mates[0]
        four = range(4)
        held = [column.at[zs[k]] for k in four]
        own = [slot(y, c, zs[k], x) for k in four]
        from_x = [slot(y, c, zs[k], 1 - x) for k in four]
        from_y = [slot(1 - y, c, zs[k], x) for k in four]
        across = [slot(1 - y, c, zs[k], 1 - x) for k in four]
        first = [upper, lower, upper, lower]
        second = [lower, upper, lower, upper]
        self.local = [pltpu.make_async_copy(held[k], own[k], local_sems.at[k]) for k in four]
        self.to_x = [make(held[k], own[k], over_x) for k in four]
        self.to_y = [make(held[k], own[k], over_y) for k in four]
        self.x_to_y = [make(from_x[k].at[first[k]], from_x[k].at[first[k]], over_y) for k in four]
        self.y_to_x = [make(from_y[k].at[second[k]], from_y[k].at[second[k]], over_x) for k in four]
        self.pair = [make(held[k], own[k], beside) for k in four]
        self.pair_x = [make(s, s, beside) for s in from_x]
        self.pair_y = [make(s, s, beside) for s in from_y]
        self.pair_across = [make(s, s, beside) for s in across]

    def start(self):
        for k in range(4):
            self.to_x[k].start()
            self.to_y[k].start()
        for k in range(4):
            self.pair[k].start()
            self.local[k].start()

    def pass_across(self, k):
        self.to_x[k].wait_recv()
        self.x_to_y[k].start()
        self.pair_x[k].start()
        self.to_y[k].wait_recv()
        self.y_to_x[k].start()
        self.pair_y[k].start()

    def pass_pair(self, k):
        self.x_to_y[k].wait_recv()
        self.y_to_x[k].wait_recv()
        self.pair_across[k].start()

    def finish(self):
        for copy in self.local:
            copy.wait()
        for copy in self.pair + self.pair_x + self.pair_y + self.pair_across:
            copy.wait_recv()
        for copy in self.copies.made:
            copy.wait_send()


SCATTER_COPIES = 24


class Scatter:
    def __init__(self, place, parts, bufs, column, send_sems, recv_sems):
        x, y, zs = place.x, place.y, place.zs
        self.place, self.parts, self.column = place, parts, column
        self.by_x, self.by_y, self.from_x, self.from_y = [bufs.at[k] for k in range(4)]
        self.copies = Copies(send_sems, recv_sems)
        make = self.copies.make
        self.upper, self.lower = (0, UPPER), (UPPER, SHARD - UPPER)
        a, b = pl.ds(*self.upper), pl.ds(*self.lower)
        over_x, over_y = place.device(x=1 - x), place.device(y=1 - y)
        four = range(4)
        self.across_y = [
            make(parts.at[1 - y, zs[k], 1 - x, a], self.by_y.at[k, a], over_y) for k in four
        ]
        self.across_x = [
            make(parts.at[1 - y, zs[k], 1 - x, b], self.by_x.at[k, b], over_x) for k in four
        ]
        self.x_lower = [make(parts.at[y, zs[k], 1 - x, b], self.from_x.at[k, b], over_x) for k in four]
        self.y_upper = [make(parts.at[1 - y, zs[k], x, a], self.from_y.at[k, a], over_y) for k in four]
        self.x_upper = [make(self.by_y.at[k, a], self.from_x.at[k, a], over_x) for k in four]
        self.y_lower = [make(self.by_x.at[k, b], self.from_y.at[k, b], over_y) for k in four]

    def start(self, k):
        self.across_y[k].start()
        self.across_x[k].start()

    def follow(self, k):
        self.x_lower[k].start()
        self.y_upper[k].start()

    def add(self, target, k, index, rows):
        for at in range(0, rows[1], 16):
            here = pl.ds(rows[0] + at, 16)
            total = self.parts[(*index, here)].astype(F32) + target[k, here].astype(F32)
            target[k, here] = total.astype(BF16)

    def pass_across(self, k):
        x, y, z = self.place.x, self.place.y, self.place.zs[k]
        self.across_y[k].wait_recv()
        self.add(self.by_y, k, (y, z, 1 - x), self.upper)
        self.x_upper[k].start()
        self.across_x[k].wait_recv()
        self.add(self.by_x, k, (1 - y, z, x), self.lower)
        self.y_lower[k].start()

    def collect(self, k):
        x, y, z = self.place.x, self.place.y, self.place.zs[k]
        for copy in (self.x_upper[k], self.x_lower[k], self.y_upper[k], self.y_lower[k]):
            copy.wait_recv()
        for at in range(0, SHARD, 16):
            here = pl.ds(at, 16)
            total = self.parts[y, z, x, here].astype(F32) + self.from_x[k, here].astype(F32)
            self.column[k, here] = (total + self.from_y[k, here].astype(F32)).astype(BF16)

    def finish(self):
        for copy in self.copies.made:
            copy.wait_send()


class Along:
    def __init__(self, place, column, from_z, out, send_sems, recv_sems):
        copies = Copies(send_sems, recv_sems)
        self.column, self.from_z, self.out = column, from_z, out
        self.copies = [
            copies.make(column.at[k], from_z.at[k - 1], place.device(z=place.zs[k])) for k in (1, 2, 3)
        ]

    def start(self, k):
        self.copies[k - 1].start()

    def close(self):
        for copy in self.copies:
            copy.wait()
        for at in range(0, SHARD, 16):
            here = pl.ds(at, 16)
            total = self.column[0, here].astype(F32)
            for k in range(3):
                total = total + self.from_z[k, here].astype(F32)
            self.out[here] = total


ORDER = (1, 2, 3, 0)
DMA = pltpu.SemaphoreType.DMA


def add_rows(target, rows, left, right):
    def body(i, carry):
        here = pl.ds(pl.multiple_of(16 * i, 16), 16)
        target(here, (left(here).astype(F32) + right(here).astype(F32)).astype(BF16))
        return carry

    lax.fori_loop(0, rows // 16, body, 0)


class Pair:
    def __init__(self, place, buffers, parts, send_sems, recv_sems):
        self.place, self.buffers, self.parts = place, buffers, parts
        self.send_sems, self.recv_sems = send_sems, recv_sems

    def copy(self, m):
        y = lax.div(m, 2)
        return pltpu.make_async_remote_copy(
            src_ref=self.buffers.at[lax.rem(m, 2)],
            dst_ref=self.parts.at[y],
            send_sem=self.send_sems.at[y],
            recv_sem=self.recv_sems.at[y],
            device_id=self.place.mates[0],
            device_id_type=MESH,
        )

    def send(self, m):
        @pl.when(lax.rem(m, 2) != self.place.c)
        def _():
            self.copy(m).start()

    def free(self, m):
        @pl.when(lax.rem(m, 2) != self.place.c)
        def _():
            self.copy(m).wait_send()

    def take(self, m):
        @pl.when(lax.rem(m, 2) == self.place.c)
        def _():
            y, buffer = lax.div(m, 2), lax.rem(m, 2)
            self.copy(m).wait_recv()

            def store(here, value):
                self.parts[y, here] = value

            add_rows(
                store, D, lambda here: self.buffers[buffer, here], lambda here: self.parts[y, here]
            )


def attend_kernel(
    x_ref, weight_ref, mods_ref, qkv_bias_ref, out_bias_ref, column_ref, row_ref, slot_ref,
    groups_ref, mask_ref, up_ref, down_ref,
    first_ref, heads_ref, mixed_ref, lse_ref, attn_ref, after_ref, arrived_ref, picked_ref, out_weight_ref,
    up_out, down_out,
    bias_ref, parts_ref, second_ref,
    send_sems, recv_sems, local_sems, down_send, down_recv, down_local,
):
    place = Place()
    place.meet()
    ups = Spread(
        place, up_ref, lambda y, c, z, x: up_out.at[y, c, z, x], send_sems, recv_sems, local_sems
    )
    downs = Column(place, down_ref, down_out, down_send, down_recv, down_local.at[0])
    ups.start()
    downs.start()
    crop_mask(bias_ref, column_ref, row_ref)

    def norm(i, carry):
        here = rows_at(i)
        segment = column_ref[here, :]
        normed, _ = normalise(x_ref[here, :].astype(F32))
        shift, scale = per_crop(mods_ref[0], segment), per_crop(mods_ref[1], segment)
        first_ref[here, :] = (normed * (1.0 + scale) + shift).astype(BF16)
        return carry

    lax.fori_loop(0, 3, norm, 0)
    for j in range(4):
        out_weight_ref[:, OUT_SHARD * j : OUT_SHARD * (j + 1)] = weight_ref[j, :, QKV_SHARD:]

    def project(i, carry):
        j = lax.div(i, 3)
        here = rows_at(lax.rem(i, 3))
        triple = (dot(first_ref[here, :], weight_ref[j, :, :PAD_SHARD]) + qkv_bias_ref[j]).astype(BF16)
        zero = jnp.zeros((BLOCK, 128 - HEAD_DIM), BF16)
        for h in range(12):
            part = triple[:, HEAD_DIM * h : HEAD_DIM * (h + 1)]
            heads_ref[12 * j + h, here, :] = jnp.concatenate([part, zero], axis=1)
        return carry

    lax.fori_loop(0, 12, project, 0)

    def head(h, carry):
        for k in range(4):

            @pl.when(h == 7 + k)
            def _():
                ups.pass_across(k)

        keys, values = heads_ref[16 + h], heads_ref[32 + h]
        for i in range(3):
            here = pl.ds(i * BLOCK, BLOCK)
            scores = dot(heads_ref[h, here, :], keys, NT) * SOFT + bias_ref[here, :]
            top = jnp.max(scores, axis=1, keepdims=True)
            weights = jnp.exp2(scores - top)
            total = jnp.sum(weights, axis=1, keepdims=True)
            keep = head_keep(mask_ref, h, column_ref[here, :])
            parts_ref[h, here, :] = (dot(weights.astype(BF16), values) * (keep / total)).astype(BF16)
            spread = jnp.broadcast_to(top + jnp.log2(total), (BLOCK, 128))
            lse_ref[h, :, here] = jnp.transpose(spread)[:1, :]
        return carry

    lax.fori_loop(0, HEADS, head, 0)
    for h in range(HEADS):
        mixed_ref[:, HEAD_DIM * h : HEAD_DIM * (h + 1)] = parts_ref[h][:, :HEAD_DIM]
    for k in range(4):
        ups.pass_pair(k)

    def close(i, carry):
        here = rows_at(i)
        segment = column_ref[here, :]
        attn = dot(mixed_ref[here, :], out_weight_ref[...]) + out_bias_ref[...]
        attn_ref[here, :] = attn.astype(BF16)
        after = x_ref[here, :].astype(F32) + per_crop(mods_ref[2], segment) * attn
        after_ref[here, :] = after
        normed, _ = normalise(after)
        shift, scale = per_crop(mods_ref[3], segment), per_crop(mods_ref[4], segment)
        second_ref[here, :] = (normed * (1.0 + scale) + shift).astype(BF16)
        return carry

    lax.fori_loop(0, 3, close, 0)
    for i in range(2):
        here = pl.ds(i * BLOCK, BLOCK)
        choice = places_of(slot_ref[...], i)
        arrived_ref[here, :] = dot(choice, second_ref[...]).astype(BF16)
        picked_ref[here, :] = dot(choice, groups_ref[...]).astype(BF16)
    ups.finish()
    downs.finish()


def shape_of(*shape, dtype=BF16):
    return jax.ShapeDtypeStruct(shape, dtype)


def talking(number):
    return pltpu.CompilerParams(
        collective_id=number, has_side_effects=True, vmem_limit_bytes=VMEM_BYTES
    )


IN_VMEM = pl.BlockSpec(memory_space=pltpu.VMEM)
IN_SMEM = pl.BlockSpec(memory_space=pltpu.SMEM)
ANYWHERE = pl.BlockSpec(memory_space=pl.ANY)


def attend(x, weight, mods, qkv_bias, out_bias, column, row, slot_row, groups, mask, up, down):
    return pl.pallas_call(
        attend_kernel,
        out_shape=[
            shape_of(TOK_DEV, D),
            shape_of(3 * HEADS, TOK_DEV, 128),
            shape_of(TOK_DEV, D),
            shape_of(HEADS, 1, TOK_DEV, dtype=F32),
            shape_of(TOK_DEV, D),
            shape_of(TOK_DEV, D, dtype=F32),
            shape_of(PLACES, D),
            shape_of(PLACES, 128),
            shape_of(D, D),
            shape_of(2, 2, 4, 2, SHARD, D),
            shape_of(4, SHARD, D),
        ],
        in_specs=[IN_VMEM] * 9 + [IN_SMEM] + [ANYWHERE] * 2,
        out_specs=[IN_VMEM] * 9 + [ANYWHERE] * 2,
        scratch_shapes=[
            pltpu.VMEM((TOK_DEV, TOK_DEV), F32),
            pltpu.VMEM((HEADS, TOK_DEV, 128), BF16),
            pltpu.VMEM((TOK_DEV, D), BF16),
            DMA((SPREAD_COPIES,)),
            DMA((SPREAD_COPIES,)),
            DMA((4,)),
            DMA((3,)),
            DMA((3,)),
            DMA((1,)),
        ],
        compiler_params=talking(2),
    )(x, weight, mods, qkv_bias, out_bias, column, row, slot_row, groups, mask, up, down)


ROOT = math.sqrt(2.0 / math.pi)


def feed_kernel(
    up_ref, arrived_ref, picked_ref, up_bias_ref, down_bias_ref, cot_ref, after_ref,
    mods_ref, column_ref, slot_column_ref, slot_row_ref, down_ref,
    pull_ref, grad_rows_ref, block_out_ref, gate_ref, bias_ref, parts_ref, down_out,
    active_ref, total_ref, branch_ref, buffers_ref, halves_ref, tiles_ref,
    send_sems, recv_sems, local_sems, pair_send, pair_recv, tile_sems,
):
    step = pl.program_id(0)
    place = Place()
    downs = Spread(
        place, down_ref, lambda y, c, z, x: down_out.at[z, x, y, c], send_sems, recv_sems, local_sems
    )

    def rows_of(x, y, c):
        return pl.ds(pl.multiple_of((4 * x + 2 * y + c) * SHARD, 16), SHARD)

    def pair(m, x, y):
        return pltpu.make_async_remote_copy(
            src_ref=buffers_ref.at[lax.rem(m, 2), rows_of(x, y, 1 - place.c)],
            dst_ref=halves_ref.at[y, m, x],
            send_sem=pair_send.at[m, x, y],
            recv_sem=pair_recv.at[m, x, y],
            device_id=place.mates[0],
            device_id_type=MESH,
        )

    def take(m):
        for x in range(2):
            for y in range(2):
                pair(m, x, y).wait_recv()
                own = rows_of(x, y, place.c)
                mine = buffers_ref.at[lax.rem(m, 2), own]
                for at in range(0, SHARD, 16):
                    here = pl.ds(at, 16)
                    total = mine[here].astype(F32) + halves_ref[y, m, x, here].astype(F32)
                    parts_ref[y, m, x, here] = total.astype(BF16)

    def free(m):
        for x in range(2):
            for y in range(2):
                pair(m, x, y).wait_send()

    def tile(m):
        return [
            pltpu.make_async_copy(
                down_out.at[m, x, y],
                tiles_ref.at[lax.rem(m, 2), x, y],
                tile_sems.at[lax.rem(m, 2), x, y],
            )
            for x in range(2)
            for y in range(2)
        ]

    @pl.when(step == 0)
    def _():
        place.meet()
        downs.start()
        for i in range(3):
            here = pl.ds(i * BLOCK, BLOCK)
            gate = per_crop(mods_ref[5], column_ref[here, :])
            block_out_ref[here, :] = (gate * cot_ref[here, :].astype(F32)).astype(BF16)
        for i in range(2):
            here = pl.ds(i * BLOCK, BLOCK)
            choice = places_of(slot_row_ref[...], i)
            grad_rows_ref[here, :] = dot(choice, block_out_ref[...]).astype(BF16)
        bias_ref[...] = jnp.sum(grad_rows_ref[...].astype(F32), axis=0, keepdims=True)
        total_ref[...] = jnp.zeros_like(total_ref)

    @pl.when(step < 4)
    def _():
        group = lax.broadcasted_iota(jnp.int32, (128, D), 0) - 4 * step
        unit = lax.broadcasted_iota(jnp.int32, (128, D), 1)
        width = FF // GROUPS
        spread = ((unit >= group * width) & (unit < (group + 1) * width)).astype(BF16)
        for i in range(2):
            here = pl.ds(i * BLOCK, BLOCK)
            hidden = dot(arrived_ref[here, :], up_ref[0]) + up_bias_ref[0]
            keep = dot(picked_ref[here, :], spread)
            square = hidden * hidden
            curve = jnp.tanh(ROOT * hidden * (1.0 + 0.044715 * square))
            half = 0.5 * (1.0 + curve)
            slope = half + 0.5 * hidden * (1.0 - curve * curve) * (
                ROOT * (1.0 + 3.0 * 0.044715 * square)
            )
            active_ref[step, here, :] = (hidden * half * keep).astype(BF16)
            pull_ref[0, here, :] = (slope * keep).astype(BF16)

        def grad(i, carry):
            here = pl.ds(pl.multiple_of(i * 384, 384), 384)
            part = dot(active_ref[step, :, here], grad_rows_ref[...], TN).astype(BF16)
            buffers_ref[lax.rem(step, 2), here, :] = part
            return carry

        @pl.when(step >= 2)
        def _():
            free(step - 2)

        lax.fori_loop(0, 3, grad, 0)
        for x in range(2):
            for y in range(2):
                pair(step, x, y).start()

    @pl.when((step >= 1) & (step < 5))
    def _():
        take(step - 1)

    @pl.when(step == 3)
    def _():
        for k in range(4):
            downs.pass_across(k)

    @pl.when(step == 4)
    def _():
        free(2)
        free(3)
        for k in range(4):
            downs.pass_pair(k)
        downs.finish()
        for m in (0, 1):
            for copy in tile(m):
                copy.start()

    @pl.when(step >= 4)
    def _():
        m = step - 4
        for copy in tile(m):
            copy.wait()
        weights = tiles_ref[lax.rem(m, 2)].reshape(D, D)
        for i in range(2):
            here = pl.ds(i * BLOCK, BLOCK)
            total_ref[here, :] += dot(active_ref[m, here, :], weights)

        @pl.when(m < 2)
        def _():
            for copy in tile(m + 2):
                copy.start()

    @pl.when(step == 7)
    def _():
        branch_ref[...] = (total_ref[...] + down_bias_ref[...]).astype(BF16)
        gates = jnp.zeros((8, D), F32)
        for i in range(3):
            here = pl.ds(i * BLOCK, BLOCK)
            segment = column_ref[here, :]
            branch = dot(tokens_of(slot_column_ref[here, :]), branch_ref[...])
            gate = per_crop(mods_ref[5], segment)
            block_out_ref[here, :] = (after_ref[here, :] + gate * branch).astype(BF16)
            gates = gates + crop_sums(segment, cot_ref[here, :].astype(F32) * branch)
        gate_ref[...] = gates


def whole(*shape):
    return pl.BlockSpec(shape, lambda i: (0,) * len(shape), pipeline_mode=pl.Buffered(1))


def feed(up, arrived, picked, up_bias, down_bias, cot, after, mods, column, slot_column, slot_row, down):
    early = lambda *tail: pl.BlockSpec((1, *tail), lambda i: (jnp.minimum(i, 3), 0, 0))
    return pl.pallas_call(
        feed_kernel,
        grid=(8,),
        out_shape=[
            shape_of(4, PLACES, D),
            shape_of(PLACES, D),
            shape_of(TOK_DEV, D),
            shape_of(8, D, dtype=F32),
            shape_of(1, D, dtype=F32),
            shape_of(2, 4, 2, SHARD, D),
            shape_of(4, 2, 2, 2, SHARD, D),
        ],
        in_specs=[
            early(D, D), whole(PLACES, D), whole(PLACES, 128), early(1, D), whole(1, D),
            whole(TOK_DEV, D), whole(TOK_DEV, D), whole(6, 8, D), whole(TOK_DEV, 1), whole(TOK_DEV, 1),
            whole(1, TOK_DEV), ANYWHERE,
        ],
        out_specs=[
            early(PLACES, D), whole(PLACES, D), whole(TOK_DEV, D), whole(8, D), whole(1, D),
            whole(2, 4, 2, SHARD, D), ANYWHERE,
        ],
        scratch_shapes=[
            pltpu.VMEM((4, PLACES, D), BF16),
            pltpu.VMEM((PLACES, D), F32),
            pltpu.VMEM((PLACES, D), BF16),
            pltpu.VMEM((2, D, D), BF16),
            pltpu.VMEM((2, 4, 2, SHARD, D), BF16),
            pltpu.VMEM((2, 2, 2, 2, SHARD, D), BF16),
            DMA((SPREAD_COPIES,)),
            DMA((SPREAD_COPIES,)),
            DMA((4,)),
            DMA((4, 2, 2)),
            DMA((4, 2, 2)),
            DMA((2, 2, 2)),
        ],
        compiler_params=talking(3),
    )(up, arrived, picked, up_bias, down_bias, cot, after, mods, column, slot_column, slot_row, down)


def unfeed_kernel(
    down_ref, up_ref, pull_ref, grad_rows_ref, arrived_ref, after_ref, cot_ref, attn_ref, mods_ref,
    column_ref, slot_column_ref, given_ref,
    up_bias_ref, mid_ref, grad_attn_ref, sums_ref, out_bias_ref, parts_out, plane_ref,
    hidden_ref, total_ref, back_ref, buffers_ref, parts_ref, bufs_ref,
    send_sems, recv_sems, pair_send, pair_recv, out_sem,
):
    step = pl.program_id(0)
    place = Place()
    scatter = Scatter(place, given_ref, bufs_ref, plane_ref, send_sems, recv_sems)
    pair = Pair(place, buffers_ref, parts_ref, pair_send, pair_recv)

    @pl.when(step == 0)
    def _():
        place.meet()
        for k in ORDER:
            scatter.start(k)
        total_ref[...] = jnp.zeros_like(total_ref)

    bias = jnp.zeros((1, D), F32)
    for i in range(2):
        here = pl.ds(i * BLOCK, BLOCK)
        grad = dot(grad_rows_ref[here, :], down_ref[0], NT) * pull_ref[0, here, :].astype(F32)
        low = grad.astype(BF16)
        hidden_ref[here, :] = low
        bias = bias + jnp.sum(low.astype(F32), axis=0, keepdims=True)
        total_ref[here, :] += dot(low, up_ref[0], NT)
    up_bias_ref[0] = bias

    def grad_of(i, carry):
        here = pl.ds(pl.multiple_of(i * 384, 384), 384)
        part = dot(arrived_ref[:, here], hidden_ref[...], TN).astype(BF16)
        buffers_ref[lax.rem(step, 2), here, :] = part
        return carry

    @pl.when(step >= 2)
    def _():
        pair.free(step - 2)

    lax.fori_loop(0, 3, grad_of, 0)
    pair.send(step)

    @pl.when(step >= 1)
    def _():
        pair.take(step - 1)

    @pl.when(step == 0)
    def _():
        for k in ORDER:
            scatter.follow(k)

    for here_step, ks in ((1, (1, 2)), (2, (3, 0))):

        @pl.when(step == here_step)
        def _():
            for k in ks:
                scatter.pass_across(k)

    @pl.when(step == 3)
    def _():
        back_ref[...] = total_ref[...].astype(BF16)
        shifts, scales = jnp.zeros((8, D), F32), jnp.zeros((8, D), F32)
        gates, out_bias = jnp.zeros((8, D), F32), jnp.zeros((1, D), F32)
        for i in range(3):
            here = pl.ds(i * BLOCK, BLOCK)
            segment = column_ref[here, :]
            second = dot(tokens_of(slot_column_ref[here, :]), back_ref[...])
            normed, inverse = normalise(after_ref[here, :])
            grad = second * (1.0 + per_crop(mods_ref[4], segment))
            mean = jnp.mean(grad, axis=1, keepdims=True)
            slant = jnp.mean(grad * normed, axis=1, keepdims=True)
            mid = cot_ref[here, :].astype(F32) + inverse * (grad - mean - normed * slant)
            mid_ref[here, :] = mid
            low = (per_crop(mods_ref[2], segment) * mid).astype(BF16)
            grad_attn_ref[here, :] = low
            out_bias = out_bias + jnp.sum(low.astype(F32), axis=0, keepdims=True)
            shifts = shifts + crop_sums(segment, second)
            scales = scales + crop_sums(segment, second * normed)
            gates = gates + crop_sums(segment, mid * attn_ref[here, :].astype(F32))
        sums_ref[0], sums_ref[1], sums_ref[2] = gates, shifts, scales
        out_bias_ref[...] = out_bias
        pair.free(2)
        pair.free(3)
        pair.take(3)
        leave = pltpu.make_async_copy(parts_ref, parts_out, out_sem.at[0])
        leave.start()
        for k in ORDER:
            scatter.collect(k)
        scatter.finish()
        leave.wait()


def unfeed(down, up, pull, grad_rows, arrived, after, cot, attn, mods, column, slot_column, given):
    block = lambda *tail: pl.BlockSpec((1, *tail), lambda i: (i, 0, 0))
    return pl.pallas_call(
        unfeed_kernel,
        grid=(4,),
        out_shape=[
            shape_of(4, 1, D, dtype=F32),
            shape_of(TOK_DEV, D, dtype=F32),
            shape_of(TOK_DEV, D),
            shape_of(3, 8, D, dtype=F32),
            shape_of(1, D, dtype=F32),
            shape_of(2, D, D),
            shape_of(4, SHARD, D),
        ],
        in_specs=[
            block(D, D), block(D, D), block(PLACES, D), whole(PLACES, D), whole(PLACES, D),
            whole(TOK_DEV, D), whole(TOK_DEV, D), whole(TOK_DEV, D), whole(6, 8, D), whole(TOK_DEV, 1),
            whole(TOK_DEV, 1), whole(2, 4, 2, SHARD, D),
        ],
        out_specs=[
            block(1, D), whole(TOK_DEV, D), whole(TOK_DEV, D), whole(3, 8, D), whole(1, D), ANYWHERE, whole(4, SHARD, D),
        ],
        scratch_shapes=[
            pltpu.VMEM((PLACES, D), BF16),
            pltpu.VMEM((PLACES, D), F32),
            pltpu.VMEM((PLACES, D), BF16),
            pltpu.VMEM((2, D, D), BF16),
            pltpu.VMEM((2, D, D), BF16),
            pltpu.VMEM((4, 4, SHARD, D), BF16),
            DMA((SCATTER_COPIES,)),
            DMA((SCATTER_COPIES,)),
            DMA((2,)),
            DMA((2,)),
            DMA((1,)),
        ],
        compiler_params=talking(4),
    )(down, up, pull, grad_rows, arrived, after, cot, attn, mods, column, slot_column, given)


def unattend_kernel(
    grad_ref, out_weight_ref, heads_ref, lse_ref, column_ref, row_ref, given_ref, plane_ref, mask_ref,
    triple_ref, sums_ref, share_ref, plane_out, split_ref,
    bias_ref, mixed_ref, grads_ref, key_ref, value_ref, bufs_ref, from_z_ref,
    send_sems, recv_sems, along_send, along_recv,
):
    place = Place()
    place.meet()
    scatter = Scatter(place, given_ref, bufs_ref, plane_out, send_sems, recv_sems)
    along = Along(place, plane_ref, from_z_ref, share_ref, along_send, along_recv)
    for k in ORDER:
        scatter.start(k)
    for k in (1, 2, 3):
        along.start(k)
    crop_mask(bias_ref, column_ref, row_ref)

    def spread(i, carry):
        here = rows_at(i)
        segment = column_ref[here, :]
        mixed = dot(grad_ref[here, :], out_weight_ref[...], NT)
        zero = jnp.zeros((BLOCK, 128 - HEAD_DIM), BF16)
        for h in range(HEADS):
            part = mixed[:, HEAD_DIM * h : HEAD_DIM * (h + 1)] * head_keep(mask_ref, h, segment)
            mixed_ref[h, here, :] = jnp.concatenate([part.astype(BF16), zero], axis=1)
        return carry

    lax.fori_loop(0, 3, spread, 0)
    factor = HEAD_DIM**-0.5

    def head(h, carry):
        @pl.when(h == 1)
        def _():
            for k in ORDER:
                scatter.follow(k)

        for at, k in enumerate(ORDER):

            @pl.when(h == 4 + at)
            def _():
                scatter.pass_across(k)

        keys, values = heads_ref[16 + h], heads_ref[32 + h]
        turned = jnp.transpose(keys)
        for i in range(3):
            here = pl.ds(i * BLOCK, BLOCK)
            queries, grads = heads_ref[h, here, :], mixed_ref[h, here, :]
            scores = dot(keys, queries, NT) * SOFT + bias_ref[:, here]
            probs = jnp.exp2(scores - lse_ref[h, :, here])
            product = probs * dot(values, grads, NT)
            total = jnp.sum(product, axis=0, keepdims=True)
            low = (product - probs * total).astype(BF16)
            for_values, for_keys = dot(probs.astype(BF16), grads), dot(low, queries)
            if i == 0:
                value_ref[...], key_ref[...] = for_values, for_keys
            else:
                value_ref[...] += for_values
                key_ref[...] += for_keys
            grads_ref[h, here, :] = jnp.transpose(dot(turned, low) * factor).astype(BF16)
        grads_ref[16 + h] = (key_ref[...] * factor).astype(BF16)
        grads_ref[32 + h] = value_ref[...].astype(BF16)
        return carry

    lax.fori_loop(0, HEADS, head, 0)
    for j in range(4):
        triple_ref[j, :, QKV_SHARD:] = jnp.zeros((TOK_DEV, PAD_SHARD - QKV_SHARD), BF16)
        for h in range(12):
            triple_ref[j, :, HEAD_DIM * h : HEAD_DIM * (h + 1)] = grads_ref[12 * j + h][:, :HEAD_DIM]
        sums_ref[j] = jnp.sum(triple_ref[j].astype(F32), axis=0, keepdims=True)
    for j in range(4):
        split_ref[j] = grad_ref[:, OUT_SHARD * j : OUT_SHARD * (j + 1)]
    along.close()
    for k in ORDER:
        scatter.collect(k)
    scatter.finish()


def unattend(grad_attn, out_weight, heads, lse, column, row, given, plane, mask):
    return pl.pallas_call(
        unattend_kernel,
        out_shape=[
            shape_of(4, TOK_DEV, PAD_SHARD),
            shape_of(4, 1, PAD_SHARD, dtype=F32),
            shape_of(SHARD, D, dtype=F32),
            shape_of(4, SHARD, D),
            shape_of(4, TOK_DEV, OUT_SHARD),
        ],
        in_specs=[IN_VMEM] * 8 + [IN_SMEM],
        out_specs=[IN_VMEM] * 5,
        scratch_shapes=[
            pltpu.VMEM((TOK_DEV, TOK_DEV), F32),
            pltpu.VMEM((HEADS, TOK_DEV, 128), BF16),
            pltpu.VMEM((3 * HEADS, TOK_DEV, 128), BF16),
            pltpu.VMEM((TOK_DEV, 128), F32),
            pltpu.VMEM((TOK_DEV, 128), F32),
            pltpu.VMEM((4, 4, SHARD, D), BF16),
            pltpu.VMEM((3, SHARD, D), BF16),
            DMA((SCATTER_COPIES,)),
            DMA((SCATTER_COPIES,)),
            DMA((3,)),
            DMA((3,)),
        ],
        compiler_params=talking(5),
    )(grad_attn, out_weight, heads, lse, column, row, given, plane, mask)


def unproject_kernel(
    weight_ref, triple_ref, split_ref, first_ref, mixed_ref, x_ref, mid_ref, mods_ref, column_ref,
    plane_up_ref, rest_ref, conds_ref,
    grad_in_ref, share_up_ref, share_ref, ada_ref, sums_ref,
    total_ref, buffers_ref, parts_ref, bufs_ref, plane_ref, up_z_ref, from_z_ref,
    mod_ref, mates_ref, packed_ref, every_ref,
    send_sems, recv_sems, pair_send, pair_recv, up_send, up_recv, along_send, along_recv,
    small_send, small_recv,
):
    step = pl.program_id(0)
    place = Place()
    pair = Pair(place, buffers_ref, parts_ref, pair_send, pair_recv)
    blocks = parts_ref.reshape(2, 4, 2, SHARD, D)
    scatter = Scatter(place, blocks, bufs_ref, plane_ref, send_sems, recv_sems)
    along_up = Along(place, plane_up_ref, up_z_ref, share_up_ref, up_send, up_recv)
    along = Along(place, plane_ref, from_z_ref, share_ref, along_send, along_recv)
    small = Copies(small_send, small_recv)
    to_mates = [
        small.make(mod_ref.at[other], mates_ref.at[place.index], mate)
        for other, mate in zip(place.mate_index, place.mates)
    ]
    to_z = [
        small.make(packed_ref, every_ref.at[place.peer], place.device(z=place.zs[k]))
        for k in (1, 2, 3)
    ]
    to_x = []
    for k in range(4):
        held = every_ref.at[2 * place.zs[k] + place.x]
        to_x.append(small.make(held, held, place.device(x=1 - place.x)))

    @pl.when(step == 0)
    def _():
        place.meet()
        for k in (1, 2, 3):
            along_up.start(k)

    @pl.when(step < 4)
    def _():
        def grad(i, carry):
            here = pl.ds(pl.multiple_of(i * 384, 384), 384)
            buffer = lax.rem(step, 2)
            part = dot(first_ref[:, here], triple_ref[0], TN).astype(BF16)
            buffers_ref[buffer, here, :PAD_SHARD] = part
            part = dot(mixed_ref[:, here], split_ref[0], TN).astype(BF16)
            buffers_ref[buffer, here, QKV_SHARD:] = part
            return carry

        @pl.when(step >= 2)
        def _():
            pair.free(step - 2)

        lax.fori_loop(0, 3, grad, 0)
        pair.send(step)

    @pl.when((step >= 1) & (step < 5))
    def _():
        pair.take(step - 1)

    @pl.when(step == 4)
    def _():
        pair.free(2)
        pair.free(3)
        for k in ORDER:
            scatter.start(k)

    @pl.when(step == 5)
    def _():
        for k in ORDER:
            scatter.follow(k)

    @pl.when(step >= 4)
    def _():
        for i in range(3):
            here = pl.ds(i * BLOCK, BLOCK)
            part = dot(triple_ref[0, here, :], weight_ref[0, :, :PAD_SHARD], NT)
            total_ref[here, :] = jnp.where(step == 4, part, total_ref[here, :] + part)

    @pl.when(step == 7)
    def _():
        for k in ORDER[:2]:
            scatter.pass_across(k)
        shifts, scales = jnp.zeros((8, D), F32), jnp.zeros((8, D), F32)
        for i in range(3):
            here = pl.ds(i * BLOCK, BLOCK)
            segment = column_ref[here, :]
            first = total_ref[here, :]
            normed, inverse = normalise(x_ref[here, :].astype(F32))
            grads = first * (1.0 + per_crop(mods_ref[1], segment))
            mean = jnp.mean(grads, axis=1, keepdims=True)
            slant = jnp.mean(grads * normed, axis=1, keepdims=True)
            grad_in_ref[here, :] = mid_ref[here, :] + inverse * (grads - mean - normed * slant)
            shifts = shifts + crop_sums(segment, first)
            scales = scales + crop_sums(segment, first * normed)
        mod_ref[...] = rest_ref[...]
        mod_ref[0, :CROPS, :D] = shifts[:CROPS]
        mod_ref[0, :CROPS, D:] = scales[:CROPS, : D // 2]
        mod_ref[1, :CROPS, : D // 2] = scales[:CROPS, D // 2 :]
        for copy in to_mates:
            copy.start()
        mates_ref[place.index] = mod_ref[place.index]
        for k in ORDER[2:]:
            scatter.pass_across(k)
        for copy in to_mates:
            copy.wait_recv()
        packed_ref[...] = jnp.zeros_like(packed_ref)
        for j in range(4):
            packed_ref[CROPS * j : CROPS * (j + 1), :] = mates_ref[j, :CROPS, :]
            packed_ref[12:14, :] += mates_ref[j, CROPS : CROPS + 2, :]
        for copy in to_z:
            copy.start()
        every_ref[place.peer] = packed_ref[...]
        along_up.close()
        for copy in to_z:
            copy.wait_recv()
        for copy in to_x:
            copy.start()
        for k in ORDER[:3]:
            scatter.collect(k)
            along.start(k)
        for copy in to_x:
            copy.wait_recv()
        close_ada(conds_ref, every_ref, ada_ref, sums_ref)
        scatter.collect(0)
        along.close()
        scatter.finish()
        for copy in small.made:
            copy.wait_send()


def unproject(weight, triple, split, first, mixed, x, mid, mods, column, plane_up, rest, conds):
    block = lambda *tail: pl.BlockSpec((1, *tail), lambda i: (lax.rem(i, 4), 0, 0))
    early = lambda *tail: pl.BlockSpec((1, *tail), lambda i: (jnp.minimum(i, 3), 0, 0))
    late = lambda *tail: pl.BlockSpec((1, *tail), lambda i: (jnp.maximum(i - 4, 0), 0, 0))
    wide = rest.shape[2]
    vmem = pltpu.VMEM
    return pl.pallas_call(
        unproject_kernel,
        grid=(8,),
        out_shape=[
            shape_of(TOK_DEV, D, dtype=F32),
            shape_of(SHARD, D, dtype=F32),
            shape_of(SHARD, D, dtype=F32),
            shape_of(SHARD, wide, dtype=F32),
            shape_of(8, wide, dtype=F32),
        ],
        in_specs=[
            late(D, D), block(TOK_DEV, PAD_SHARD), early(TOK_DEV, OUT_SHARD), whole(TOK_DEV, D),
            whole(TOK_DEV, D), whole(TOK_DEV, D), whole(TOK_DEV, D), whole(6, 8, D), whole(TOK_DEV, 1),
            whole(4, SHARD, D), whole(4, 8, wide), whole(8, 16, 256),
        ],
        out_specs=[
            whole(TOK_DEV, D), whole(SHARD, D), whole(SHARD, D), whole(SHARD, wide), whole(8, wide),
        ],
        scratch_shapes=[
            vmem((TOK_DEV, D), F32),
            vmem((2, D, D), BF16),
            vmem((2, D, D), BF16),
            vmem((4, 4, SHARD, D), BF16),
            vmem((4, SHARD, D), BF16),
            vmem((3, SHARD, D), BF16),
            vmem((3, SHARD, D), BF16),
            vmem((4, 8, wide), F32),
            vmem((4, 8, wide), F32),
            vmem((16, wide), F32),
            vmem((8, 16, wide), F32),
            DMA((SCATTER_COPIES,)),
            DMA((SCATTER_COPIES,)),
            DMA((2,)),
            DMA((2,)),
            DMA((3,)),
            DMA((3,)),
            DMA((3,)),
            DMA((3,)),
            DMA((10,)),
            DMA((10,)),
        ],
        compiler_params=talking(6),
    )(weight, triple, split, first, mixed, x, mid, mods, column, plane_up, rest, conds)


CROPS = 3


def gather_kernel(
    mixed_ref, up_ref, cond_ref, ada_ref, ada_bias_ref, bias_ref,
    mixed_out, up_out, mods_ref, biases_ref, conds_ref,
    send_sems, recv_sems, local_sem, up_send, up_recv, up_local, small_send, small_recv, local_small,
    all_cond, own_cond, partial_ref, from_x, from_z, column_ref,
):
    place = Place()
    place.meet()
    x, zs = place.x, place.zs

    first = Gather(
        place,
        mixed_ref,
        lambda y, c, z, x: mixed_out.at[y, c, z, x],
        send_sems,
        recv_sems,
        local_sem.at[0],
        False,
    )
    ups = Column(place, up_ref, up_out, up_send, up_recv, up_local.at[0])
    small = Copies(small_send, small_recv)
    to_mates = [small.make(cond_ref, all_cond.at[place.index], mate) for mate in place.mates]
    to_mates += [small.make(bias_ref, biases_ref.at[place.index], mate) for mate in place.mates]
    others = [(k, far) for k in range(4) for far in (0, 1) if k or far]
    to_peers = []
    for k, far in others:
        there = 1 - x if far else x
        to_peers.append(
            small.make(
                own_cond.at[2 * zs[k] + there],
                conds_ref.at[place.peer],
                place.device(z=zs[k], x=there),
            )
        )
    over_x = [
        small.make(partial_ref.at[2 * zs[k] + 1 - x], from_x.at[k], place.device(x=1 - x))
        for k in range(4)
    ]
    along = [
        small.make(partial_ref.at[2 * zs[k] + x], from_z.at[k - 1], place.device(z=zs[k]))
        for k in (1, 2, 3)
    ]
    finals = [
        small.make(column_ref.at[other], mods_ref.at[place.index], mate)
        for other, mate in zip(place.mate_index, place.mates)
    ]
    own_bias = pltpu.make_async_copy(bias_ref, biases_ref.at[place.index], local_small.at[0])

    for copy in to_mates:
        copy.start()
    own_bias.start()
    first.start()
    all_cond[place.index] = cond_ref[...]
    own_cond[...] = jnp.zeros_like(own_cond)
    for copy in to_mates:
        copy.wait_recv()
    for j in range(4):
        own_cond[:, CROPS * j : CROPS * (j + 1), :] = all_cond[j, :, :CROPS, :]
    for copy in to_peers:
        copy.start()
    conds_ref[place.peer] = own_cond[place.peer]
    first.pass_along(1)
    for copy in to_peers:
        copy.wait_recv()
    for i in range(8):
        partial_ref[i] = dot(conds_ref[i][:, :SHARD].astype(BF16), ada_ref[...])
    for copy in over_x:
        copy.start()
    first.pass_along(2)
    first.pass_along(3)
    for k in range(4):
        over_x[k].wait_recv()
        partial_ref[2 * zs[k] + x] += from_x[k]
    for copy in along:
        copy.start()
    for k in range(2):
        first.pass_across(k)
    for copy in along:
        copy.wait_recv()
    total = partial_ref[place.peer] + from_z[0] + from_z[1] + from_z[2] + ada_bias_ref[...]
    column_ref[...] = jnp.zeros_like(column_ref)
    for j in range(4):
        column_ref[j, :CROPS, :] = total[CROPS * j : CROPS * (j + 1)]
    for copy in finals:
        copy.start()
    mods_ref[place.index] = column_ref[place.index]
    for k in range(2, 4):
        first.pass_across(k)
    ups.start()
    for k in range(4):
        first.pass_pair(k)
    for copy in finals:
        copy.wait_recv()
    own_bias.wait()
    first.finish()
    ups.finish()
    for copy in small.made:
        copy.wait_send()


def gather_all(mixed, up, cond, ada, ada_bias, bias):
    vmem = pltpu.VMEM
    wide = ada.shape[1]
    return pl.pallas_call(
        gather_kernel,
        out_shape=[shape_of(2, 2, 4, 2, SHARD, D), shape_of(4, SHARD, D)]
        + [shape_of(4, 8, wide, dtype=F32), shape_of(4, 32, 128), shape_of(8, 16, 256, dtype=F32)],
        in_specs=[ANYWHERE] * 2 + [IN_VMEM] * 4,
        out_specs=[ANYWHERE] * 2 + [IN_VMEM] * 3,
        scratch_shapes=[DMA((GATHER_COPIES,))] * 2
        + [DMA((1,)), DMA((3,)), DMA((3,)), DMA((1,)), DMA((23,)), DMA((23,)), DMA((1,))]
        + [
            vmem((4, 8, 8, 256), F32),
            vmem((8, 16, 256), F32),
            vmem((8, 16, wide), F32),
            vmem((4, 16, wide), F32),
            vmem((3, 16, wide), F32),
            vmem((4, 8, wide), F32),
        ],
        compiler_params=pltpu.CompilerParams(
            collective_id=1, has_side_effects=True, vmem_limit_bytes=VMEM_BYTES
        ),
    )(mixed, up, cond, ada, ada_bias, bias)


def close_ada(conds_ref, every, ada_ref, sums_ref):
    total = jnp.zeros(ada_ref.shape, F32)
    rows = jnp.zeros((16, ada_ref.shape[1]), F32)
    for i in range(0, 8, 2):
        rows = rows + every[i] + every[i + 1]
        cond = jnp.concatenate([conds_ref[i][:, :SHARD], conds_ref[i + 1][:, :SHARD]], axis=0)
        rest = jnp.concatenate([every[i], every[i + 1]], axis=0)
        for _ in range(3):
            part = rest.astype(BF16)
            total = total + dot(cond.astype(BF16), part, TN)
            rest = rest - part.astype(F32)
    ada_ref[...] = total
    sums_ref[...] = jnp.zeros_like(sums_ref)
    sums_ref[0:1, :] = jnp.sum(rows[:12], axis=0, keepdims=True)
    sums_ref[1:3, :] = rows[12:14]


def block_shards(
    block_in, condition, lengths, head_mask, group_mask, buffer_slot, ada_weight, ada_bias, qkv_weight,
    query_bias, value_bias, out_weight, out_bias, up_weight, up_bias, down_weight, down_bias, cotangent,
):
    x, cot = block_in[0], cotangent[0]
    finish = jnp.cumsum(lengths[0])
    position = jnp.arange(TOK_DEV, dtype=jnp.int32)
    segment = jnp.sum((position[:, None] >= finish[None, :]).astype(jnp.int32), axis=1)
    column, row = segment[:, None], segment[None, :]
    slot = buffer_slot[0].astype(jnp.int32)
    slot_column, slot_row = slot[:, None], slot[None, :]
    mask = head_mask[0].T.astype(F32)
    chosen = (segment[:, None] == jnp.arange(CROPS)[None, :])[:, :, None]
    groups = jnp.sum(jnp.where(chosen, group_mask[0].astype(F32)[None], 0.0), axis=1)
    groups = jnp.pad(groups, ((0, 0), (0, 128 - GROUPS))).astype(BF16)
    cond = jax.nn.silu(condition[0].astype(F32)).astype(BF16).astype(F32)
    cond = cond.reshape(CROPS, 8, SHARD).transpose(1, 0, 2)
    cond = jnp.pad(cond, ((0, 0), (0, 8 - CROPS), (0, 256 - SHARD)))
    vectors = jnp.concatenate([query_bias, value_bias, out_bias, up_bias, down_bias])
    packed = jnp.pad(vectors.reshape(18, 128), ((0, 14), (0, 0)))
    down_rows = lax.all_to_all(down_weight, "fsdp", split_axis=0, concat_axis=1, tiled=True)
    mixed_block = jnp.concatenate([qkv_weight, out_weight], axis=1)
    mixed_weight, up_column, mods, biases, conds = gather_all(
        mixed_block, up_weight, cond, ada_weight, ada_bias.astype(F32)[None], packed
    )
    mixed_weight = mixed_weight.reshape(4, D, D)
    mods = mods.transpose(1, 0, 2).reshape(8, 6, D).transpose(1, 0, 2)
    biases = biases[:, :18].reshape(4, 2304).astype(F32)
    edges = (0, 288, 576, 864, 2016, 2304)
    bias_query, bias_value, bias_out, bias_up, bias_down = [
        biases[:, low:high].reshape(1, -1) for low, high in zip(edges[:-1], edges[1:])
    ]
    qkv_bias = jnp.concatenate([bias_query, jnp.zeros_like(bias_query), bias_value], axis=1)
    qkv_bias = jnp.pad(qkv_bias.reshape(4, 1, QKV_SHARD), ((0, 0), (0, 0), (0, PAD_SHARD - QKV_SHARD)))
    first, heads, mixed, lse, attn, after, arrived, picked, full_out, up, down_column = attend(
        x, mixed_weight, mods, qkv_bias, bias_out, column, row, slot_row, groups, mask, up_column,
        down_rows,
    )
    up = up.reshape(4, D, D)
    pull, grad_rows, block_out, gate_two, grad_down_bias, parts_down, down = feed(
        up, arrived, picked, bias_up.reshape(4, 1, D), bias_down, cot, after, mods, column,
        slot_column, slot_row, down_column,
    )
    down = down.reshape(4, D, D)
    grad_up_bias, mid, grad_attn, sums, grad_out_bias, parts_up, plane_down = unfeed(
        down, up, pull, grad_rows, arrived, after, cot, attn, mods, column, slot_column, parts_down
    )
    triple, triple_sums, share_down, plane_up, grad_split = unattend(
        grad_attn, full_out, heads, lse, column, row, parts_up.reshape(2, 4, 2, SHARD, D), plane_down,
        mask,
    )
    triple_sums = triple_sums[:, 0, :QKV_SHARD].reshape(3 * D)
    blank = jnp.zeros((8, 2 * D), F32)
    mod_grads = jnp.concatenate([blank, sums[0], sums[1], sums[2], gate_two], axis=1)[:CROPS]
    mod_grads = mod_grads.reshape(CROPS, 4, -1).transpose(1, 0, 2)
    bias_grads = (
        triple_sums[:D], triple_sums[2 * D :], grad_out_bias, grad_up_bias, grad_down_bias,
    )
    bias_grads = jnp.concatenate([vector.reshape(4, -1) for vector in bias_grads], axis=1)
    wide = mod_grads.shape[2]
    bias_grads = jnp.pad(bias_grads, ((0, 0), (0, 5 * wide - 2304))).reshape(4, 5, wide)
    rest = jnp.concatenate([mod_grads, bias_grads], axis=1)
    grad_in, share_up, share_mixed, grad_ada, totals = unproject(
        mixed_weight, triple, grad_split, first, mixed, x, mid, mods, column, plane_up, rest, conds
    )
    share_down = lax.all_to_all(share_down, "fsdp", split_axis=1, concat_axis=0, tiled=True)
    bias_totals = totals[1:3].reshape(-1)
    grad_query, grad_value, grad_out, grad_ups, grad_downs = [
        bias_totals[low:high] for low, high in zip(edges[:-1], edges[1:])
    ]
    return (
        block_out[None],
        grad_in[None],
        grad_ada,
        totals[0],
        share_mixed[:, :QKV_SHARD],
        grad_query,
        grad_value,
        share_mixed[:, QKV_SHARD:],
        grad_out,
        share_up,
        grad_ups,
        share_down,
        grad_downs,
    )


def layer_norm(values):
    center = values - jnp.mean(values, axis=-1, keepdims=True)
    variance = jnp.mean(center * center, axis=-1, keepdims=True)
    inverse = lax.rsqrt(variance + epsilon)
    return (center * inverse, inverse)


def norm_back(grad_normed, normed, inverse):
    first_mean = jnp.mean(grad_normed, axis=-1, keepdims=True)
    second_mean = jnp.mean(grad_normed * normed, axis=-1, keepdims=True)
    return inverse * (grad_normed - first_mean - normed * second_mean)


def attention_scores(query_part, key_part, allowed, factor):
    raw_scores = (
        jnp.einsum("qhd,khd->hqk", query_part, key_part, preferred_element_type=jnp.float32)
        * factor
    )
    return jnp.where(allowed[None], raw_scores, -1e30)


def gelu_tanh(values):
    return jax.nn.gelu(values, approximate=True)


def shards(
    block_in,
    condition,
    lengths,
    head_mask,
    group_mask,
    buffer_slot,
    ada_weight,
    ada_bias,
    qkv_weight,
    query_bias,
    value_bias,
    out_weight,
    out_bias,
    up_weight,
    up_bias,
    down_weight,
    down_bias,
    cotangent,
):
    peers = lax.axis_size("dp")
    mates = lax.axis_size("fsdp")

    def gather_matrix(shard):
        stacked = lax.all_gather(shard, ("dp", "fsdp"), axis=0, tiled=False)
        rows, columns = shard.shape
        stacked = stacked.reshape(peers, mates, rows, columns).transpose(0, 2, 1, 3)
        return stacked.reshape(peers * rows, mates * columns)

    full_qkv, full_out, full_up, full_down = [
        gather_matrix(shard) for shard in (qkv_weight, out_weight, up_weight, down_weight)
    ]
    vectors = (query_bias, value_bias, out_bias, up_bias, down_bias)
    packed_bias = lax.all_gather(jnp.concatenate(vectors), "fsdp", axis=0, tiled=False)
    edges = [0]
    for vector in vectors:
        edges.append(edges[-1] + vector.shape[0])
    bias_query, bias_value, bias_out, bias_up, bias_down = [
        packed_bias[:, low:high].reshape(-1).astype(jnp.float32)
        for low, high in zip(edges[:-1], edges[1:])
    ]
    inputs = block_in[0].astype(jnp.float32)
    crop_length = lengths[0]
    finish = jnp.cumsum(crop_length)
    opening = finish - crop_length
    position = jnp.arange(TOK_DEV, dtype=jnp.int32)
    member = (
        (position[:, None] >= opening[None, :]) & (position[:, None] < finish[None, :])
    ).astype(jnp.float32)
    segment = jnp.sum((position[:, None] >= finish[None, :]).astype(jnp.int32), axis=1)
    cond_act = jax.nn.silu(condition[0].astype(jnp.float32)).astype(jnp.bfloat16)
    crops = cond_act.shape[0]
    cond_all = lax.all_gather(cond_act, ("dp", "fsdp"), axis=0, tiled=True)
    depth = ada_weight.shape[0]
    cond_slice = lax.dynamic_slice_in_dim(cond_all, lax.axis_index("dp") * depth, depth, axis=1)
    partial_mod = jnp.dot(cond_slice, ada_weight, preferred_element_type=jnp.float32)
    column_mod = lax.psum_scatter(partial_mod, "dp", scatter_dimension=0, tiled=True)
    column_mod = column_mod + ada_bias.astype(jnp.float32)
    modulation = lax.all_to_all(column_mod, "fsdp", split_axis=0, concat_axis=1, tiled=True)
    pieces = [
        jnp.dot(member, modulation[:, number * D : (number + 1) * D], precision=highest)
        for number in range(6)
    ]
    shift_one, scale_one, gate_one, shift_two, scale_two, gate_two = pieces
    head_keep = jnp.dot(member, head_mask[0].astype(jnp.float32), precision=highest)
    group_keep = jnp.dot(member, group_mask[0].astype(jnp.float32), precision=highest)
    normed_one, inverse_one = layer_norm(inputs)
    first_in = (normed_one * (1.0 + scale_one) + shift_one).astype(jnp.bfloat16)
    qkv_bias = jnp.concatenate([bias_query, jnp.zeros_like(bias_query), bias_value])
    triple = (jnp.dot(first_in, full_qkv, preferred_element_type=jnp.float32) + qkv_bias).astype(
        jnp.bfloat16
    )
    queries = triple[:, :D].reshape(TOK_DEV, HEADS, HEAD_DIM)
    keys_all = triple[:, D : 2 * D].reshape(TOK_DEV, HEADS, HEAD_DIM)
    values_all = triple[:, 2 * D :].reshape(TOK_DEV, HEADS, HEAD_DIM)
    factor = HEAD_DIM ** (-0.5)
    row_block = min(768, TOK_DEV)
    group_size = min(4, HEADS)
    log_totals = {}
    head_parts = []
    for head_start in range(0, HEADS, group_size):
        heads_here = slice(head_start, head_start + group_size)
        row_start = 0
        rows_here = slice(row_start, row_start + row_block)
        allowed = segment[:, None] == segment[None, :]
        scores = attention_scores(
            queries[rows_here, heads_here], keys_all[:, heads_here], allowed, factor
        )
        row_max = jnp.max(scores, axis=-1, keepdims=True)
        log_total = row_max + jnp.log(jnp.sum(jnp.exp(scores - row_max), axis=-1, keepdims=True))
        weights_low = jnp.exp(scores - log_total).astype(jnp.bfloat16)
        row_parts = jnp.einsum(
            "hqk,khd->qhd",
            weights_low,
            values_all[:, heads_here],
            preferred_element_type=jnp.float32,
        )
        log_totals[head_start, row_start] = log_total
        head_parts.append(row_parts)
    attended = jnp.concatenate(head_parts, axis=1)
    mixed = (attended * head_keep[:, :, None]).astype(jnp.bfloat16).reshape(TOK_DEV, D)
    attn_out = jnp.dot(mixed, full_out, preferred_element_type=jnp.float32) + bias_out
    after_attn = inputs + gate_one * attn_out
    normed_two, inverse_two = layer_norm(after_attn)
    second_in = (normed_two * (1.0 + scale_two) + shift_two).astype(jnp.bfloat16)
    keep = (buffer_slot[0] >= 0).astype(jnp.float32)[:, None]
    places = 2 * TOK_DEV // 3
    chooser = (buffer_slot[0][:, None] == jnp.arange(places, dtype=jnp.int32)[None, :]).astype(
        jnp.bfloat16
    )
    arrived = jnp.einsum(
        "tb,td->bd", chooser, second_in, preferred_element_type=jnp.float32
    ).astype(jnp.bfloat16)
    groups_float = jnp.einsum(
        "tb,tg->bg",
        chooser,
        group_keep.astype(jnp.bfloat16),
        preferred_element_type=jnp.float32,
    )
    channel_keep = jnp.repeat(groups_float, FF // GROUPS, axis=1)
    hidden = jnp.dot(arrived, full_up, preferred_element_type=jnp.float32) + bias_up
    active = (gelu_tanh(hidden) * channel_keep).astype(jnp.bfloat16)
    branch = (jnp.dot(active, full_down, preferred_element_type=jnp.float32) + bias_down).astype(
        jnp.bfloat16
    )
    branch_tok = jnp.einsum(
        "tb,bd->td", chooser, branch, preferred_element_type=jnp.float32
    )
    after_mlp = after_attn + gate_two * branch_tok
    block_out = after_mlp.astype(jnp.bfloat16)[None]
    grad_after = cotangent[0].astype(jnp.float32)
    grad_gate_two = grad_after * branch_tok
    grad_branch = (gate_two * keep * grad_after).astype(jnp.bfloat16)
    grad_rows = jnp.einsum(
        "tb,td->bd", chooser, grad_branch, preferred_element_type=jnp.float32
    ).astype(jnp.bfloat16)
    back_qkv, back_out, back_up, back_down = full_qkv, full_out, full_up, full_down
    grad_down_bias = jnp.sum(grad_rows.astype(jnp.float32), axis=0)
    grad_down = jnp.einsum("bf,bd->fd", active, grad_rows, preferred_element_type=jnp.float32)
    grad_active = jnp.einsum("bd,fd->bf", grad_rows, back_down, preferred_element_type=jnp.float32)
    gelu_pull = jax.vjp(gelu_tanh, hidden)[1]
    grad_hidden = gelu_pull(grad_active * channel_keep)[0].astype(jnp.bfloat16)
    grad_up_bias = jnp.sum(grad_hidden.astype(jnp.float32), axis=0)
    grad_up = jnp.einsum("bd,bf->df", arrived, grad_hidden, preferred_element_type=jnp.float32)
    grad_arrived = jnp.einsum(
        "bf,df->bd", grad_hidden, back_up, preferred_element_type=jnp.float32
    ).astype(jnp.bfloat16)
    grad_second = jnp.einsum(
        "tb,bd->td", chooser, grad_arrived, preferred_element_type=jnp.float32
    )
    grad_scale_two = grad_second * normed_two
    grad_mid = grad_after + norm_back(grad_second * (1.0 + scale_two), normed_two, inverse_two)
    grad_gate_one = grad_mid * attn_out
    grad_attn = (gate_one * grad_mid).astype(jnp.bfloat16)
    grad_out_bias = jnp.sum(grad_attn.astype(jnp.float32), axis=0)
    grad_out = jnp.einsum("te,tf->ef", mixed, grad_attn, preferred_element_type=jnp.float32)
    grad_mixed = jnp.einsum(
        "tf,ef->te", grad_attn, back_out, preferred_element_type=jnp.float32
    ).astype(jnp.bfloat16)
    grad_attended = (
        grad_mixed.reshape(TOK_DEV, HEADS, HEAD_DIM).astype(jnp.float32) * head_keep[:, :, None]
    ).astype(jnp.bfloat16)
    query_heads = []
    key_heads = []
    value_heads = []
    for head_start in range(0, HEADS, group_size):
        heads_here = slice(head_start, head_start + group_size)
        row_start = 0
        rows_here = slice(row_start, row_start + row_block)
        allowed = segment[:, None] == segment[None, :]
        scores = attention_scores(
            queries[rows_here, heads_here], keys_all[:, heads_here], allowed, factor
        )
        probs = jnp.exp(scores - log_totals[head_start, row_start])
        grad_piece = grad_attended[rows_here, heads_here]
        grad_values = jnp.einsum(
            "hqk,qhd->khd",
            probs.astype(jnp.bfloat16),
            grad_piece,
            preferred_element_type=jnp.float32,
        )
        grad_probs = jnp.einsum(
            "qhd,khd->hqk",
            grad_piece,
            values_all[:, heads_here],
            preferred_element_type=jnp.float32,
        )
        grad_scores = (
            probs * (grad_probs - jnp.sum(probs * grad_probs, axis=-1, keepdims=True))
        ).astype(jnp.bfloat16)
        query_rows = (
            jnp.einsum(
                "hqk,khd->qhd",
                grad_scores,
                keys_all[:, heads_here],
                preferred_element_type=jnp.float32,
            )
            * factor
        )
        grad_keys = (
            jnp.einsum(
                "hqk,qhd->khd",
                grad_scores,
                queries[rows_here, heads_here],
                preferred_element_type=jnp.float32,
            )
            * factor
        )
        query_heads.append(query_rows)
        key_heads.append(grad_keys)
        value_heads.append(grad_values)
    grad_triple = jnp.concatenate(
        [
            jnp.concatenate(query_heads, axis=1).reshape(TOK_DEV, D),
            jnp.concatenate(key_heads, axis=1).reshape(TOK_DEV, D),
            jnp.concatenate(value_heads, axis=1).reshape(TOK_DEV, D),
        ],
        axis=1,
    ).astype(jnp.bfloat16)
    grad_query_bias = jnp.sum(grad_triple[:, :D].astype(jnp.float32), axis=0)
    grad_value_bias = jnp.sum(grad_triple[:, 2 * D :].astype(jnp.float32), axis=0)
    grad_qkv = jnp.einsum("td,te->de", first_in, grad_triple, preferred_element_type=jnp.float32)
    grad_first = jnp.einsum("te,de->td", grad_triple, back_qkv, preferred_element_type=jnp.float32)
    grad_scale_one = grad_first * normed_one
    grad_inputs = grad_mid + norm_back(grad_first * (1.0 + scale_one), normed_one, inverse_one)
    token_grads = [
        grad_first,
        grad_scale_one,
        grad_gate_one,
        grad_second,
        grad_scale_two,
        grad_gate_two,
    ]
    grad_modulation = jnp.concatenate(
        [jnp.einsum("ts,td->sd", member, single, precision=highest) for single in token_grads],
        axis=1,
    )
    mod_columns = lax.all_to_all(
        grad_modulation, "fsdp", split_axis=1, concat_axis=0, tiled=True
    )
    mod_all = lax.all_gather(mod_columns, "dp", axis=0, tiled=True)
    grad_ada_bias = jnp.sum(mod_all, axis=0)
    grad_ada = jnp.einsum(
        "sd,se->de", cond_slice.astype(jnp.float32), mod_all, precision=highest
    )

    def scatter_matrix(full):
        rows, columns = full.shape[0] // peers, full.shape[1] // mates
        blocks = full.astype(jnp.bfloat16).reshape(peers, rows, mates, columns)
        blocks = blocks.transpose(0, 2, 1, 3).reshape(peers * mates * rows, columns)
        share = lax.psum_scatter(blocks, ("dp", "fsdp"), scatter_dimension=0, tiled=True)
        return share.astype(jnp.float32)

    shares = [scatter_matrix(full) for full in (grad_qkv, grad_out, grad_up, grad_down)]
    bias_grads = (grad_query_bias, grad_value_bias, grad_out_bias, grad_up_bias, grad_down_bias)
    packed = jnp.concatenate([vector.reshape(mates, -1) for vector in bias_grads], axis=1)
    packed = lax.psum_scatter(packed, "fsdp", scatter_dimension=0, tiled=True)
    packed = lax.psum(packed[0], "dp")
    totals = [packed[low:high] for low, high in zip(edges[:-1], edges[1:])]
    return (
        block_out,
        grad_inputs[None],
        grad_ada,
        grad_ada_bias,
        shares[0],
        totals[0],
        totals[1],
        shares[1],
        totals[2],
        shares[2],
        totals[3],
        shares[3],
        totals[4],
    )


def solution(mesh):
    placed = (
        P(("dp", "fsdp"), None, None),
        P(("dp", "fsdp"), None, None),
        P(("dp", "fsdp"), None),
        P(("dp", "fsdp"), None, None),
        P(("dp", "fsdp"), None, None),
        P(("dp", "fsdp"), None),
        P("dp", "fsdp"),
        P("fsdp"),
        P("dp", "fsdp"),
        P("fsdp"),
        P("fsdp"),
        P("dp", "fsdp"),
        P("fsdp"),
        P("dp", "fsdp"),
        P("fsdp"),
        P("dp", "fsdp"),
        P("fsdp"),
        P(("dp", "fsdp"), None, None),
    )
    on_block = dict(mesh.shape) == {"dp": 8, "fsdp": 4}
    return jax.shard_map(
        block_shards if on_block else shards,
        mesh=mesh,
        in_specs=placed,
        out_specs=(
            P(("dp", "fsdp"), None, None),
            P(("dp", "fsdp"), None, None),
            P("dp", "fsdp"),
            P("fsdp"),
            P("dp", "fsdp"),
            P("fsdp"),
            P("fsdp"),
            P("dp", "fsdp"),
            P("fsdp"),
            P("dp", "fsdp"),
            P("fsdp"),
            P("dp", "fsdp"),
            P("fsdp"),
        ),
        check_vma=False,
    )
```

```python
import math

import jax
import jax.numpy as jnp
from jax import lax
from jax.experimental import pallas as pl
from jax.experimental.pallas import tpu as pltpu
from jax.sharding import PartitionSpec as P

D = 1152
HEADS = 16
HEAD_DIM = 72
FF = 4608
GROUPS = 16
TOK_DEV = 768


highest = lax.Precision.HIGHEST
epsilon = 1e-06


NT = (((1,), (1,)), ((), ()))
TN = (((0,), (0,)), ((), ()))
NN = (((1,), (0,)), ((), ()))
PLACES = 512
BLOCK = 256
BF16, F32 = jnp.bfloat16, jnp.float32
SOFT = HEAD_DIM**-0.5 * math.log2(math.e)
QKV_SHARD, OUT_SHARD, PAD_SHARD = 864, 288, 896
VMEM_BYTES = 60 * 2**20


def dot(left, right, dims=NN):
    return lax.dot_general(left, right, dims, preferred_element_type=F32)


def rows_at(i):
    return pl.ds(pl.multiple_of(i * BLOCK, BLOCK), BLOCK)


def per_crop(table, segment):
    return jnp.where(
        segment == 0, table[0:1], jnp.where(segment == 1, table[1:2], table[2:3])
    )


def normalise(values):
    center = values - jnp.mean(values, axis=1, keepdims=True)
    variance = jnp.mean(center * center, axis=1, keepdims=True)
    inverse = lax.rsqrt(variance + epsilon)
    return center * inverse, inverse


def crop_sums(segment, values):
    lanes = lax.broadcasted_iota(jnp.int32, (values.shape[0], 128), 1)
    member = (lanes == segment).astype(BF16)
    high = values.astype(BF16)
    low = (values - high.astype(F32)).astype(BF16)
    return (dot(member, high, TN) + dot(member, low, TN))[:8]


def crop_mask(bias_ref, column_ref, row_ref):
    for i in range(TOK_DEV // BLOCK):
        here = pl.ds(i * BLOCK, BLOCK)
        bias_ref[here, :] = jnp.where(column_ref[here, :] == row_ref[...], 0.0, -1e30).astype(F32)


def places_of(slot_row, i):
    place = lax.broadcasted_iota(jnp.int32, (BLOCK, TOK_DEV), 0) + i * BLOCK
    return (place == slot_row).astype(BF16)


def tokens_of(slot_column):
    place = lax.broadcasted_iota(jnp.int32, (BLOCK, PLACES), 1)
    return (place == slot_column).astype(BF16)


def head_keep(mask_ref, h, segment):
    keep = jnp.where(
        segment == 0, mask_ref[0, h], jnp.where(segment == 1, mask_ref[1, h], mask_ref[2, h])
    )
    return keep.astype(F32)


MESH = pl.DeviceIdType.MESH
SHARD = 144
UPPER = 80


class Place:
    def __init__(self):
        dp, fsdp = lax.axis_index("dp"), lax.axis_index("fsdp")
        self.z, self.x = lax.div(dp, 2), lax.rem(dp, 2)
        self.y, self.c = lax.div(fsdp, 2), lax.rem(fsdp, 2)
        z = self.z
        self.zs = (z, z + 1 - 2 * lax.rem(z, 2), lax.rem(z + 2, 4), 3 - z)
        self.mates = (
            self.device(c=1 - self.c),
            self.device(y=1 - self.y),
            self.device(y=1 - self.y, c=1 - self.c),
        )
        self.mate_index = (
            2 * self.y + 1 - self.c,
            2 * (1 - self.y) + self.c,
            2 * (1 - self.y) + 1 - self.c,
        )
        self.index = 2 * self.y + self.c
        self.peer = 2 * z + self.x

    def device(self, z=None, x=None, y=None, c=None):
        z, x = self.z if z is None else z, self.x if x is None else x
        y, c = self.y if y is None else y, self.c if c is None else c
        return (2 * z + x, 2 * y + c)

    def meet(self):
        barrier = pltpu.get_barrier_semaphore()
        others = [self.device(z=self.zs[k]) for k in (1, 2, 3)]
        others += [self.device(z=self.zs[k], x=1 - self.x) for k in range(4)]
        others += self.mates
        for other in others:
            pl.semaphore_signal(barrier, inc=1, device_id=other, device_id_type=MESH)
        pl.semaphore_wait(barrier, len(others))


class Copies:
    def __init__(self, send_sems, recv_sems):
        self.send_sems, self.recv_sems, self.made = send_sems, recv_sems, []

    def make(self, source, target, device):
        index = len(self.made)
        copy = pltpu.make_async_remote_copy(
            src_ref=source,
            dst_ref=target,
            send_sem=self.send_sems.at[index],
            recv_sem=self.recv_sems.at[index],
            device_id=device,
            device_id_type=MESH,
        )
        self.made.append(copy)
        return copy


GATHER_COPIES = 35


class Gather:
    def __init__(self, place, source, slot, send_sems, recv_sems, local_sem, swap):
        x, y, c, zs = place.x, place.y, place.c, place.zs
        self.copies = Copies(send_sems, recv_sems)
        make = self.copies.make
        first, second = (SHARD - UPPER, UPPER) if swap else (0, UPPER)
        upper = pl.ds(first, second)
        lower = pl.ds(0, SHARD - UPPER) if swap else pl.ds(UPPER, SHARD - UPPER)
        over_x, over_y, beside = (
            place.device(x=1 - x),
            place.device(y=1 - y),
            place.device(c=1 - c),
        )
        own = [slot(y, c, zs[k], x) for k in range(4)]
        held = [source] + own[1:]
        from_x = [slot(y, c, zs[k], 1 - x) for k in range(4)]
        from_y = [slot(1 - y, c, zs[k], x) for k in range(4)]
        across = [slot(1 - y, c, zs[k], 1 - x) for k in range(4)]
        self.local = pltpu.make_async_copy(source, own[0], local_sem)
        self.along = [None] + [make(source, own[0], place.device(z=zs[k])) for k in (1, 2, 3)]
        self.to_x = [make(held[k], own[k], over_x) for k in range(4)]
        self.to_y = [make(held[k], own[k], over_y) for k in range(4)]
        self.x_to_y = [make(s.at[upper], s.at[upper], over_y) for s in from_x]
        self.y_to_x = [make(s.at[lower], s.at[lower], over_x) for s in from_y]
        self.pair = [make(held[k], own[k], beside) for k in range(4)]
        self.pair_x = [make(s, s, beside) for s in from_x]
        self.pair_y = [make(s, s, beside) for s in from_y]
        self.pair_across = [make(s, s, beside) for s in across]

    def start(self):
        self.along[1].start()
        self.to_x[0].start()
        self.to_y[0].start()
        self.along[2].start()
        self.along[3].start()
        self.pair[0].start()
        self.local.start()

    def pass_along(self, k):
        self.along[k].wait_recv()
        self.to_x[k].start()
        self.to_y[k].start()
        self.pair[k].start()

    def pass_across(self, k):
        self.to_x[k].wait_recv()
        self.x_to_y[k].start()
        self.pair_x[k].start()
        self.to_y[k].wait_recv()
        self.y_to_x[k].start()
        self.pair_y[k].start()

    def pass_pair(self, k):
        self.x_to_y[k].wait_recv()
        self.y_to_x[k].wait_recv()
        self.pair_across[k].start()

    def finish(self):
        self.local.wait()
        for copy in self.pair + self.pair_x + self.pair_y + self.pair_across:
            copy.wait_recv()
        for copy in self.copies.made:
            copy.wait_send()


class Column:
    def __init__(self, place, source, column, send_sems, recv_sems, local_sem):
        copies = Copies(send_sems, recv_sems)
        self.local = pltpu.make_async_copy(source, column.at[place.z], local_sem)
        self.along = [
            copies.make(source, column.at[place.z], place.device(z=place.zs[k])) for k in (1, 2, 3)
        ]

    def start(self):
        for copy in self.along:
            copy.start()
        self.local.start()

    def finish(self):
        for copy in self.along:
            copy.wait()
        self.local.wait()


SPREAD_COPIES = 32


class Spread:
    def __init__(self, place, column, slot, send_sems, recv_sems, local_sems):
        x, y, c, zs = place.x, place.y, place.c, place.zs
        self.copies = Copies(send_sems, recv_sems)
        make = self.copies.make
        upper, lower = pl.ds(0, UPPER), pl.ds(UPPER, SHARD - UPPER)
        over_x, over_y, beside = place.device(x=1 - x), place.device(y=1 - y), place.mates[0]
        four = range(4)
        held = [column.at[zs[k]] for k in four]
        own = [slot(y, c, zs[k], x) for k in four]
        from_x = [slot(y, c, zs[k], 1 - x) for k in four]
        from_y = [slot(1 - y, c, zs[k], x) for k in four]
        across = [slot(1 - y, c, zs[k], 1 - x) for k in four]
        first = [upper, lower, upper, lower]
        second = [lower, upper, lower, upper]
        self.local = [pltpu.make_async_copy(held[k], own[k], local_sems.at[k]) for k in four]
        self.to_x = [make(held[k], own[k], over_x) for k in four]
        self.to_y = [make(held[k], own[k], over_y) for k in four]
        self.x_to_y = [make(from_x[k].at[first[k]], from_x[k].at[first[k]], over_y) for k in four]
        self.y_to_x = [make(from_y[k].at[second[k]], from_y[k].at[second[k]], over_x) for k in four]
        self.pair = [make(held[k], own[k], beside) for k in four]
        self.pair_x = [make(s, s, beside) for s in from_x]
        self.pair_y = [make(s, s, beside) for s in from_y]
        self.pair_across = [make(s, s, beside) for s in across]

    def start(self):
        for k in range(4):
            self.to_x[k].start()
            self.to_y[k].start()
        for k in range(4):
            self.pair[k].start()
            self.local[k].start()

    def pass_across(self, k):
        self.to_x[k].wait_recv()
        self.x_to_y[k].start()
        self.pair_x[k].start()
        self.to_y[k].wait_recv()
        self.y_to_x[k].start()
        self.pair_y[k].start()

    def pass_pair(self, k):
        self.x_to_y[k].wait_recv()
        self.y_to_x[k].wait_recv()
        self.pair_across[k].start()

    def finish(self):
        for copy in self.local:
            copy.wait()
        for copy in self.pair + self.pair_x + self.pair_y + self.pair_across:
            copy.wait_recv()
        for copy in self.copies.made:
            copy.wait_send()


SCATTER_COPIES = 24


class Scatter:
    def __init__(self, place, parts, bufs, column, send_sems, recv_sems):
        x, y, zs = place.x, place.y, place.zs
        self.place, self.parts, self.column = place, parts, column
        self.by_x, self.by_y, self.from_x, self.from_y = [bufs.at[k] for k in range(4)]
        self.copies = Copies(send_sems, recv_sems)
        make = self.copies.make
        self.upper, self.lower = (0, UPPER), (UPPER, SHARD - UPPER)
        a, b = pl.ds(*self.upper), pl.ds(*self.lower)
        over_x, over_y = place.device(x=1 - x), place.device(y=1 - y)
        four = range(4)
        self.across_y = [
            make(parts.at[1 - y, zs[k], 1 - x, a], self.by_y.at[k, a], over_y) for k in four
        ]
        self.across_x = [
            make(parts.at[1 - y, zs[k], 1 - x, b], self.by_x.at[k, b], over_x) for k in four
        ]
        self.x_lower = [make(parts.at[y, zs[k], 1 - x, b], self.from_x.at[k, b], over_x) for k in four]
        self.y_upper = [make(parts.at[1 - y, zs[k], x, a], self.from_y.at[k, a], over_y) for k in four]
        self.x_upper = [make(self.by_y.at[k, a], self.from_x.at[k, a], over_x) for k in four]
        self.y_lower = [make(self.by_x.at[k, b], self.from_y.at[k, b], over_y) for k in four]

    def start(self, k):
        self.across_y[k].start()
        self.across_x[k].start()

    def follow(self, k):
        self.x_lower[k].start()
        self.y_upper[k].start()

    def add(self, target, k, index, rows):
        for at in range(0, rows[1], 16):
            here = pl.ds(rows[0] + at, 16)
            total = self.parts[(*index, here)].astype(F32) + target[k, here].astype(F32)
            target[k, here] = total.astype(BF16)

    def pass_across(self, k):
        x, y, z = self.place.x, self.place.y, self.place.zs[k]
        self.across_y[k].wait_recv()
        self.add(self.by_y, k, (y, z, 1 - x), self.upper)
        self.x_upper[k].start()
        self.across_x[k].wait_recv()
        self.add(self.by_x, k, (1 - y, z, x), self.lower)
        self.y_lower[k].start()

    def collect(self, k):
        x, y, z = self.place.x, self.place.y, self.place.zs[k]
        for copy in (self.x_upper[k], self.x_lower[k], self.y_upper[k], self.y_lower[k]):
            copy.wait_recv()
        for at in range(0, SHARD, 16):
            here = pl.ds(at, 16)
            total = self.parts[y, z, x, here].astype(F32) + self.from_x[k, here].astype(F32)
            self.column[k, here] = (total + self.from_y[k, here].astype(F32)).astype(BF16)

    def finish(self):
        for copy in self.copies.made:
            copy.wait_send()


class Along:
    def __init__(self, place, column, from_z, out, send_sems, recv_sems):
        copies = Copies(send_sems, recv_sems)
        self.column, self.from_z, self.out = column, from_z, out
        self.copies = [
            copies.make(column.at[k], from_z.at[k - 1], place.device(z=place.zs[k])) for k in (1, 2, 3)
        ]

    def start(self, k):
        self.copies[k - 1].start()

    def close(self):
        for copy in self.copies:
            copy.wait()
        for at in range(0, SHARD, 16):
            here = pl.ds(at, 16)
            total = self.column[0, here].astype(F32)
            for k in range(3):
                total = total + self.from_z[k, here].astype(F32)
            self.out[here] = total


ORDER = (1, 2, 3, 0)
DMA = pltpu.SemaphoreType.DMA


def add_rows(target, rows, left, right):
    def body(i, carry):
        here = pl.ds(pl.multiple_of(16 * i, 16), 16)
        target(here, (left(here).astype(F32) + right(here).astype(F32)).astype(BF16))
        return carry

    lax.fori_loop(0, rows // 16, body, 0)


class Pair:
    def __init__(self, place, buffers, parts, send_sems, recv_sems):
        self.place, self.buffers, self.parts = place, buffers, parts
        self.send_sems, self.recv_sems = send_sems, recv_sems

    def copy(self, m):
        y = lax.div(m, 2)
        return pltpu.make_async_remote_copy(
            src_ref=self.buffers.at[lax.rem(m, 2)],
            dst_ref=self.parts.at[y],
            send_sem=self.send_sems.at[y],
            recv_sem=self.recv_sems.at[y],
            device_id=self.place.mates[0],
            device_id_type=MESH,
        )

    def send(self, m):
        @pl.when(lax.rem(m, 2) != self.place.c)
        def _():
            self.copy(m).start()

    def free(self, m):
        @pl.when(lax.rem(m, 2) != self.place.c)
        def _():
            self.copy(m).wait_send()

    def take(self, m):
        @pl.when(lax.rem(m, 2) == self.place.c)
        def _():
            y, buffer = lax.div(m, 2), lax.rem(m, 2)
            self.copy(m).wait_recv()

            def store(here, value):
                self.parts[y, here] = value

            add_rows(
                store, D, lambda here: self.buffers[buffer, here], lambda here: self.parts[y, here]
            )


def attend_kernel(
    x_ref, weight_in, mods_ref, qkv_bias_ref, out_bias_ref, column_ref, row_ref, slot_ref,
    groups_ref, mask_ref, up_ref, down_ref,
    first_out, heads_out, mixed_out, lse_ref, attn_ref, after_ref, arrived_ref, picked_ref, weight_out,
    up_out, down_out,
    weight_ref, first_ref, heads_ref, mixed_ref, out_weight_ref, load_sems, save_sems,
    bias_ref, parts_ref, second_ref,
    send_sems, recv_sems, local_sems, down_send, down_recv, down_local,
):
    place = Place()
    place.meet()
    ups = Spread(
        place, up_ref, lambda y, c, z, x: up_out.at[y, c, z, x], send_sems, recv_sems, local_sems
    )
    downs = Column(place, down_ref, down_out, down_send, down_recv, down_local.at[0])
    loads = [
        pltpu.make_async_copy(weight_in.at[j], weight_ref.at[j], load_sems.at[j]) for j in range(4)
    ]
    saves = [
        pltpu.make_async_copy(source, target, save_sems.at[n])
        for n, (source, target) in enumerate(
            (
                (first_ref, first_out),
                (heads_ref, heads_out),
                (out_weight_ref, weight_out),
                (mixed_ref, mixed_out),
            )
        )
    ]
    ups.start()
    for copy in loads:
        copy.start()
    downs.start()
    crop_mask(bias_ref, column_ref, row_ref)

    def norm(i, carry):
        here = rows_at(i)
        segment = column_ref[here, :]
        normed, _ = normalise(x_ref[here, :].astype(F32))
        shift, scale = per_crop(mods_ref[0], segment), per_crop(mods_ref[1], segment)
        first_ref[here, :] = (normed * (1.0 + scale) + shift).astype(BF16)
        return carry

    lax.fori_loop(0, 3, norm, 0)
    saves[0].start()
    for copy in loads:
        copy.wait()
    for j in range(4):
        out_weight_ref[:, OUT_SHARD * j : OUT_SHARD * (j + 1)] = weight_ref[j, :, QKV_SHARD:]
    saves[2].start()

    def project(i, carry):
        j = lax.div(i, 3)
        here = rows_at(lax.rem(i, 3))
        triple = (dot(first_ref[here, :], weight_ref[j, :, :PAD_SHARD]) + qkv_bias_ref[j]).astype(BF16)
        zero = jnp.zeros((BLOCK, 128 - HEAD_DIM), BF16)
        for h in range(12):
            part = triple[:, HEAD_DIM * h : HEAD_DIM * (h + 1)]
            heads_ref[12 * j + h, here, :] = jnp.concatenate([part, zero], axis=1)
        return carry

    lax.fori_loop(0, 12, project, 0)
    saves[1].start()

    def head(h, carry):
        for k in range(4):

            @pl.when(h == 7 + k)
            def _():
                ups.pass_across(k)

        keys, values = heads_ref[16 + h], heads_ref[32 + h]
        for i in range(3):
            here = pl.ds(i * BLOCK, BLOCK)
            scores = dot(heads_ref[h, here, :], keys, NT) * SOFT + bias_ref[here, :]
            top = jnp.max(scores, axis=1, keepdims=True)
            weights = jnp.exp2(scores - top)
            total = jnp.sum(weights, axis=1, keepdims=True)
            keep = head_keep(mask_ref, h, column_ref[here, :])
            parts_ref[h, here, :] = (dot(weights.astype(BF16), values) * (keep / total)).astype(BF16)
            spread = jnp.broadcast_to(top + jnp.log2(total), (BLOCK, 128))
            lse_ref[h, :, here] = jnp.transpose(spread)[:1, :]
        return carry

    lax.fori_loop(0, HEADS, head, 0)
    for h in range(HEADS):
        mixed_ref[:, HEAD_DIM * h : HEAD_DIM * (h + 1)] = parts_ref[h][:, :HEAD_DIM]
    saves[3].start()
    for k in range(4):
        ups.pass_pair(k)

    def close(i, carry):
        here = rows_at(i)
        segment = column_ref[here, :]
        attn = dot(mixed_ref[here, :], out_weight_ref[...]) + out_bias_ref[...]
        attn_ref[here, :] = attn.astype(BF16)
        after = x_ref[here, :].astype(F32) + per_crop(mods_ref[2], segment) * attn
        after_ref[here, :] = after
        normed, _ = normalise(after)
        shift, scale = per_crop(mods_ref[3], segment), per_crop(mods_ref[4], segment)
        second_ref[here, :] = (normed * (1.0 + scale) + shift).astype(BF16)
        return carry

    lax.fori_loop(0, 3, close, 0)
    for i in range(2):
        here = pl.ds(i * BLOCK, BLOCK)
        choice = places_of(slot_ref[...], i)
        arrived_ref[here, :] = dot(choice, second_ref[...]).astype(BF16)
        picked_ref[here, :] = dot(choice, groups_ref[...]).astype(BF16)
    ups.finish()
    downs.finish()
    for copy in saves:
        copy.wait()


def shape_of(*shape, dtype=BF16):
    return jax.ShapeDtypeStruct(shape, dtype)


def talking(number):
    return pltpu.CompilerParams(
        collective_id=number, has_side_effects=True, vmem_limit_bytes=VMEM_BYTES
    )


IN_VMEM = pl.BlockSpec(memory_space=pltpu.VMEM)
IN_SMEM = pl.BlockSpec(memory_space=pltpu.SMEM)
ANYWHERE = pl.BlockSpec(memory_space=pl.ANY)


def attend(x, weight, mods, qkv_bias, out_bias, column, row, slot_row, groups, mask, up, down):
    return pl.pallas_call(
        attend_kernel,
        out_shape=[
            shape_of(TOK_DEV, D),
            shape_of(3 * HEADS, TOK_DEV, 128),
            shape_of(TOK_DEV, D),
            shape_of(HEADS, 1, TOK_DEV, dtype=F32),
            shape_of(TOK_DEV, D),
            shape_of(TOK_DEV, D, dtype=F32),
            shape_of(PLACES, D),
            shape_of(PLACES, 128),
            shape_of(D, D),
            shape_of(2, 2, 4, 2, SHARD, D),
            shape_of(4, SHARD, D),
        ],
        in_specs=[IN_VMEM, ANYWHERE] + [IN_VMEM] * 7 + [IN_SMEM] + [ANYWHERE] * 2,
        out_specs=[ANYWHERE] * 3 + [IN_VMEM] * 5 + [ANYWHERE] * 3,
        scratch_shapes=[
            pltpu.VMEM((4, D, D), BF16),
            pltpu.VMEM((TOK_DEV, D), BF16),
            pltpu.VMEM((3 * HEADS, TOK_DEV, 128), BF16),
            pltpu.VMEM((TOK_DEV, D), BF16),
            pltpu.VMEM((D, D), BF16),
            DMA((4,)),
            DMA((4,)),
            pltpu.VMEM((TOK_DEV, TOK_DEV), F32),
            pltpu.VMEM((HEADS, TOK_DEV, 128), BF16),
            pltpu.VMEM((TOK_DEV, D), BF16),
            DMA((SPREAD_COPIES,)),
            DMA((SPREAD_COPIES,)),
            DMA((4,)),
            DMA((3,)),
            DMA((3,)),
            DMA((1,)),
        ],
        compiler_params=talking(2),
    )(x, weight, mods, qkv_bias, out_bias, column, row, slot_row, groups, mask, up, down)


ROOT = math.sqrt(2.0 / math.pi)


def feed_kernel(
    up_ref, arrived_ref, picked_ref, up_bias_ref, down_bias_ref, cot_ref, after_ref,
    mods_ref, column_ref, slot_column_ref, slot_row_ref, down_ref,
    pull_ref, grad_rows_ref, block_out_ref, gate_ref, bias_ref, parts_ref, down_out,
    active_ref, total_ref, branch_ref, buffers_ref, halves_ref, tiles_ref,
    send_sems, recv_sems, local_sems, pair_send, pair_recv, tile_sems,
):
    step = pl.program_id(0)
    place = Place()
    downs = Spread(
        place, down_ref, lambda y, c, z, x: down_out.at[z, x, y, c], send_sems, recv_sems, local_sems
    )

    def rows_of(x, y, c):
        return pl.ds(pl.multiple_of((4 * x + 2 * y + c) * SHARD, 16), SHARD)

    def pair(m, x, y):
        return pltpu.make_async_remote_copy(
            src_ref=buffers_ref.at[lax.rem(m, 2), rows_of(x, y, 1 - place.c)],
            dst_ref=halves_ref.at[y, m, x],
            send_sem=pair_send.at[m, x, y],
            recv_sem=pair_recv.at[m, x, y],
            device_id=place.mates[0],
            device_id_type=MESH,
        )

    def take(m):
        for x in range(2):
            for y in range(2):
                pair(m, x, y).wait_recv()
                own = rows_of(x, y, place.c)
                mine = buffers_ref.at[lax.rem(m, 2), own]
                for at in range(0, SHARD, 16):
                    here = pl.ds(at, 16)
                    total = mine[here].astype(F32) + halves_ref[y, m, x, here].astype(F32)
                    parts_ref[y, m, x, here] = total.astype(BF16)

    def free(m):
        for x in range(2):
            for y in range(2):
                pair(m, x, y).wait_send()

    def tile(m):
        return [
            pltpu.make_async_copy(
                down_out.at[m, x, y],
                tiles_ref.at[lax.rem(m, 2), x, y],
                tile_sems.at[lax.rem(m, 2), x, y],
            )
            for x in range(2)
            for y in range(2)
        ]

    @pl.when(step == 0)
    def _():
        place.meet()
        downs.start()
        for i in range(3):
            here = pl.ds(i * BLOCK, BLOCK)
            gate = per_crop(mods_ref[5], column_ref[here, :])
            block_out_ref[here, :] = (gate * cot_ref[here, :].astype(F32)).astype(BF16)
        for i in range(2):
            here = pl.ds(i * BLOCK, BLOCK)
            choice = places_of(slot_row_ref[...], i)
            grad_rows_ref[here, :] = dot(choice, block_out_ref[...]).astype(BF16)
        bias_ref[...] = jnp.sum(grad_rows_ref[...].astype(F32), axis=0, keepdims=True)
        total_ref[...] = jnp.zeros_like(total_ref)

    @pl.when(step < 4)
    def _():
        group = lax.broadcasted_iota(jnp.int32, (128, D), 0) - 4 * step
        unit = lax.broadcasted_iota(jnp.int32, (128, D), 1)
        width = FF // GROUPS
        spread = ((unit >= group * width) & (unit < (group + 1) * width)).astype(BF16)
        for i in range(2):
            here = pl.ds(i * BLOCK, BLOCK)
            hidden = dot(arrived_ref[here, :], up_ref[0]) + up_bias_ref[0]
            keep = dot(picked_ref[here, :], spread)
            square = hidden * hidden
            curve = jnp.tanh(ROOT * hidden * (1.0 + 0.044715 * square))
            half = 0.5 * (1.0 + curve)
            slope = half + 0.5 * hidden * (1.0 - curve * curve) * (
                ROOT * (1.0 + 3.0 * 0.044715 * square)
            )
            active_ref[step, here, :] = (hidden * half * keep).astype(BF16)
            pull_ref[0, here, :] = (slope * keep).astype(BF16)

        def grad(i, carry):
            here = pl.ds(pl.multiple_of(i * 384, 384), 384)
            part = dot(active_ref[step, :, here], grad_rows_ref[...], TN).astype(BF16)
            buffers_ref[lax.rem(step, 2), here, :] = part
            return carry

        @pl.when(step >= 2)
        def _():
            free(step - 2)

        lax.fori_loop(0, 3, grad, 0)
        for x in range(2):
            for y in range(2):
                pair(step, x, y).start()

    @pl.when((step >= 1) & (step < 5))
    def _():
        take(step - 1)

    @pl.when(step == 3)
    def _():
        for k in range(4):
            downs.pass_across(k)

    @pl.when(step == 4)
    def _():
        free(2)
        free(3)
        for k in range(4):
            downs.pass_pair(k)
        downs.finish()
        for m in (0, 1):
            for copy in tile(m):
                copy.start()

    @pl.when(step >= 4)
    def _():
        m = step - 4
        for copy in tile(m):
            copy.wait()
        weights = tiles_ref[lax.rem(m, 2)].reshape(D, D)
        for i in range(2):
            here = pl.ds(i * BLOCK, BLOCK)
            total_ref[here, :] += dot(active_ref[m, here, :], weights)

        @pl.when(m < 2)
        def _():
            for copy in tile(m + 2):
                copy.start()

    @pl.when(step == 7)
    def _():
        branch_ref[...] = (total_ref[...] + down_bias_ref[...]).astype(BF16)
        gates = jnp.zeros((8, D), F32)
        for i in range(3):
            here = pl.ds(i * BLOCK, BLOCK)
            segment = column_ref[here, :]
            branch = dot(tokens_of(slot_column_ref[here, :]), branch_ref[...])
            gate = per_crop(mods_ref[5], segment)
            block_out_ref[here, :] = (after_ref[here, :] + gate * branch).astype(BF16)
            gates = gates + crop_sums(segment, cot_ref[here, :].astype(F32) * branch)
        gate_ref[...] = gates


def whole(*shape):
    return pl.BlockSpec(shape, lambda i: (0,) * len(shape), pipeline_mode=pl.Buffered(1))


def feed(up, arrived, picked, up_bias, down_bias, cot, after, mods, column, slot_column, slot_row, down):
    early = lambda *tail: pl.BlockSpec((1, *tail), lambda i: (jnp.minimum(i, 3), 0, 0))
    return pl.pallas_call(
        feed_kernel,
        grid=(8,),
        out_shape=[
            shape_of(4, PLACES, D),
            shape_of(PLACES, D),
            shape_of(TOK_DEV, D),
            shape_of(8, D, dtype=F32),
            shape_of(1, D, dtype=F32),
            shape_of(2, 4, 2, SHARD, D),
            shape_of(4, 2, 2, 2, SHARD, D),
        ],
        in_specs=[
            early(D, D), whole(PLACES, D), whole(PLACES, 128), early(1, D), whole(1, D),
            whole(TOK_DEV, D), whole(TOK_DEV, D), whole(6, 8, D), whole(TOK_DEV, 1), whole(TOK_DEV, 1),
            whole(1, TOK_DEV), ANYWHERE,
        ],
        out_specs=[
            early(PLACES, D), whole(PLACES, D), whole(TOK_DEV, D), whole(8, D), whole(1, D),
            whole(2, 4, 2, SHARD, D), ANYWHERE,
        ],
        scratch_shapes=[
            pltpu.VMEM((4, PLACES, D), BF16),
            pltpu.VMEM((PLACES, D), F32),
            pltpu.VMEM((PLACES, D), BF16),
            pltpu.VMEM((2, D, D), BF16),
            pltpu.VMEM((2, 4, 2, SHARD, D), BF16),
            pltpu.VMEM((2, 2, 2, 2, SHARD, D), BF16),
            DMA((SPREAD_COPIES,)),
            DMA((SPREAD_COPIES,)),
            DMA((4,)),
            DMA((4, 2, 2)),
            DMA((4, 2, 2)),
            DMA((2, 2, 2)),
        ],
        compiler_params=talking(3),
    )(up, arrived, picked, up_bias, down_bias, cot, after, mods, column, slot_column, slot_row, down)


def unfeed_kernel(
    down_ref, up_ref, pull_ref, grad_rows_ref, arrived_ref, after_ref, cot_ref, attn_ref, mods_ref,
    column_ref, slot_column_ref, given_ref,
    up_bias_ref, mid_ref, grad_attn_ref, sums_ref, out_bias_ref, parts_out, plane_ref,
    hidden_ref, total_ref, back_ref, buffers_ref, parts_ref, bufs_ref,
    send_sems, recv_sems, pair_send, pair_recv, out_sem,
):
    step = pl.program_id(0)
    place = Place()
    scatter = Scatter(place, given_ref, bufs_ref, plane_ref, send_sems, recv_sems)
    pair = Pair(place, buffers_ref, parts_ref, pair_send, pair_recv)

    @pl.when(step == 0)
    def _():
        place.meet()
        for k in ORDER:
            scatter.start(k)
        total_ref[...] = jnp.zeros_like(total_ref)

    bias = jnp.zeros((1, D), F32)
    for i in range(2):
        here = pl.ds(i * BLOCK, BLOCK)
        grad = dot(grad_rows_ref[here, :], down_ref[0], NT) * pull_ref[0, here, :].astype(F32)
        low = grad.astype(BF16)
        hidden_ref[here, :] = low
        bias = bias + jnp.sum(low.astype(F32), axis=0, keepdims=True)
        total_ref[here, :] += dot(low, up_ref[0], NT)
    up_bias_ref[0] = bias

    def grad_of(i, carry):
        here = pl.ds(pl.multiple_of(i * 384, 384), 384)
        part = dot(arrived_ref[:, here], hidden_ref[...], TN).astype(BF16)
        buffers_ref[lax.rem(step, 2), here, :] = part
        return carry

    @pl.when(step >= 2)
    def _():
        pair.free(step - 2)

    lax.fori_loop(0, 3, grad_of, 0)
    pair.send(step)

    @pl.when(step >= 1)
    def _():
        pair.take(step - 1)

    @pl.when(step == 0)
    def _():
        for k in ORDER:
            scatter.follow(k)

    for here_step, ks in ((1, (1, 2)), (2, (3, 0))):

        @pl.when(step == here_step)
        def _():
            for k in ks:
                scatter.pass_across(k)

    @pl.when(step == 3)
    def _():
        back_ref[...] = total_ref[...].astype(BF16)
        shifts, scales = jnp.zeros((8, D), F32), jnp.zeros((8, D), F32)
        gates, out_bias = jnp.zeros((8, D), F32), jnp.zeros((1, D), F32)
        for i in range(3):
            here = pl.ds(i * BLOCK, BLOCK)
            segment = column_ref[here, :]
            second = dot(tokens_of(slot_column_ref[here, :]), back_ref[...])
            normed, inverse = normalise(after_ref[here, :])
            grad = second * (1.0 + per_crop(mods_ref[4], segment))
            mean = jnp.mean(grad, axis=1, keepdims=True)
            slant = jnp.mean(grad * normed, axis=1, keepdims=True)
            mid = cot_ref[here, :].astype(F32) + inverse * (grad - mean - normed * slant)
            mid_ref[here, :] = mid
            low = (per_crop(mods_ref[2], segment) * mid).astype(BF16)
            grad_attn_ref[here, :] = low
            out_bias = out_bias + jnp.sum(low.astype(F32), axis=0, keepdims=True)
            shifts = shifts + crop_sums(segment, second)
            scales = scales + crop_sums(segment, second * normed)
            gates = gates + crop_sums(segment, mid * attn_ref[here, :].astype(F32))
        sums_ref[0], sums_ref[1], sums_ref[2] = gates, shifts, scales
        out_bias_ref[...] = out_bias
        pair.free(2)
        pair.free(3)
        pair.take(3)
        leave = pltpu.make_async_copy(parts_ref, parts_out, out_sem.at[0])
        leave.start()
        for k in ORDER:
            scatter.collect(k)
        scatter.finish()
        leave.wait()


def unfeed(down, up, pull, grad_rows, arrived, after, cot, attn, mods, column, slot_column, given):
    block = lambda *tail: pl.BlockSpec((1, *tail), lambda i: (i, 0, 0))
    return pl.pallas_call(
        unfeed_kernel,
        grid=(4,),
        out_shape=[
            shape_of(4, 1, D, dtype=F32),
            shape_of(TOK_DEV, D, dtype=F32),
            shape_of(TOK_DEV, D),
            shape_of(3, 8, D, dtype=F32),
            shape_of(1, D, dtype=F32),
            shape_of(2, D, D),
            shape_of(4, SHARD, D),
        ],
        in_specs=[
            block(D, D), block(D, D), block(PLACES, D), whole(PLACES, D), whole(PLACES, D),
            whole(TOK_DEV, D), whole(TOK_DEV, D), whole(TOK_DEV, D), whole(6, 8, D), whole(TOK_DEV, 1),
            whole(TOK_DEV, 1), whole(2, 4, 2, SHARD, D),
        ],
        out_specs=[
            block(1, D), whole(TOK_DEV, D), whole(TOK_DEV, D), whole(3, 8, D), whole(1, D), ANYWHERE, whole(4, SHARD, D),
        ],
        scratch_shapes=[
            pltpu.VMEM((PLACES, D), BF16),
            pltpu.VMEM((PLACES, D), F32),
            pltpu.VMEM((PLACES, D), BF16),
            pltpu.VMEM((2, D, D), BF16),
            pltpu.VMEM((2, D, D), BF16),
            pltpu.VMEM((4, 4, SHARD, D), BF16),
            DMA((SCATTER_COPIES,)),
            DMA((SCATTER_COPIES,)),
            DMA((2,)),
            DMA((2,)),
            DMA((1,)),
        ],
        compiler_params=talking(4),
    )(down, up, pull, grad_rows, arrived, after, cot, attn, mods, column, slot_column, given)


def unattend_kernel(
    grad_ref, weight_in, heads_in, lse_ref, column_ref, row_ref, given_in, plane_ref, mask_ref,
    triple_ref, sums_ref, share_ref, plane_out, split_out,
    out_weight_ref, heads_ref, given_ref, split_ref, load_sems,
    bias_ref, mixed_ref, grads_ref, key_ref, value_ref, bufs_ref, from_z_ref,
    send_sems, recv_sems, along_send, along_recv,
):
    place = Place()
    place.meet()
    scatter = Scatter(place, given_ref, bufs_ref, plane_out, send_sems, recv_sems)
    along = Along(place, plane_ref, from_z_ref, share_ref, along_send, along_recv)
    loads = [
        pltpu.make_async_copy(source, target, load_sems.at[n])
        for n, (source, target) in enumerate(
            ((given_in, given_ref), (weight_in, out_weight_ref), (heads_in, heads_ref))
        )
    ]
    save = pltpu.make_async_copy(split_ref, split_out, load_sems.at[3])
    for copy in loads:
        copy.start()
    for k in (1, 2, 3):
        along.start(k)
    for j in range(4):
        split_ref[j] = grad_ref[:, OUT_SHARD * j : OUT_SHARD * (j + 1)]
    save.start()
    loads[0].wait()
    for k in ORDER:
        scatter.start(k)
    loads[1].wait()
    crop_mask(bias_ref, column_ref, row_ref)

    def spread(i, carry):
        here = rows_at(i)
        segment = column_ref[here, :]
        mixed = dot(grad_ref[here, :], out_weight_ref[...], NT)
        zero = jnp.zeros((BLOCK, 128 - HEAD_DIM), BF16)
        for h in range(HEADS):
            part = mixed[:, HEAD_DIM * h : HEAD_DIM * (h + 1)] * head_keep(mask_ref, h, segment)
            mixed_ref[h, here, :] = jnp.concatenate([part.astype(BF16), zero], axis=1)
        return carry

    lax.fori_loop(0, 3, spread, 0)
    factor = HEAD_DIM**-0.5
    loads[2].wait()

    def head(h, carry):
        @pl.when(h == 1)
        def _():
            for k in ORDER:
                scatter.follow(k)

        for at, k in enumerate(ORDER):

            @pl.when(h == 4 + at)
            def _():
                scatter.pass_across(k)

        keys, values = heads_ref[16 + h], heads_ref[32 + h]
        turned = jnp.transpose(keys)
        for i in range(3):
            here = pl.ds(i * BLOCK, BLOCK)
            queries, grads = heads_ref[h, here, :], mixed_ref[h, here, :]
            scores = dot(keys, queries, NT) * SOFT + bias_ref[:, here]
            probs = jnp.exp2(scores - lse_ref[h, :, here])
            product = probs * dot(values, grads, NT)
            total = jnp.sum(product, axis=0, keepdims=True)
            low = (product - probs * total).astype(BF16)
            for_values, for_keys = dot(probs.astype(BF16), grads), dot(low, queries)
            if i == 0:
                value_ref[...], key_ref[...] = for_values, for_keys
            else:
                value_ref[...] += for_values
                key_ref[...] += for_keys
            grads_ref[h, here, :] = jnp.transpose(dot(turned, low) * factor).astype(BF16)
        grads_ref[16 + h] = (key_ref[...] * factor).astype(BF16)
        grads_ref[32 + h] = value_ref[...].astype(BF16)
        return carry

    lax.fori_loop(0, HEADS, head, 0)
    for j in range(4):
        triple_ref[j, :, QKV_SHARD:] = jnp.zeros((TOK_DEV, PAD_SHARD - QKV_SHARD), BF16)
        for h in range(12):
            triple_ref[j, :, HEAD_DIM * h : HEAD_DIM * (h + 1)] = grads_ref[12 * j + h][:, :HEAD_DIM]
        sums_ref[j] = jnp.sum(triple_ref[j].astype(F32), axis=0, keepdims=True)
    save.wait()
    along.close()
    for k in ORDER:
        scatter.collect(k)
    scatter.finish()


def unattend(grad_attn, out_weight, heads, lse, column, row, given, plane, mask):
    return pl.pallas_call(
        unattend_kernel,
        out_shape=[
            shape_of(4, TOK_DEV, PAD_SHARD),
            shape_of(4, 1, PAD_SHARD, dtype=F32),
            shape_of(SHARD, D, dtype=F32),
            shape_of(4, SHARD, D),
            shape_of(4, TOK_DEV, OUT_SHARD),
        ],
        in_specs=[IN_VMEM] + [ANYWHERE] * 2 + [IN_VMEM] * 3 + [ANYWHERE, IN_VMEM, IN_SMEM],
        out_specs=[IN_VMEM] * 4 + [ANYWHERE],
        scratch_shapes=[
            pltpu.VMEM((D, D), BF16),
            pltpu.VMEM((3 * HEADS, TOK_DEV, 128), BF16),
            pltpu.VMEM((2, 4, 2, SHARD, D), BF16),
            pltpu.VMEM((4, TOK_DEV, OUT_SHARD), BF16),
            DMA((4,)),
            pltpu.VMEM((TOK_DEV, TOK_DEV), F32),
            pltpu.VMEM((HEADS, TOK_DEV, 128), BF16),
            pltpu.VMEM((3 * HEADS, TOK_DEV, 128), BF16),
            pltpu.VMEM((TOK_DEV, 128), F32),
            pltpu.VMEM((TOK_DEV, 128), F32),
            pltpu.VMEM((4, 4, SHARD, D), BF16),
            pltpu.VMEM((3, SHARD, D), BF16),
            DMA((SCATTER_COPIES,)),
            DMA((SCATTER_COPIES,)),
            DMA((3,)),
            DMA((3,)),
        ],
        compiler_params=talking(5),
    )(grad_attn, out_weight, heads, lse, column, row, given, plane, mask)


def unproject_kernel(
    weight_ref, triple_ref, split_ref, first_ref, mixed_ref, x_ref, mid_ref, mods_ref, column_ref,
    plane_up_ref, rest_ref, conds_ref, down_ref,
    grad_in_ref, share_up_ref, qkv_ref, out_ref, ada_ref, sums_ref, share_down_ref,
    share_ref, turn_ref, turned_ref, total_ref, buffers_ref, parts_ref, bufs_ref, plane_ref, up_z_ref, from_z_ref,
    mod_ref, mates_ref, rows_ref, packed_ref, every_ref,
    send_sems, recv_sems, pair_send, pair_recv, up_send, up_recv, along_send, along_recv,
    small_send, small_recv,
):
    step = pl.program_id(0)
    place = Place()
    pair = Pair(place, buffers_ref, parts_ref, pair_send, pair_recv)
    blocks = parts_ref.reshape(2, 4, 2, SHARD, D)
    scatter = Scatter(place, blocks, bufs_ref, plane_ref, send_sems, recv_sems)
    along_up = Along(place, plane_up_ref, up_z_ref, share_up_ref, up_send, up_recv)
    along = Along(place, plane_ref, from_z_ref, share_ref, along_send, along_recv)
    small = Copies(small_send, small_recv)
    to_mates = [
        small.make(mod_ref.at[other], mates_ref.at[place.index], mate)
        for other, mate in zip(place.mate_index, place.mates)
    ]
    to_peers = []
    for k in range(4):
        for there in (place.x, 1 - place.x) if k else (1 - place.x,):
            other = place.device(z=place.zs[k], x=there)
            to_peers.append(small.make(packed_ref, every_ref.at[place.peer], other))
    swaps = [
        small.make(turn_ref.at[other], turned_ref.at[place.index], mate)
        for other, mate in zip(place.mate_index, place.mates)
    ]
    @pl.when(step == 0)
    def _():
        place.meet()
        for k in (2, 3, 1):
            along_up.start(k)
        for j in range(4):
            turn_ref[j] = down_ref[:, OUT_SHARD * j : OUT_SHARD * (j + 1)]
        for copy in swaps:
            copy.start()
        turned_ref[place.index] = turn_ref[place.index]

    @pl.when(step < 4)
    def _():
        def grad(i, carry):
            here = pl.ds(pl.multiple_of(i * 384, 384), 384)
            buffer = lax.rem(step, 2)
            part = dot(first_ref[:, here], triple_ref[0], TN).astype(BF16)
            buffers_ref[buffer, here, :PAD_SHARD] = part
            part = dot(mixed_ref[:, here], split_ref[0], TN).astype(BF16)
            buffers_ref[buffer, here, QKV_SHARD:] = part
            return carry

        @pl.when(step >= 2)
        def _():
            pair.free(step - 2)

        lax.fori_loop(0, 3, grad, 0)
        pair.send(step)

    @pl.when((step >= 1) & (step < 5))
    def _():
        pair.take(step - 1)

    @pl.when(step == 4)
    def _():
        pair.free(2)
        pair.free(3)
        scatter.start(2)
        scatter.follow(2)
        scatter.start(3)

    for at, now, then in ((5, 2, 3), (6, 3, 1), (7, 1, 0)):

        @pl.when(step == at)
        def _():
            scatter.pass_across(now)
            scatter.follow(then)
            if at < 7:
                scatter.start(1 if at == 5 else 0)

    @pl.when(step >= 4)
    def _():
        for i in range(3):
            here = pl.ds(i * BLOCK, BLOCK)
            part = dot(triple_ref[0, here, :], weight_ref[0, :, :PAD_SHARD], NT)
            total_ref[here, :] = jnp.where(step == 4, part, total_ref[here, :] + part)

    @pl.when(step == 7)
    def _():
        scatter.collect(2)
        along.start(2)
        scatter.pass_across(0)
        shifts, scales = jnp.zeros((8, D), F32), jnp.zeros((8, D), F32)
        for i in range(3):
            here = pl.ds(i * BLOCK, BLOCK)
            segment = column_ref[here, :]
            first = total_ref[here, :]
            normed, inverse = normalise(x_ref[here, :].astype(F32))
            grads = first * (1.0 + per_crop(mods_ref[1], segment))
            mean = jnp.mean(grads, axis=1, keepdims=True)
            slant = jnp.mean(grads * normed, axis=1, keepdims=True)
            grad_in_ref[here, :] = mid_ref[here, :] + inverse * (grads - mean - normed * slant)
            shifts = shifts + crop_sums(segment, first)
            scales = scales + crop_sums(segment, first * normed)
        mod_ref[...] = rest_ref[...]
        mod_ref[0, :CROPS, :D] = shifts[:CROPS]
        mod_ref[0, :CROPS, D:] = scales[:CROPS, : D // 2]
        mod_ref[1, :CROPS, : D // 2] = scales[:CROPS, D // 2 :]
        for copy in to_mates:
            copy.start()
        mates_ref[place.index] = mod_ref[place.index]
        scatter.collect(3)
        along.start(3)
        for copy in to_mates:
            copy.wait_recv()
        rows_ref[...] = jnp.zeros_like(rows_ref)
        for j in range(4):
            rows_ref[CROPS * j : CROPS * (j + 1), :] = mates_ref[j, :CROPS, :]
            rows_ref[12:14, :] += mates_ref[j, CROPS : CROPS + 2, :]
        packed_ref[...] = rows_ref[...].astype(BF16)
        for copy in to_peers:
            copy.start()
        every_ref[place.peer] = packed_ref[...]
        scatter.collect(1)
        along.start(1)
        along_up.close()
        for copy in swaps:
            copy.wait_recv()
        share_down_ref[...] = turned_ref[...]
        scatter.collect(0)
        for copy in to_peers:
            copy.wait_recv()
        close_ada(conds_ref, every_ref, ada_ref, sums_ref)
        along.close()
        qkv_ref[...] = share_ref[:, :QKV_SHARD]
        out_ref[...] = share_ref[:, QKV_SHARD:]
        scatter.finish()
        for copy in small.made:
            copy.wait_send()


def unproject(weight, triple, split, first, mixed, x, mid, mods, column, plane_up, rest, conds, down):
    block = lambda *tail: pl.BlockSpec((1, *tail), lambda i: (lax.rem(i, 4), 0, 0))
    early = lambda *tail: pl.BlockSpec((1, *tail), lambda i: (jnp.minimum(i, 3), 0, 0))
    late = lambda *tail: pl.BlockSpec((1, *tail), lambda i: (jnp.maximum(i - 4, 0), 0, 0))
    wide = rest.shape[2]
    vmem = pltpu.VMEM
    return pl.pallas_call(
        unproject_kernel,
        grid=(8,),
        out_shape=[
            shape_of(TOK_DEV, D, dtype=F32),
            shape_of(SHARD, D, dtype=F32),
            shape_of(SHARD, QKV_SHARD, dtype=F32),
            shape_of(SHARD, OUT_SHARD, dtype=F32),
            shape_of(SHARD, wide, dtype=F32),
            shape_of(8, wide, dtype=F32),
            shape_of(4, SHARD, OUT_SHARD, dtype=F32),
        ],
        in_specs=[
            late(D, D), block(TOK_DEV, PAD_SHARD), early(TOK_DEV, OUT_SHARD), whole(TOK_DEV, D),
            whole(TOK_DEV, D), whole(TOK_DEV, D), whole(TOK_DEV, D), whole(6, 8, D), whole(TOK_DEV, 1),
            whole(4, SHARD, D), whole(4, 8, wide), whole(8, 16, 256), whole(SHARD, D),
        ],
        out_specs=[
            whole(TOK_DEV, D), whole(SHARD, D), whole(SHARD, QKV_SHARD), whole(SHARD, OUT_SHARD),
            whole(SHARD, wide), whole(8, wide), whole(4, SHARD, OUT_SHARD),
        ],
        scratch_shapes=[
            vmem((SHARD, D), F32),
            vmem((4, SHARD, OUT_SHARD), F32),
            vmem((4, SHARD, OUT_SHARD), F32),
            vmem((TOK_DEV, D), F32),
            vmem((2, D, D), BF16),
            vmem((2, D, D), BF16),
            vmem((4, 4, SHARD, D), BF16),
            vmem((4, SHARD, D), BF16),
            vmem((3, SHARD, D), BF16),
            vmem((3, SHARD, D), BF16),
            vmem((4, 8, wide), F32),
            vmem((4, 8, wide), F32),
            vmem((16, wide), F32),
            vmem((16, wide), BF16),
            vmem((8, 16, wide), BF16),
            DMA((SCATTER_COPIES,)),
            DMA((SCATTER_COPIES,)),
            DMA((2,)),
            DMA((2,)),
            DMA((3,)),
            DMA((3,)),
            DMA((3,)),
            DMA((3,)),
            DMA((13,)),
            DMA((13,)),
        ],
        compiler_params=talking(6),
    )(weight, triple, split, first, mixed, x, mid, mods, column, plane_up, rest, conds, down)


CROPS = 3


def gather_kernel(
    qkv_ref, out_ref, up_ref, down_ref, cond_ref, ada_ref, vectors_ref, slot_ref, groups_ref, lengths_ref,
    mixed_out, up_out, down_out, mods_ref, conds_ref, qkv_bias_ref, up_bias_ref, out_bias_ref,
    down_bias_ref, column_ref, row_ref, slot_column_ref, token_groups_ref,
    send_sems, recv_sems, local_sem, up_send, up_recv, up_local, small_send, small_recv, local_small,
    mixed_ref, stage_ref, own_small, all_small, own_cond, partial_ref, from_x, from_z, rows_ref, tables_ref,
    query_ref, value_ref,
):
    place = Place()
    place.meet()
    x, zs = place.x, place.zs
    mixed_ref[:, :QKV_SHARD] = qkv_ref[...]
    mixed_ref[:, QKV_SHARD:] = out_ref[...]
    first = Gather(
        place,
        mixed_ref,
        lambda y, c, z, x: mixed_out.at[y, c, z, x],
        send_sems,
        recv_sems,
        local_sem.at[0],
        False,
    )
    ups = Column(place, up_ref, up_out, up_send, up_recv, up_local.at[0])
    small = Copies(small_send, small_recv)
    to_mates = [small.make(own_small, all_small.at[place.index], mate) for mate in place.mates]
    others = [(k, far) for k in range(4) for far in (0, 1) if k or far]
    to_peers = []
    for k, far in others:
        there = 1 - x if far else x
        to_peers.append(
            small.make(
                own_cond.at[2 * zs[k] + there],
                conds_ref.at[place.peer],
                place.device(z=zs[k], x=there),
            )
        )
    over_x = [
        small.make(partial_ref.at[2 * zs[k] + 1 - x], from_x.at[k], place.device(x=1 - x))
        for k in range(4)
    ]
    along = [
        small.make(partial_ref.at[2 * zs[k] + x], from_z.at[k - 1], place.device(z=zs[k]))
        for k in (1, 2, 3)
    ]
    finals = [
        small.make(rows_ref.at[other], tables_ref.at[place.index], mate)
        for other, mate in zip(place.mate_index, place.mates)
    ]

    def down_rows(index):
        return down_ref.at[pl.ds(pl.multiple_of(index * SHARD, 16), SHARD)]

    swaps = [
        small.make(down_rows(other), stage_ref.at[place.index], mate)
        for other, mate in zip(place.mate_index, place.mates)
    ]
    own_stage = pltpu.make_async_copy(
        down_rows(place.index), stage_ref.at[place.index], local_small.at[0]
    )

    first.start()
    cond = cond_ref[...].astype(F32)
    own_small[...] = jnp.zeros_like(own_small)
    own_small[:CROPS, :] = (cond / (1.0 + jnp.exp(-cond))).astype(BF16).astype(F32)
    own_small[CROPS : CROPS + 1, :] = vectors_ref[:, :D]
    own_small[CROPS + 1 : CROPS + 2, :] = vectors_ref[:, D : 2 * D]
    for copy in to_mates:
        copy.start()
    own_stage.start()
    all_small[place.index] = own_small[...]
    own_cond[...] = jnp.zeros_like(own_cond)
    for copy in to_mates:
        copy.wait_recv()
    for i in range(8):
        for j in range(4):
            part = all_small[j, :CROPS, SHARD * i : SHARD * (i + 1)]
            own_cond[i, CROPS * j : CROPS * (j + 1), :SHARD] = part
    for copy in to_peers:
        copy.start()
    conds_ref[place.peer] = own_cond[place.peer]
    for copy in to_peers:
        copy.wait_recv()
    every_cond = conds_ref[...].reshape(128, 256)[:, :SHARD].astype(BF16)
    partial_ref[...] = dot(every_cond, ada_ref[...]).reshape(partial_ref.shape)
    for k in ORDER:
        over_x[k].start()
    first.pass_across(0)
    for k in (1, 2, 3):
        first.pass_along(k)
    for k in ORDER:
        over_x[k].wait_recv()
        partial_ref[2 * zs[k] + x] += from_x[k]
        if k:
            along[k - 1].start()
    first_end = lengths_ref[0, 0]
    second_end = first_end + lengths_ref[0, 1]
    tokens = lax.broadcasted_iota(jnp.int32, (TOK_DEV, 1), 0)
    column_ref[...] = (tokens >= first_end).astype(jnp.int32) + (tokens >= second_end).astype(jnp.int32)
    tokens = lax.broadcasted_iota(jnp.int32, (1, TOK_DEV), 1)
    row_ref[...] = (tokens >= first_end).astype(jnp.int32) + (tokens >= second_end).astype(jnp.int32)
    spread = jnp.broadcast_to(slot_ref[...].astype(F32), (128, TOK_DEV))
    slot_column_ref[...] = jnp.transpose(spread)[:, :1].astype(jnp.int32)
    token_groups_ref[...] = jnp.zeros_like(token_groups_ref)
    token_groups_ref[:, :GROUPS] = per_crop(groups_ref[...].astype(F32), column_ref[...]).astype(BF16)
    first.pass_across(1)
    for copy in along:
        copy.wait_recv()
    total = partial_ref[place.peer] + from_z[0] + from_z[1] + from_z[2] + vectors_ref[:, 2 * D :]
    rows_ref[...] = jnp.zeros_like(rows_ref)
    for j in range(4):
        rows_ref[j, :CROPS, :] = total[CROPS * j : CROPS * (j + 1)]
    for copy in finals:
        copy.start()
    tables_ref[place.index] = rows_ref[place.index]
    ups.start()
    for copy in swaps:
        copy.start()
    first.pass_across(2)
    for copy in finals:
        copy.wait_recv()
    for j in (0, 2):
        mods_ref[3 * j // 2] = tables_ref[j, :, :D]
        mods_ref[3 * j // 2 + 1, :, : D // 2] = tables_ref[j, :, D:]
        mods_ref[3 * j // 2 + 1, :, D // 2 :] = tables_ref[j + 1, :, : D // 2]
        mods_ref[3 * j // 2 + 2] = tables_ref[j + 1, :, D // 2 :]
    first.pass_pair(0)
    first.pass_across(3)
    for copy in swaps:
        copy.wait_recv()
    own_stage.wait()
    for j in range(4):
        here = slice(OUT_SHARD * j, OUT_SHARD * (j + 1))
        down_out[:, here] = stage_ref[j]
        up_bias_ref[j] = all_small[j, CROPS : CROPS + 1, :]
        row = all_small[j, CROPS + 1 : CROPS + 2, :]
        query_ref[:, here] = row[:, :OUT_SHARD]
        value_ref[:, here] = row[:, OUT_SHARD : 2 * OUT_SHARD]
        out_bias_ref[:, here] = row[:, 2 * OUT_SHARD : 3 * OUT_SHARD]
        down_bias_ref[:, here] = row[:, 3 * OUT_SHARD :]
    qkv_bias_ref[...] = jnp.zeros_like(qkv_bias_ref)
    qkv_bias_ref[0, :, :QKV_SHARD] = query_ref[:, :QKV_SHARD]
    qkv_bias_ref[1, :, :OUT_SHARD] = query_ref[:, QKV_SHARD:]
    qkv_bias_ref[2, :, 2 * OUT_SHARD : QKV_SHARD] = value_ref[:, :OUT_SHARD]
    qkv_bias_ref[3, :, :QKV_SHARD] = value_ref[:, OUT_SHARD:]
    for k in (1, 2, 3):
        first.pass_pair(k)
    first.finish()
    ups.finish()
    for copy in small.made:
        copy.wait_send()


def gather_all(qkv, out, up, down, cond, ada, vectors, slot, groups, lengths):
    vmem = pltpu.VMEM
    wide = ada.shape[1]
    return pl.pallas_call(
        gather_kernel,
        out_shape=[
            shape_of(2, 2, 4, 2, SHARD, D),
            shape_of(4, SHARD, D),
            shape_of(SHARD, D),
            shape_of(6, 8, D, dtype=F32),
            shape_of(8, 16, 256, dtype=F32),
            shape_of(4, 1, PAD_SHARD, dtype=F32),
            shape_of(4, 1, D, dtype=F32),
            shape_of(1, D, dtype=F32),
            shape_of(1, D, dtype=F32),
            shape_of(TOK_DEV, 1, dtype=jnp.int32),
            shape_of(1, TOK_DEV, dtype=jnp.int32),
            shape_of(TOK_DEV, 1, dtype=jnp.int32),
            shape_of(TOK_DEV, 128),
        ],
        in_specs=[IN_VMEM] * 2 + [ANYWHERE] * 2 + [IN_VMEM] * 5 + [IN_SMEM],
        out_specs=[ANYWHERE] * 2 + [IN_VMEM] * 11,
        scratch_shapes=[DMA((GATHER_COPIES,))] * 2
        + [DMA((1,)), DMA((3,)), DMA((3,)), DMA((1,)), DMA((23,)), DMA((23,)), DMA((1,))]
        + [
            vmem((SHARD, D), BF16),
            vmem((4, SHARD, OUT_SHARD), BF16),
            vmem((8, D), F32),
            vmem((4, 8, D), F32),
            vmem((8, 16, 256), F32),
            vmem((8, 16, wide), F32),
            vmem((4, 16, wide), F32),
            vmem((3, 16, wide), F32),
            vmem((4, 8, wide), F32),
            vmem((4, 8, wide), F32),
            vmem((1, D), F32),
            vmem((1, D), F32),
        ],
        compiler_params=talking(1),
    )(qkv, out, up, down, cond, ada, vectors, slot, groups, lengths)


def close_ada(conds_ref, every, ada_ref, sums_ref):
    rows = jnp.zeros((16, ada_ref.shape[1]), F32)
    for i in range(8):
        rows = rows + every[i].astype(F32)
    cond = conds_ref[...].reshape(128, 256)[:, :SHARD].astype(BF16)
    total = dot(cond, every[...].reshape(128, ada_ref.shape[1]), TN)
    ada_ref[...] = total
    sums_ref[...] = jnp.zeros_like(sums_ref)
    sums_ref[0:1, :] = jnp.sum(rows[:12], axis=0, keepdims=True)
    sums_ref[1:3, :] = rows[12:14]


def block_shards(
    block_in, condition, lengths, head_mask, group_mask, buffer_slot, ada_weight, ada_bias, qkv_weight,
    query_bias, value_bias, out_weight, out_bias, up_weight, up_bias, down_weight, down_bias, cotangent,
):
    x, cot, slot_row, mask = block_in[0], cotangent[0], buffer_slot.astype(jnp.int32), head_mask[0]
    vectors = (up_bias, query_bias, value_bias, out_bias, down_bias, ada_bias)
    total = sum(vector.shape[0] for vector in vectors)
    starts = (0, 1152, 1440, 1728, 2016, 2304)
    padded = [
        jnp.pad(vector.astype(F32), (start, total - start - vector.shape[0]))
        for start, vector in zip(starts, vectors)
    ]
    vectors = sum(padded)[None]
    (
        mixed_weight, up_column, down_rows, mods, conds, qkv_bias, bias_up, bias_out, bias_down,
        column, row, slot_column, groups,
    ) = gather_all(
        qkv_weight, out_weight, up_weight, down_weight, condition[0], ada_weight, vectors, slot_row,
        group_mask[0], lengths,
    )
    mixed_weight = mixed_weight.reshape(4, D, D)
    edges = (0, 288, 576, 864, 2016, 2304)
    first, heads, mixed, lse, attn, after, arrived, picked, full_out, up, down_column = attend(
        x, mixed_weight, mods, qkv_bias, bias_out, column, row, slot_row, groups, mask, up_column,
        down_rows,
    )
    up = up.reshape(4, D, D)
    pull, grad_rows, block_out, gate_two, grad_down_bias, parts_down, down = feed(
        up, arrived, picked, bias_up, bias_down, cot, after, mods, column,
        slot_column, slot_row, down_column,
    )
    down = down.reshape(4, D, D)
    grad_up_bias, mid, grad_attn, sums, grad_out_bias, parts_up, plane_down = unfeed(
        down, up, pull, grad_rows, arrived, after, cot, attn, mods, column, slot_column, parts_down
    )
    triple, triple_sums, share_down, plane_up, grad_split = unattend(
        grad_attn, full_out, heads, lse, column, row, parts_up.reshape(2, 4, 2, SHARD, D), plane_down,
        mask,
    )
    triple_sums = triple_sums[:, 0, :QKV_SHARD].reshape(3 * D)
    blank = jnp.zeros((8, 2 * D), F32)
    mod_grads = jnp.concatenate([blank, sums[0], sums[1], sums[2], gate_two], axis=1)[:CROPS]
    mod_grads = mod_grads.reshape(CROPS, 4, -1).transpose(1, 0, 2)
    bias_grads = (
        triple_sums[:D], triple_sums[2 * D :], grad_out_bias, grad_up_bias, grad_down_bias,
    )
    bias_grads = jnp.concatenate([vector.reshape(4, -1) for vector in bias_grads], axis=1)
    wide = mod_grads.shape[2]
    bias_grads = jnp.pad(bias_grads, ((0, 0), (0, 5 * wide - 2304))).reshape(4, 5, wide)
    rest = jnp.concatenate([mod_grads, bias_grads], axis=1)
    grad_in, share_up, share_qkv, share_out, grad_ada, totals, share_down = unproject(
        mixed_weight, triple, grad_split, first, mixed, x, mid, mods, column, plane_up, rest, conds,
        share_down,
    )
    share_down = share_down.reshape(4 * SHARD, OUT_SHARD)
    bias_totals = totals[1:3].reshape(-1)
    grad_query, grad_value, grad_out, grad_ups, grad_downs = [
        bias_totals[low:high] for low, high in zip(edges[:-1], edges[1:])
    ]
    return (
        block_out[None],
        grad_in[None],
        grad_ada,
        totals[0],
        share_qkv,
        grad_query,
        grad_value,
        share_out,
        grad_out,
        share_up,
        grad_ups,
        share_down,
        grad_downs,
    )


def layer_norm(values):
    center = values - jnp.mean(values, axis=-1, keepdims=True)
    variance = jnp.mean(center * center, axis=-1, keepdims=True)
    inverse = lax.rsqrt(variance + epsilon)
    return (center * inverse, inverse)


def norm_back(grad_normed, normed, inverse):
    first_mean = jnp.mean(grad_normed, axis=-1, keepdims=True)
    second_mean = jnp.mean(grad_normed * normed, axis=-1, keepdims=True)
    return inverse * (grad_normed - first_mean - normed * second_mean)


def attention_scores(query_part, key_part, allowed, factor):
    raw_scores = (
        jnp.einsum("qhd,khd->hqk", query_part, key_part, preferred_element_type=jnp.float32)
        * factor
    )
    return jnp.where(allowed[None], raw_scores, -1e30)


def gelu_tanh(values):
    return jax.nn.gelu(values, approximate=True)


def shards(
    block_in,
    condition,
    lengths,
    head_mask,
    group_mask,
    buffer_slot,
    ada_weight,
    ada_bias,
    qkv_weight,
    query_bias,
    value_bias,
    out_weight,
    out_bias,
    up_weight,
    up_bias,
    down_weight,
    down_bias,
    cotangent,
):
    peers = lax.axis_size("dp")
    mates = lax.axis_size("fsdp")

    def gather_matrix(shard):
        stacked = lax.all_gather(shard, ("dp", "fsdp"), axis=0, tiled=False)
        rows, columns = shard.shape
        stacked = stacked.reshape(peers, mates, rows, columns).transpose(0, 2, 1, 3)
        return stacked.reshape(peers * rows, mates * columns)

    full_qkv, full_out, full_up, full_down = [
        gather_matrix(shard) for shard in (qkv_weight, out_weight, up_weight, down_weight)
    ]
    vectors = (query_bias, value_bias, out_bias, up_bias, down_bias)
    packed_bias = lax.all_gather(jnp.concatenate(vectors), "fsdp", axis=0, tiled=False)
    edges = [0]
    for vector in vectors:
        edges.append(edges[-1] + vector.shape[0])
    bias_query, bias_value, bias_out, bias_up, bias_down = [
        packed_bias[:, low:high].reshape(-1).astype(jnp.float32)
        for low, high in zip(edges[:-1], edges[1:])
    ]
    inputs = block_in[0].astype(jnp.float32)
    crop_length = lengths[0]
    finish = jnp.cumsum(crop_length)
    opening = finish - crop_length
    position = jnp.arange(TOK_DEV, dtype=jnp.int32)
    member = (
        (position[:, None] >= opening[None, :]) & (position[:, None] < finish[None, :])
    ).astype(jnp.float32)
    segment = jnp.sum((position[:, None] >= finish[None, :]).astype(jnp.int32), axis=1)
    cond_act = jax.nn.silu(condition[0].astype(jnp.float32)).astype(jnp.bfloat16)
    crops = cond_act.shape[0]
    cond_all = lax.all_gather(cond_act, ("dp", "fsdp"), axis=0, tiled=True)
    depth = ada_weight.shape[0]
    cond_slice = lax.dynamic_slice_in_dim(cond_all, lax.axis_index("dp") * depth, depth, axis=1)
    partial_mod = jnp.dot(cond_slice, ada_weight, preferred_element_type=jnp.float32)
    column_mod = lax.psum_scatter(partial_mod, "dp", scatter_dimension=0, tiled=True)
    column_mod = column_mod + ada_bias.astype(jnp.float32)
    modulation = lax.all_to_all(column_mod, "fsdp", split_axis=0, concat_axis=1, tiled=True)
    pieces = [
        jnp.dot(member, modulation[:, number * D : (number + 1) * D], precision=highest)
        for number in range(6)
    ]
    shift_one, scale_one, gate_one, shift_two, scale_two, gate_two = pieces
    head_keep = jnp.dot(member, head_mask[0].astype(jnp.float32), precision=highest)
    group_keep = jnp.dot(member, group_mask[0].astype(jnp.float32), precision=highest)
    normed_one, inverse_one = layer_norm(inputs)
    first_in = (normed_one * (1.0 + scale_one) + shift_one).astype(jnp.bfloat16)
    qkv_bias = jnp.concatenate([bias_query, jnp.zeros_like(bias_query), bias_value])
    triple = (jnp.dot(first_in, full_qkv, preferred_element_type=jnp.float32) + qkv_bias).astype(
        jnp.bfloat16
    )
    queries = triple[:, :D].reshape(TOK_DEV, HEADS, HEAD_DIM)
    keys_all = triple[:, D : 2 * D].reshape(TOK_DEV, HEADS, HEAD_DIM)
    values_all = triple[:, 2 * D :].reshape(TOK_DEV, HEADS, HEAD_DIM)
    factor = HEAD_DIM ** (-0.5)
    row_block = min(768, TOK_DEV)
    group_size = min(4, HEADS)
    log_totals = {}
    head_parts = []
    for head_start in range(0, HEADS, group_size):
        heads_here = slice(head_start, head_start + group_size)
        row_start = 0
        rows_here = slice(row_start, row_start + row_block)
        allowed = segment[:, None] == segment[None, :]
        scores = attention_scores(
            queries[rows_here, heads_here], keys_all[:, heads_here], allowed, factor
        )
        row_max = jnp.max(scores, axis=-1, keepdims=True)
        log_total = row_max + jnp.log(jnp.sum(jnp.exp(scores - row_max), axis=-1, keepdims=True))
        weights_low = jnp.exp(scores - log_total).astype(jnp.bfloat16)
        row_parts = jnp.einsum(
            "hqk,khd->qhd",
            weights_low,
            values_all[:, heads_here],
            preferred_element_type=jnp.float32,
        )
        log_totals[head_start, row_start] = log_total
        head_parts.append(row_parts)
    attended = jnp.concatenate(head_parts, axis=1)
    mixed = (attended * head_keep[:, :, None]).astype(jnp.bfloat16).reshape(TOK_DEV, D)
    attn_out = jnp.dot(mixed, full_out, preferred_element_type=jnp.float32) + bias_out
    after_attn = inputs + gate_one * attn_out
    normed_two, inverse_two = layer_norm(after_attn)
    second_in = (normed_two * (1.0 + scale_two) + shift_two).astype(jnp.bfloat16)
    keep = (buffer_slot[0] >= 0).astype(jnp.float32)[:, None]
    places = 2 * TOK_DEV // 3
    chooser = (buffer_slot[0][:, None] == jnp.arange(places, dtype=jnp.int32)[None, :]).astype(
        jnp.bfloat16
    )
    arrived = jnp.einsum(
        "tb,td->bd", chooser, second_in, preferred_element_type=jnp.float32
    ).astype(jnp.bfloat16)
    groups_float = jnp.einsum(
        "tb,tg->bg",
        chooser,
        group_keep.astype(jnp.bfloat16),
        preferred_element_type=jnp.float32,
    )
    channel_keep = jnp.repeat(groups_float, FF // GROUPS, axis=1)
    hidden = jnp.dot(arrived, full_up, preferred_element_type=jnp.float32) + bias_up
    active = (gelu_tanh(hidden) * channel_keep).astype(jnp.bfloat16)
    branch = (jnp.dot(active, full_down, preferred_element_type=jnp.float32) + bias_down).astype(
        jnp.bfloat16
    )
    branch_tok = jnp.einsum(
        "tb,bd->td", chooser, branch, preferred_element_type=jnp.float32
    )
    after_mlp = after_attn + gate_two * branch_tok
    block_out = after_mlp.astype(jnp.bfloat16)[None]
    grad_after = cotangent[0].astype(jnp.float32)
    grad_gate_two = grad_after * branch_tok
    grad_branch = (gate_two * keep * grad_after).astype(jnp.bfloat16)
    grad_rows = jnp.einsum(
        "tb,td->bd", chooser, grad_branch, preferred_element_type=jnp.float32
    ).astype(jnp.bfloat16)
    back_qkv, back_out, back_up, back_down = full_qkv, full_out, full_up, full_down
    grad_down_bias = jnp.sum(grad_rows.astype(jnp.float32), axis=0)
    grad_down = jnp.einsum("bf,bd->fd", active, grad_rows, preferred_element_type=jnp.float32)
    grad_active = jnp.einsum("bd,fd->bf", grad_rows, back_down, preferred_element_type=jnp.float32)
    gelu_pull = jax.vjp(gelu_tanh, hidden)[1]
    grad_hidden = gelu_pull(grad_active * channel_keep)[0].astype(jnp.bfloat16)
    grad_up_bias = jnp.sum(grad_hidden.astype(jnp.float32), axis=0)
    grad_up = jnp.einsum("bd,bf->df", arrived, grad_hidden, preferred_element_type=jnp.float32)
    grad_arrived = jnp.einsum(
        "bf,df->bd", grad_hidden, back_up, preferred_element_type=jnp.float32
    ).astype(jnp.bfloat16)
    grad_second = jnp.einsum(
        "tb,bd->td", chooser, grad_arrived, preferred_element_type=jnp.float32
    )
    grad_scale_two = grad_second * normed_two
    grad_mid = grad_after + norm_back(grad_second * (1.0 + scale_two), normed_two, inverse_two)
    grad_gate_one = grad_mid * attn_out
    grad_attn = (gate_one * grad_mid).astype(jnp.bfloat16)
    grad_out_bias = jnp.sum(grad_attn.astype(jnp.float32), axis=0)
    grad_out = jnp.einsum("te,tf->ef", mixed, grad_attn, preferred_element_type=jnp.float32)
    grad_mixed = jnp.einsum(
        "tf,ef->te", grad_attn, back_out, preferred_element_type=jnp.float32
    ).astype(jnp.bfloat16)
    grad_attended = (
        grad_mixed.reshape(TOK_DEV, HEADS, HEAD_DIM).astype(jnp.float32) * head_keep[:, :, None]
    ).astype(jnp.bfloat16)
    query_heads = []
    key_heads = []
    value_heads = []
    for head_start in range(0, HEADS, group_size):
        heads_here = slice(head_start, head_start + group_size)
        row_start = 0
        rows_here = slice(row_start, row_start + row_block)
        allowed = segment[:, None] == segment[None, :]
        scores = attention_scores(
            queries[rows_here, heads_here], keys_all[:, heads_here], allowed, factor
        )
        probs = jnp.exp(scores - log_totals[head_start, row_start])
        grad_piece = grad_attended[rows_here, heads_here]
        grad_values = jnp.einsum(
            "hqk,qhd->khd",
            probs.astype(jnp.bfloat16),
            grad_piece,
            preferred_element_type=jnp.float32,
        )
        grad_probs = jnp.einsum(
            "qhd,khd->hqk",
            grad_piece,
            values_all[:, heads_here],
            preferred_element_type=jnp.float32,
        )
        grad_scores = (
            probs * (grad_probs - jnp.sum(probs * grad_probs, axis=-1, keepdims=True))
        ).astype(jnp.bfloat16)
        query_rows = (
            jnp.einsum(
                "hqk,khd->qhd",
                grad_scores,
                keys_all[:, heads_here],
                preferred_element_type=jnp.float32,
            )
            * factor
        )
        grad_keys = (
            jnp.einsum(
                "hqk,qhd->khd",
                grad_scores,
                queries[rows_here, heads_here],
                preferred_element_type=jnp.float32,
            )
            * factor
        )
        query_heads.append(query_rows)
        key_heads.append(grad_keys)
        value_heads.append(grad_values)
    grad_triple = jnp.concatenate(
        [
            jnp.concatenate(query_heads, axis=1).reshape(TOK_DEV, D),
            jnp.concatenate(key_heads, axis=1).reshape(TOK_DEV, D),
            jnp.concatenate(value_heads, axis=1).reshape(TOK_DEV, D),
        ],
        axis=1,
    ).astype(jnp.bfloat16)
    grad_query_bias = jnp.sum(grad_triple[:, :D].astype(jnp.float32), axis=0)
    grad_value_bias = jnp.sum(grad_triple[:, 2 * D :].astype(jnp.float32), axis=0)
    grad_qkv = jnp.einsum("td,te->de", first_in, grad_triple, preferred_element_type=jnp.float32)
    grad_first = jnp.einsum("te,de->td", grad_triple, back_qkv, preferred_element_type=jnp.float32)
    grad_scale_one = grad_first * normed_one
    grad_inputs = grad_mid + norm_back(grad_first * (1.0 + scale_one), normed_one, inverse_one)
    token_grads = [
        grad_first,
        grad_scale_one,
        grad_gate_one,
        grad_second,
        grad_scale_two,
        grad_gate_two,
    ]
    grad_modulation = jnp.concatenate(
        [jnp.einsum("ts,td->sd", member, single, precision=highest) for single in token_grads],
        axis=1,
    )
    mod_columns = lax.all_to_all(
        grad_modulation, "fsdp", split_axis=1, concat_axis=0, tiled=True
    )
    mod_all = lax.all_gather(mod_columns, "dp", axis=0, tiled=True)
    grad_ada_bias = jnp.sum(mod_all, axis=0)
    grad_ada = jnp.einsum(
        "sd,se->de", cond_slice.astype(jnp.float32), mod_all, precision=highest
    )

    def scatter_matrix(full):
        rows, columns = full.shape[0] // peers, full.shape[1] // mates
        blocks = full.astype(jnp.bfloat16).reshape(peers, rows, mates, columns)
        blocks = blocks.transpose(0, 2, 1, 3).reshape(peers * mates * rows, columns)
        share = lax.psum_scatter(blocks, ("dp", "fsdp"), scatter_dimension=0, tiled=True)
        return share.astype(jnp.float32)

    shares = [scatter_matrix(full) for full in (grad_qkv, grad_out, grad_up, grad_down)]
    bias_grads = (grad_query_bias, grad_value_bias, grad_out_bias, grad_up_bias, grad_down_bias)
    packed = jnp.concatenate([vector.reshape(mates, -1) for vector in bias_grads], axis=1)
    packed = lax.psum_scatter(packed, "fsdp", scatter_dimension=0, tiled=True)
    packed = lax.psum(packed[0], "dp")
    totals = [packed[low:high] for low, high in zip(edges[:-1], edges[1:])]
    return (
        block_out,
        grad_inputs[None],
        grad_ada,
        grad_ada_bias,
        shares[0],
        totals[0],
        totals[1],
        shares[1],
        totals[2],
        shares[2],
        totals[3],
        shares[3],
        totals[4],
    )


def solution(mesh):
    placed = (
        P(("dp", "fsdp"), None, None),
        P(("dp", "fsdp"), None, None),
        P(("dp", "fsdp"), None),
        P(("dp", "fsdp"), None, None),
        P(("dp", "fsdp"), None, None),
        P(("dp", "fsdp"), None),
        P("dp", "fsdp"),
        P("fsdp"),
        P("dp", "fsdp"),
        P("fsdp"),
        P("fsdp"),
        P("dp", "fsdp"),
        P("fsdp"),
        P("dp", "fsdp"),
        P("fsdp"),
        P("dp", "fsdp"),
        P("fsdp"),
        P(("dp", "fsdp"), None, None),
    )
    on_block = dict(mesh.shape) == {"dp": 8, "fsdp": 4}
    return jax.shard_map(
        block_shards if on_block else shards,
        mesh=mesh,
        in_specs=placed,
        out_specs=(
            P(("dp", "fsdp"), None, None),
            P(("dp", "fsdp"), None, None),
            P("dp", "fsdp"),
            P("fsdp"),
            P("dp", "fsdp"),
            P("fsdp"),
            P("fsdp"),
            P("dp", "fsdp"),
            P("fsdp"),
            P("dp", "fsdp"),
            P("fsdp"),
            P("dp", "fsdp"),
            P("fsdp"),
        ),
        check_vma=False,
    )
```

```python
import math

import jax
import jax.numpy as jnp
from jax import lax
from jax.experimental import pallas as pl
from jax.experimental.pallas import tpu as pltpu
from jax.sharding import PartitionSpec as P

D = 1152
HEADS = 16
HEAD_DIM = 72
FF = 4608
GROUPS = 16
TOK_DEV = 768


highest = lax.Precision.HIGHEST
epsilon = 1e-06


NT = (((1,), (1,)), ((), ()))
TN = (((0,), (0,)), ((), ()))
NN = (((1,), (0,)), ((), ()))
PLACES = 512
BLOCK = 256
BF16, F32 = jnp.bfloat16, jnp.float32
SOFT = HEAD_DIM**-0.5 * math.log2(math.e)
QKV_SHARD, OUT_SHARD, PAD_SHARD = 864, 288, 896
VMEM_BYTES = 60 * 2**20


def dot(left, right, dims=NN):
    return lax.dot_general(left, right, dims, preferred_element_type=F32)


def rows_at(i):
    return pl.ds(pl.multiple_of(i * BLOCK, BLOCK), BLOCK)


def per_crop(table, segment):
    return jnp.where(
        segment == 0, table[0:1], jnp.where(segment == 1, table[1:2], table[2:3])
    )


def normalise(values):
    center = values - jnp.mean(values, axis=1, keepdims=True)
    variance = jnp.mean(center * center, axis=1, keepdims=True)
    inverse = lax.rsqrt(variance + epsilon)
    return center * inverse, inverse


def crop_sums(segment, values):
    lanes = lax.broadcasted_iota(jnp.int32, (values.shape[0], 128), 1)
    member = (lanes == segment).astype(BF16)
    high = values.astype(BF16)
    low = (values - high.astype(F32)).astype(BF16)
    return (dot(member, high, TN) + dot(member, low, TN))[:8]


def crop_mask(bias_ref, column_ref, row_ref):
    for i in range(TOK_DEV // BLOCK):
        here = pl.ds(i * BLOCK, BLOCK)
        bias_ref[here, :] = jnp.where(column_ref[here, :] == row_ref[...], 0.0, -1e30).astype(F32)


def places_of(slot_row, i):
    place = lax.broadcasted_iota(jnp.int32, (BLOCK, TOK_DEV), 0) + i * BLOCK
    return (place == slot_row).astype(BF16)


def tokens_of(slot_column):
    place = lax.broadcasted_iota(jnp.int32, (BLOCK, PLACES), 1)
    return (place == slot_column).astype(BF16)


def head_keep(mask_ref, h, segment):
    keep = jnp.where(
        segment == 0, mask_ref[0, h], jnp.where(segment == 1, mask_ref[1, h], mask_ref[2, h])
    )
    return keep.astype(F32)


MESH = pl.DeviceIdType.MESH
SHARD = 144
UPPER = 80


class Place:
    def __init__(self):
        dp, fsdp = lax.axis_index("dp"), lax.axis_index("fsdp")
        self.z, self.x = lax.div(dp, 2), lax.rem(dp, 2)
        self.y, self.c = lax.div(fsdp, 2), lax.rem(fsdp, 2)
        z = self.z
        self.zs = (z, z + 1 - 2 * lax.rem(z, 2), lax.rem(z + 2, 4), 3 - z)
        self.mates = (
            self.device(c=1 - self.c),
            self.device(y=1 - self.y),
            self.device(y=1 - self.y, c=1 - self.c),
        )
        self.mate_index = (
            2 * self.y + 1 - self.c,
            2 * (1 - self.y) + self.c,
            2 * (1 - self.y) + 1 - self.c,
        )
        self.index = 2 * self.y + self.c
        self.peer = 2 * z + self.x

    def device(self, z=None, x=None, y=None, c=None):
        z, x = self.z if z is None else z, self.x if x is None else x
        y, c = self.y if y is None else y, self.c if c is None else c
        return (2 * z + x, 2 * y + c)

    def meet(self):
        barrier = pltpu.get_barrier_semaphore()
        others = [self.device(z=self.zs[k]) for k in (1, 2, 3)]
        others += [self.device(z=self.zs[k], x=1 - self.x) for k in range(4)]
        others += self.mates
        for other in others:
            pl.semaphore_signal(barrier, inc=1, device_id=other, device_id_type=MESH)
        pl.semaphore_wait(barrier, len(others))


class Copies:
    def __init__(self, send_sems, recv_sems):
        self.send_sems, self.recv_sems, self.made = send_sems, recv_sems, []

    def make(self, source, target, device):
        index = len(self.made)
        copy = pltpu.make_async_remote_copy(
            src_ref=source,
            dst_ref=target,
            send_sem=self.send_sems.at[index],
            recv_sem=self.recv_sems.at[index],
            device_id=device,
            device_id_type=MESH,
        )
        self.made.append(copy)
        return copy


GATHER_COPIES = 35


class Gather:
    def __init__(self, place, source, slot, send_sems, recv_sems, local_sem, swap):
        x, y, c, zs = place.x, place.y, place.c, place.zs
        self.copies = Copies(send_sems, recv_sems)
        make = self.copies.make
        first, second = (SHARD - UPPER, UPPER) if swap else (0, UPPER)
        upper = pl.ds(first, second)
        lower = pl.ds(0, SHARD - UPPER) if swap else pl.ds(UPPER, SHARD - UPPER)
        over_x, over_y, beside = (
            place.device(x=1 - x),
            place.device(y=1 - y),
            place.device(c=1 - c),
        )
        own = [slot(y, c, zs[k], x) for k in range(4)]
        held = [source] + own[1:]
        from_x = [slot(y, c, zs[k], 1 - x) for k in range(4)]
        from_y = [slot(1 - y, c, zs[k], x) for k in range(4)]
        across = [slot(1 - y, c, zs[k], 1 - x) for k in range(4)]
        self.local = pltpu.make_async_copy(source, own[0], local_sem)
        self.along = [None] + [make(source, own[0], place.device(z=zs[k])) for k in (1, 2, 3)]
        self.to_x = [make(held[k], own[k], over_x) for k in range(4)]
        self.to_y = [make(held[k], own[k], over_y) for k in range(4)]
        self.x_to_y = [make(s.at[upper], s.at[upper], over_y) for s in from_x]
        self.y_to_x = [make(s.at[lower], s.at[lower], over_x) for s in from_y]
        self.pair = [make(held[k], own[k], beside) for k in range(4)]
        self.pair_x = [make(s, s, beside) for s in from_x]
        self.pair_y = [make(s, s, beside) for s in from_y]
        self.pair_across = [make(s, s, beside) for s in across]

    def start(self):
        self.along[1].start()
        self.to_x[0].start()
        self.to_y[0].start()
        self.along[2].start()
        self.along[3].start()
        self.pair[0].start()
        self.local.start()

    def pass_along(self, k):
        self.along[k].wait_recv()
        self.to_x[k].start()
        self.to_y[k].start()
        self.pair[k].start()

    def pass_across(self, k):
        self.to_x[k].wait_recv()
        self.x_to_y[k].start()
        self.pair_x[k].start()
        self.to_y[k].wait_recv()
        self.y_to_x[k].start()
        self.pair_y[k].start()

    def pass_pair(self, k):
        self.x_to_y[k].wait_recv()
        self.y_to_x[k].wait_recv()
        self.pair_across[k].start()

    def finish(self):
        self.local.wait()
        for copy in self.pair + self.pair_x + self.pair_y + self.pair_across:
            copy.wait_recv()
        for copy in self.copies.made:
            copy.wait_send()


class Column:
    def __init__(self, place, source, column, send_sems, recv_sems, local_sem):
        copies = Copies(send_sems, recv_sems)
        self.local = pltpu.make_async_copy(source, column.at[place.z], local_sem)
        self.along = [
            copies.make(source, column.at[place.z], place.device(z=place.zs[k])) for k in (1, 2, 3)
        ]

    def start(self):
        for copy in self.along:
            copy.start()
        self.local.start()

    def finish(self):
        for copy in self.along:
            copy.wait()
        self.local.wait()


SPREAD_COPIES = 32


class Spread:
    def __init__(self, place, column, slot, send_sems, recv_sems, local_sems):
        x, y, c, zs = place.x, place.y, place.c, place.zs
        self.copies = Copies(send_sems, recv_sems)
        make = self.copies.make
        upper, lower = pl.ds(0, UPPER), pl.ds(UPPER, SHARD - UPPER)
        over_x, over_y, beside = place.device(x=1 - x), place.device(y=1 - y), place.mates[0]
        four = range(4)
        held = [column.at[zs[k]] for k in four]
        own = [slot(y, c, zs[k], x) for k in four]
        from_x = [slot(y, c, zs[k], 1 - x) for k in four]
        from_y = [slot(1 - y, c, zs[k], x) for k in four]
        across = [slot(1 - y, c, zs[k], 1 - x) for k in four]
        first = [upper, lower, upper, lower]
        second = [lower, upper, lower, upper]
        self.local = [pltpu.make_async_copy(held[k], own[k], local_sems.at[k]) for k in four]
        self.to_x = [make(held[k], own[k], over_x) for k in four]
        self.to_y = [make(held[k], own[k], over_y) for k in four]
        self.x_to_y = [make(from_x[k].at[first[k]], from_x[k].at[first[k]], over_y) for k in four]
        self.y_to_x = [make(from_y[k].at[second[k]], from_y[k].at[second[k]], over_x) for k in four]
        self.pair = [make(held[k], own[k], beside) for k in four]
        self.pair_x = [make(s, s, beside) for s in from_x]
        self.pair_y = [make(s, s, beside) for s in from_y]
        self.pair_across = [make(s, s, beside) for s in across]

    def start(self):
        for k in range(4):
            self.to_x[k].start()
            self.to_y[k].start()
        for k in range(4):
            self.pair[k].start()
            self.local[k].start()

    def pass_across(self, k):
        self.to_x[k].wait_recv()
        self.x_to_y[k].start()
        self.pair_x[k].start()
        self.to_y[k].wait_recv()
        self.y_to_x[k].start()
        self.pair_y[k].start()

    def pass_pair(self, k):
        self.x_to_y[k].wait_recv()
        self.y_to_x[k].wait_recv()
        self.pair_across[k].start()

    def finish(self):
        for copy in self.local:
            copy.wait()
        for copy in self.pair + self.pair_x + self.pair_y + self.pair_across:
            copy.wait_recv()
        for copy in self.copies.made:
            copy.wait_send()


SCATTER_COPIES = 24


class Corner:
    def __init__(self, place, parts, across, copies):
        x, y, zs = place.x, place.y, place.zs
        a, b = pl.ds(0, UPPER), pl.ds(UPPER, SHARD - UPPER)
        over_x, over_y = place.device(x=1 - x), place.device(y=1 - y)
        self.over_y, self.over_x = [], []
        for k in range(4):
            block = parts.at[1 - y, zs[k], 1 - x]
            self.over_y.append(copies.make(block.at[a], across.at[k, a], over_y))
            self.over_x.append(copies.make(block.at[b], across.at[k, b], over_x))

    def start(self, k):
        self.over_y[k].start()
        self.over_x[k].start()


class Scatter:
    def __init__(self, place, parts, bufs, column, send_sems, recv_sems, early=None):
        x, y, zs = place.x, place.y, place.zs
        self.place, self.parts, self.column = place, parts, column
        self.across, self.from_x, self.from_y = [bufs.at[k] for k in range(3)]
        self.early = early
        self.copies = Copies(send_sems, recv_sems)
        make = self.copies.make
        self.upper, self.lower = (0, UPPER), (UPPER, SHARD - UPPER)
        a, b = pl.ds(*self.upper), pl.ds(*self.lower)
        over_x, over_y = place.device(x=1 - x), place.device(y=1 - y)
        four = range(4)
        if early is None:
            self.corner = Corner(place, parts, self.across, self.copies)
        self.x_lower = [make(parts.at[y, zs[k], 1 - x, b], self.from_x.at[k, b], over_x) for k in four]
        self.y_upper = [make(parts.at[1 - y, zs[k], x, a], self.from_y.at[k, a], over_y) for k in four]
        self.x_upper = [make(self.across.at[k, a], self.from_x.at[k, a], over_x) for k in four]
        self.y_lower = [make(self.across.at[k, b], self.from_y.at[k, b], over_y) for k in four]

    def start(self, k):
        self.corner.start(k)

    def follow(self, k):
        self.x_lower[k].start()
        self.y_upper[k].start()

    def add(self, k, index, rows):
        given = self.across if self.early is None else self.early
        for at in range(0, rows[1], 16):
            here = pl.ds(rows[0] + at, 16)
            total = self.parts[(*index, here)].astype(F32) + given[k, here].astype(F32)
            self.across[k, here] = total.astype(BF16)

    def pass_across(self, k):
        x, y, z = self.place.x, self.place.y, self.place.zs[k]
        if self.early is None:
            self.corner.over_y[k].wait_recv()
        self.add(k, (y, z, 1 - x), self.upper)
        self.x_upper[k].start()
        if self.early is None:
            self.corner.over_x[k].wait_recv()
        self.add(k, (1 - y, z, x), self.lower)
        self.y_lower[k].start()

    def collect(self, k):
        x, y, z = self.place.x, self.place.y, self.place.zs[k]
        for copy in (self.x_upper[k], self.x_lower[k], self.y_upper[k], self.y_lower[k]):
            copy.wait_recv()
        for at in range(0, SHARD, 16):
            here = pl.ds(at, 16)
            total = self.parts[y, z, x, here].astype(F32) + self.from_x[k, here].astype(F32)
            self.column[k, here] = (total + self.from_y[k, here].astype(F32)).astype(BF16)

    def finish(self):
        for copy in self.copies.made:
            copy.wait_send()


class Along:
    def __init__(self, place, column, from_z, out, send_sems, recv_sems):
        copies = Copies(send_sems, recv_sems)
        self.column, self.from_z, self.out = column, from_z, out
        self.copies = [
            copies.make(column.at[k], from_z.at[k - 1], place.device(z=place.zs[k])) for k in (1, 2, 3)
        ]

    def start(self, k):
        self.copies[k - 1].start()

    def close(self):
        for copy in self.copies:
            copy.wait()
        for at in range(0, SHARD, 16):
            here = pl.ds(at, 16)
            total = self.column[0, here].astype(F32)
            for k in range(3):
                total = total + self.from_z[k, here].astype(F32)
            self.out[here] = total


ORDER = (1, 2, 3, 0)
DMA = pltpu.SemaphoreType.DMA


def add_rows(target, rows, left, right):
    def body(i, carry):
        here = pl.ds(pl.multiple_of(16 * i, 16), 16)
        target(here, (left(here).astype(F32) + right(here).astype(F32)).astype(BF16))
        return carry

    lax.fori_loop(0, rows // 16, body, 0)


class Pair:
    def __init__(self, place, buffers, parts, send_sems, recv_sems):
        self.place, self.buffers, self.parts = place, buffers, parts
        self.send_sems, self.recv_sems = send_sems, recv_sems

    def copy(self, m):
        y = lax.div(m, 2)
        return pltpu.make_async_remote_copy(
            src_ref=self.buffers.at[lax.rem(m, 2)],
            dst_ref=self.parts.at[y],
            send_sem=self.send_sems.at[y],
            recv_sem=self.recv_sems.at[y],
            device_id=self.place.mates[0],
            device_id_type=MESH,
        )

    def send(self, m):
        @pl.when(lax.rem(m, 2) != self.place.c)
        def _():
            self.copy(m).start()

    def free(self, m):
        @pl.when(lax.rem(m, 2) != self.place.c)
        def _():
            self.copy(m).wait_send()

    def take(self, m):
        @pl.when(lax.rem(m, 2) == self.place.c)
        def _():
            y, buffer = lax.div(m, 2), lax.rem(m, 2)
            self.copy(m).wait_recv()

            def store(here, value):
                self.parts[y, here] = value

            add_rows(
                store, D, lambda here: self.buffers[buffer, here], lambda here: self.parts[y, here]
            )


def attend_kernel(
    x_ref, weight_in, mods_ref, qkv_bias_ref, out_bias_ref, column_ref, row_ref, slot_ref,
    groups_ref, mask_ref, up_ref, down_ref,
    first_out, heads_out, mixed_out, lse_ref, attn_ref, after_ref, arrived_ref, picked_ref, weight_out,
    up_out, down_out,
    weight_ref, first_ref, heads_ref, mixed_ref, out_weight_ref, load_sems, save_sems,
    bias_ref, parts_ref, second_ref,
    send_sems, recv_sems, local_sems, down_send, down_recv, down_local,
):
    place = Place()
    place.meet()
    ups = Spread(
        place, up_ref, lambda y, c, z, x: up_out.at[y, c, z, x], send_sems, recv_sems, local_sems
    )
    downs = Column(place, down_ref, down_out, down_send, down_recv, down_local.at[0])
    loads = [
        pltpu.make_async_copy(weight_in.at[j], weight_ref.at[j], load_sems.at[j]) for j in range(4)
    ]
    saves = [
        pltpu.make_async_copy(source, target, save_sems.at[n])
        for n, (source, target) in enumerate(
            (
                (first_ref, first_out),
                (heads_ref, heads_out),
                (out_weight_ref, weight_out),
                (mixed_ref, mixed_out),
            )
        )
    ]
    ups.start()
    for copy in loads:
        copy.start()
    downs.start()
    crop_mask(bias_ref, column_ref, row_ref)

    def norm(i, carry):
        here = rows_at(i)
        segment = column_ref[here, :]
        normed, _ = normalise(x_ref[here, :].astype(F32))
        shift, scale = per_crop(mods_ref[0], segment), per_crop(mods_ref[1], segment)
        first_ref[here, :] = (normed * (1.0 + scale) + shift).astype(BF16)
        return carry

    lax.fori_loop(0, 3, norm, 0)
    saves[0].start()
    for copy in loads:
        copy.wait()
    for j in range(4):
        out_weight_ref[:, OUT_SHARD * j : OUT_SHARD * (j + 1)] = weight_ref[j, :, QKV_SHARD:]
    saves[2].start()

    def project(i, carry):
        j = lax.div(i, 3)
        here = rows_at(lax.rem(i, 3))
        triple = (dot(first_ref[here, :], weight_ref[j, :, :PAD_SHARD]) + qkv_bias_ref[j]).astype(BF16)
        zero = jnp.zeros((BLOCK, 128 - HEAD_DIM), BF16)
        for h in range(12):
            part = triple[:, HEAD_DIM * h : HEAD_DIM * (h + 1)]
            heads_ref[12 * j + h, here, :] = jnp.concatenate([part, zero], axis=1)
        return carry

    lax.fori_loop(0, 12, project, 0)
    saves[1].start()

    def head(h, carry):
        for k in range(4):

            @pl.when(h == 7 + k)
            def _():
                ups.pass_across(k)

        keys, values = heads_ref[16 + h], heads_ref[32 + h]
        for i in range(3):
            here = pl.ds(i * BLOCK, BLOCK)
            scores = dot(heads_ref[h, here, :], keys, NT) * SOFT + bias_ref[here, :]
            top = jnp.max(scores, axis=1, keepdims=True)
            weights = jnp.exp2(scores - top)
            total = jnp.sum(weights, axis=1, keepdims=True)
            keep = head_keep(mask_ref, h, column_ref[here, :])
            parts_ref[h, here, :] = (dot(weights.astype(BF16), values) * (keep / total)).astype(BF16)
            spread = jnp.broadcast_to(top + jnp.log2(total), (BLOCK, 128))
            lse_ref[h, :, here] = jnp.transpose(spread)[:1, :]
        return carry

    lax.fori_loop(0, HEADS, head, 0)
    for h in range(HEADS):
        mixed_ref[:, HEAD_DIM * h : HEAD_DIM * (h + 1)] = parts_ref[h][:, :HEAD_DIM]
    saves[3].start()
    for k in range(4):
        ups.pass_pair(k)

    def close(i, carry):
        here = rows_at(i)
        segment = column_ref[here, :]
        attn = dot(mixed_ref[here, :], out_weight_ref[...]) + out_bias_ref[...]
        attn_ref[here, :] = attn.astype(BF16)
        after = x_ref[here, :].astype(F32) + per_crop(mods_ref[2], segment) * attn
        after_ref[here, :] = after
        normed, _ = normalise(after)
        shift, scale = per_crop(mods_ref[3], segment), per_crop(mods_ref[4], segment)
        second_ref[here, :] = (normed * (1.0 + scale) + shift).astype(BF16)
        return carry

    lax.fori_loop(0, 3, close, 0)
    for i in range(2):
        here = pl.ds(i * BLOCK, BLOCK)
        choice = places_of(slot_ref[...], i)
        arrived_ref[here, :] = dot(choice, second_ref[...]).astype(BF16)
        picked_ref[here, :] = dot(choice, groups_ref[...]).astype(BF16)
    ups.finish()
    downs.finish()
    for copy in saves:
        copy.wait()


def shape_of(*shape, dtype=BF16):
    return jax.ShapeDtypeStruct(shape, dtype)


def talking(number):
    return pltpu.CompilerParams(
        collective_id=number, has_side_effects=True, vmem_limit_bytes=VMEM_BYTES
    )


IN_VMEM = pl.BlockSpec(memory_space=pltpu.VMEM)
IN_SMEM = pl.BlockSpec(memory_space=pltpu.SMEM)
ANYWHERE = pl.BlockSpec(memory_space=pl.ANY)


def attend(x, weight, mods, qkv_bias, out_bias, column, row, slot_row, groups, mask, up, down):
    return pl.pallas_call(
        attend_kernel,
        out_shape=[
            shape_of(TOK_DEV, D),
            shape_of(3 * HEADS, TOK_DEV, 128),
            shape_of(TOK_DEV, D),
            shape_of(HEADS, 1, TOK_DEV, dtype=F32),
            shape_of(TOK_DEV, D),
            shape_of(TOK_DEV, D, dtype=F32),
            shape_of(PLACES, D),
            shape_of(PLACES, 128),
            shape_of(D, D),
            shape_of(2, 2, 4, 2, SHARD, D),
            shape_of(4, SHARD, D),
        ],
        in_specs=[IN_VMEM, ANYWHERE] + [IN_VMEM] * 7 + [IN_SMEM] + [ANYWHERE] * 2,
        out_specs=[ANYWHERE] * 3 + [IN_VMEM] * 5 + [ANYWHERE] * 3,
        scratch_shapes=[
            pltpu.VMEM((4, D, D), BF16),
            pltpu.VMEM((TOK_DEV, D), BF16),
            pltpu.VMEM((3 * HEADS, TOK_DEV, 128), BF16),
            pltpu.VMEM((TOK_DEV, D), BF16),
            pltpu.VMEM((D, D), BF16),
            DMA((4,)),
            DMA((4,)),
            pltpu.VMEM((TOK_DEV, TOK_DEV), F32),
            pltpu.VMEM((HEADS, TOK_DEV, 128), BF16),
            pltpu.VMEM((TOK_DEV, D), BF16),
            DMA((SPREAD_COPIES,)),
            DMA((SPREAD_COPIES,)),
            DMA((4,)),
            DMA((3,)),
            DMA((3,)),
            DMA((1,)),
        ],
        compiler_params=talking(2),
    )(x, weight, mods, qkv_bias, out_bias, column, row, slot_row, groups, mask, up, down)


ROOT = math.sqrt(2.0 / math.pi)


def feed_kernel(
    up_ref, arrived_ref, picked_ref, up_bias_ref, down_bias_ref, cot_ref, after_ref,
    mods_ref, column_ref, slot_column_ref, slot_row_ref, down_ref,
    pull_ref, grad_rows_ref, block_out_ref, gate_ref, bias_ref, parts_ref, down_out, across_out,
    active_ref, total_ref, branch_ref, buffers_ref, halves_ref, tiles_ref, across_ref,
    send_sems, recv_sems, local_sems, pair_send, pair_recv, tile_sems, corner_send, corner_recv,
):
    step = pl.program_id(0)
    place = Place()
    downs = Spread(
        place, down_ref, lambda y, c, z, x: down_out.at[z, x, y, c], send_sems, recv_sems, local_sems
    )

    corners = Copies(corner_send, corner_recv)
    corner = Corner(place, parts_ref, across_ref, corners)

    def rows_of(x, y, c):
        return pl.ds(pl.multiple_of((4 * x + 2 * y + c) * SHARD, 16), SHARD)

    def pair(m, x, y):
        return pltpu.make_async_remote_copy(
            src_ref=buffers_ref.at[lax.rem(m, 2), rows_of(x, y, 1 - place.c)],
            dst_ref=halves_ref.at[y, m, x],
            send_sem=pair_send.at[m, x, y],
            recv_sem=pair_recv.at[m, x, y],
            device_id=place.mates[0],
            device_id_type=MESH,
        )

    def take(m):
        for x in range(2):
            for y in range(2):
                pair(m, x, y).wait_recv()
                own = rows_of(x, y, place.c)
                mine = buffers_ref.at[lax.rem(m, 2), own]
                for at in range(0, SHARD, 16):
                    here = pl.ds(at, 16)
                    total = mine[here].astype(F32) + halves_ref[y, m, x, here].astype(F32)
                    parts_ref[y, m, x, here] = total.astype(BF16)

    def free(m):
        for x in range(2):
            for y in range(2):
                pair(m, x, y).wait_send()

    def tile(m):
        return [
            pltpu.make_async_copy(
                down_out.at[m, x, y],
                tiles_ref.at[lax.rem(m, 2), x, y],
                tile_sems.at[lax.rem(m, 2), x, y],
            )
            for x in range(2)
            for y in range(2)
        ]

    @pl.when(step == 0)
    def _():
        place.meet()
        downs.start()
        for i in range(3):
            here = pl.ds(i * BLOCK, BLOCK)
            gate = per_crop(mods_ref[5], column_ref[here, :])
            block_out_ref[here, :] = (gate * cot_ref[here, :].astype(F32)).astype(BF16)
        for i in range(2):
            here = pl.ds(i * BLOCK, BLOCK)
            choice = places_of(slot_row_ref[...], i)
            grad_rows_ref[here, :] = dot(choice, block_out_ref[...]).astype(BF16)
        bias_ref[...] = jnp.sum(grad_rows_ref[...].astype(F32), axis=0, keepdims=True)
        total_ref[...] = jnp.zeros_like(total_ref)

    @pl.when(step < 4)
    def _():
        group = lax.broadcasted_iota(jnp.int32, (128, D), 0) - 4 * step
        unit = lax.broadcasted_iota(jnp.int32, (128, D), 1)
        width = FF // GROUPS
        spread = ((unit >= group * width) & (unit < (group + 1) * width)).astype(BF16)
        for i in range(2):
            here = pl.ds(i * BLOCK, BLOCK)
            hidden = dot(arrived_ref[here, :], up_ref[0]) + up_bias_ref[0]
            keep = dot(picked_ref[here, :], spread)
            square = hidden * hidden
            curve = jnp.tanh(ROOT * hidden * (1.0 + 0.044715 * square))
            half = 0.5 * (1.0 + curve)
            slope = half + 0.5 * hidden * (1.0 - curve * curve) * (
                ROOT * (1.0 + 3.0 * 0.044715 * square)
            )
            active_ref[step, here, :] = (hidden * half * keep).astype(BF16)
            pull_ref[0, here, :] = (slope * keep).astype(BF16)

        def grad(i, carry):
            here = pl.ds(pl.multiple_of(i * 384, 384), 384)
            part = dot(active_ref[step, :, here], grad_rows_ref[...], TN).astype(BF16)
            buffers_ref[lax.rem(step, 2), here, :] = part
            return carry

        @pl.when(step >= 2)
        def _():
            free(step - 2)

        lax.fori_loop(0, 3, grad, 0)
        for x in range(2):
            for y in range(2):
                pair(step, x, y).start()

    @pl.when((step >= 1) & (step < 5))
    def _():
        take(step - 1)

    @pl.when(step == 3)
    def _():
        for k in range(4):
            downs.pass_across(k)

    @pl.when(step == 4)
    def _():
        free(2)
        free(3)
        for k in range(4):
            corner.start(k)
        for k in range(4):
            downs.pass_pair(k)
        downs.finish()
        for m in (0, 1):
            for copy in tile(m):
                copy.start()

    @pl.when(step >= 4)
    def _():
        m = step - 4
        for copy in tile(m):
            copy.wait()
        weights = tiles_ref[lax.rem(m, 2)].reshape(D, D)
        for i in range(2):
            here = pl.ds(i * BLOCK, BLOCK)
            total_ref[here, :] += dot(active_ref[m, here, :], weights)

        @pl.when(m < 2)
        def _():
            for copy in tile(m + 2):
                copy.start()

    @pl.when(step == 7)
    def _():
        branch_ref[...] = (total_ref[...] + down_bias_ref[...]).astype(BF16)
        gates = jnp.zeros((8, D), F32)
        for i in range(3):
            here = pl.ds(i * BLOCK, BLOCK)
            segment = column_ref[here, :]
            branch = dot(tokens_of(slot_column_ref[here, :]), branch_ref[...])
            gate = per_crop(mods_ref[5], segment)
            block_out_ref[here, :] = (after_ref[here, :] + gate * branch).astype(BF16)
            gates = gates + crop_sums(segment, cot_ref[here, :].astype(F32) * branch)
        gate_ref[...] = gates
        for copy in corners.made:
            copy.wait()
        leave = pltpu.make_async_copy(across_ref, across_out, local_sems.at[0])
        leave.start()
        leave.wait()


def whole(*shape):
    return pl.BlockSpec(shape, lambda i: (0,) * len(shape), pipeline_mode=pl.Buffered(1))


def feed(up, arrived, picked, up_bias, down_bias, cot, after, mods, column, slot_column, slot_row, down):
    early = lambda *tail: pl.BlockSpec((1, *tail), lambda i: (jnp.minimum(i, 3), 0, 0))
    return pl.pallas_call(
        feed_kernel,
        grid=(8,),
        out_shape=[
            shape_of(4, PLACES, D),
            shape_of(PLACES, D),
            shape_of(TOK_DEV, D),
            shape_of(8, D, dtype=F32),
            shape_of(1, D, dtype=F32),
            shape_of(2, 4, 2, SHARD, D),
            shape_of(4, 2, 2, 2, SHARD, D),
            shape_of(4, SHARD, D),
        ],
        in_specs=[
            early(D, D), whole(PLACES, D), whole(PLACES, 128), early(1, D), whole(1, D),
            whole(TOK_DEV, D), whole(TOK_DEV, D), whole(6, 8, D), whole(TOK_DEV, 1), whole(TOK_DEV, 1),
            whole(1, TOK_DEV), ANYWHERE,
        ],
        out_specs=[
            early(PLACES, D), whole(PLACES, D), whole(TOK_DEV, D), whole(8, D), whole(1, D),
            whole(2, 4, 2, SHARD, D), ANYWHERE, ANYWHERE,
        ],
        scratch_shapes=[
            pltpu.VMEM((4, PLACES, D), BF16),
            pltpu.VMEM((PLACES, D), F32),
            pltpu.VMEM((PLACES, D), BF16),
            pltpu.VMEM((2, D, D), BF16),
            pltpu.VMEM((2, 4, 2, SHARD, D), BF16),
            pltpu.VMEM((2, 2, 2, 2, SHARD, D), BF16),
            pltpu.VMEM((4, SHARD, D), BF16),
            DMA((SPREAD_COPIES,)),
            DMA((SPREAD_COPIES,)),
            DMA((4,)),
            DMA((4, 2, 2)),
            DMA((4, 2, 2)),
            DMA((2, 2, 2)),
            DMA((8,)),
            DMA((8,)),
        ],
        compiler_params=talking(3),
    )(up, arrived, picked, up_bias, down_bias, cot, after, mods, column, slot_column, slot_row, down)


def unfeed_kernel(
    down_ref, up_ref, pull_ref, grad_rows_ref, arrived_ref, after_ref, cot_ref, attn_ref, mods_ref,
    column_ref, slot_column_ref, given_ref, early_ref,
    up_bias_ref, mid_ref, grad_attn_ref, sums_ref, out_bias_ref, parts_out, plane_ref,
    hidden_ref, total_ref, back_ref, buffers_ref, parts_ref, bufs_ref,
    send_sems, recv_sems, pair_send, pair_recv, out_sem,
):
    step = pl.program_id(0)
    place = Place()
    scatter = Scatter(place, given_ref, bufs_ref, plane_ref, send_sems, recv_sems, early_ref)
    pair = Pair(place, buffers_ref, parts_ref, pair_send, pair_recv)

    @pl.when(step == 0)
    def _():
        place.meet()
        for k in ORDER:
            scatter.follow(k)
            scatter.pass_across(k)
        total_ref[...] = jnp.zeros_like(total_ref)

    bias = jnp.zeros((1, D), F32)
    for i in range(2):
        here = pl.ds(i * BLOCK, BLOCK)
        grad = dot(grad_rows_ref[here, :], down_ref[0], NT) * pull_ref[0, here, :].astype(F32)
        low = grad.astype(BF16)
        hidden_ref[here, :] = low
        bias = bias + jnp.sum(low.astype(F32), axis=0, keepdims=True)
        total_ref[here, :] += dot(low, up_ref[0], NT)
    up_bias_ref[0] = bias

    def grad_of(i, carry):
        here = pl.ds(pl.multiple_of(i * 384, 384), 384)
        part = dot(arrived_ref[:, here], hidden_ref[...], TN).astype(BF16)
        buffers_ref[lax.rem(step, 2), here, :] = part
        return carry

    @pl.when(step >= 2)
    def _():
        pair.free(step - 2)

    lax.fori_loop(0, 3, grad_of, 0)
    pair.send(step)

    @pl.when(step >= 1)
    def _():
        pair.take(step - 1)

    @pl.when(step == 3)
    def _():
        back_ref[...] = total_ref[...].astype(BF16)
        shifts, scales = jnp.zeros((8, D), F32), jnp.zeros((8, D), F32)
        gates, out_bias = jnp.zeros((8, D), F32), jnp.zeros((1, D), F32)
        for i in range(3):
            here = pl.ds(i * BLOCK, BLOCK)
            segment = column_ref[here, :]
            second = dot(tokens_of(slot_column_ref[here, :]), back_ref[...])
            normed, inverse = normalise(after_ref[here, :])
            grad = second * (1.0 + per_crop(mods_ref[4], segment))
            mean = jnp.mean(grad, axis=1, keepdims=True)
            slant = jnp.mean(grad * normed, axis=1, keepdims=True)
            mid = cot_ref[here, :].astype(F32) + inverse * (grad - mean - normed * slant)
            mid_ref[here, :] = mid
            low = (per_crop(mods_ref[2], segment) * mid).astype(BF16)
            grad_attn_ref[here, :] = low
            out_bias = out_bias + jnp.sum(low.astype(F32), axis=0, keepdims=True)
            shifts = shifts + crop_sums(segment, second)
            scales = scales + crop_sums(segment, second * normed)
            gates = gates + crop_sums(segment, mid * attn_ref[here, :].astype(F32))
        sums_ref[0], sums_ref[1], sums_ref[2] = gates, shifts, scales
        out_bias_ref[...] = out_bias
        pair.free(2)
        pair.free(3)
        pair.take(3)
        leave = pltpu.make_async_copy(parts_ref, parts_out, out_sem.at[0])
        leave.start()
        for k in ORDER:
            scatter.collect(k)
        scatter.finish()
        leave.wait()


def unfeed(down, up, pull, grad_rows, arrived, after, cot, attn, mods, column, slot_column, given, early):
    block = lambda *tail: pl.BlockSpec((1, *tail), lambda i: (i, 0, 0))
    return pl.pallas_call(
        unfeed_kernel,
        grid=(4,),
        out_shape=[
            shape_of(4, 1, D, dtype=F32),
            shape_of(TOK_DEV, D, dtype=F32),
            shape_of(TOK_DEV, D),
            shape_of(3, 8, D, dtype=F32),
            shape_of(1, D, dtype=F32),
            shape_of(2, D, D),
            shape_of(4, SHARD, D),
        ],
        in_specs=[
            block(D, D), block(D, D), block(PLACES, D), whole(PLACES, D), whole(PLACES, D),
            whole(TOK_DEV, D), whole(TOK_DEV, D), whole(TOK_DEV, D), whole(6, 8, D), whole(TOK_DEV, 1),
            whole(TOK_DEV, 1), whole(2, 4, 2, SHARD, D), whole(4, SHARD, D),
        ],
        out_specs=[
            block(1, D), whole(TOK_DEV, D), whole(TOK_DEV, D), whole(3, 8, D), whole(1, D), ANYWHERE, whole(4, SHARD, D),
        ],
        scratch_shapes=[
            pltpu.VMEM((PLACES, D), BF16),
            pltpu.VMEM((PLACES, D), F32),
            pltpu.VMEM((PLACES, D), BF16),
            pltpu.VMEM((2, D, D), BF16),
            pltpu.VMEM((2, D, D), BF16),
            pltpu.VMEM((3, 4, SHARD, D), BF16),
            DMA((SCATTER_COPIES,)),
            DMA((SCATTER_COPIES,)),
            DMA((2,)),
            DMA((2,)),
            DMA((1,)),
        ],
        compiler_params=talking(4),
    )(down, up, pull, grad_rows, arrived, after, cot, attn, mods, column, slot_column, given, early)


def unattend_kernel(
    grad_ref, weight_in, heads_in, lse_ref, column_ref, row_ref, given_in, plane_ref, mask_ref,
    triple_ref, sums_ref, share_ref, plane_out, split_out,
    out_weight_ref, heads_ref, given_ref, split_ref, load_sems,
    bias_ref, mixed_ref, grads_ref, key_ref, value_ref, bufs_ref, from_z_ref,
    send_sems, recv_sems, along_send, along_recv,
):
    place = Place()
    place.meet()
    scatter = Scatter(place, given_ref, bufs_ref, plane_out, send_sems, recv_sems)
    along = Along(place, plane_ref, from_z_ref, share_ref, along_send, along_recv)
    loads = [
        pltpu.make_async_copy(source, target, load_sems.at[n])
        for n, (source, target) in enumerate(
            ((given_in, given_ref), (weight_in, out_weight_ref), (heads_in, heads_ref))
        )
    ]
    save = pltpu.make_async_copy(split_ref, split_out, load_sems.at[3])
    for copy in loads:
        copy.start()
    for k in (1, 2, 3):
        along.start(k)
    for j in range(4):
        split_ref[j] = grad_ref[:, OUT_SHARD * j : OUT_SHARD * (j + 1)]
    save.start()
    loads[0].wait()
    for k in ORDER:
        scatter.start(k)
    loads[1].wait()
    crop_mask(bias_ref, column_ref, row_ref)

    def spread(i, carry):
        here = rows_at(i)
        segment = column_ref[here, :]
        mixed = dot(grad_ref[here, :], out_weight_ref[...], NT)
        zero = jnp.zeros((BLOCK, 128 - HEAD_DIM), BF16)
        for h in range(HEADS):
            part = mixed[:, HEAD_DIM * h : HEAD_DIM * (h + 1)] * head_keep(mask_ref, h, segment)
            mixed_ref[h, here, :] = jnp.concatenate([part.astype(BF16), zero], axis=1)
        return carry

    lax.fori_loop(0, 3, spread, 0)
    factor = HEAD_DIM**-0.5
    loads[2].wait()

    def head(h, carry):
        @pl.when(h == 1)
        def _():
            for k in ORDER:
                scatter.follow(k)

        for at, k in enumerate(ORDER):

            @pl.when(h == 4 + at)
            def _():
                scatter.pass_across(k)

        keys, values = heads_ref[16 + h], heads_ref[32 + h]
        turned = jnp.transpose(keys)
        for i in range(3):
            here = pl.ds(i * BLOCK, BLOCK)
            queries, grads = heads_ref[h, here, :], mixed_ref[h, here, :]
            scores = dot(keys, queries, NT) * SOFT + bias_ref[:, here]
            probs = jnp.exp2(scores - lse_ref[h, :, here])
            product = probs * dot(values, grads, NT)
            total = jnp.sum(product, axis=0, keepdims=True)
            low = (product - probs * total).astype(BF16)
            for_values, for_keys = dot(probs.astype(BF16), grads), dot(low, queries)
            if i == 0:
                value_ref[...], key_ref[...] = for_values, for_keys
            else:
                value_ref[...] += for_values
                key_ref[...] += for_keys
            grads_ref[h, here, :] = jnp.transpose(dot(turned, low) * factor).astype(BF16)
        grads_ref[16 + h] = (key_ref[...] * factor).astype(BF16)
        grads_ref[32 + h] = value_ref[...].astype(BF16)
        return carry

    lax.fori_loop(0, HEADS, head, 0)
    for j in range(4):
        triple_ref[j, :, QKV_SHARD:] = jnp.zeros((TOK_DEV, PAD_SHARD - QKV_SHARD), BF16)
        for h in range(12):
            triple_ref[j, :, HEAD_DIM * h : HEAD_DIM * (h + 1)] = grads_ref[12 * j + h][:, :HEAD_DIM]
        sums_ref[j] = jnp.sum(triple_ref[j].astype(F32), axis=0, keepdims=True)
    save.wait()
    along.close()
    for k in ORDER:
        scatter.collect(k)
    scatter.finish()


def unattend(grad_attn, out_weight, heads, lse, column, row, given, plane, mask):
    return pl.pallas_call(
        unattend_kernel,
        out_shape=[
            shape_of(4, TOK_DEV, PAD_SHARD),
            shape_of(4, 1, PAD_SHARD, dtype=F32),
            shape_of(SHARD, D, dtype=F32),
            shape_of(4, SHARD, D),
            shape_of(4, TOK_DEV, OUT_SHARD),
        ],
        in_specs=[IN_VMEM] + [ANYWHERE] * 2 + [IN_VMEM] * 3 + [ANYWHERE, IN_VMEM, IN_SMEM],
        out_specs=[IN_VMEM] * 4 + [ANYWHERE],
        scratch_shapes=[
            pltpu.VMEM((D, D), BF16),
            pltpu.VMEM((3 * HEADS, TOK_DEV, 128), BF16),
            pltpu.VMEM((2, 4, 2, SHARD, D), BF16),
            pltpu.VMEM((4, TOK_DEV, OUT_SHARD), BF16),
            DMA((4,)),
            pltpu.VMEM((TOK_DEV, TOK_DEV), F32),
            pltpu.VMEM((HEADS, TOK_DEV, 128), BF16),
            pltpu.VMEM((3 * HEADS, TOK_DEV, 128), BF16),
            pltpu.VMEM((TOK_DEV, 128), F32),
            pltpu.VMEM((TOK_DEV, 128), F32),
            pltpu.VMEM((3, 4, SHARD, D), BF16),
            pltpu.VMEM((3, SHARD, D), BF16),
            DMA((SCATTER_COPIES,)),
            DMA((SCATTER_COPIES,)),
            DMA((3,)),
            DMA((3,)),
        ],
        compiler_params=talking(5),
    )(grad_attn, out_weight, heads, lse, column, row, given, plane, mask)


def unproject_kernel(
    weight_ref, triple_ref, split_ref, first_ref, mixed_ref, x_ref, mid_ref, mods_ref, column_ref,
    plane_up_ref, rest_ref, conds_ref, down_ref,
    grad_in_ref, share_up_ref, qkv_ref, out_ref, ada_ref, sums_ref, share_down_ref,
    share_ref, turn_ref, turned_ref, total_ref, buffers_ref, parts_ref, bufs_ref, plane_ref, up_z_ref, from_z_ref,
    mod_ref, mates_ref, rows_ref, packed_ref, every_ref,
    send_sems, recv_sems, pair_send, pair_recv, up_send, up_recv, along_send, along_recv,
    small_send, small_recv,
):
    step = pl.program_id(0)
    place = Place()
    pair = Pair(place, buffers_ref, parts_ref, pair_send, pair_recv)
    blocks = parts_ref.reshape(2, 4, 2, SHARD, D)
    scatter = Scatter(place, blocks, bufs_ref, plane_ref, send_sems, recv_sems)
    along_up = Along(place, plane_up_ref, up_z_ref, share_up_ref, up_send, up_recv)
    along = Along(place, plane_ref, from_z_ref, share_ref, along_send, along_recv)
    small = Copies(small_send, small_recv)
    to_mates = [
        small.make(mod_ref.at[other], mates_ref.at[place.index], mate)
        for other, mate in zip(place.mate_index, place.mates)
    ]
    to_peers = []
    for k in range(4):
        for there in (place.x, 1 - place.x) if k else (1 - place.x,):
            other = place.device(z=place.zs[k], x=there)
            to_peers.append(small.make(packed_ref, every_ref.at[place.peer], other))
    swaps = [
        small.make(turn_ref.at[other], turned_ref.at[place.index], mate)
        for other, mate in zip(place.mate_index, place.mates)
    ]
    @pl.when(step == 0)
    def _():
        place.meet()
        for k in (2, 3, 1):
            along_up.start(k)
        for j in range(4):
            turn_ref[j] = down_ref[:, OUT_SHARD * j : OUT_SHARD * (j + 1)]
        for copy in swaps:
            copy.start()
        turned_ref[place.index] = turn_ref[place.index]

    @pl.when(step < 4)
    def _():
        def grad(i, carry):
            here = pl.ds(pl.multiple_of(i * 384, 384), 384)
            buffer = lax.rem(step, 2)
            part = dot(first_ref[:, here], triple_ref[0], TN).astype(BF16)
            buffers_ref[buffer, here, :PAD_SHARD] = part
            part = dot(mixed_ref[:, here], split_ref[0], TN).astype(BF16)
            buffers_ref[buffer, here, QKV_SHARD:] = part
            return carry

        @pl.when(step >= 2)
        def _():
            pair.free(step - 2)

        lax.fori_loop(0, 3, grad, 0)
        pair.send(step)

    @pl.when((step >= 1) & (step < 5))
    def _():
        pair.take(step - 1)

    @pl.when(step == 4)
    def _():
        pair.free(2)
        pair.free(3)
        scatter.start(2)
        scatter.follow(2)
        scatter.start(3)

    for at, now, then in ((5, 2, 3), (6, 3, 1), (7, 1, 0)):

        @pl.when(step == at)
        def _():
            scatter.pass_across(now)
            scatter.follow(then)
            if at < 7:
                scatter.start(1 if at == 5 else 0)

    @pl.when(step >= 4)
    def _():
        for i in range(3):
            here = pl.ds(i * BLOCK, BLOCK)
            part = dot(triple_ref[0, here, :], weight_ref[0, :, :PAD_SHARD], NT)
            total_ref[here, :] = jnp.where(step == 4, part, total_ref[here, :] + part)

    @pl.when(step == 7)
    def _():
        scatter.collect(2)
        along.start(2)
        scatter.pass_across(0)
        shifts, scales = jnp.zeros((8, D), F32), jnp.zeros((8, D), F32)
        for i in range(3):
            here = pl.ds(i * BLOCK, BLOCK)
            segment = column_ref[here, :]
            first = total_ref[here, :]
            normed, inverse = normalise(x_ref[here, :].astype(F32))
            grads = first * (1.0 + per_crop(mods_ref[1], segment))
            mean = jnp.mean(grads, axis=1, keepdims=True)
            slant = jnp.mean(grads * normed, axis=1, keepdims=True)
            grad_in_ref[here, :] = mid_ref[here, :] + inverse * (grads - mean - normed * slant)
            shifts = shifts + crop_sums(segment, first)
            scales = scales + crop_sums(segment, first * normed)
        mod_ref[...] = rest_ref[...]
        mod_ref[0, :CROPS, :D] = shifts[:CROPS]
        mod_ref[0, :CROPS, D:] = scales[:CROPS, : D // 2]
        mod_ref[1, :CROPS, : D // 2] = scales[:CROPS, D // 2 :]
        for copy in to_mates:
            copy.start()
        mates_ref[place.index] = mod_ref[place.index]
        scatter.collect(3)
        along.start(3)
        for copy in to_mates:
            copy.wait_recv()
        rows_ref[...] = jnp.zeros_like(rows_ref)
        for j in range(4):
            rows_ref[CROPS * j : CROPS * (j + 1), :] = mates_ref[j, :CROPS, :]
            rows_ref[12:14, :] += mates_ref[j, CROPS : CROPS + 2, :]
        packed_ref[...] = rows_ref[...].astype(BF16)
        for copy in to_peers:
            copy.start()
        every_ref[place.peer] = packed_ref[...]
        scatter.collect(1)
        along.start(1)
        along_up.close()
        for copy in swaps:
            copy.wait_recv()
        share_down_ref[...] = turned_ref[...]
        scatter.collect(0)
        for copy in to_peers:
            copy.wait_recv()
        close_ada(conds_ref, every_ref, ada_ref, sums_ref)
        along.close()
        qkv_ref[...] = share_ref[:, :QKV_SHARD]
        out_ref[...] = share_ref[:, QKV_SHARD:]
        scatter.finish()
        for copy in small.made:
            copy.wait_send()


def unproject(weight, triple, split, first, mixed, x, mid, mods, column, plane_up, rest, conds, down):
    block = lambda *tail: pl.BlockSpec((1, *tail), lambda i: (lax.rem(i, 4), 0, 0))
    early = lambda *tail: pl.BlockSpec((1, *tail), lambda i: (jnp.minimum(i, 3), 0, 0))
    late = lambda *tail: pl.BlockSpec((1, *tail), lambda i: (jnp.maximum(i - 4, 0), 0, 0))
    wide = rest.shape[2]
    vmem = pltpu.VMEM
    return pl.pallas_call(
        unproject_kernel,
        grid=(8,),
        out_shape=[
            shape_of(TOK_DEV, D, dtype=F32),
            shape_of(SHARD, D, dtype=F32),
            shape_of(SHARD, QKV_SHARD, dtype=F32),
            shape_of(SHARD, OUT_SHARD, dtype=F32),
            shape_of(SHARD, wide, dtype=F32),
            shape_of(8, wide, dtype=F32),
            shape_of(4, SHARD, OUT_SHARD, dtype=F32),
        ],
        in_specs=[
            late(D, D), block(TOK_DEV, PAD_SHARD), early(TOK_DEV, OUT_SHARD), whole(TOK_DEV, D),
            whole(TOK_DEV, D), whole(TOK_DEV, D), whole(TOK_DEV, D), whole(6, 8, D), whole(TOK_DEV, 1),
            whole(4, SHARD, D), whole(4, 8, wide), whole(8, 16, 256), whole(SHARD, D),
        ],
        out_specs=[
            whole(TOK_DEV, D), whole(SHARD, D), whole(SHARD, QKV_SHARD), whole(SHARD, OUT_SHARD),
            whole(SHARD, wide), whole(8, wide), whole(4, SHARD, OUT_SHARD),
        ],
        scratch_shapes=[
            vmem((SHARD, D), F32),
            vmem((4, SHARD, OUT_SHARD), F32),
            vmem((4, SHARD, OUT_SHARD), F32),
            vmem((TOK_DEV, D), F32),
            vmem((2, D, D), BF16),
            vmem((2, D, D), BF16),
            vmem((3, 4, SHARD, D), BF16),
            vmem((4, SHARD, D), BF16),
            vmem((3, SHARD, D), BF16),
            vmem((3, SHARD, D), BF16),
            vmem((4, 8, wide), F32),
            vmem((4, 8, wide), F32),
            vmem((16, wide), F32),
            vmem((16, wide), BF16),
            vmem((8, 16, wide), BF16),
            DMA((SCATTER_COPIES,)),
            DMA((SCATTER_COPIES,)),
            DMA((2,)),
            DMA((2,)),
            DMA((3,)),
            DMA((3,)),
            DMA((3,)),
            DMA((3,)),
            DMA((13,)),
            DMA((13,)),
        ],
        compiler_params=talking(6),
    )(weight, triple, split, first, mixed, x, mid, mods, column, plane_up, rest, conds, down)


CROPS = 3


def gather_kernel(
    qkv_ref, out_ref, up_ref, down_ref, cond_ref, ada_ref, vectors_ref, slot_ref, groups_ref, lengths_ref,
    mixed_out, up_out, down_out, mods_ref, conds_ref, qkv_bias_ref, up_bias_ref, out_bias_ref,
    down_bias_ref, column_ref, row_ref, slot_column_ref, token_groups_ref,
    send_sems, recv_sems, local_sem, up_send, up_recv, up_local, small_send, small_recv, local_small,
    mixed_ref, stage_ref, own_small, all_small, crop_rows, own_crops, all_crops, ada_parts, ada_all,
    product_ref, columns_ref, total_ref, rows_ref, tables_ref,
    query_ref, value_ref,
):
    place = Place()
    place.meet()
    x, zs = place.x, place.zs
    mixed_ref[:, :QKV_SHARD] = qkv_ref[...]
    mixed_ref[:, QKV_SHARD:] = out_ref[...]
    first = Gather(
        place,
        mixed_ref,
        lambda y, c, z, x: mixed_out.at[y, c, z, x],
        send_sems,
        recv_sems,
        local_sem.at[0],
        False,
    )
    ups = Column(place, up_ref, up_out, up_send, up_recv, up_local.at[0])
    small = Copies(small_send, small_recv)
    to_mates = [small.make(own_small, all_small.at[place.index], mate) for mate in place.mates]
    others = [(k, far) for k in range(4) for far in (0, 1) if k or far]

    def to_peers(source, target):
        copies = []
        for k, far in others:
            there = 1 - x if far else x
            copies.append(
                small.make(
                    source(2 * zs[k] + there), target.at[place.peer], place.device(z=zs[k], x=there)
                )
            )
        return copies

    crops = to_peers(lambda peer: own_crops, all_crops)
    ada = to_peers(lambda peer: ada_parts.at[peer], ada_all)
    products = to_peers(lambda peer: product_ref.at[peer], columns_ref)
    finals = [
        small.make(rows_ref.at[other], tables_ref.at[place.index], mate)
        for other, mate in zip(place.mate_index, place.mates)
    ]

    def down_rows(index):
        return down_ref.at[pl.ds(pl.multiple_of(index * SHARD, 16), SHARD)]

    swaps = [
        small.make(down_rows(other), stage_ref.at[place.index], mate)
        for other, mate in zip(place.mate_index, place.mates)
    ]
    own_stage = pltpu.make_async_copy(
        down_rows(place.index), stage_ref.at[place.index], local_small.at[0]
    )

    first.start()
    cond = cond_ref[...].astype(F32)
    own_small[...] = jnp.zeros_like(own_small)
    own_small[:CROPS, :] = (cond / (1.0 + jnp.exp(-cond))).astype(BF16).astype(F32)
    own_small[CROPS : CROPS + 1, :] = vectors_ref[:, :D]
    own_small[CROPS + 1 : CROPS + 2, :] = vectors_ref[:, D : 2 * D]
    for copy in to_mates:
        copy.start()
    own_stage.start()
    all_small[place.index] = own_small[...]
    thin = ada_ref.shape[1] // 8
    ada_parts[...] = jnp.zeros_like(ada_parts)
    for i in range(8):
        ada_parts[i, :, :thin] = ada_ref[:, thin * i : thin * (i + 1)]
    for copy in ada:
        copy.start()
    ada_all[place.peer] = ada_parts[place.peer]
    crop_rows[...] = jnp.zeros_like(crop_rows)
    for copy in to_mates:
        copy.wait_recv()
    for j in range(4):
        crop_rows[CROPS * j : CROPS * (j + 1), :] = all_small[j, :CROPS, :]
    own_crops[...] = crop_rows[...].astype(BF16)
    for copy in crops:
        copy.start()
    all_crops[place.peer] = own_crops[...]
    first.pass_across(0)
    first_end = lengths_ref[0, 0]
    second_end = first_end + lengths_ref[0, 1]
    tokens = lax.broadcasted_iota(jnp.int32, (TOK_DEV, 1), 0)
    column_ref[...] = (tokens >= first_end).astype(jnp.int32) + (tokens >= second_end).astype(jnp.int32)
    tokens = lax.broadcasted_iota(jnp.int32, (1, TOK_DEV), 1)
    row_ref[...] = (tokens >= first_end).astype(jnp.int32) + (tokens >= second_end).astype(jnp.int32)
    spread = jnp.broadcast_to(slot_ref[...].astype(F32), (128, TOK_DEV))
    slot_column_ref[...] = jnp.transpose(spread)[:, :1].astype(jnp.int32)
    token_groups_ref[...] = jnp.zeros_like(token_groups_ref)
    token_groups_ref[:, :GROUPS] = per_crop(groups_ref[...].astype(F32), column_ref[...]).astype(BF16)
    for k in (1, 2, 3):
        first.pass_along(k)
    first.pass_across(1)
    for copy in crops + ada:
        copy.wait_recv()
    every_crop = all_crops[...].reshape(128, D)
    product = dot(every_crop, ada_all[...].reshape(D, ada_all.shape[2]))
    product_ref[...] = product.reshape(product_ref.shape)
    for copy in products:
        copy.start()
    ups.start()
    columns_ref[place.peer] = product_ref[place.peer]
    conds_ref[...] = jnp.zeros_like(conds_ref)
    mine = jnp.zeros((128, SHARD), F32)
    for i in range(8):
        part = every_crop[:, SHARD * i : SHARD * (i + 1)].astype(F32)
        mine = mine + jnp.where(place.peer == i, part, 0.0)
    conds_ref[:, :, :SHARD] = mine.reshape(8, 16, SHARD)
    first.pass_across(2)
    for copy in products:
        copy.wait_recv()
    for i in range(8):
        total_ref[:, thin * i : thin * (i + 1)] = columns_ref[i, :, :thin]
    total = total_ref[...] + vectors_ref[:, 2 * D :]
    rows_ref[...] = jnp.zeros_like(rows_ref)
    for j in range(4):
        rows_ref[j, :CROPS, :] = total[CROPS * j : CROPS * (j + 1)]
    for copy in finals:
        copy.start()
    tables_ref[place.index] = rows_ref[place.index]
    for copy in swaps:
        copy.start()
    first.pass_across(3)
    first.pass_pair(0)
    first.pass_pair(1)
    for copy in finals:
        copy.wait_recv()
    for j in (0, 2):
        mods_ref[3 * j // 2] = tables_ref[j, :, :D]
        mods_ref[3 * j // 2 + 1, :, : D // 2] = tables_ref[j, :, D:]
        mods_ref[3 * j // 2 + 1, :, D // 2 :] = tables_ref[j + 1, :, : D // 2]
        mods_ref[3 * j // 2 + 2] = tables_ref[j + 1, :, D // 2 :]
    for copy in swaps:
        copy.wait_recv()
    own_stage.wait()
    for j in range(4):
        here = slice(OUT_SHARD * j, OUT_SHARD * (j + 1))
        down_out[:, here] = stage_ref[j]
        up_bias_ref[j] = all_small[j, CROPS : CROPS + 1, :]
        row = all_small[j, CROPS + 1 : CROPS + 2, :]
        query_ref[:, here] = row[:, :OUT_SHARD]
        value_ref[:, here] = row[:, OUT_SHARD : 2 * OUT_SHARD]
        out_bias_ref[:, here] = row[:, 2 * OUT_SHARD : 3 * OUT_SHARD]
        down_bias_ref[:, here] = row[:, 3 * OUT_SHARD :]
    qkv_bias_ref[...] = jnp.zeros_like(qkv_bias_ref)
    qkv_bias_ref[0, :, :QKV_SHARD] = query_ref[:, :QKV_SHARD]
    qkv_bias_ref[1, :, :OUT_SHARD] = query_ref[:, QKV_SHARD:]
    qkv_bias_ref[2, :, 2 * OUT_SHARD : QKV_SHARD] = value_ref[:, :OUT_SHARD]
    qkv_bias_ref[3, :, :QKV_SHARD] = value_ref[:, OUT_SHARD:]
    for k in (2, 3):
        first.pass_pair(k)
    first.finish()
    ups.finish()
    for copy in small.made:
        copy.wait_send()


def gather_all(qkv, out, up, down, cond, ada, vectors, slot, groups, lengths):
    vmem = pltpu.VMEM
    wide = ada.shape[1]
    return pl.pallas_call(
        gather_kernel,
        out_shape=[
            shape_of(2, 2, 4, 2, SHARD, D),
            shape_of(4, SHARD, D),
            shape_of(SHARD, D),
            shape_of(6, 8, D, dtype=F32),
            shape_of(8, 16, 256, dtype=F32),
            shape_of(4, 1, PAD_SHARD, dtype=F32),
            shape_of(4, 1, D, dtype=F32),
            shape_of(1, D, dtype=F32),
            shape_of(1, D, dtype=F32),
            shape_of(TOK_DEV, 1, dtype=jnp.int32),
            shape_of(1, TOK_DEV, dtype=jnp.int32),
            shape_of(TOK_DEV, 1, dtype=jnp.int32),
            shape_of(TOK_DEV, 128),
        ],
        in_specs=[IN_VMEM] * 2 + [ANYWHERE] * 2 + [IN_VMEM] * 5 + [IN_SMEM],
        out_specs=[ANYWHERE] * 2 + [IN_VMEM] * 11,
        scratch_shapes=[DMA((GATHER_COPIES,))] * 2
        + [DMA((1,)), DMA((3,)), DMA((3,)), DMA((1,)), DMA((30,)), DMA((30,)), DMA((1,))]
        + [
            vmem((SHARD, D), BF16),
            vmem((4, SHARD, OUT_SHARD), BF16),
            vmem((8, D), F32),
            vmem((4, 8, D), F32),
            vmem((16, D), F32),
            vmem((16, D), BF16),
            vmem((8, 16, D), BF16),
            vmem((8, SHARD, 256), BF16),
            vmem((8, SHARD, 256), BF16),
            vmem((8, 16, 256), F32),
            vmem((8, 16, 256), F32),
            vmem((16, wide), F32),
            vmem((4, 8, wide), F32),
            vmem((4, 8, wide), F32),
            vmem((1, D), F32),
            vmem((1, D), F32),
        ],
        compiler_params=talking(1),
    )(qkv, out, up, down, cond, ada, vectors, slot, groups, lengths)


def close_ada(conds_ref, every, ada_ref, sums_ref):
    rows = jnp.zeros((16, ada_ref.shape[1]), F32)
    for i in range(8):
        rows = rows + every[i].astype(F32)
    cond = conds_ref[...].reshape(128, 256)[:, :SHARD].astype(BF16)
    total = dot(cond, every[...].reshape(128, ada_ref.shape[1]), TN)
    ada_ref[...] = total
    sums_ref[...] = jnp.zeros_like(sums_ref)
    sums_ref[0:1, :] = jnp.sum(rows[:12], axis=0, keepdims=True)
    sums_ref[1:3, :] = rows[12:14]


def block_shards(
    block_in, condition, lengths, head_mask, group_mask, buffer_slot, ada_weight, ada_bias, qkv_weight,
    query_bias, value_bias, out_weight, out_bias, up_weight, up_bias, down_weight, down_bias, cotangent,
):
    x, cot, slot_row, mask = block_in[0], cotangent[0], buffer_slot.astype(jnp.int32), head_mask[0]
    vectors = (up_bias, query_bias, value_bias, out_bias, down_bias, ada_bias)
    total = sum(vector.shape[0] for vector in vectors)
    starts = (0, 1152, 1440, 1728, 2016, 2304)
    padded = [
        jnp.pad(vector.astype(F32), (start, total - start - vector.shape[0]))
        for start, vector in zip(starts, vectors)
    ]
    vectors = sum(padded)[None]
    (
        mixed_weight, up_column, down_rows, mods, conds, qkv_bias, bias_up, bias_out, bias_down,
        column, row, slot_column, groups,
    ) = gather_all(
        qkv_weight, out_weight, up_weight, down_weight, condition[0], ada_weight, vectors, slot_row,
        group_mask[0], lengths,
    )
    mixed_weight = mixed_weight.reshape(4, D, D)
    edges = (0, 288, 576, 864, 2016, 2304)
    first, heads, mixed, lse, attn, after, arrived, picked, full_out, up, down_column = attend(
        x, mixed_weight, mods, qkv_bias, bias_out, column, row, slot_row, groups, mask, up_column,
        down_rows,
    )
    up = up.reshape(4, D, D)
    pull, grad_rows, block_out, gate_two, grad_down_bias, parts_down, down, early_down = feed(
        up, arrived, picked, bias_up, bias_down, cot, after, mods, column,
        slot_column, slot_row, down_column,
    )
    down = down.reshape(4, D, D)
    grad_up_bias, mid, grad_attn, sums, grad_out_bias, parts_up, plane_down = unfeed(
        down, up, pull, grad_rows, arrived, after, cot, attn, mods, column, slot_column, parts_down, early_down
    )
    triple, triple_sums, share_down, plane_up, grad_split = unattend(
        grad_attn, full_out, heads, lse, column, row, parts_up.reshape(2, 4, 2, SHARD, D), plane_down,
        mask,
    )
    triple_sums = triple_sums[:, 0, :QKV_SHARD].reshape(3 * D)
    blank = jnp.zeros((8, 2 * D), F32)
    mod_grads = jnp.concatenate([blank, sums[0], sums[1], sums[2], gate_two], axis=1)[:CROPS]
    mod_grads = mod_grads.reshape(CROPS, 4, -1).transpose(1, 0, 2)
    bias_grads = (
        triple_sums[:D], triple_sums[2 * D :], grad_out_bias, grad_up_bias, grad_down_bias,
    )
    bias_grads = jnp.concatenate([vector.reshape(4, -1) for vector in bias_grads], axis=1)
    wide = mod_grads.shape[2]
    bias_grads = jnp.pad(bias_grads, ((0, 0), (0, 5 * wide - 2304))).reshape(4, 5, wide)
    rest = jnp.concatenate([mod_grads, bias_grads], axis=1)
    grad_in, share_up, share_qkv, share_out, grad_ada, totals, share_down = unproject(
        mixed_weight, triple, grad_split, first, mixed, x, mid, mods, column, plane_up, rest, conds,
        share_down,
    )
    share_down = share_down.reshape(4 * SHARD, OUT_SHARD)
    bias_totals = totals[1:3].reshape(-1)
    grad_query, grad_value, grad_out, grad_ups, grad_downs = [
        bias_totals[low:high] for low, high in zip(edges[:-1], edges[1:])
    ]
    return (
        block_out[None],
        grad_in[None],
        grad_ada,
        totals[0],
        share_qkv,
        grad_query,
        grad_value,
        share_out,
        grad_out,
        share_up,
        grad_ups,
        share_down,
        grad_downs,
    )


def layer_norm(values):
    center = values - jnp.mean(values, axis=-1, keepdims=True)
    variance = jnp.mean(center * center, axis=-1, keepdims=True)
    inverse = lax.rsqrt(variance + epsilon)
    return (center * inverse, inverse)


def norm_back(grad_normed, normed, inverse):
    first_mean = jnp.mean(grad_normed, axis=-1, keepdims=True)
    second_mean = jnp.mean(grad_normed * normed, axis=-1, keepdims=True)
    return inverse * (grad_normed - first_mean - normed * second_mean)


def attention_scores(query_part, key_part, allowed, factor):
    raw_scores = (
        jnp.einsum("qhd,khd->hqk", query_part, key_part, preferred_element_type=jnp.float32)
        * factor
    )
    return jnp.where(allowed[None], raw_scores, -1e30)


def gelu_tanh(values):
    return jax.nn.gelu(values, approximate=True)


def shards(
    block_in,
    condition,
    lengths,
    head_mask,
    group_mask,
    buffer_slot,
    ada_weight,
    ada_bias,
    qkv_weight,
    query_bias,
    value_bias,
    out_weight,
    out_bias,
    up_weight,
    up_bias,
    down_weight,
    down_bias,
    cotangent,
):
    peers = lax.axis_size("dp")
    mates = lax.axis_size("fsdp")

    def gather_matrix(shard):
        stacked = lax.all_gather(shard, ("dp", "fsdp"), axis=0, tiled=False)
        rows, columns = shard.shape
        stacked = stacked.reshape(peers, mates, rows, columns).transpose(0, 2, 1, 3)
        return stacked.reshape(peers * rows, mates * columns)

    full_qkv, full_out, full_up, full_down = [
        gather_matrix(shard) for shard in (qkv_weight, out_weight, up_weight, down_weight)
    ]
    vectors = (query_bias, value_bias, out_bias, up_bias, down_bias)
    packed_bias = lax.all_gather(jnp.concatenate(vectors), "fsdp", axis=0, tiled=False)
    edges = [0]
    for vector in vectors:
        edges.append(edges[-1] + vector.shape[0])
    bias_query, bias_value, bias_out, bias_up, bias_down = [
        packed_bias[:, low:high].reshape(-1).astype(jnp.float32)
        for low, high in zip(edges[:-1], edges[1:])
    ]
    inputs = block_in[0].astype(jnp.float32)
    crop_length = lengths[0]
    finish = jnp.cumsum(crop_length)
    opening = finish - crop_length
    position = jnp.arange(TOK_DEV, dtype=jnp.int32)
    member = (
        (position[:, None] >= opening[None, :]) & (position[:, None] < finish[None, :])
    ).astype(jnp.float32)
    segment = jnp.sum((position[:, None] >= finish[None, :]).astype(jnp.int32), axis=1)
    cond_act = jax.nn.silu(condition[0].astype(jnp.float32)).astype(jnp.bfloat16)
    crops = cond_act.shape[0]
    cond_all = lax.all_gather(cond_act, ("dp", "fsdp"), axis=0, tiled=True)
    depth = ada_weight.shape[0]
    cond_slice = lax.dynamic_slice_in_dim(cond_all, lax.axis_index("dp") * depth, depth, axis=1)
    partial_mod = jnp.dot(cond_slice, ada_weight, preferred_element_type=jnp.float32)
    column_mod = lax.psum_scatter(partial_mod, "dp", scatter_dimension=0, tiled=True)
    column_mod = column_mod + ada_bias.astype(jnp.float32)
    modulation = lax.all_to_all(column_mod, "fsdp", split_axis=0, concat_axis=1, tiled=True)
    pieces = [
        jnp.dot(member, modulation[:, number * D : (number + 1) * D], precision=highest)
        for number in range(6)
    ]
    shift_one, scale_one, gate_one, shift_two, scale_two, gate_two = pieces
    head_keep = jnp.dot(member, head_mask[0].astype(jnp.float32), precision=highest)
    group_keep = jnp.dot(member, group_mask[0].astype(jnp.float32), precision=highest)
    normed_one, inverse_one = layer_norm(inputs)
    first_in = (normed_one * (1.0 + scale_one) + shift_one).astype(jnp.bfloat16)
    qkv_bias = jnp.concatenate([bias_query, jnp.zeros_like(bias_query), bias_value])
    triple = (jnp.dot(first_in, full_qkv, preferred_element_type=jnp.float32) + qkv_bias).astype(
        jnp.bfloat16
    )
    queries = triple[:, :D].reshape(TOK_DEV, HEADS, HEAD_DIM)
    keys_all = triple[:, D : 2 * D].reshape(TOK_DEV, HEADS, HEAD_DIM)
    values_all = triple[:, 2 * D :].reshape(TOK_DEV, HEADS, HEAD_DIM)
    factor = HEAD_DIM ** (-0.5)
    row_block = min(768, TOK_DEV)
    group_size = min(4, HEADS)
    log_totals = {}
    head_parts = []
    for head_start in range(0, HEADS, group_size):
        heads_here = slice(head_start, head_start + group_size)
        row_start = 0
        rows_here = slice(row_start, row_start + row_block)
        allowed = segment[:, None] == segment[None, :]
        scores = attention_scores(
            queries[rows_here, heads_here], keys_all[:, heads_here], allowed, factor
        )
        row_max = jnp.max(scores, axis=-1, keepdims=True)
        log_total = row_max + jnp.log(jnp.sum(jnp.exp(scores - row_max), axis=-1, keepdims=True))
        weights_low = jnp.exp(scores - log_total).astype(jnp.bfloat16)
        row_parts = jnp.einsum(
            "hqk,khd->qhd",
            weights_low,
            values_all[:, heads_here],
            preferred_element_type=jnp.float32,
        )
        log_totals[head_start, row_start] = log_total
        head_parts.append(row_parts)
    attended = jnp.concatenate(head_parts, axis=1)
    mixed = (attended * head_keep[:, :, None]).astype(jnp.bfloat16).reshape(TOK_DEV, D)
    attn_out = jnp.dot(mixed, full_out, preferred_element_type=jnp.float32) + bias_out
    after_attn = inputs + gate_one * attn_out
    normed_two, inverse_two = layer_norm(after_attn)
    second_in = (normed_two * (1.0 + scale_two) + shift_two).astype(jnp.bfloat16)
    keep = (buffer_slot[0] >= 0).astype(jnp.float32)[:, None]
    places = 2 * TOK_DEV // 3
    chooser = (buffer_slot[0][:, None] == jnp.arange(places, dtype=jnp.int32)[None, :]).astype(
        jnp.bfloat16
    )
    arrived = jnp.einsum(
        "tb,td->bd", chooser, second_in, preferred_element_type=jnp.float32
    ).astype(jnp.bfloat16)
    groups_float = jnp.einsum(
        "tb,tg->bg",
        chooser,
        group_keep.astype(jnp.bfloat16),
        preferred_element_type=jnp.float32,
    )
    channel_keep = jnp.repeat(groups_float, FF // GROUPS, axis=1)
    hidden = jnp.dot(arrived, full_up, preferred_element_type=jnp.float32) + bias_up
    active = (gelu_tanh(hidden) * channel_keep).astype(jnp.bfloat16)
    branch = (jnp.dot(active, full_down, preferred_element_type=jnp.float32) + bias_down).astype(
        jnp.bfloat16
    )
    branch_tok = jnp.einsum(
        "tb,bd->td", chooser, branch, preferred_element_type=jnp.float32
    )
    after_mlp = after_attn + gate_two * branch_tok
    block_out = after_mlp.astype(jnp.bfloat16)[None]
    grad_after = cotangent[0].astype(jnp.float32)
    grad_gate_two = grad_after * branch_tok
    grad_branch = (gate_two * keep * grad_after).astype(jnp.bfloat16)
    grad_rows = jnp.einsum(
        "tb,td->bd", chooser, grad_branch, preferred_element_type=jnp.float32
    ).astype(jnp.bfloat16)
    back_qkv, back_out, back_up, back_down = full_qkv, full_out, full_up, full_down
    grad_down_bias = jnp.sum(grad_rows.astype(jnp.float32), axis=0)
    grad_down = jnp.einsum("bf,bd->fd", active, grad_rows, preferred_element_type=jnp.float32)
    grad_active = jnp.einsum("bd,fd->bf", grad_rows, back_down, preferred_element_type=jnp.float32)
    gelu_pull = jax.vjp(gelu_tanh, hidden)[1]
    grad_hidden = gelu_pull(grad_active * channel_keep)[0].astype(jnp.bfloat16)
    grad_up_bias = jnp.sum(grad_hidden.astype(jnp.float32), axis=0)
    grad_up = jnp.einsum("bd,bf->df", arrived, grad_hidden, preferred_element_type=jnp.float32)
    grad_arrived = jnp.einsum(
        "bf,df->bd", grad_hidden, back_up, preferred_element_type=jnp.float32
    ).astype(jnp.bfloat16)
    grad_second = jnp.einsum(
        "tb,bd->td", chooser, grad_arrived, preferred_element_type=jnp.float32
    )
    grad_scale_two = grad_second * normed_two
    grad_mid = grad_after + norm_back(grad_second * (1.0 + scale_two), normed_two, inverse_two)
    grad_gate_one = grad_mid * attn_out
    grad_attn = (gate_one * grad_mid).astype(jnp.bfloat16)
    grad_out_bias = jnp.sum(grad_attn.astype(jnp.float32), axis=0)
    grad_out = jnp.einsum("te,tf->ef", mixed, grad_attn, preferred_element_type=jnp.float32)
    grad_mixed = jnp.einsum(
        "tf,ef->te", grad_attn, back_out, preferred_element_type=jnp.float32
    ).astype(jnp.bfloat16)
    grad_attended = (
        grad_mixed.reshape(TOK_DEV, HEADS, HEAD_DIM).astype(jnp.float32) * head_keep[:, :, None]
    ).astype(jnp.bfloat16)
    query_heads = []
    key_heads = []
    value_heads = []
    for head_start in range(0, HEADS, group_size):
        heads_here = slice(head_start, head_start + group_size)
        row_start = 0
        rows_here = slice(row_start, row_start + row_block)
        allowed = segment[:, None] == segment[None, :]
        scores = attention_scores(
            queries[rows_here, heads_here], keys_all[:, heads_here], allowed, factor
        )
        probs = jnp.exp(scores - log_totals[head_start, row_start])
        grad_piece = grad_attended[rows_here, heads_here]
        grad_values = jnp.einsum(
            "hqk,qhd->khd",
            probs.astype(jnp.bfloat16),
            grad_piece,
            preferred_element_type=jnp.float32,
        )
        grad_probs = jnp.einsum(
            "qhd,khd->hqk",
            grad_piece,
            values_all[:, heads_here],
            preferred_element_type=jnp.float32,
        )
        grad_scores = (
            probs * (grad_probs - jnp.sum(probs * grad_probs, axis=-1, keepdims=True))
        ).astype(jnp.bfloat16)
        query_rows = (
            jnp.einsum(
                "hqk,khd->qhd",
                grad_scores,
                keys_all[:, heads_here],
                preferred_element_type=jnp.float32,
            )
            * factor
        )
        grad_keys = (
            jnp.einsum(
                "hqk,qhd->khd",
                grad_scores,
                queries[rows_here, heads_here],
                preferred_element_type=jnp.float32,
            )
            * factor
        )
        query_heads.append(query_rows)
        key_heads.append(grad_keys)
        value_heads.append(grad_values)
    grad_triple = jnp.concatenate(
        [
            jnp.concatenate(query_heads, axis=1).reshape(TOK_DEV, D),
            jnp.concatenate(key_heads, axis=1).reshape(TOK_DEV, D),
            jnp.concatenate(value_heads, axis=1).reshape(TOK_DEV, D),
        ],
        axis=1,
    ).astype(jnp.bfloat16)
    grad_query_bias = jnp.sum(grad_triple[:, :D].astype(jnp.float32), axis=0)
    grad_value_bias = jnp.sum(grad_triple[:, 2 * D :].astype(jnp.float32), axis=0)
    grad_qkv = jnp.einsum("td,te->de", first_in, grad_triple, preferred_element_type=jnp.float32)
    grad_first = jnp.einsum("te,de->td", grad_triple, back_qkv, preferred_element_type=jnp.float32)
    grad_scale_one = grad_first * normed_one
    grad_inputs = grad_mid + norm_back(grad_first * (1.0 + scale_one), normed_one, inverse_one)
    token_grads = [
        grad_first,
        grad_scale_one,
        grad_gate_one,
        grad_second,
        grad_scale_two,
        grad_gate_two,
    ]
    grad_modulation = jnp.concatenate(
        [jnp.einsum("ts,td->sd", member, single, precision=highest) for single in token_grads],
        axis=1,
    )
    mod_columns = lax.all_to_all(
        grad_modulation, "fsdp", split_axis=1, concat_axis=0, tiled=True
    )
    mod_all = lax.all_gather(mod_columns, "dp", axis=0, tiled=True)
    grad_ada_bias = jnp.sum(mod_all, axis=0)
    grad_ada = jnp.einsum(
        "sd,se->de", cond_slice.astype(jnp.float32), mod_all, precision=highest
    )

    def scatter_matrix(full):
        rows, columns = full.shape[0] // peers, full.shape[1] // mates
        blocks = full.astype(jnp.bfloat16).reshape(peers, rows, mates, columns)
        blocks = blocks.transpose(0, 2, 1, 3).reshape(peers * mates * rows, columns)
        share = lax.psum_scatter(blocks, ("dp", "fsdp"), scatter_dimension=0, tiled=True)
        return share.astype(jnp.float32)

    shares = [scatter_matrix(full) for full in (grad_qkv, grad_out, grad_up, grad_down)]
    bias_grads = (grad_query_bias, grad_value_bias, grad_out_bias, grad_up_bias, grad_down_bias)
    packed = jnp.concatenate([vector.reshape(mates, -1) for vector in bias_grads], axis=1)
    packed = lax.psum_scatter(packed, "fsdp", scatter_dimension=0, tiled=True)
    packed = lax.psum(packed[0], "dp")
    totals = [packed[low:high] for low, high in zip(edges[:-1], edges[1:])]
    return (
        block_out,
        grad_inputs[None],
        grad_ada,
        grad_ada_bias,
        shares[0],
        totals[0],
        totals[1],
        shares[1],
        totals[2],
        shares[2],
        totals[3],
        shares[3],
        totals[4],
    )


def solution(mesh):
    placed = (
        P(("dp", "fsdp"), None, None),
        P(("dp", "fsdp"), None, None),
        P(("dp", "fsdp"), None),
        P(("dp", "fsdp"), None, None),
        P(("dp", "fsdp"), None, None),
        P(("dp", "fsdp"), None),
        P("dp", "fsdp"),
        P("fsdp"),
        P("dp", "fsdp"),
        P("fsdp"),
        P("fsdp"),
        P("dp", "fsdp"),
        P("fsdp"),
        P("dp", "fsdp"),
        P("fsdp"),
        P("dp", "fsdp"),
        P("fsdp"),
        P(("dp", "fsdp"), None, None),
    )
    on_block = dict(mesh.shape) == {"dp": 8, "fsdp": 4}
    return jax.shard_map(
        block_shards if on_block else shards,
        mesh=mesh,
        in_specs=placed,
        out_specs=(
            P(("dp", "fsdp"), None, None),
            P(("dp", "fsdp"), None, None),
            P("dp", "fsdp"),
            P("fsdp"),
            P("dp", "fsdp"),
            P("fsdp"),
            P("fsdp"),
            P("dp", "fsdp"),
            P("fsdp"),
            P("dp", "fsdp"),
            P("fsdp"),
            P("dp", "fsdp"),
            P("fsdp"),
        ),
        check_vma=False,
    )
```

```python
import math

import jax
import jax.numpy as jnp
from jax import lax
from jax.experimental import pallas as pl
from jax.experimental.pallas import tpu as pltpu
from jax.sharding import PartitionSpec as P

D = 1152
HEADS = 16
HEAD_DIM = 72
FF = 4608
GROUPS = 16
TOK_DEV = 768


highest = lax.Precision.HIGHEST
epsilon = 1e-06


NT = (((1,), (1,)), ((), ()))
TN = (((0,), (0,)), ((), ()))
NN = (((1,), (0,)), ((), ()))
PLACES = 512
BLOCK = 256
BF16, F32 = jnp.bfloat16, jnp.float32
SOFT = HEAD_DIM**-0.5 * math.log2(math.e)
QKV_SHARD, OUT_SHARD, PAD_SHARD = 864, 288, 896
VMEM_BYTES = 60 * 2**20


def dot(left, right, dims=NN):
    return lax.dot_general(left, right, dims, preferred_element_type=F32)


def rows_at(i):
    return pl.ds(pl.multiple_of(i * BLOCK, BLOCK), BLOCK)


def per_crop(table, segment):
    return jnp.where(
        segment == 0, table[0:1], jnp.where(segment == 1, table[1:2], table[2:3])
    )


def normalise(values):
    center = values - jnp.mean(values, axis=1, keepdims=True)
    variance = jnp.mean(center * center, axis=1, keepdims=True)
    inverse = lax.rsqrt(variance + epsilon)
    return center * inverse, inverse


def crop_sums(segment, values):
    lanes = lax.broadcasted_iota(jnp.int32, (values.shape[0], 128), 1)
    member = (lanes == segment).astype(BF16)
    high = values.astype(BF16)
    low = (values - high.astype(F32)).astype(BF16)
    return (dot(member, high, TN) + dot(member, low, TN))[:8]


def crop_mask(bias_ref, column_ref, row_ref):
    for i in range(TOK_DEV // BLOCK):
        here = pl.ds(i * BLOCK, BLOCK)
        bias_ref[here, :] = jnp.where(column_ref[here, :] == row_ref[...], 0.0, -1e30).astype(F32)


def places_of(slot_row, i):
    place = lax.broadcasted_iota(jnp.int32, (BLOCK, TOK_DEV), 0) + i * BLOCK
    return (place == slot_row).astype(BF16)


def tokens_of(slot_column):
    place = lax.broadcasted_iota(jnp.int32, (BLOCK, PLACES), 1)
    return (place == slot_column).astype(BF16)


def head_keep(mask_ref, h, segment):
    keep = jnp.where(
        segment == 0, mask_ref[0, h], jnp.where(segment == 1, mask_ref[1, h], mask_ref[2, h])
    )
    return keep.astype(F32)


MESH = pl.DeviceIdType.MESH
SHARD = 144
UPPER = 80


class Place:
    def __init__(self):
        dp, fsdp = lax.axis_index("dp"), lax.axis_index("fsdp")
        self.z, self.x = lax.div(dp, 2), lax.rem(dp, 2)
        self.y, self.c = lax.div(fsdp, 2), lax.rem(fsdp, 2)
        z = self.z
        self.zs = (z, z + 1 - 2 * lax.rem(z, 2), lax.rem(z + 2, 4), 3 - z)
        self.mates = (
            self.device(c=1 - self.c),
            self.device(y=1 - self.y),
            self.device(y=1 - self.y, c=1 - self.c),
        )
        self.mate_index = (
            2 * self.y + 1 - self.c,
            2 * (1 - self.y) + self.c,
            2 * (1 - self.y) + 1 - self.c,
        )
        self.index = 2 * self.y + self.c
        self.peer = 2 * z + self.x

    def device(self, z=None, x=None, y=None, c=None):
        z, x = self.z if z is None else z, self.x if x is None else x
        y, c = self.y if y is None else y, self.c if c is None else c
        return (2 * z + x, 2 * y + c)

    def meet(self):
        barrier = pltpu.get_barrier_semaphore()
        others = [self.device(z=self.zs[k]) for k in (1, 2, 3)]
        others += [self.device(z=self.zs[k], x=1 - self.x) for k in range(4)]
        others += self.mates
        for other in others:
            pl.semaphore_signal(barrier, inc=1, device_id=other, device_id_type=MESH)
        pl.semaphore_wait(barrier, len(others))


class Copies:
    def __init__(self, send_sems, recv_sems):
        self.send_sems, self.recv_sems, self.made = send_sems, recv_sems, []

    def make(self, source, target, device):
        index = len(self.made)
        copy = pltpu.make_async_remote_copy(
            src_ref=source,
            dst_ref=target,
            send_sem=self.send_sems.at[index],
            recv_sem=self.recv_sems.at[index],
            device_id=device,
            device_id_type=MESH,
        )
        self.made.append(copy)
        return copy


GATHER_COPIES = 35


class Gather:
    def __init__(self, place, source, slot, send_sems, recv_sems, local_sem, swap):
        x, y, c, zs = place.x, place.y, place.c, place.zs
        self.copies = Copies(send_sems, recv_sems)
        make = self.copies.make
        first, second = (SHARD - UPPER, UPPER) if swap else (0, UPPER)
        upper = pl.ds(first, second)
        lower = pl.ds(0, SHARD - UPPER) if swap else pl.ds(UPPER, SHARD - UPPER)
        over_x, over_y, beside = (
            place.device(x=1 - x),
            place.device(y=1 - y),
            place.device(c=1 - c),
        )
        own = [slot(y, c, zs[k], x) for k in range(4)]
        held = [source] + own[1:]
        from_x = [slot(y, c, zs[k], 1 - x) for k in range(4)]
        from_y = [slot(1 - y, c, zs[k], x) for k in range(4)]
        across = [slot(1 - y, c, zs[k], 1 - x) for k in range(4)]
        self.local = pltpu.make_async_copy(source, own[0], local_sem)
        self.along = [None] + [make(source, own[0], place.device(z=zs[k])) for k in (1, 2, 3)]
        self.to_x = [make(held[k], own[k], over_x) for k in range(4)]
        self.to_y = [make(held[k], own[k], over_y) for k in range(4)]
        self.x_to_y = [make(s.at[upper], s.at[upper], over_y) for s in from_x]
        self.y_to_x = [make(s.at[lower], s.at[lower], over_x) for s in from_y]
        self.pair = [make(held[k], own[k], beside) for k in range(4)]
        self.pair_x = [make(s, s, beside) for s in from_x]
        self.pair_y = [make(s, s, beside) for s in from_y]
        self.pair_across = [make(s, s, beside) for s in across]

    def start(self):
        self.along[1].start()
        self.to_x[0].start()
        self.to_y[0].start()
        self.along[2].start()
        self.along[3].start()
        self.pair[0].start()
        self.local.start()

    def pass_along(self, k):
        self.along[k].wait_recv()
        self.to_x[k].start()
        self.to_y[k].start()
        self.pair[k].start()

    def pass_across(self, k):
        self.to_x[k].wait_recv()
        self.x_to_y[k].start()
        self.pair_x[k].start()
        self.to_y[k].wait_recv()
        self.y_to_x[k].start()
        self.pair_y[k].start()

    def pass_pair(self, k):
        self.x_to_y[k].wait_recv()
        self.y_to_x[k].wait_recv()
        self.pair_across[k].start()

    def finish(self):
        self.local.wait()
        for copy in self.pair + self.pair_x + self.pair_y + self.pair_across:
            copy.wait_recv()
        for copy in self.copies.made:
            copy.wait_send()


class Column:
    def __init__(self, place, source, column, send_sems, recv_sems, local_sem):
        copies = Copies(send_sems, recv_sems)
        self.local = pltpu.make_async_copy(source, column.at[place.z], local_sem)
        self.along = [
            copies.make(source, column.at[place.z], place.device(z=place.zs[k])) for k in (1, 2, 3)
        ]

    def start(self):
        for copy in self.along:
            copy.start()
        self.local.start()

    def finish(self):
        for copy in self.along:
            copy.wait()
        self.local.wait()


SPREAD_COPIES = 32


class Spread:
    def __init__(self, place, column, slot, send_sems, recv_sems, local_sems):
        x, y, c, zs = place.x, place.y, place.c, place.zs
        self.copies = Copies(send_sems, recv_sems)
        make = self.copies.make
        upper, lower = pl.ds(0, UPPER), pl.ds(UPPER, SHARD - UPPER)
        over_x, over_y, beside = place.device(x=1 - x), place.device(y=1 - y), place.mates[0]
        four = range(4)
        held = [column.at[zs[k]] for k in four]
        own = [slot(y, c, zs[k], x) for k in four]
        from_x = [slot(y, c, zs[k], 1 - x) for k in four]
        from_y = [slot(1 - y, c, zs[k], x) for k in four]
        across = [slot(1 - y, c, zs[k], 1 - x) for k in four]
        first = [upper, lower, upper, lower]
        second = [lower, upper, lower, upper]
        self.local = [pltpu.make_async_copy(held[k], own[k], local_sems.at[k]) for k in four]
        self.to_x = [make(held[k], own[k], over_x) for k in four]
        self.to_y = [make(held[k], own[k], over_y) for k in four]
        self.x_to_y = [make(from_x[k].at[first[k]], from_x[k].at[first[k]], over_y) for k in four]
        self.y_to_x = [make(from_y[k].at[second[k]], from_y[k].at[second[k]], over_x) for k in four]
        self.pair = [make(held[k], own[k], beside) for k in four]
        self.pair_x = [make(s, s, beside) for s in from_x]
        self.pair_y = [make(s, s, beside) for s in from_y]
        self.pair_across = [make(s, s, beside) for s in across]

    def start(self):
        for k in range(4):
            self.to_x[k].start()
            self.to_y[k].start()
        for k in range(4):
            self.pair[k].start()
            self.local[k].start()

    def pass_across(self, k):
        self.to_x[k].wait_recv()
        self.x_to_y[k].start()
        self.pair_x[k].start()
        self.to_y[k].wait_recv()
        self.y_to_x[k].start()
        self.pair_y[k].start()

    def pass_pair(self, k):
        self.x_to_y[k].wait_recv()
        self.y_to_x[k].wait_recv()
        self.pair_across[k].start()

    def finish(self):
        for copy in self.local:
            copy.wait()
        for copy in self.pair + self.pair_x + self.pair_y + self.pair_across:
            copy.wait_recv()
        for copy in self.copies.made:
            copy.wait_send()


SCATTER_COPIES = 24


class Corner:
    def __init__(self, place, parts, across, copies):
        x, y, zs = place.x, place.y, place.zs
        a, b = pl.ds(0, UPPER), pl.ds(UPPER, SHARD - UPPER)
        over_x, over_y = place.device(x=1 - x), place.device(y=1 - y)
        self.over_y, self.over_x = [], []
        for k in range(4):
            block = parts.at[1 - y, zs[k], 1 - x]
            self.over_y.append(copies.make(block.at[a], across.at[k, a], over_y))
            self.over_x.append(copies.make(block.at[b], across.at[k, b], over_x))

    def start(self, k):
        self.over_y[k].start()
        self.over_x[k].start()


class Scatter:
    def __init__(self, place, parts, bufs, column, send_sems, recv_sems, early=None):
        x, y, zs = place.x, place.y, place.zs
        self.place, self.parts, self.column = place, parts, column
        self.across, self.from_x, self.from_y = [bufs.at[k] for k in range(3)]
        self.early = early
        self.copies = Copies(send_sems, recv_sems)
        make = self.copies.make
        self.upper, self.lower = (0, UPPER), (UPPER, SHARD - UPPER)
        a, b = pl.ds(*self.upper), pl.ds(*self.lower)
        over_x, over_y = place.device(x=1 - x), place.device(y=1 - y)
        four = range(4)
        if early is None:
            self.corner = Corner(place, parts, self.across, self.copies)
        self.x_lower = [make(parts.at[y, zs[k], 1 - x, b], self.from_x.at[k, b], over_x) for k in four]
        self.y_upper = [make(parts.at[1 - y, zs[k], x, a], self.from_y.at[k, a], over_y) for k in four]
        self.x_upper = [make(self.across.at[k, a], self.from_x.at[k, a], over_x) for k in four]
        self.y_lower = [make(self.across.at[k, b], self.from_y.at[k, b], over_y) for k in four]

    def start(self, k):
        self.corner.start(k)

    def follow(self, k):
        self.x_lower[k].start()
        self.y_upper[k].start()

    def add(self, k, index, rows):
        given = self.across if self.early is None else self.early
        for at in range(0, rows[1], 16):
            here = pl.ds(rows[0] + at, 16)
            total = self.parts[(*index, here)].astype(F32) + given[k, here].astype(F32)
            self.across[k, here] = total.astype(BF16)

    def pass_across(self, k):
        x, y, z = self.place.x, self.place.y, self.place.zs[k]
        if self.early is None:
            self.corner.over_y[k].wait_recv()
        self.add(k, (y, z, 1 - x), self.upper)
        self.x_upper[k].start()
        if self.early is None:
            self.corner.over_x[k].wait_recv()
        self.add(k, (1 - y, z, x), self.lower)
        self.y_lower[k].start()

    def collect(self, k):
        x, y, z = self.place.x, self.place.y, self.place.zs[k]
        for copy in (self.x_upper[k], self.x_lower[k], self.y_upper[k], self.y_lower[k]):
            copy.wait_recv()
        for at in range(0, SHARD, 16):
            here = pl.ds(at, 16)
            total = self.parts[y, z, x, here].astype(F32) + self.from_x[k, here].astype(F32)
            self.column[k, here] = (total + self.from_y[k, here].astype(F32)).astype(BF16)

    def finish(self):
        for copy in self.copies.made:
            copy.wait_send()


class Along:
    def __init__(self, place, column, from_z, out, send_sems, recv_sems):
        copies = Copies(send_sems, recv_sems)
        self.column, self.from_z, self.out = column, from_z, out
        self.copies = [
            copies.make(column.at[k], from_z.at[k - 1], place.device(z=place.zs[k])) for k in (1, 2, 3)
        ]

    def start(self, k):
        self.copies[k - 1].start()

    def close(self):
        for copy in self.copies:
            copy.wait()
        for at in range(0, SHARD, 16):
            here = pl.ds(at, 16)
            total = self.column[0, here].astype(F32)
            for k in range(3):
                total = total + self.from_z[k, here].astype(F32)
            self.out[here] = total


ORDER = (1, 2, 3, 0)
DMA = pltpu.SemaphoreType.DMA


def add_rows(target, rows, left, right):
    def body(i, carry):
        here = pl.ds(pl.multiple_of(16 * i, 16), 16)
        target(here, (left(here).astype(F32) + right(here).astype(F32)).astype(BF16))
        return carry

    lax.fori_loop(0, rows // 16, body, 0)


class Pair:
    def __init__(self, place, buffers, parts, send_sems, recv_sems):
        self.place, self.buffers, self.parts = place, buffers, parts
        self.send_sems, self.recv_sems = send_sems, recv_sems

    def copy(self, m):
        y = lax.div(m, 2)
        return pltpu.make_async_remote_copy(
            src_ref=self.buffers.at[lax.rem(m, 2)],
            dst_ref=self.parts.at[y],
            send_sem=self.send_sems.at[y],
            recv_sem=self.recv_sems.at[y],
            device_id=self.place.mates[0],
            device_id_type=MESH,
        )

    def send(self, m):
        @pl.when(lax.rem(m, 2) != self.place.c)
        def _():
            self.copy(m).start()

    def free(self, m):
        @pl.when(lax.rem(m, 2) != self.place.c)
        def _():
            self.copy(m).wait_send()

    def take(self, m):
        @pl.when(lax.rem(m, 2) == self.place.c)
        def _():
            y, buffer = lax.div(m, 2), lax.rem(m, 2)
            self.copy(m).wait_recv()

            def store(here, value):
                self.parts[y, here] = value

            add_rows(
                store, D, lambda here: self.buffers[buffer, here], lambda here: self.parts[y, here]
            )


def attend_kernel(
    x_ref, weight_in, mods_ref, qkv_bias_ref, out_bias_ref, column_ref, row_ref, slot_ref,
    groups_ref, mask_ref, up_ref, down_ref,
    first_out, heads_out, mixed_out, lse_ref, attn_ref, after_ref, arrived_ref, picked_ref, weight_out,
    up_out, down_out,
    weight_ref, first_ref, heads_ref, mixed_ref, out_weight_ref, load_sems, save_sems,
    bias_ref, parts_ref, second_ref,
    send_sems, recv_sems, local_sems, down_send, down_recv, down_local,
):
    place = Place()
    place.meet()
    ups = Spread(
        place, up_ref, lambda y, c, z, x: up_out.at[y, c, z, x], send_sems, recv_sems, local_sems
    )
    downs = Column(place, down_ref, down_out, down_send, down_recv, down_local.at[0])
    loads = [
        pltpu.make_async_copy(weight_in.at[j], weight_ref.at[j], load_sems.at[j]) for j in range(4)
    ]
    saves = [
        pltpu.make_async_copy(source, target, save_sems.at[n])
        for n, (source, target) in enumerate(
            (
                (first_ref, first_out),
                (heads_ref, heads_out),
                (out_weight_ref, weight_out),
                (mixed_ref, mixed_out),
            )
        )
    ]
    ups.start()
    for copy in loads:
        copy.start()
    downs.start()
    crop_mask(bias_ref, column_ref, row_ref)

    def norm(i, carry):
        here = rows_at(i)
        segment = column_ref[here, :]
        normed, _ = normalise(x_ref[here, :].astype(F32))
        shift, scale = per_crop(mods_ref[0], segment), per_crop(mods_ref[1], segment)
        first_ref[here, :] = (normed * (1.0 + scale) + shift).astype(BF16)
        return carry

    lax.fori_loop(0, 3, norm, 0)
    saves[0].start()
    for copy in loads:
        copy.wait()
    for j in range(4):
        out_weight_ref[:, OUT_SHARD * j : OUT_SHARD * (j + 1)] = weight_ref[j, :, QKV_SHARD:]
    saves[2].start()

    def project(i, carry):
        j = lax.div(i, 3)
        here = rows_at(lax.rem(i, 3))
        triple = (dot(first_ref[here, :], weight_ref[j, :, :PAD_SHARD]) + qkv_bias_ref[j]).astype(BF16)
        zero = jnp.zeros((BLOCK, 128 - HEAD_DIM), BF16)
        for h in range(12):
            part = triple[:, HEAD_DIM * h : HEAD_DIM * (h + 1)]
            heads_ref[12 * j + h, here, :] = jnp.concatenate([part, zero], axis=1)
        return carry

    lax.fori_loop(0, 12, project, 0)
    saves[1].start()

    def head(h, carry):
        for k in range(4):

            @pl.when(h == 7 + k)
            def _():
                ups.pass_across(k)

        keys, values = heads_ref[16 + h], heads_ref[32 + h]
        for i in range(3):
            here = pl.ds(i * BLOCK, BLOCK)
            scores = dot(heads_ref[h, here, :], keys, NT) * SOFT + bias_ref[here, :]
            top = jnp.max(scores, axis=1, keepdims=True)
            weights = jnp.exp2(scores - top)
            total = jnp.sum(weights, axis=1, keepdims=True)
            keep = head_keep(mask_ref, h, column_ref[here, :])
            parts_ref[h, here, :] = (dot(weights.astype(BF16), values) * (keep / total)).astype(BF16)
            spread = jnp.broadcast_to(top + jnp.log2(total), (BLOCK, 128))
            lse_ref[h, :, here] = jnp.transpose(spread)[:1, :]
        return carry

    lax.fori_loop(0, HEADS, head, 0)
    for h in range(HEADS):
        mixed_ref[:, HEAD_DIM * h : HEAD_DIM * (h + 1)] = parts_ref[h][:, :HEAD_DIM]
    saves[3].start()
    for k in range(4):
        ups.pass_pair(k)

    def close(i, carry):
        here = rows_at(i)
        segment = column_ref[here, :]
        attn = dot(mixed_ref[here, :], out_weight_ref[...]) + out_bias_ref[...]
        attn_ref[here, :] = attn.astype(BF16)
        after = x_ref[here, :].astype(F32) + per_crop(mods_ref[2], segment) * attn
        after_ref[here, :] = after
        normed, _ = normalise(after)
        shift, scale = per_crop(mods_ref[3], segment), per_crop(mods_ref[4], segment)
        second_ref[here, :] = (normed * (1.0 + scale) + shift).astype(BF16)
        return carry

    lax.fori_loop(0, 3, close, 0)
    for i in range(2):
        here = pl.ds(i * BLOCK, BLOCK)
        choice = places_of(slot_ref[...], i)
        arrived_ref[here, :] = dot(choice, second_ref[...]).astype(BF16)
        picked_ref[here, :] = dot(choice, groups_ref[...]).astype(BF16)
    ups.finish()
    downs.finish()
    for copy in saves:
        copy.wait()


def shape_of(*shape, dtype=BF16):
    return jax.ShapeDtypeStruct(shape, dtype)


def talking(number):
    return pltpu.CompilerParams(
        collective_id=number, has_side_effects=True, vmem_limit_bytes=VMEM_BYTES
    )


IN_VMEM = pl.BlockSpec(memory_space=pltpu.VMEM)
IN_SMEM = pl.BlockSpec(memory_space=pltpu.SMEM)
ANYWHERE = pl.BlockSpec(memory_space=pl.ANY)


def attend(x, weight, mods, qkv_bias, out_bias, column, row, slot_row, groups, mask, up, down):
    return pl.pallas_call(
        attend_kernel,
        out_shape=[
            shape_of(TOK_DEV, D),
            shape_of(3 * HEADS, TOK_DEV, 128),
            shape_of(TOK_DEV, D),
            shape_of(HEADS, 1, TOK_DEV, dtype=F32),
            shape_of(TOK_DEV, D),
            shape_of(TOK_DEV, D, dtype=F32),
            shape_of(PLACES, D),
            shape_of(PLACES, 128),
            shape_of(D, D),
            shape_of(2, 2, 4, 2, SHARD, D),
            shape_of(4, SHARD, D),
        ],
        in_specs=[IN_VMEM, ANYWHERE] + [IN_VMEM] * 7 + [IN_SMEM] + [ANYWHERE] * 2,
        out_specs=[ANYWHERE] * 3 + [IN_VMEM] * 5 + [ANYWHERE] * 3,
        scratch_shapes=[
            pltpu.VMEM((4, D, D), BF16),
            pltpu.VMEM((TOK_DEV, D), BF16),
            pltpu.VMEM((3 * HEADS, TOK_DEV, 128), BF16),
            pltpu.VMEM((TOK_DEV, D), BF16),
            pltpu.VMEM((D, D), BF16),
            DMA((4,)),
            DMA((4,)),
            pltpu.VMEM((TOK_DEV, TOK_DEV), F32),
            pltpu.VMEM((HEADS, TOK_DEV, 128), BF16),
            pltpu.VMEM((TOK_DEV, D), BF16),
            DMA((SPREAD_COPIES,)),
            DMA((SPREAD_COPIES,)),
            DMA((4,)),
            DMA((3,)),
            DMA((3,)),
            DMA((1,)),
        ],
        compiler_params=talking(2),
    )(x, weight, mods, qkv_bias, out_bias, column, row, slot_row, groups, mask, up, down)


ROOT = math.sqrt(2.0 / math.pi)


def feed_kernel(
    up_ref, arrived_ref, picked_ref, up_bias_ref, down_bias_ref, cot_ref, after_ref,
    mods_ref, column_ref, slot_column_ref, slot_row_ref, down_ref,
    pull_ref, grad_rows_ref, block_out_ref, gate_ref, bias_ref, parts_ref, down_out, across_out,
    active_ref, total_ref, branch_ref, buffers_ref, halves_ref, tiles_ref, across_ref,
    send_sems, recv_sems, local_sems, pair_send, pair_recv, tile_sems, corner_send, corner_recv,
):
    step = pl.program_id(0)
    place = Place()
    downs = Spread(
        place, down_ref, lambda y, c, z, x: down_out.at[z, x, y, c], send_sems, recv_sems, local_sems
    )

    corners = Copies(corner_send, corner_recv)
    corner = Corner(place, parts_ref, across_ref, corners)

    def rows_of(x, y, c):
        return pl.ds(pl.multiple_of((4 * x + 2 * y + c) * SHARD, 16), SHARD)

    def pair(m, x, y):
        return pltpu.make_async_remote_copy(
            src_ref=buffers_ref.at[lax.rem(m, 2), rows_of(x, y, 1 - place.c)],
            dst_ref=halves_ref.at[y, m, x],
            send_sem=pair_send.at[m, x, y],
            recv_sem=pair_recv.at[m, x, y],
            device_id=place.mates[0],
            device_id_type=MESH,
        )

    def take(m):
        for x in range(2):
            for y in range(2):
                pair(m, x, y).wait_recv()
                own = rows_of(x, y, place.c)
                mine = buffers_ref.at[lax.rem(m, 2), own]
                for at in range(0, SHARD, 16):
                    here = pl.ds(at, 16)
                    total = mine[here].astype(F32) + halves_ref[y, m, x, here].astype(F32)
                    parts_ref[y, m, x, here] = total.astype(BF16)

    def free(m):
        for x in range(2):
            for y in range(2):
                pair(m, x, y).wait_send()

    def tile(m):
        return [
            pltpu.make_async_copy(
                down_out.at[m, x, y],
                tiles_ref.at[lax.rem(m, 2), x, y],
                tile_sems.at[lax.rem(m, 2), x, y],
            )
            for x in range(2)
            for y in range(2)
        ]

    @pl.when(step == 0)
    def _():
        place.meet()
        downs.start()
        for i in range(3):
            here = pl.ds(i * BLOCK, BLOCK)
            gate = per_crop(mods_ref[5], column_ref[here, :])
            block_out_ref[here, :] = (gate * cot_ref[here, :].astype(F32)).astype(BF16)
        for i in range(2):
            here = pl.ds(i * BLOCK, BLOCK)
            choice = places_of(slot_row_ref[...], i)
            grad_rows_ref[here, :] = dot(choice, block_out_ref[...]).astype(BF16)
        bias_ref[...] = jnp.sum(grad_rows_ref[...].astype(F32), axis=0, keepdims=True)
        total_ref[...] = jnp.zeros_like(total_ref)

    @pl.when(step < 4)
    def _():
        group = lax.broadcasted_iota(jnp.int32, (128, D), 0) - 4 * step
        unit = lax.broadcasted_iota(jnp.int32, (128, D), 1)
        width = FF // GROUPS
        spread = ((unit >= group * width) & (unit < (group + 1) * width)).astype(BF16)
        for i in range(2):
            here = pl.ds(i * BLOCK, BLOCK)
            hidden = dot(arrived_ref[here, :], up_ref[0]) + up_bias_ref[0]
            keep = dot(picked_ref[here, :], spread)
            square = hidden * hidden
            curve = jnp.tanh(ROOT * hidden * (1.0 + 0.044715 * square))
            half = 0.5 * (1.0 + curve)
            slope = half + 0.5 * hidden * (1.0 - curve * curve) * (
                ROOT * (1.0 + 3.0 * 0.044715 * square)
            )
            active_ref[step, here, :] = (hidden * half * keep).astype(BF16)
            pull_ref[0, here, :] = (slope * keep).astype(BF16)

        def grad(i, carry):
            here = pl.ds(pl.multiple_of(i * 384, 384), 384)
            part = dot(active_ref[step, :, here], grad_rows_ref[...], TN).astype(BF16)
            buffers_ref[lax.rem(step, 2), here, :] = part
            return carry

        @pl.when(step >= 2)
        def _():
            free(step - 2)

        lax.fori_loop(0, 3, grad, 0)
        for x in range(2):
            for y in range(2):
                pair(step, x, y).start()

    @pl.when((step >= 1) & (step < 5))
    def _():
        take(step - 1)

    @pl.when(step == 3)
    def _():
        for k in range(4):
            downs.pass_across(k)

    @pl.when(step == 4)
    def _():
        free(2)
        free(3)
        for k in range(4):
            corner.start(k)
        for k in range(4):
            downs.pass_pair(k)
        downs.finish()
        for m in (0, 1):
            for copy in tile(m):
                copy.start()

    @pl.when(step >= 4)
    def _():
        m = step - 4
        for copy in tile(m):
            copy.wait()
        weights = tiles_ref[lax.rem(m, 2)].reshape(D, D)
        for i in range(2):
            here = pl.ds(i * BLOCK, BLOCK)
            total_ref[here, :] += dot(active_ref[m, here, :], weights)

        @pl.when(m < 2)
        def _():
            for copy in tile(m + 2):
                copy.start()

    @pl.when(step == 7)
    def _():
        branch_ref[...] = (total_ref[...] + down_bias_ref[...]).astype(BF16)
        gates = jnp.zeros((8, D), F32)
        for i in range(3):
            here = pl.ds(i * BLOCK, BLOCK)
            segment = column_ref[here, :]
            branch = dot(tokens_of(slot_column_ref[here, :]), branch_ref[...])
            gate = per_crop(mods_ref[5], segment)
            block_out_ref[here, :] = (after_ref[here, :] + gate * branch).astype(BF16)
            gates = gates + crop_sums(segment, cot_ref[here, :].astype(F32) * branch)
        gate_ref[...] = gates
        for copy in corners.made:
            copy.wait()
        leave = pltpu.make_async_copy(across_ref, across_out, local_sems.at[0])
        leave.start()
        leave.wait()


def whole(*shape):
    return pl.BlockSpec(shape, lambda i: (0,) * len(shape), pipeline_mode=pl.Buffered(1))


def feed(up, arrived, picked, up_bias, down_bias, cot, after, mods, column, slot_column, slot_row, down):
    early = lambda *tail: pl.BlockSpec((1, *tail), lambda i: (jnp.minimum(i, 3), 0, 0))
    return pl.pallas_call(
        feed_kernel,
        grid=(8,),
        out_shape=[
            shape_of(4, PLACES, D),
            shape_of(PLACES, D),
            shape_of(TOK_DEV, D),
            shape_of(8, D, dtype=F32),
            shape_of(1, D, dtype=F32),
            shape_of(2, 4, 2, SHARD, D),
            shape_of(4, 2, 2, 2, SHARD, D),
            shape_of(4, SHARD, D),
        ],
        in_specs=[
            early(D, D), whole(PLACES, D), whole(PLACES, 128), early(1, D), whole(1, D),
            whole(TOK_DEV, D), whole(TOK_DEV, D), whole(6, 8, D), whole(TOK_DEV, 1), whole(TOK_DEV, 1),
            whole(1, TOK_DEV), ANYWHERE,
        ],
        out_specs=[
            early(PLACES, D), whole(PLACES, D), whole(TOK_DEV, D), whole(8, D), whole(1, D),
            whole(2, 4, 2, SHARD, D), ANYWHERE, ANYWHERE,
        ],
        scratch_shapes=[
            pltpu.VMEM((4, PLACES, D), BF16),
            pltpu.VMEM((PLACES, D), F32),
            pltpu.VMEM((PLACES, D), BF16),
            pltpu.VMEM((2, D, D), BF16),
            pltpu.VMEM((2, 4, 2, SHARD, D), BF16),
            pltpu.VMEM((2, 2, 2, 2, SHARD, D), BF16),
            pltpu.VMEM((4, SHARD, D), BF16),
            DMA((SPREAD_COPIES,)),
            DMA((SPREAD_COPIES,)),
            DMA((4,)),
            DMA((4, 2, 2)),
            DMA((4, 2, 2)),
            DMA((2, 2, 2)),
            DMA((8,)),
            DMA((8,)),
        ],
        compiler_params=talking(3),
    )(up, arrived, picked, up_bias, down_bias, cot, after, mods, column, slot_column, slot_row, down)


def unfeed_kernel(
    down_ref, up_ref, pull_ref, grad_rows_ref, arrived_ref, after_ref, cot_ref, attn_ref, mods_ref,
    column_ref, slot_column_ref, given_ref, early_ref,
    up_bias_ref, mid_ref, grad_attn_ref, sums_ref, out_bias_ref, parts_out, plane_ref,
    hidden_ref, total_ref, back_ref, buffers_ref, parts_ref, bufs_ref,
    send_sems, recv_sems, pair_send, pair_recv, out_sem,
):
    step = pl.program_id(0)
    place = Place()
    scatter = Scatter(place, given_ref, bufs_ref, plane_ref, send_sems, recv_sems, early_ref)
    pair = Pair(place, buffers_ref, parts_ref, pair_send, pair_recv)

    @pl.when(step == 0)
    def _():
        place.meet()
        for k in ORDER:
            scatter.follow(k)
            scatter.pass_across(k)
        total_ref[...] = jnp.zeros_like(total_ref)

    bias = jnp.zeros((1, D), F32)
    for i in range(2):
        here = pl.ds(i * BLOCK, BLOCK)
        grad = dot(grad_rows_ref[here, :], down_ref[0], NT) * pull_ref[0, here, :].astype(F32)
        low = grad.astype(BF16)
        hidden_ref[here, :] = low
        bias = bias + jnp.sum(low.astype(F32), axis=0, keepdims=True)
        total_ref[here, :] += dot(low, up_ref[0], NT)
    up_bias_ref[0] = bias

    def grad_of(i, carry):
        here = pl.ds(pl.multiple_of(i * 384, 384), 384)
        part = dot(arrived_ref[:, here], hidden_ref[...], TN).astype(BF16)
        buffers_ref[lax.rem(step, 2), here, :] = part
        return carry

    @pl.when(step >= 2)
    def _():
        pair.free(step - 2)

    lax.fori_loop(0, 3, grad_of, 0)
    pair.send(step)

    @pl.when(step >= 1)
    def _():
        pair.take(step - 1)

    @pl.when(step == 3)
    def _():
        back_ref[...] = total_ref[...].astype(BF16)
        shifts, scales = jnp.zeros((8, D), F32), jnp.zeros((8, D), F32)
        gates, out_bias = jnp.zeros((8, D), F32), jnp.zeros((1, D), F32)
        for i in range(3):
            here = pl.ds(i * BLOCK, BLOCK)
            segment = column_ref[here, :]
            second = dot(tokens_of(slot_column_ref[here, :]), back_ref[...])
            normed, inverse = normalise(after_ref[here, :])
            grad = second * (1.0 + per_crop(mods_ref[4], segment))
            mean = jnp.mean(grad, axis=1, keepdims=True)
            slant = jnp.mean(grad * normed, axis=1, keepdims=True)
            mid = cot_ref[here, :].astype(F32) + inverse * (grad - mean - normed * slant)
            mid_ref[here, :] = mid
            low = (per_crop(mods_ref[2], segment) * mid).astype(BF16)
            grad_attn_ref[here, :] = low
            out_bias = out_bias + jnp.sum(low.astype(F32), axis=0, keepdims=True)
            shifts = shifts + crop_sums(segment, second)
            scales = scales + crop_sums(segment, second * normed)
            gates = gates + crop_sums(segment, mid * attn_ref[here, :].astype(F32))
        sums_ref[0], sums_ref[1], sums_ref[2] = gates, shifts, scales
        out_bias_ref[...] = out_bias
        pair.free(2)
        pair.free(3)
        pair.take(3)
        leave = pltpu.make_async_copy(parts_ref, parts_out, out_sem.at[0])
        leave.start()
        for k in ORDER:
            scatter.collect(k)
        scatter.finish()
        leave.wait()


def unfeed(down, up, pull, grad_rows, arrived, after, cot, attn, mods, column, slot_column, given, early):
    block = lambda *tail: pl.BlockSpec((1, *tail), lambda i: (i, 0, 0))
    return pl.pallas_call(
        unfeed_kernel,
        grid=(4,),
        out_shape=[
            shape_of(4, 1, D, dtype=F32),
            shape_of(TOK_DEV, D, dtype=F32),
            shape_of(TOK_DEV, D),
            shape_of(3, 8, D, dtype=F32),
            shape_of(1, D, dtype=F32),
            shape_of(2, D, D),
            shape_of(4, SHARD, D),
        ],
        in_specs=[
            block(D, D), block(D, D), block(PLACES, D), whole(PLACES, D), whole(PLACES, D),
            whole(TOK_DEV, D), whole(TOK_DEV, D), whole(TOK_DEV, D), whole(6, 8, D), whole(TOK_DEV, 1),
            whole(TOK_DEV, 1), whole(2, 4, 2, SHARD, D), whole(4, SHARD, D),
        ],
        out_specs=[
            block(1, D), whole(TOK_DEV, D), whole(TOK_DEV, D), whole(3, 8, D), whole(1, D), ANYWHERE, whole(4, SHARD, D),
        ],
        scratch_shapes=[
            pltpu.VMEM((PLACES, D), BF16),
            pltpu.VMEM((PLACES, D), F32),
            pltpu.VMEM((PLACES, D), BF16),
            pltpu.VMEM((2, D, D), BF16),
            pltpu.VMEM((2, D, D), BF16),
            pltpu.VMEM((3, 4, SHARD, D), BF16),
            DMA((SCATTER_COPIES,)),
            DMA((SCATTER_COPIES,)),
            DMA((2,)),
            DMA((2,)),
            DMA((1,)),
        ],
        compiler_params=talking(4),
    )(down, up, pull, grad_rows, arrived, after, cot, attn, mods, column, slot_column, given, early)


def unattend_kernel(
    grad_ref, weight_in, heads_in, lse_ref, column_ref, row_ref, given_in, plane_ref, mask_ref,
    triple_ref, sums_ref, share_ref, plane_out, split_out,
    out_weight_ref, heads_ref, given_ref, split_ref, load_sems,
    bias_ref, mixed_ref, grads_ref, key_ref, value_ref, bufs_ref, from_z_ref,
    send_sems, recv_sems, along_send, along_recv,
):
    place = Place()
    place.meet()
    scatter = Scatter(place, given_ref, bufs_ref, plane_out, send_sems, recv_sems)
    along = Along(place, plane_ref, from_z_ref, share_ref, along_send, along_recv)
    loads = [
        pltpu.make_async_copy(source, target, load_sems.at[n])
        for n, (source, target) in enumerate(
            ((given_in, given_ref), (weight_in, out_weight_ref), (heads_in, heads_ref))
        )
    ]
    save = pltpu.make_async_copy(split_ref, split_out, load_sems.at[3])
    for copy in loads:
        copy.start()
    for k in (1, 2, 3):
        along.start(k)
    for j in range(4):
        split_ref[j] = grad_ref[:, OUT_SHARD * j : OUT_SHARD * (j + 1)]
    save.start()
    loads[0].wait()
    for k in ORDER:
        scatter.start(k)
    loads[1].wait()
    crop_mask(bias_ref, column_ref, row_ref)

    def spread(i, carry):
        here = rows_at(i)
        segment = column_ref[here, :]
        mixed = dot(grad_ref[here, :], out_weight_ref[...], NT)
        zero = jnp.zeros((BLOCK, 128 - HEAD_DIM), BF16)
        for h in range(HEADS):
            part = mixed[:, HEAD_DIM * h : HEAD_DIM * (h + 1)] * head_keep(mask_ref, h, segment)
            mixed_ref[h, here, :] = jnp.concatenate([part.astype(BF16), zero], axis=1)
        return carry

    lax.fori_loop(0, 3, spread, 0)
    factor = HEAD_DIM**-0.5
    loads[2].wait()

    def head(h, carry):
        @pl.when(h == 1)
        def _():
            for k in ORDER:
                scatter.follow(k)

        for at, k in enumerate(ORDER):

            @pl.when(h == 4 + at)
            def _():
                scatter.pass_across(k)

        keys, values = heads_ref[16 + h], heads_ref[32 + h]
        turned = jnp.transpose(keys)
        for i in range(3):
            here = pl.ds(i * BLOCK, BLOCK)
            queries, grads = heads_ref[h, here, :], mixed_ref[h, here, :]
            scores = dot(keys, queries, NT) * SOFT + bias_ref[:, here]
            probs = jnp.exp2(scores - lse_ref[h, :, here])
            product = probs * dot(values, grads, NT)
            total = jnp.sum(product, axis=0, keepdims=True)
            low = (product - probs * total).astype(BF16)
            for_values, for_keys = dot(probs.astype(BF16), grads), dot(low, queries)
            if i == 0:
                value_ref[...], key_ref[...] = for_values, for_keys
            else:
                value_ref[...] += for_values
                key_ref[...] += for_keys
            grads_ref[h, here, :] = jnp.transpose(dot(turned, low) * factor).astype(BF16)
        grads_ref[16 + h] = (key_ref[...] * factor).astype(BF16)
        grads_ref[32 + h] = value_ref[...].astype(BF16)
        return carry

    lax.fori_loop(0, HEADS, head, 0)
    for j in range(4):
        triple_ref[j, :, QKV_SHARD:] = jnp.zeros((TOK_DEV, PAD_SHARD - QKV_SHARD), BF16)
        for h in range(12):
            triple_ref[j, :, HEAD_DIM * h : HEAD_DIM * (h + 1)] = grads_ref[12 * j + h][:, :HEAD_DIM]
        sums_ref[j] = jnp.sum(triple_ref[j].astype(F32), axis=0, keepdims=True)
    save.wait()
    along.close()
    for k in ORDER:
        scatter.collect(k)
    scatter.finish()


def unattend(grad_attn, out_weight, heads, lse, column, row, given, plane, mask):
    return pl.pallas_call(
        unattend_kernel,
        out_shape=[
            shape_of(4, TOK_DEV, PAD_SHARD),
            shape_of(4, 1, PAD_SHARD, dtype=F32),
            shape_of(SHARD, D, dtype=F32),
            shape_of(4, SHARD, D),
            shape_of(4, TOK_DEV, OUT_SHARD),
        ],
        in_specs=[IN_VMEM] + [ANYWHERE] * 2 + [IN_VMEM] * 3 + [ANYWHERE, IN_VMEM, IN_SMEM],
        out_specs=[IN_VMEM] * 4 + [ANYWHERE],
        scratch_shapes=[
            pltpu.VMEM((D, D), BF16),
            pltpu.VMEM((3 * HEADS, TOK_DEV, 128), BF16),
            pltpu.VMEM((2, 4, 2, SHARD, D), BF16),
            pltpu.VMEM((4, TOK_DEV, OUT_SHARD), BF16),
            DMA((4,)),
            pltpu.VMEM((TOK_DEV, TOK_DEV), F32),
            pltpu.VMEM((HEADS, TOK_DEV, 128), BF16),
            pltpu.VMEM((3 * HEADS, TOK_DEV, 128), BF16),
            pltpu.VMEM((TOK_DEV, 128), F32),
            pltpu.VMEM((TOK_DEV, 128), F32),
            pltpu.VMEM((3, 4, SHARD, D), BF16),
            pltpu.VMEM((3, SHARD, D), BF16),
            DMA((SCATTER_COPIES,)),
            DMA((SCATTER_COPIES,)),
            DMA((3,)),
            DMA((3,)),
        ],
        compiler_params=talking(5),
    )(grad_attn, out_weight, heads, lse, column, row, given, plane, mask)


def unproject_kernel(
    weight_ref, triple_ref, split_ref, first_ref, mixed_ref, x_ref, mid_ref, mods_ref, column_ref,
    plane_up_ref, rest_ref, conds_ref, down_ref,
    grad_in_ref, share_up_ref, qkv_ref, out_ref, ada_ref, sums_ref, share_down_ref,
    share_ref, turn_ref, turned_ref, total_ref, buffers_ref, parts_ref, bufs_ref, plane_ref, up_z_ref, from_z_ref,
    mod_ref, mates_ref, rows_ref, packed_ref, every_ref,
    send_sems, recv_sems, pair_send, pair_recv, up_send, up_recv, along_send, along_recv,
    small_send, small_recv,
):
    step = pl.program_id(0)
    place = Place()

    def block_at(step):
        return lax.rem(step + 2 * (1 - place.y), 4)

    pair = Pair(place, buffers_ref, parts_ref, pair_send, pair_recv)
    blocks = parts_ref.reshape(2, 4, 2, SHARD, D)
    scatter = Scatter(place, blocks, bufs_ref, plane_ref, send_sems, recv_sems)
    along_up = Along(place, plane_up_ref, up_z_ref, share_up_ref, up_send, up_recv)
    along = Along(place, plane_ref, from_z_ref, share_ref, along_send, along_recv)
    small = Copies(small_send, small_recv)
    to_mates = [
        small.make(mod_ref.at[other], mates_ref.at[place.index], mate)
        for other, mate in zip(place.mate_index, place.mates)
    ]
    to_peers = []
    for k in range(4):
        for there in (place.x, 1 - place.x) if k else (1 - place.x,):
            other = place.device(z=place.zs[k], x=there)
            to_peers.append(small.make(packed_ref, every_ref.at[place.peer], other))
    swaps = [
        small.make(turn_ref.at[other], turned_ref.at[place.index], mate)
        for other, mate in zip(place.mate_index, place.mates)
    ]
    @pl.when(step == 0)
    def _():
        place.meet()
        for k in (2, 3, 1):
            along_up.start(k)
        for j in range(4):
            turn_ref[j] = down_ref[:, OUT_SHARD * j : OUT_SHARD * (j + 1)]
        for copy in swaps:
            copy.start()
        turned_ref[place.index] = turn_ref[place.index]

    @pl.when(step < 4)
    def _():
        def grad(i, carry):
            here = pl.ds(pl.multiple_of(i * 384, 384), 384)
            buffer = lax.rem(step, 2)
            part = dot(first_ref[:, here], triple_ref[block_at(step)], TN).astype(BF16)
            buffers_ref[buffer, here, :PAD_SHARD] = part
            part = dot(mixed_ref[:, here], split_ref[block_at(step)], TN).astype(BF16)
            buffers_ref[buffer, here, QKV_SHARD:] = part
            return carry

        @pl.when(step >= 2)
        def _():
            pair.free(block_at(step - 2))

        lax.fori_loop(0, 3, grad, 0)
        pair.send(block_at(step))

    @pl.when((step >= 1) & (step < 5))
    def _():
        pair.take(block_at(step - 1))

    @pl.when(step == 2)
    def _():
        for k in (2, 3):
            scatter.start(k)
            scatter.y_upper[k].start()

    @pl.when(step == 4)
    def _():
        pair.free(block_at(2))
        pair.free(block_at(3))
        scatter.x_lower[2].start()
        scatter.pass_across(2)
        scatter.x_lower[3].start()

    for at, now, then, last in ((4, None, None, 1), (5, 3, 1, 0), (6, 1, 0, None)):

        @pl.when(step == at)
        def _():
            if now is not None:
                scatter.pass_across(now)
                scatter.x_lower[then].start()
            if last is not None:
                scatter.start(last)
                scatter.y_upper[last].start()

    @pl.when(step >= 4)
    def _():
        for i in range(3):
            here = pl.ds(i * BLOCK, BLOCK)
            part = dot(triple_ref[step - 4, here, :], weight_ref[0, :, :PAD_SHARD], NT)
            total_ref[here, :] = jnp.where(step == 4, part, total_ref[here, :] + part)

    @pl.when(step == 7)
    def _():
        scatter.collect(2)
        along.start(2)
        scatter.pass_across(0)
        shifts, scales = jnp.zeros((8, D), F32), jnp.zeros((8, D), F32)
        for i in range(3):
            here = pl.ds(i * BLOCK, BLOCK)
            segment = column_ref[here, :]
            first = total_ref[here, :]
            normed, inverse = normalise(x_ref[here, :].astype(F32))
            grads = first * (1.0 + per_crop(mods_ref[1], segment))
            mean = jnp.mean(grads, axis=1, keepdims=True)
            slant = jnp.mean(grads * normed, axis=1, keepdims=True)
            grad_in_ref[here, :] = mid_ref[here, :] + inverse * (grads - mean - normed * slant)
            shifts = shifts + crop_sums(segment, first)
            scales = scales + crop_sums(segment, first * normed)
        mod_ref[...] = rest_ref[...]
        mod_ref[0, :CROPS, :D] = shifts[:CROPS]
        mod_ref[0, :CROPS, D:] = scales[:CROPS, : D // 2]
        mod_ref[1, :CROPS, : D // 2] = scales[:CROPS, D // 2 :]
        for copy in to_mates:
            copy.start()
        mates_ref[place.index] = mod_ref[place.index]
        scatter.collect(3)
        along.start(3)
        for copy in to_mates:
            copy.wait_recv()
        rows_ref[...] = jnp.zeros_like(rows_ref)
        for j in range(4):
            rows_ref[CROPS * j : CROPS * (j + 1), :] = mates_ref[j, :CROPS, :]
            rows_ref[12:14, :] += mates_ref[j, CROPS : CROPS + 2, :]
        packed_ref[...] = rows_ref[...].astype(BF16)
        for copy in to_peers:
            copy.start()
        every_ref[place.peer] = packed_ref[...]
        scatter.collect(1)
        along.start(1)
        along_up.close()
        for copy in swaps:
            copy.wait_recv()
        share_down_ref[...] = turned_ref[...]
        scatter.collect(0)
        for copy in to_peers:
            copy.wait_recv()
        close_ada(conds_ref, every_ref, ada_ref, sums_ref)
        along.close()
        qkv_ref[...] = share_ref[:, :QKV_SHARD]
        out_ref[...] = share_ref[:, QKV_SHARD:]
        scatter.finish()
        for copy in small.made:
            copy.wait_send()


def unproject(weight, triple, split, first, mixed, x, mid, mods, column, plane_up, rest, conds, down):
    block = lambda *tail: pl.BlockSpec((1, *tail), lambda i: (lax.rem(i, 4), 0, 0))
    early = lambda *tail: pl.BlockSpec((1, *tail), lambda i: (jnp.minimum(i, 3), 0, 0))
    late = lambda *tail: pl.BlockSpec((1, *tail), lambda i: (jnp.maximum(i - 4, 0), 0, 0))
    wide = rest.shape[2]
    vmem = pltpu.VMEM
    return pl.pallas_call(
        unproject_kernel,
        grid=(8,),
        out_shape=[
            shape_of(TOK_DEV, D, dtype=F32),
            shape_of(SHARD, D, dtype=F32),
            shape_of(SHARD, QKV_SHARD, dtype=F32),
            shape_of(SHARD, OUT_SHARD, dtype=F32),
            shape_of(SHARD, wide, dtype=F32),
            shape_of(8, wide, dtype=F32),
            shape_of(4, SHARD, OUT_SHARD, dtype=F32),
        ],
        in_specs=[
            late(D, D), whole(4, TOK_DEV, PAD_SHARD), whole(4, TOK_DEV, OUT_SHARD), whole(TOK_DEV, D),
            whole(TOK_DEV, D), whole(TOK_DEV, D), whole(TOK_DEV, D), whole(6, 8, D), whole(TOK_DEV, 1),
            whole(4, SHARD, D), whole(4, 8, wide), whole(8, 16, 256), whole(SHARD, D),
        ],
        out_specs=[
            whole(TOK_DEV, D), whole(SHARD, D), whole(SHARD, QKV_SHARD), whole(SHARD, OUT_SHARD),
            whole(SHARD, wide), whole(8, wide), whole(4, SHARD, OUT_SHARD),
        ],
        scratch_shapes=[
            vmem((SHARD, D), F32),
            vmem((4, SHARD, OUT_SHARD), F32),
            vmem((4, SHARD, OUT_SHARD), F32),
            vmem((TOK_DEV, D), F32),
            vmem((2, D, D), BF16),
            vmem((2, D, D), BF16),
            vmem((3, 4, SHARD, D), BF16),
            vmem((4, SHARD, D), BF16),
            vmem((3, SHARD, D), BF16),
            vmem((3, SHARD, D), BF16),
            vmem((4, 8, wide), F32),
            vmem((4, 8, wide), F32),
            vmem((16, wide), F32),
            vmem((16, wide), BF16),
            vmem((8, 16, wide), BF16),
            DMA((SCATTER_COPIES,)),
            DMA((SCATTER_COPIES,)),
            DMA((2,)),
            DMA((2,)),
            DMA((3,)),
            DMA((3,)),
            DMA((3,)),
            DMA((3,)),
            DMA((13,)),
            DMA((13,)),
        ],
        compiler_params=talking(6),
    )(weight, triple, split, first, mixed, x, mid, mods, column, plane_up, rest, conds, down)


CROPS = 3


def gather_kernel(
    qkv_ref, out_ref, up_ref, down_ref, cond_ref, ada_ref, vectors_ref, slot_ref, groups_ref, lengths_ref,
    mixed_out, up_out, down_out, mods_ref, conds_ref, qkv_bias_ref, up_bias_ref, out_bias_ref,
    down_bias_ref, column_ref, row_ref, slot_column_ref, token_groups_ref,
    send_sems, recv_sems, local_sem, up_send, up_recv, up_local, small_send, small_recv, local_small,
    mixed_ref, stage_ref, own_small, all_small, crop_rows, own_crops, all_crops, ada_parts, ada_all,
    product_ref, columns_ref, total_ref, rows_ref, tables_ref,
    query_ref, value_ref,
):
    place = Place()
    place.meet()
    x, zs = place.x, place.zs
    mixed_ref[:, :QKV_SHARD] = qkv_ref[...]
    mixed_ref[:, QKV_SHARD:] = out_ref[...]
    first = Gather(
        place,
        mixed_ref,
        lambda y, c, z, x: mixed_out.at[y, c, z, x],
        send_sems,
        recv_sems,
        local_sem.at[0],
        False,
    )
    ups = Column(place, up_ref, up_out, up_send, up_recv, up_local.at[0])
    small = Copies(small_send, small_recv)
    to_mates = [small.make(own_small, all_small.at[place.index], mate) for mate in place.mates]
    others = [(k, far) for k in range(4) for far in (0, 1) if k or far]

    def to_peers(source, target):
        copies = []
        for k, far in others:
            there = 1 - x if far else x
            copies.append(
                small.make(
                    source(2 * zs[k] + there), target.at[place.peer], place.device(z=zs[k], x=there)
                )
            )
        return copies

    crops = to_peers(lambda peer: own_crops, all_crops)
    ada = to_peers(lambda peer: ada_parts.at[peer], ada_all)
    products = to_peers(lambda peer: product_ref.at[peer], columns_ref)
    finals = [
        small.make(rows_ref.at[other], tables_ref.at[place.index], mate)
        for other, mate in zip(place.mate_index, place.mates)
    ]

    def down_rows(index):
        return down_ref.at[pl.ds(pl.multiple_of(index * SHARD, 16), SHARD)]

    swaps = [
        small.make(down_rows(other), stage_ref.at[place.index], mate)
        for other, mate in zip(place.mate_index, place.mates)
    ]
    own_stage = pltpu.make_async_copy(
        down_rows(place.index), stage_ref.at[place.index], local_small.at[0]
    )

    first.start()
    cond = cond_ref[...].astype(F32)
    own_small[...] = jnp.zeros_like(own_small)
    own_small[:CROPS, :] = (cond / (1.0 + jnp.exp(-cond))).astype(BF16).astype(F32)
    own_small[CROPS : CROPS + 1, :] = vectors_ref[:, :D]
    own_small[CROPS + 1 : CROPS + 2, :] = vectors_ref[:, D : 2 * D]
    for copy in to_mates:
        copy.start()
    own_stage.start()
    all_small[place.index] = own_small[...]
    thin = ada_ref.shape[1] // 8
    ada_parts[...] = jnp.zeros_like(ada_parts)
    for i in range(8):
        ada_parts[i, :, :thin] = ada_ref[:, thin * i : thin * (i + 1)]
    for copy in ada:
        copy.start()
    ada_all[place.peer] = ada_parts[place.peer]
    crop_rows[...] = jnp.zeros_like(crop_rows)
    for copy in to_mates:
        copy.wait_recv()
    for j in range(4):
        crop_rows[CROPS * j : CROPS * (j + 1), :] = all_small[j, :CROPS, :]
    own_crops[...] = crop_rows[...].astype(BF16)
    for copy in crops:
        copy.start()
    all_crops[place.peer] = own_crops[...]
    first.pass_across(0)
    first_end = lengths_ref[0, 0]
    second_end = first_end + lengths_ref[0, 1]
    tokens = lax.broadcasted_iota(jnp.int32, (TOK_DEV, 1), 0)
    column_ref[...] = (tokens >= first_end).astype(jnp.int32) + (tokens >= second_end).astype(jnp.int32)
    tokens = lax.broadcasted_iota(jnp.int32, (1, TOK_DEV), 1)
    row_ref[...] = (tokens >= first_end).astype(jnp.int32) + (tokens >= second_end).astype(jnp.int32)
    spread = jnp.broadcast_to(slot_ref[...].astype(F32), (128, TOK_DEV))
    slot_column_ref[...] = jnp.transpose(spread)[:, :1].astype(jnp.int32)
    token_groups_ref[...] = jnp.zeros_like(token_groups_ref)
    token_groups_ref[:, :GROUPS] = per_crop(groups_ref[...].astype(F32), column_ref[...]).astype(BF16)
    for k in (1, 2, 3):
        first.pass_along(k)
    first.pass_across(1)
    for copy in crops + ada:
        copy.wait_recv()
    every_crop = all_crops[...].reshape(128, D)
    product = dot(every_crop, ada_all[...].reshape(D, ada_all.shape[2]))
    product_ref[...] = product.reshape(product_ref.shape)
    for copy in products:
        copy.start()
    ups.start()
    columns_ref[place.peer] = product_ref[place.peer]
    conds_ref[...] = jnp.zeros_like(conds_ref)
    mine = jnp.zeros((128, SHARD), F32)
    for i in range(8):
        part = every_crop[:, SHARD * i : SHARD * (i + 1)].astype(F32)
        mine = mine + jnp.where(place.peer == i, part, 0.0)
    conds_ref[:, :, :SHARD] = mine.reshape(8, 16, SHARD)
    first.pass_across(2)
    for copy in products:
        copy.wait_recv()
    for i in range(8):
        total_ref[:, thin * i : thin * (i + 1)] = columns_ref[i, :, :thin]
    total = total_ref[...] + vectors_ref[:, 2 * D :]
    rows_ref[...] = jnp.zeros_like(rows_ref)
    for j in range(4):
        rows_ref[j, :CROPS, :] = total[CROPS * j : CROPS * (j + 1)]
    for copy in finals:
        copy.start()
    tables_ref[place.index] = rows_ref[place.index]
    for copy in swaps:
        copy.start()
    first.pass_across(3)
    first.pass_pair(0)
    first.pass_pair(1)
    for copy in finals:
        copy.wait_recv()
    for j in (0, 2):
        mods_ref[3 * j // 2] = tables_ref[j, :, :D]
        mods_ref[3 * j // 2 + 1, :, : D // 2] = tables_ref[j, :, D:]
        mods_ref[3 * j // 2 + 1, :, D // 2 :] = tables_ref[j + 1, :, : D // 2]
        mods_ref[3 * j // 2 + 2] = tables_ref[j + 1, :, D // 2 :]
    for copy in swaps:
        copy.wait_recv()
    own_stage.wait()
    for j in range(4):
        here = slice(OUT_SHARD * j, OUT_SHARD * (j + 1))
        down_out[:, here] = stage_ref[j]
        up_bias_ref[j] = all_small[j, CROPS : CROPS + 1, :]
        row = all_small[j, CROPS + 1 : CROPS + 2, :]
        query_ref[:, here] = row[:, :OUT_SHARD]
        value_ref[:, here] = row[:, OUT_SHARD : 2 * OUT_SHARD]
        out_bias_ref[:, here] = row[:, 2 * OUT_SHARD : 3 * OUT_SHARD]
        down_bias_ref[:, here] = row[:, 3 * OUT_SHARD :]
    qkv_bias_ref[...] = jnp.zeros_like(qkv_bias_ref)
    qkv_bias_ref[0, :, :QKV_SHARD] = query_ref[:, :QKV_SHARD]
    qkv_bias_ref[1, :, :OUT_SHARD] = query_ref[:, QKV_SHARD:]
    qkv_bias_ref[2, :, 2 * OUT_SHARD : QKV_SHARD] = value_ref[:, :OUT_SHARD]
    qkv_bias_ref[3, :, :QKV_SHARD] = value_ref[:, OUT_SHARD:]
    for k in (2, 3):
        first.pass_pair(k)
    first.finish()
    ups.finish()
    for copy in small.made:
        copy.wait_send()


def gather_all(qkv, out, up, down, cond, ada, vectors, slot, groups, lengths):
    vmem = pltpu.VMEM
    wide = ada.shape[1]
    return pl.pallas_call(
        gather_kernel,
        out_shape=[
            shape_of(2, 2, 4, 2, SHARD, D),
            shape_of(4, SHARD, D),
            shape_of(SHARD, D),
            shape_of(6, 8, D, dtype=F32),
            shape_of(8, 16, 256, dtype=F32),
            shape_of(4, 1, PAD_SHARD, dtype=F32),
            shape_of(4, 1, D, dtype=F32),
            shape_of(1, D, dtype=F32),
            shape_of(1, D, dtype=F32),
            shape_of(TOK_DEV, 1, dtype=jnp.int32),
            shape_of(1, TOK_DEV, dtype=jnp.int32),
            shape_of(TOK_DEV, 1, dtype=jnp.int32),
            shape_of(TOK_DEV, 128),
        ],
        in_specs=[IN_VMEM] * 2 + [ANYWHERE] * 2 + [IN_VMEM] * 5 + [IN_SMEM],
        out_specs=[ANYWHERE] * 2 + [IN_VMEM] * 11,
        scratch_shapes=[DMA((GATHER_COPIES,))] * 2
        + [DMA((1,)), DMA((3,)), DMA((3,)), DMA((1,)), DMA((30,)), DMA((30,)), DMA((1,))]
        + [
            vmem((SHARD, D), BF16),
            vmem((4, SHARD, OUT_SHARD), BF16),
            vmem((8, D), F32),
            vmem((4, 8, D), F32),
            vmem((16, D), F32),
            vmem((16, D), BF16),
            vmem((8, 16, D), BF16),
            vmem((8, SHARD, 256), BF16),
            vmem((8, SHARD, 256), BF16),
            vmem((8, 16, 256), F32),
            vmem((8, 16, 256), F32),
            vmem((16, wide), F32),
            vmem((4, 8, wide), F32),
            vmem((4, 8, wide), F32),
            vmem((1, D), F32),
            vmem((1, D), F32),
        ],
        compiler_params=talking(1),
    )(qkv, out, up, down, cond, ada, vectors, slot, groups, lengths)


def close_ada(conds_ref, every, ada_ref, sums_ref):
    rows = jnp.zeros((16, ada_ref.shape[1]), F32)
    for i in range(8):
        rows = rows + every[i].astype(F32)
    cond = conds_ref[...].reshape(128, 256)[:, :SHARD].astype(BF16)
    total = dot(cond, every[...].reshape(128, ada_ref.shape[1]), TN)
    ada_ref[...] = total
    sums_ref[...] = jnp.zeros_like(sums_ref)
    sums_ref[0:1, :] = jnp.sum(rows[:12], axis=0, keepdims=True)
    sums_ref[1:3, :] = rows[12:14]


def block_shards(
    block_in, condition, lengths, head_mask, group_mask, buffer_slot, ada_weight, ada_bias, qkv_weight,
    query_bias, value_bias, out_weight, out_bias, up_weight, up_bias, down_weight, down_bias, cotangent,
):
    x, cot, slot_row, mask = block_in[0], cotangent[0], buffer_slot.astype(jnp.int32), head_mask[0]
    vectors = (up_bias, query_bias, value_bias, out_bias, down_bias, ada_bias)
    total = sum(vector.shape[0] for vector in vectors)
    starts = (0, 1152, 1440, 1728, 2016, 2304)
    padded = [
        jnp.pad(vector.astype(F32), (start, total - start - vector.shape[0]))
        for start, vector in zip(starts, vectors)
    ]
    vectors = sum(padded)[None]
    (
        mixed_weight, up_column, down_rows, mods, conds, qkv_bias, bias_up, bias_out, bias_down,
        column, row, slot_column, groups,
    ) = gather_all(
        qkv_weight, out_weight, up_weight, down_weight, condition[0], ada_weight, vectors, slot_row,
        group_mask[0], lengths,
    )
    mixed_weight = mixed_weight.reshape(4, D, D)
    edges = (0, 288, 576, 864, 2016, 2304)
    first, heads, mixed, lse, attn, after, arrived, picked, full_out, up, down_column = attend(
        x, mixed_weight, mods, qkv_bias, bias_out, column, row, slot_row, groups, mask, up_column,
        down_rows,
    )
    up = up.reshape(4, D, D)
    pull, grad_rows, block_out, gate_two, grad_down_bias, parts_down, down, early_down = feed(
        up, arrived, picked, bias_up, bias_down, cot, after, mods, column,
        slot_column, slot_row, down_column,
    )
    down = down.reshape(4, D, D)
    grad_up_bias, mid, grad_attn, sums, grad_out_bias, parts_up, plane_down = unfeed(
        down, up, pull, grad_rows, arrived, after, cot, attn, mods, column, slot_column, parts_down, early_down
    )
    triple, triple_sums, share_down, plane_up, grad_split = unattend(
        grad_attn, full_out, heads, lse, column, row, parts_up.reshape(2, 4, 2, SHARD, D), plane_down,
        mask,
    )
    triple_sums = triple_sums[:, 0, :QKV_SHARD].reshape(3 * D)
    blank = jnp.zeros((8, 2 * D), F32)
    mod_grads = jnp.concatenate([blank, sums[0], sums[1], sums[2], gate_two], axis=1)[:CROPS]
    mod_grads = mod_grads.reshape(CROPS, 4, -1).transpose(1, 0, 2)
    bias_grads = (
        triple_sums[:D], triple_sums[2 * D :], grad_out_bias, grad_up_bias, grad_down_bias,
    )
    bias_grads = jnp.concatenate([vector.reshape(4, -1) for vector in bias_grads], axis=1)
    wide = mod_grads.shape[2]
    bias_grads = jnp.pad(bias_grads, ((0, 0), (0, 5 * wide - 2304))).reshape(4, 5, wide)
    rest = jnp.concatenate([mod_grads, bias_grads], axis=1)
    grad_in, share_up, share_qkv, share_out, grad_ada, totals, share_down = unproject(
        mixed_weight, triple, grad_split, first, mixed, x, mid, mods, column, plane_up, rest, conds,
        share_down,
    )
    share_down = share_down.reshape(4 * SHARD, OUT_SHARD)
    bias_totals = totals[1:3].reshape(-1)
    grad_query, grad_value, grad_out, grad_ups, grad_downs = [
        bias_totals[low:high] for low, high in zip(edges[:-1], edges[1:])
    ]
    return (
        block_out[None],
        grad_in[None],
        grad_ada,
        totals[0],
        share_qkv,
        grad_query,
        grad_value,
        share_out,
        grad_out,
        share_up,
        grad_ups,
        share_down,
        grad_downs,
    )


def layer_norm(values):
    center = values - jnp.mean(values, axis=-1, keepdims=True)
    variance = jnp.mean(center * center, axis=-1, keepdims=True)
    inverse = lax.rsqrt(variance + epsilon)
    return (center * inverse, inverse)


def norm_back(grad_normed, normed, inverse):
    first_mean = jnp.mean(grad_normed, axis=-1, keepdims=True)
    second_mean = jnp.mean(grad_normed * normed, axis=-1, keepdims=True)
    return inverse * (grad_normed - first_mean - normed * second_mean)


def attention_scores(query_part, key_part, allowed, factor):
    raw_scores = (
        jnp.einsum("qhd,khd->hqk", query_part, key_part, preferred_element_type=jnp.float32)
        * factor
    )
    return jnp.where(allowed[None], raw_scores, -1e30)


def gelu_tanh(values):
    return jax.nn.gelu(values, approximate=True)


def shards(
    block_in,
    condition,
    lengths,
    head_mask,
    group_mask,
    buffer_slot,
    ada_weight,
    ada_bias,
    qkv_weight,
    query_bias,
    value_bias,
    out_weight,
    out_bias,
    up_weight,
    up_bias,
    down_weight,
    down_bias,
    cotangent,
):
    peers = lax.axis_size("dp")
    mates = lax.axis_size("fsdp")

    def gather_matrix(shard):
        stacked = lax.all_gather(shard, ("dp", "fsdp"), axis=0, tiled=False)
        rows, columns = shard.shape
        stacked = stacked.reshape(peers, mates, rows, columns).transpose(0, 2, 1, 3)
        return stacked.reshape(peers * rows, mates * columns)

    full_qkv, full_out, full_up, full_down = [
        gather_matrix(shard) for shard in (qkv_weight, out_weight, up_weight, down_weight)
    ]
    vectors = (query_bias, value_bias, out_bias, up_bias, down_bias)
    packed_bias = lax.all_gather(jnp.concatenate(vectors), "fsdp", axis=0, tiled=False)
    edges = [0]
    for vector in vectors:
        edges.append(edges[-1] + vector.shape[0])
    bias_query, bias_value, bias_out, bias_up, bias_down = [
        packed_bias[:, low:high].reshape(-1).astype(jnp.float32)
        for low, high in zip(edges[:-1], edges[1:])
    ]
    inputs = block_in[0].astype(jnp.float32)
    crop_length = lengths[0]
    finish = jnp.cumsum(crop_length)
    opening = finish - crop_length
    position = jnp.arange(TOK_DEV, dtype=jnp.int32)
    member = (
        (position[:, None] >= opening[None, :]) & (position[:, None] < finish[None, :])
    ).astype(jnp.float32)
    segment = jnp.sum((position[:, None] >= finish[None, :]).astype(jnp.int32), axis=1)
    cond_act = jax.nn.silu(condition[0].astype(jnp.float32)).astype(jnp.bfloat16)
    crops = cond_act.shape[0]
    cond_all = lax.all_gather(cond_act, ("dp", "fsdp"), axis=0, tiled=True)
    depth = ada_weight.shape[0]
    cond_slice = lax.dynamic_slice_in_dim(cond_all, lax.axis_index("dp") * depth, depth, axis=1)
    partial_mod = jnp.dot(cond_slice, ada_weight, preferred_element_type=jnp.float32)
    column_mod = lax.psum_scatter(partial_mod, "dp", scatter_dimension=0, tiled=True)
    column_mod = column_mod + ada_bias.astype(jnp.float32)
    modulation = lax.all_to_all(column_mod, "fsdp", split_axis=0, concat_axis=1, tiled=True)
    pieces = [
        jnp.dot(member, modulation[:, number * D : (number + 1) * D], precision=highest)
        for number in range(6)
    ]
    shift_one, scale_one, gate_one, shift_two, scale_two, gate_two = pieces
    head_keep = jnp.dot(member, head_mask[0].astype(jnp.float32), precision=highest)
    group_keep = jnp.dot(member, group_mask[0].astype(jnp.float32), precision=highest)
    normed_one, inverse_one = layer_norm(inputs)
    first_in = (normed_one * (1.0 + scale_one) + shift_one).astype(jnp.bfloat16)
    qkv_bias = jnp.concatenate([bias_query, jnp.zeros_like(bias_query), bias_value])
    triple = (jnp.dot(first_in, full_qkv, preferred_element_type=jnp.float32) + qkv_bias).astype(
        jnp.bfloat16
    )
    queries = triple[:, :D].reshape(TOK_DEV, HEADS, HEAD_DIM)
    keys_all = triple[:, D : 2 * D].reshape(TOK_DEV, HEADS, HEAD_DIM)
    values_all = triple[:, 2 * D :].reshape(TOK_DEV, HEADS, HEAD_DIM)
    factor = HEAD_DIM ** (-0.5)
    row_block = min(768, TOK_DEV)
    group_size = min(4, HEADS)
    log_totals = {}
    head_parts = []
    for head_start in range(0, HEADS, group_size):
        heads_here = slice(head_start, head_start + group_size)
        row_start = 0
        rows_here = slice(row_start, row_start + row_block)
        allowed = segment[:, None] == segment[None, :]
        scores = attention_scores(
            queries[rows_here, heads_here], keys_all[:, heads_here], allowed, factor
        )
        row_max = jnp.max(scores, axis=-1, keepdims=True)
        log_total = row_max + jnp.log(jnp.sum(jnp.exp(scores - row_max), axis=-1, keepdims=True))
        weights_low = jnp.exp(scores - log_total).astype(jnp.bfloat16)
        row_parts = jnp.einsum(
            "hqk,khd->qhd",
            weights_low,
            values_all[:, heads_here],
            preferred_element_type=jnp.float32,
        )
        log_totals[head_start, row_start] = log_total
        head_parts.append(row_parts)
    attended = jnp.concatenate(head_parts, axis=1)
    mixed = (attended * head_keep[:, :, None]).astype(jnp.bfloat16).reshape(TOK_DEV, D)
    attn_out = jnp.dot(mixed, full_out, preferred_element_type=jnp.float32) + bias_out
    after_attn = inputs + gate_one * attn_out
    normed_two, inverse_two = layer_norm(after_attn)
    second_in = (normed_two * (1.0 + scale_two) + shift_two).astype(jnp.bfloat16)
    keep = (buffer_slot[0] >= 0).astype(jnp.float32)[:, None]
    places = 2 * TOK_DEV // 3
    chooser = (buffer_slot[0][:, None] == jnp.arange(places, dtype=jnp.int32)[None, :]).astype(
        jnp.bfloat16
    )
    arrived = jnp.einsum(
        "tb,td->bd", chooser, second_in, preferred_element_type=jnp.float32
    ).astype(jnp.bfloat16)
    groups_float = jnp.einsum(
        "tb,tg->bg",
        chooser,
        group_keep.astype(jnp.bfloat16),
        preferred_element_type=jnp.float32,
    )
    channel_keep = jnp.repeat(groups_float, FF // GROUPS, axis=1)
    hidden = jnp.dot(arrived, full_up, preferred_element_type=jnp.float32) + bias_up
    active = (gelu_tanh(hidden) * channel_keep).astype(jnp.bfloat16)
    branch = (jnp.dot(active, full_down, preferred_element_type=jnp.float32) + bias_down).astype(
        jnp.bfloat16
    )
    branch_tok = jnp.einsum(
        "tb,bd->td", chooser, branch, preferred_element_type=jnp.float32
    )
    after_mlp = after_attn + gate_two * branch_tok
    block_out = after_mlp.astype(jnp.bfloat16)[None]
    grad_after = cotangent[0].astype(jnp.float32)
    grad_gate_two = grad_after * branch_tok
    grad_branch = (gate_two * keep * grad_after).astype(jnp.bfloat16)
    grad_rows = jnp.einsum(
        "tb,td->bd", chooser, grad_branch, preferred_element_type=jnp.float32
    ).astype(jnp.bfloat16)
    back_qkv, back_out, back_up, back_down = full_qkv, full_out, full_up, full_down
    grad_down_bias = jnp.sum(grad_rows.astype(jnp.float32), axis=0)
    grad_down = jnp.einsum("bf,bd->fd", active, grad_rows, preferred_element_type=jnp.float32)
    grad_active = jnp.einsum("bd,fd->bf", grad_rows, back_down, preferred_element_type=jnp.float32)
    gelu_pull = jax.vjp(gelu_tanh, hidden)[1]
    grad_hidden = gelu_pull(grad_active * channel_keep)[0].astype(jnp.bfloat16)
    grad_up_bias = jnp.sum(grad_hidden.astype(jnp.float32), axis=0)
    grad_up = jnp.einsum("bd,bf->df", arrived, grad_hidden, preferred_element_type=jnp.float32)
    grad_arrived = jnp.einsum(
        "bf,df->bd", grad_hidden, back_up, preferred_element_type=jnp.float32
    ).astype(jnp.bfloat16)
    grad_second = jnp.einsum(
        "tb,bd->td", chooser, grad_arrived, preferred_element_type=jnp.float32
    )
    grad_scale_two = grad_second * normed_two
    grad_mid = grad_after + norm_back(grad_second * (1.0 + scale_two), normed_two, inverse_two)
    grad_gate_one = grad_mid * attn_out
    grad_attn = (gate_one * grad_mid).astype(jnp.bfloat16)
    grad_out_bias = jnp.sum(grad_attn.astype(jnp.float32), axis=0)
    grad_out = jnp.einsum("te,tf->ef", mixed, grad_attn, preferred_element_type=jnp.float32)
    grad_mixed = jnp.einsum(
        "tf,ef->te", grad_attn, back_out, preferred_element_type=jnp.float32
    ).astype(jnp.bfloat16)
    grad_attended = (
        grad_mixed.reshape(TOK_DEV, HEADS, HEAD_DIM).astype(jnp.float32) * head_keep[:, :, None]
    ).astype(jnp.bfloat16)
    query_heads = []
    key_heads = []
    value_heads = []
    for head_start in range(0, HEADS, group_size):
        heads_here = slice(head_start, head_start + group_size)
        row_start = 0
        rows_here = slice(row_start, row_start + row_block)
        allowed = segment[:, None] == segment[None, :]
        scores = attention_scores(
            queries[rows_here, heads_here], keys_all[:, heads_here], allowed, factor
        )
        probs = jnp.exp(scores - log_totals[head_start, row_start])
        grad_piece = grad_attended[rows_here, heads_here]
        grad_values = jnp.einsum(
            "hqk,qhd->khd",
            probs.astype(jnp.bfloat16),
            grad_piece,
            preferred_element_type=jnp.float32,
        )
        grad_probs = jnp.einsum(
            "qhd,khd->hqk",
            grad_piece,
            values_all[:, heads_here],
            preferred_element_type=jnp.float32,
        )
        grad_scores = (
            probs * (grad_probs - jnp.sum(probs * grad_probs, axis=-1, keepdims=True))
        ).astype(jnp.bfloat16)
        query_rows = (
            jnp.einsum(
                "hqk,khd->qhd",
                grad_scores,
                keys_all[:, heads_here],
                preferred_element_type=jnp.float32,
            )
            * factor
        )
        grad_keys = (
            jnp.einsum(
                "hqk,qhd->khd",
                grad_scores,
                queries[rows_here, heads_here],
                preferred_element_type=jnp.float32,
            )
            * factor
        )
        query_heads.append(query_rows)
        key_heads.append(grad_keys)
        value_heads.append(grad_values)
    grad_triple = jnp.concatenate(
        [
            jnp.concatenate(query_heads, axis=1).reshape(TOK_DEV, D),
            jnp.concatenate(key_heads, axis=1).reshape(TOK_DEV, D),
            jnp.concatenate(value_heads, axis=1).reshape(TOK_DEV, D),
        ],
        axis=1,
    ).astype(jnp.bfloat16)
    grad_query_bias = jnp.sum(grad_triple[:, :D].astype(jnp.float32), axis=0)
    grad_value_bias = jnp.sum(grad_triple[:, 2 * D :].astype(jnp.float32), axis=0)
    grad_qkv = jnp.einsum("td,te->de", first_in, grad_triple, preferred_element_type=jnp.float32)
    grad_first = jnp.einsum("te,de->td", grad_triple, back_qkv, preferred_element_type=jnp.float32)
    grad_scale_one = grad_first * normed_one
    grad_inputs = grad_mid + norm_back(grad_first * (1.0 + scale_one), normed_one, inverse_one)
    token_grads = [
        grad_first,
        grad_scale_one,
        grad_gate_one,
        grad_second,
        grad_scale_two,
        grad_gate_two,
    ]
    grad_modulation = jnp.concatenate(
        [jnp.einsum("ts,td->sd", member, single, precision=highest) for single in token_grads],
        axis=1,
    )
    mod_columns = lax.all_to_all(
        grad_modulation, "fsdp", split_axis=1, concat_axis=0, tiled=True
    )
    mod_all = lax.all_gather(mod_columns, "dp", axis=0, tiled=True)
    grad_ada_bias = jnp.sum(mod_all, axis=0)
    grad_ada = jnp.einsum(
        "sd,se->de", cond_slice.astype(jnp.float32), mod_all, precision=highest
    )

    def scatter_matrix(full):
        rows, columns = full.shape[0] // peers, full.shape[1] // mates
        blocks = full.astype(jnp.bfloat16).reshape(peers, rows, mates, columns)
        blocks = blocks.transpose(0, 2, 1, 3).reshape(peers * mates * rows, columns)
        share = lax.psum_scatter(blocks, ("dp", "fsdp"), scatter_dimension=0, tiled=True)
        return share.astype(jnp.float32)

    shares = [scatter_matrix(full) for full in (grad_qkv, grad_out, grad_up, grad_down)]
    bias_grads = (grad_query_bias, grad_value_bias, grad_out_bias, grad_up_bias, grad_down_bias)
    packed = jnp.concatenate([vector.reshape(mates, -1) for vector in bias_grads], axis=1)
    packed = lax.psum_scatter(packed, "fsdp", scatter_dimension=0, tiled=True)
    packed = lax.psum(packed[0], "dp")
    totals = [packed[low:high] for low, high in zip(edges[:-1], edges[1:])]
    return (
        block_out,
        grad_inputs[None],
        grad_ada,
        grad_ada_bias,
        shares[0],
        totals[0],
        totals[1],
        shares[1],
        totals[2],
        shares[2],
        totals[3],
        shares[3],
        totals[4],
    )


def solution(mesh):
    placed = (
        P(("dp", "fsdp"), None, None),
        P(("dp", "fsdp"), None, None),
        P(("dp", "fsdp"), None),
        P(("dp", "fsdp"), None, None),
        P(("dp", "fsdp"), None, None),
        P(("dp", "fsdp"), None),
        P("dp", "fsdp"),
        P("fsdp"),
        P("dp", "fsdp"),
        P("fsdp"),
        P("fsdp"),
        P("dp", "fsdp"),
        P("fsdp"),
        P("dp", "fsdp"),
        P("fsdp"),
        P("dp", "fsdp"),
        P("fsdp"),
        P(("dp", "fsdp"), None, None),
    )
    on_block = dict(mesh.shape) == {"dp": 8, "fsdp": 4}
    return jax.shard_map(
        block_shards if on_block else shards,
        mesh=mesh,
        in_specs=placed,
        out_specs=(
            P(("dp", "fsdp"), None, None),
            P(("dp", "fsdp"), None, None),
            P("dp", "fsdp"),
            P("fsdp"),
            P("dp", "fsdp"),
            P("fsdp"),
            P("fsdp"),
            P("dp", "fsdp"),
            P("fsdp"),
            P("dp", "fsdp"),
            P("fsdp"),
            P("dp", "fsdp"),
            P("fsdp"),
        ),
        check_vma=False,
    )
```
